32 devices in a mesh: dp: 2 (over y), mp: 16 (over z, x, core).
Axes of the slice: x: 2, y: 2, z: 4, core: 2. Of those that a mesh axis runs over, the one named last changes fastest.
Arguments:
- query: bfloat16 [512, 1024], P('dp', 'mp'), may hold values from -0.75 to 0.75
- kv_cache: bfloat16 [1024, 2048], P('dp', 'mp'), may hold values from -4 to 4, as said below
- out_grad: bfloat16 [512, 1024], P('dp', 'mp'), may hold values from -384 to 384
- source_lengths: int32 [2, 8], P('dp'), may hold values from 1 to 128, 512 in all within a row
- target_lengths: int32 [2, 8], P('dp'), may hold values from 1 to 64, 256 in all within a row
- low_rank: bfloat16 [1024, 32], P(('dp', 'mp')), may hold values from -0.125 to 0.125
- adapter_up_matrix: bfloat16 [32, 1024], replicated, may hold values from -0.1875 to 0.1875
Outputs:
- query_grad: bfloat16 [512, 1024], P('dp', 'mp')
- key_gradient: bfloat16 [1024, 1024], P(('dp', 'mp'))
- value_grad: bfloat16 [1024, 1024], P(('dp', 'mp'))
- low_rank_gradient: float32 [1024, 32], P(('dp', 'mp'))
- adapter_up_gradient: float32 [1024, 32], P(('dp', 'mp'))
The draws below stay inside these ranges and needn't reach their ends.
Inputs may be any that keep to these rules, and one draw needn't show every extreme that they name: `source_lengths`: each row sums to 512; its largest entry is exactly 128. `target_lengths`: each row sums to 256; its largest entry is exactly 64. `kv_cache`: the key columns lie within -0.75 to 0.75.
All inputs are finite; a program needn't handle non-finite values.
Results may differ from the reference program's by a relative error of at most 0.0053.
Values may be sent and summed in bfloat16 or wider, within the bound.
No kernel may reach another device: no remote copies, remote signals or barrier semaphores. Data moves between devices by JAX's collectives and lax.ppermute only.
A program may use at most 64 MiB of HBM per device.

```python
import math
import jax
import jax.numpy as jnp
import numpy as np
from jax import lax

HS = 64
HEADS = 16
D = 1024
ADAPTER_RANK = 16
NDOC = 8
TQ = 256
PACKS = 2
S = 512


def scaled_heads(key, rows):
    first, second = jax.random.split(key)
    scales = jnp.exp(jax.random.uniform(first, (rows, HEADS, 1), jnp.float32, math.log(0.25), 0.0))
    base = jnp.clip(0.5 * jax.random.normal(second, (rows, HEADS, HS), jnp.float32), -0.75, 0.75)
    return base * scales


def draw_query(key, part):
    rows = PACKS * TQ
    return scaled_heads(jax.random.fold_in(key, 11), rows).reshape(rows, HEADS * HS).astype(jnp.bfloat16)


def draw_kv_cache(key, part):
    rows = PACKS * S
    keys_part = scaled_heads(jax.random.fold_in(key, 23), rows)
    values_part = jnp.clip(jax.random.normal(jax.random.fold_in(key, 37), (rows, HEADS, HS), jnp.float32), -4.0, 4.0)
    both = jnp.stack([keys_part, values_part], axis=2)
    return both.reshape(rows, 2 * HEADS * HS).astype(jnp.bfloat16)


def level_of(key, dims, pieces, smallest, largest):
    level = 1.0
    for dim, blocks in pieces:
        heights = jax.random.uniform(jax.random.fold_in(jax.random.fold_in(key, 6), dim), (blocks,), jnp.float32, smallest / len(pieces), largest / len(pieces))
        level = level * jnp.repeat(jnp.exp(heights), dims[dim] // blocks).reshape((-1,) + (1,) * (len(dims) - 1 - dim))
    return level


def profile(amount, total, most, skew):
    portions = [(1 << 20) // math.isqrt(rank ** skew) + 1 for rank in range(2, amount + 1)]
    surplus, holding = total - most - (amount - 1), [1] * (amount - 1)
    while surplus > 0:
        free = [i for i in range(amount - 1) if holding[i] < most]
        whole, remaining = sum([portions[i] for i in free]), surplus
        for i in free:
            more = min(most - holding[i], max(1, remaining * portions[i] // whole), surplus)
            holding[i] = holding[i] + more
            surplus = surplus - more
    return np.array([most] + holding)


def uneven_parts(own_key, number_of, total, reach, skew):
    if number_of == 2:
        one = jax.random.randint(own_key, (), max(1, total - reach), min(reach, total - 1) + 1)
        return jnp.stack([one, total - one])
    tallies = jnp.asarray(profile(number_of, total, reach, skew), jnp.int32)
    couples = (number_of - 1) // 2
    giver, taker = tallies[1:1 + 2 * couples:2], tallies[2:2 + 2 * couples:2]
    margin = jnp.minimum(giver - 1, reach - taker)
    passed = jax.random.randint(jax.random.fold_in(own_key, 1), (couples,), 0, 1 << 20) % (margin + 1)
    tallies = tallies.at[1:1 + 2 * couples:2].set(giver - passed).at[2:2 + 2 * couples:2].set(taker + passed)
    return tallies[jax.random.permutation(jax.random.fold_in(own_key, 2), number_of)]


def gaussian(rng, extent, deviation, limit, cuts=(), kind=jnp.bfloat16):
    level = level_of(rng, extent, cuts, -0.22, 0.18) if cuts else 1.0
    drawn = jax.random.normal(rng, extent, jnp.float32) * deviation * level
    return jnp.minimum(jnp.maximum(drawn, -limit), limit).astype(kind)


def setup_inputs(seed: int = 0) -> dict:
    seeds = jax.random.split(jax.random.key(seed), 8)
    query = draw_query(jax.random.fold_in(seeds[7], 71), 0)
    kv_cache = draw_kv_cache(jax.random.fold_in(seeds[7], 71), 0)
    out_grad = gaussian(seeds[2], (PACKS * TQ, D), 64.0, 384.0, ((0, 2), (1, 16)))
    source_lengths = jax.vmap(lambda own: uneven_parts(own, NDOC, S, S // 4, 2))(jax.random.split(seeds[3], PACKS)).reshape((PACKS, NDOC)).astype(jnp.int32)
    target_lengths = jax.vmap(lambda own: uneven_parts(own, NDOC, TQ, TQ // 4, 2))(jax.random.split(seeds[4], PACKS)).reshape((PACKS, NDOC)).astype(jnp.int32)
    low_rank = gaussian(seeds[5], (PACKS * S, 2 * ADAPTER_RANK), 0.02, 0.125, ((0, 32),))
    adapter_up_matrix = gaussian(seeds[6], (2 * ADAPTER_RANK, D), D ** -0.5, 0.1875)
    return dict(query=query, kv_cache=kv_cache, out_grad=out_grad, source_lengths=source_lengths, target_lengths=target_lengths, low_rank=low_rank, adapter_up_matrix=adapter_up_matrix)


adapter_factor = 2.0


def doc_index(lengths, count):
    ends = jnp.cumsum(lengths.astype(jnp.int32)).astype(jnp.int32)
    position = jnp.arange(count, dtype=jnp.int32)
    return jnp.sum((position[:, None] >= ends[None, :]).astype(jnp.int32), axis=1)


def reference(query, kv_cache, out_grad, source_lengths, target_lengths, low_rank, adapter_up_matrix):
    query_parts = []
    key_parts = []
    value_parts = []
    for pack in range(PACKS):
        query_pack = query[pack * TQ:(pack + 1) * TQ].reshape(TQ, HEADS, HS).transpose(1, 0, 2)
        grad_pack = out_grad[pack * TQ:(pack + 1) * TQ].reshape(TQ, HEADS, HS).transpose(1, 0, 2)
        both_pack = kv_cache[pack * S:(pack + 1) * S].reshape(S, HEADS, 2, HS)
        key_pack = both_pack[:, :, 0, :].transpose(1, 0, 2)
        value_pack = both_pack[:, :, 1, :].transpose(1, 0, 2)
        allowed = doc_index(target_lengths[pack], TQ)[:, None] == doc_index(source_lengths[pack], S)[None, :]

        def one_head(operands):
            query_head, key_head, value_head, grad_head = operands
            scores = jnp.dot(query_head, key_head.T, preferred_element_type=jnp.float32)
            expo = jnp.where(allowed, jnp.exp(scores), jnp.zeros_like(scores))
            total = jnp.sum(expo, axis=1)
            dprob = jnp.dot(grad_head, value_head.T, preferred_element_type=jnp.float32)
            delta = jnp.sum(expo * dprob, axis=1) / total
            prob = expo / total[:, None]
            prob_low = prob.astype(jnp.bfloat16)
            dscore = (prob * (dprob - delta[:, None])).astype(jnp.bfloat16)
            head_query = jnp.dot(dscore, key_head, preferred_element_type=jnp.float32).astype(jnp.bfloat16)
            head_key = jnp.dot(dscore.T, query_head, preferred_element_type=jnp.float32).astype(jnp.bfloat16)
            head_value = jnp.dot(prob_low.T, grad_head, preferred_element_type=jnp.float32).astype(jnp.bfloat16)
            return head_query, head_key, head_value

        heads_query, heads_key, heads_value = lax.map(one_head, (query_pack, key_pack, value_pack, grad_pack))
        query_parts.append(heads_query.transpose(1, 0, 2).reshape(TQ, HEADS * HS))
        key_parts.append(heads_key.transpose(1, 0, 2).reshape(S, HEADS * HS))
        value_parts.append(heads_value.transpose(1, 0, 2).reshape(S, HEADS * HS))
    query_grad = jnp.concatenate(query_parts, axis=0)
    key_gradient = jnp.concatenate(key_parts, axis=0)
    value_grad = jnp.concatenate(value_parts, axis=0)
    low_rank_gradient = adapter_factor * jnp.concatenate(
        [jnp.dot(key_gradient, adapter_up_matrix[:ADAPTER_RANK].T, preferred_element_type=jnp.float32),
         jnp.dot(value_grad, adapter_up_matrix[ADAPTER_RANK:].T, preferred_element_type=jnp.float32)], axis=1)
    adapter_up_gradient = adapter_factor * jnp.concatenate(
        [jnp.dot(key_gradient.T, low_rank[:, :ADAPTER_RANK], preferred_element_type=jnp.float32),
         jnp.dot(value_grad.T, low_rank[:, ADAPTER_RANK:], preferred_element_type=jnp.float32)], axis=1)
    return query_grad, key_gradient, value_grad, low_rank_gradient, adapter_up_gradient
```

```python
import functools

import jax
import jax.numpy as jnp
from jax import lax
from jax.experimental import pallas as pl
from jax.experimental.pallas import tpu as pltpu
from jax.sharding import PartitionSpec as P

HS = 64

adapter_factor = 2.0


def doc_of(lengths_ref, shape, dim):
    position = lax.broadcasted_iota(jnp.int32, shape, dim)
    doc = jnp.zeros(shape, jnp.int32)
    end = jnp.int32(0)
    for i in range(lengths_ref.shape[1]):
        end = end + lengths_ref[0, i]
        doc = doc + (position >= end).astype(jnp.int32)
    return doc


def attention_kernel(
    source_ref, target_ref, query_ref, grad_ref, kv_ref, query_grad_ref, both_grad_ref
):
    tgt_count = query_ref.shape[1]
    src_count = kv_ref.shape[0]
    both = kv_ref[...]
    query_t = query_ref[...]
    grad_t = grad_ref[...]
    blank = jnp.zeros_like(query_t)
    query_wide = jnp.concatenate([query_t, blank], axis=0)
    grad_wide = jnp.concatenate([blank, grad_t], axis=0)
    scores = jnp.dot(both, query_wide, preferred_element_type=jnp.float32)
    dprob = jnp.dot(both, grad_wide, preferred_element_type=jnp.float32)
    tgt_doc = doc_of(target_ref, (1, tgt_count), 1)
    src_doc = doc_of(source_ref, (src_count, 1), 0)
    expo = jnp.where(src_doc == tgt_doc, jnp.exp(scores), 0.0)
    total = jnp.sum(expo, axis=0, keepdims=True)
    delta = jnp.sum(expo * dprob, axis=0, keepdims=True) / total
    prob = expo / total
    prob_low = prob.astype(jnp.bfloat16)
    dscore = (prob * (dprob - delta)).astype(jnp.bfloat16)
    nt = (((1,), (1,)), ((), ()))
    both_grad = lax.dot_general(dscore, query_wide, nt, preferred_element_type=jnp.float32)
    both_grad += lax.dot_general(prob_low, grad_wide, nt, preferred_element_type=jnp.float32)
    both_grad_ref[...] = both_grad.astype(jnp.bfloat16)
    tn = (((0,), (0,)), ((), ()))
    query_grad = lax.dot_general(both, dscore, tn, preferred_element_type=jnp.float32)
    query_grad_ref[...] = query_grad[:HS].astype(jnp.bfloat16)


def adapter_kernel(parts, both_grad_ref, *refs):
    low_refs = refs[:parts]
    out_refs = refs[parts:-1]
    low = refs[-1]
    me = lax.axis_index("mp")
    rows = low_refs[0].shape[0]
    for shift in range(parts):
        owner = lax.rem(me + parts - shift, parts)
        low[pl.ds(pl.multiple_of(owner * rows, rows), rows), :] = low_refs[shift][...]
    tn = (((0,), (0,)), ((), ()))
    share = adapter_factor * lax.dot_general(
        both_grad_ref[...], low[...], tn, preferred_element_type=jnp.float32
    )
    column = lax.broadcasted_iota(jnp.int32, (HS, share.shape[1]), 1)
    share = jnp.where(column < share.shape[1] // 2, share[:HS], share[HS:])
    step = HS // len(out_refs)
    for j, out_ref in enumerate(out_refs):
        out_ref[...] = share[j * step:(j + 1) * step]


def owner_kernel(heads, got_ref, up_ref, *refs):
    share_refs = refs[:-4]
    key_ref, value_ref, low_grad_ref, up_grad_ref = refs[-4:]
    rows = key_ref.shape[0]
    rank = up_ref.shape[0] // 2
    for pair in range(heads // 2):
        first = got_ref[2 * pair * rows:(2 * pair + 1) * rows, :]
        second = got_ref[(2 * pair + 1) * rows:(2 * pair + 2) * rows, :]
        columns = slice(2 * pair * HS, (2 * pair + 2) * HS)
        key_ref[:, columns] = jnp.concatenate([first[:, :HS], second[:, :HS]], axis=1)
        value_ref[:, columns] = jnp.concatenate([first[:, HS:], second[:, HS:]], axis=1)
    nt = (((1,), (1,)), ((), ()))
    up = up_ref[...]
    from_key = lax.dot_general(key_ref[...], up, nt, preferred_element_type=jnp.float32)
    from_value = lax.dot_general(value_ref[...], up, nt, preferred_element_type=jnp.float32)
    column = lax.broadcasted_iota(jnp.int32, from_key.shape, 1)
    low_grad_ref[...] = adapter_factor * jnp.where(column < rank, from_key, from_value)
    total = share_refs[0][...]
    for share_ref in share_refs[1:]:
        total = total + share_ref[...]
    up_grad_ref[...] = total


def local(dp, mp, query, kv_cache, out_grad, source_lengths, target_lengths, low_rank, adapter_up_matrix):
    tgt_count = query.shape[0]
    src_count = kv_cache.shape[0]
    rows = low_rank.shape[0]
    both_rank = low_rank.shape[1]
    width = adapter_up_matrix.shape[1]
    vmem = pl.BlockSpec(memory_space=pltpu.VMEM)
    smem = pl.BlockSpec(memory_space=pltpu.SMEM)
    params = pltpu.CompilerParams(vmem_limit_bytes=48 * 1024 * 1024)

    lows = [low_rank]
    for shift in range(1, mp):
        lows.append(lax.ppermute(low_rank, "mp", [(m, (m + shift) % mp) for m in range(mp)]))

    query_grad_t, both_grad = pl.pallas_call(
        attention_kernel,
        out_shape=[
            jax.ShapeDtypeStruct((HS, tgt_count), jnp.bfloat16),
            jax.ShapeDtypeStruct((src_count, 2 * HS), jnp.bfloat16),
        ],
        in_specs=[smem, smem, vmem, vmem, vmem],
        out_specs=[vmem, vmem],
        compiler_params=params,
        name="attention_backward",
    )(source_lengths, target_lengths, query.T, out_grad.T, kv_cache)

    got = lax.all_to_all(both_grad, "mp", split_axis=0, concat_axis=0, tiled=True)

    share_rows = HS // dp
    shares = pl.pallas_call(
        functools.partial(adapter_kernel, mp),
        out_shape=[jax.ShapeDtypeStruct((share_rows, both_rank), jnp.float32)] * dp,
        in_specs=[vmem] * (1 + mp),
        out_specs=[vmem] * dp,
        scratch_shapes=[pltpu.VMEM((mp * rows, both_rank), jnp.bfloat16)],
        compiler_params=params,
        name="adapter_shares",
    )(both_grad, *lows)

    mine = lax.axis_index("dp")
    arrived = []
    for step in range(dp):
        turn = (mine + step) % dp
        sent = shares[0]
        for j in range(1, dp):
            sent = jnp.where(turn == j, shares[j], sent)
        route = [(d * mp + h, h * dp + (d + step) % dp) for d in range(dp) for h in range(mp)]
        arrived.append(lax.ppermute(sent, ("dp", "mp"), route))

    key_gradient, value_grad, low_grad, up_grad = pl.pallas_call(
        functools.partial(owner_kernel, mp),
        out_shape=[
            jax.ShapeDtypeStruct((rows, width), jnp.bfloat16),
            jax.ShapeDtypeStruct((rows, width), jnp.bfloat16),
            jax.ShapeDtypeStruct((rows, both_rank), jnp.float32),
            jax.ShapeDtypeStruct((share_rows, both_rank), jnp.float32),
        ],
        in_specs=[vmem] * (2 + dp),
        out_specs=[vmem] * 4,
        compiler_params=params,
        name="owner_outputs",
    )(got, adapter_up_matrix, *arrived)
    return query_grad_t.T, key_gradient, value_grad, low_grad, up_grad


def solution(mesh):
    in_specs = (
        P("dp", "mp"),
        P("dp", "mp"),
        P("dp", "mp"),
        P("dp", None),
        P("dp", None),
        P(("dp", "mp"), None),
        P(),
    )
    out_specs = (
        P("dp", "mp"),
        P(("dp", "mp"), None),
        P(("dp", "mp"), None),
        P(("dp", "mp"), None),
        P(("dp", "mp"), None),
    )
    body = functools.partial(local, mesh.shape["dp"], mesh.shape["mp"])
    return jax.shard_map(body, mesh=mesh, in_specs=in_specs, out_specs=out_specs, check_vma=False)
```

```python
import functools

import jax
import jax.numpy as jnp
from jax import lax
from jax.experimental import pallas as pl
from jax.experimental.pallas import tpu as pltpu
from jax.sharding import PartitionSpec as P

HS = 64
LANES = 128
CUT = 16

adapter_factor = 2.0

NT = (((1,), (1,)), ((), ()))
TN = (((0,), (0,)), ((), ()))


def dot(left, right, dims):
    return lax.dot_general(left, right, dims, preferred_element_type=jnp.float32)


def source_range(source_ref, target_ref, count):
    position = lax.broadcasted_iota(jnp.int32, (1, count), 1)
    first = jnp.zeros((1, count), jnp.int32)
    last = jnp.zeros((1, count), jnp.int32)
    target_start = jnp.int32(0)
    source_start = jnp.int32(0)
    for i in range(source_ref.shape[1]):
        source_end = source_start + source_ref[0, i]
        inside = position >= target_start
        first = jnp.where(inside, source_start, first)
        last = jnp.where(inside, source_end, last)
        target_start = target_start + target_ref[0, i]
        source_start = source_end
    return first, last


def attention_kernel(dp, mp, source_any, target_any, query_ref, grad_ref, kv_ref, *refs):
    low_refs = refs[:dp]
    query_grad_ref, both_grad_ref = refs[dp:dp + 2]
    piece_refs = refs[dp + 2:dp + 2 + dp]
    source_ref, target_ref, pieces, sems = refs[dp + 2 + dp:]
    source_copy = pltpu.make_async_copy(source_any, source_ref, sems.at[0])
    target_copy = pltpu.make_async_copy(target_any, target_ref, sems.at[1])
    source_copy.start()
    target_copy.start()
    tgt_count = query_ref.shape[1]
    src_count = kv_ref.shape[0]
    rows = src_count // mp
    both = kv_ref[...]
    query_t = query_ref[...]
    grad_t = grad_ref[...]
    blank = jnp.zeros_like(query_t)
    query_wide = jnp.concatenate([query_t, blank], axis=0)
    grad_wide = jnp.concatenate([blank, grad_t], axis=0)
    scores = jnp.dot(both, query_wide, preferred_element_type=jnp.float32)
    dprob = jnp.dot(both, grad_wide, preferred_element_type=jnp.float32)
    source_copy.wait()
    target_copy.wait()
    first, last = source_range(source_ref, target_ref, tgt_count)
    position = lax.broadcasted_iota(jnp.int32, scores.shape, 0)
    allowed = jnp.logical_and(position >= first, position < last)
    expo = jnp.where(allowed, jnp.exp(scores), 0.0)
    total = jnp.sum(expo, axis=0, keepdims=True)
    delta = jnp.sum(expo * dprob, axis=0, keepdims=True) / total
    prob = expo * (1.0 / total)
    prob_low = prob.astype(jnp.bfloat16)
    dscore = (prob * (dprob - delta)).astype(jnp.bfloat16)
    both_grad = dot(dscore, query_wide, NT) + dot(prob_low, grad_wide, NT)
    both_low = both_grad.astype(jnp.bfloat16)

    both_rank = low_refs[0].shape[1]
    mine = lax.axis_index("dp")
    parts = []
    for low_ref in low_refs:
        for cut in range(rows // CUT):
            parts.append(low_ref[cut * CUT:(cut + 1) * CUT, :])
    side = LANES // both_rank
    packed = [
        jnp.concatenate(parts[at:at + side], axis=1) for at in range(0, len(parts), side)
    ]
    packed = jnp.concatenate(packed, axis=0) if len(packed) > 1 else packed[0]
    for block in range(mp):
        both_grad_ref[block, :rows, :] = both_low[block * rows:(block + 1) * rows]
        both_grad_ref[block, rows:, :] = packed

    order = []
    for cut in range(rows // CUT):
        for block in range(mp):
            start = block * rows + cut * CUT
            order.append(both_low[start:start + CUT])
    turned = jnp.concatenate(order, axis=0).astype(jnp.float32).T.astype(jnp.bfloat16)
    step = HS // dp
    for j in range(dp):
        pieces[j] = jnp.concatenate(
            [turned[j * step:(j + 1) * step], turned[HS + j * step:HS + (j + 1) * step]], axis=0
        )
    for s in range(dp):
        piece_refs[s][...] = pieces[lax.rem(mine + s, dp)]

    query_grad = dot(both, dscore, TN)
    query_grad_ref[...] = query_grad[:HS].astype(jnp.bfloat16)


def owner_kernel(dp, mp, got_ref, up_ref, *refs):
    piece_refs = refs[:dp]
    key_ref, value_ref, low_grad_ref, up_grad_ref = refs[dp:dp + 4]
    rows = key_ref.shape[0]
    both_rank = up_ref.shape[0]
    rank = both_rank // 2
    for pair in range(mp // 2):
        first = got_ref[2 * pair, :rows, :]
        second = got_ref[2 * pair + 1, :rows, :]
        columns = slice(2 * pair * HS, (2 * pair + 2) * HS)
        key_ref[:, columns] = jnp.concatenate([first[:, :HS], second[:, :HS]], axis=1)
        value_ref[:, columns] = jnp.concatenate([first[:, HS:], second[:, HS:]], axis=1)
    up = up_ref[...]
    from_key = dot(key_ref[...], up, NT)
    from_value = dot(value_ref[...], up, NT)
    column = lax.broadcasted_iota(jnp.int32, from_key.shape, 1)
    low_grad_ref[...] = adapter_factor * jnp.where(column < rank, from_key, from_value)

    me = lax.axis_index("dp") * mp + lax.axis_index("mp")
    side = LANES // both_rank
    cuts = rows // CUT
    half = mp * CUT
    step = HS // dp
    lane = lax.broadcasted_iota(jnp.int32, (2 * step, LANES), 1) // both_rank
    total = jnp.zeros((2 * step, LANES), jnp.float32)
    lows = []
    for group in range(dp * cuts // side):
        at = rows + group * CUT
        lows.append(jnp.concatenate([got_ref[block, at:at + CUT, :] for block in range(mp)], axis=0))
    for s in range(dp):
        pack = lax.rem(lax.rem(me, dp) + dp - s, dp)
        for cut in range(cuts):
            piece = piece_refs[s][:, cut * half:(cut + 1) * half]
            slot = pack * cuts + cut
            for group, low in enumerate(lows):
                product = jnp.dot(piece, low, preferred_element_type=jnp.float32)
                total += jnp.where(lane + group * side == slot, product, 0.0)
    share = total[:, :both_rank]
    for at in range(1, side):
        share += total[:, at * both_rank:(at + 1) * both_rank]
    column = lax.broadcasted_iota(jnp.int32, (step, both_rank), 1)
    up_grad_ref[...] = adapter_factor * jnp.where(column < rank, share[:step], share[step:])


def local(dp, mp, query, kv_cache, out_grad, source_lengths, target_lengths, low_rank, adapter_up_matrix):
    tgt_count = query.shape[0]
    src_count = kv_cache.shape[0]
    rows, both_rank = low_rank.shape
    width = adapter_up_matrix.shape[1]
    step = HS // dp
    low_rows = dp * rows * both_rank // LANES
    vmem = pl.BlockSpec(memory_space=pltpu.VMEM)
    hbm = pl.BlockSpec(memory_space=pl.ANY)
    params = pltpu.CompilerParams(vmem_limit_bytes=48 * 1024 * 1024)

    seen = [low_rank]
    for s in range(1, dp):
        seen.append(lax.ppermute(low_rank, "dp", [(d, (d + s) % dp) for d in range(dp)]))
    mine = lax.axis_index("dp")
    lows = []
    for pack in range(dp):
        low = seen[0]
        for s in range(1, dp):
            low = jnp.where((mine - s) % dp == pack, seen[s], low)
        lows.append(low)

    query_grad_t, sent, *pieces = pl.pallas_call(
        functools.partial(attention_kernel, dp, mp),
        out_shape=[
            jax.ShapeDtypeStruct((HS, tgt_count), jnp.bfloat16),
            jax.ShapeDtypeStruct((mp, rows + low_rows, LANES), jnp.bfloat16),
        ] + [jax.ShapeDtypeStruct((2 * step, src_count), jnp.bfloat16)] * dp,
        in_specs=[hbm, hbm] + [vmem] * (3 + dp),
        out_specs=[vmem] * (2 + dp),
        scratch_shapes=[
            pltpu.SMEM(source_lengths.shape, jnp.int32),
            pltpu.SMEM(target_lengths.shape, jnp.int32),
            pltpu.VMEM((dp, 2 * step, src_count), jnp.bfloat16),
            pltpu.SemaphoreType.DMA((2,)),
        ],
        compiler_params=params,
        name="attention_backward",
    )(source_lengths, target_lengths, query.T, out_grad.T, kv_cache, *lows)

    got = lax.all_to_all(sent, "mp", split_axis=0, concat_axis=0, tiled=True)

    arrived = []
    for s in range(dp):
        route = [(d * mp + h, h * dp + (d + s) % dp) for d in range(dp) for h in range(mp)]
        arrived.append(lax.ppermute(pieces[s], ("dp", "mp"), route))

    key_gradient, value_grad, low_grad, up_grad = pl.pallas_call(
        functools.partial(owner_kernel, dp, mp),
        out_shape=[
            jax.ShapeDtypeStruct((rows, width), jnp.bfloat16),
            jax.ShapeDtypeStruct((rows, width), jnp.bfloat16),
            jax.ShapeDtypeStruct((rows, both_rank), jnp.float32),
            jax.ShapeDtypeStruct((step, both_rank), jnp.float32),
        ],
        in_specs=[vmem] * (2 + dp),
        out_specs=[vmem] * 4,
        compiler_params=params,
        name="owner_outputs",
    )(got, adapter_up_matrix, *arrived)
    return query_grad_t.T, key_gradient, value_grad, low_grad, up_grad


def solution(mesh):
    in_specs = (
        P("dp", "mp"),
        P("dp", "mp"),
        P("dp", "mp"),
        P("dp", None),
        P("dp", None),
        P(("dp", "mp"), None),
        P(),
    )
    out_specs = (
        P("dp", "mp"),
        P(("dp", "mp"), None),
        P(("dp", "mp"), None),
        P(("dp", "mp"), None),
        P(("dp", "mp"), None),
    )
    body = functools.partial(local, mesh.shape["dp"], mesh.shape["mp"])
    return jax.shard_map(body, mesh=mesh, in_specs=in_specs, out_specs=out_specs, check_vma=False)
```

```python
import functools

import jax
import jax.numpy as jnp
from jax import lax
from jax.experimental import pallas as pl
from jax.experimental.pallas import tpu as pltpu
from jax.sharding import PartitionSpec as P

HS = 64
LANES = 128
CUT = 16

adapter_factor = 2.0

NT = (((1,), (1,)), ((), ()))
TN = (((0,), (0,)), ((), ()))


def dot(left, right, dims):
    return lax.dot_general(left, right, dims, preferred_element_type=jnp.float32)


def source_range(source_ref, target_ref, count):
    position = lax.broadcasted_iota(jnp.int32, (1, count), 1)
    first = jnp.zeros((1, count), jnp.int32)
    last = jnp.zeros((1, count), jnp.int32)
    target_start = jnp.int32(0)
    source_start = jnp.int32(0)
    for i in range(source_ref.shape[1]):
        source_end = source_start + source_ref[0, i]
        inside = position >= target_start
        first = jnp.where(inside, source_start, first)
        last = jnp.where(inside, source_end, last)
        target_start = target_start + target_ref[0, i]
        source_start = source_end
    return first, last


def attention_kernel(
    inner, outer,
    source_any, target_any, query_any, grad_any, kv_any, low_any,
    query_grad_ref, sent_ref,
    source_ref, target_ref, query_ref, grad_ref, kv_ref, low_ref, sems,
):
    pairs = [
        (kv_any, kv_ref), (query_any, query_ref), (grad_any, grad_ref),
        (source_any, source_ref), (target_any, target_ref), (low_any, low_ref),
    ]
    copies = [
        pltpu.make_async_copy(here, there, sems.at[i]) for i, (here, there) in enumerate(pairs)
    ]
    for copy in copies:
        copy.start()
    for copy in copies:
        copy.wait()
    tgt_count = query_ref.shape[1]
    rows = kv_ref.shape[0] // (inner * outer)
    both = kv_ref[...]
    query_t = query_ref[...]
    grad_t = grad_ref[...]
    blank = jnp.zeros_like(query_t)
    query_wide = jnp.concatenate([query_t, blank], axis=0)
    grad_wide = jnp.concatenate([blank, grad_t], axis=0)
    scores = jnp.dot(both, query_wide, preferred_element_type=jnp.float32)
    dprob = jnp.dot(both, grad_wide, preferred_element_type=jnp.float32)
    first, last = source_range(source_ref, target_ref, tgt_count)
    position = lax.broadcasted_iota(jnp.int32, scores.shape, 0)
    allowed = jnp.logical_and(position >= first, position < last)
    expo = jnp.where(allowed, jnp.exp(scores), 0.0)
    total = jnp.sum(expo, axis=0, keepdims=True)
    delta = jnp.sum(expo * dprob, axis=0, keepdims=True) / total
    prob = expo * (1.0 / total)
    prob_low = prob.astype(jnp.bfloat16)
    dscore = (prob * (dprob - delta)).astype(jnp.bfloat16)
    both_grad = dot(dscore, query_wide, NT) + dot(prob_low, grad_wide, NT)
    both_low = both_grad.astype(jnp.bfloat16)
    low = low_ref[...]
    cuts = rows // CUT
    spread = [low[cut * CUT:(cut + 1) * CUT] for cut in range(cuts)]
    spread.append(jnp.zeros((CUT, LANES - cuts * low.shape[1]), jnp.bfloat16))
    spread = jnp.concatenate(spread, axis=1)
    for p in range(inner):
        for z in range(outer):
            block = z * inner + p
            sent_ref[p, z * rows:(z + 1) * rows, :] = both_low[block * rows:(block + 1) * rows]
        sent_ref[p, outer * rows:, :] = spread
    query_grad = dot(both, dscore, TN)
    query_grad_ref[...] = query_grad[:HS].astype(jnp.bfloat16)


def relay_kernel(inner, outer, both_rank, got_ref, *out_refs):
    here = lax.axis_index("mp") // inner
    rows = (got_ref.shape[1] - CUT) // outer
    used = rows // CUT * both_rank
    beside = LANES // used
    groups = []
    for g in range(0, inner, beside):
        parts = [got_ref[g + q, outer * rows:, :][:, :used] for q in range(beside)]
        groups.append(jnp.concatenate(parts, axis=1))
    for l, out_ref in enumerate(out_refs):
        there = here ^ l
        for p in range(inner):
            out_ref[p * rows:(p + 1) * rows, :] = got_ref[
                p, pl.ds(pl.multiple_of(there * rows, rows), rows), :
            ]
        for g, group in enumerate(groups):
            at = inner * rows + g * CUT
            out_ref[at:at + CUT, :] = group


def share_kernel(inner, outer, both_rank, rows, sent_ref, *refs):
    plane_refs = refs[:outer]
    out_refs = refs[outer:]
    here = lax.axis_index("mp") // inner
    mine = lax.axis_index("dp")
    dp = len(out_refs)
    cuts = rows // CUT
    beside = LANES // (cuts * both_rank)
    lows = jnp.concatenate([ref[inner * rows:, :] for ref in plane_refs], axis=0)
    lane = lax.broadcasted_iota(jnp.int32, (2 * HS, LANES), 1) // both_rank
    total = jnp.zeros((2 * HS, LANES), jnp.float32)
    for q in range(beside):
        for cut in range(cuts):
            tokens = []
            for l in range(outer):
                start = (here ^ l) * rows + cut * CUT
                for g in range(inner // beside):
                    tokens.append(sent_ref[g * beside + q, pl.ds(pl.multiple_of(start, CUT), CUT), :])
            product = dot(jnp.concatenate(tokens, axis=0), lows, TN)
            total += jnp.where(lane == q * cuts + cut, product, 0.0)
    share = total[:, :both_rank]
    for at in range(1, beside * cuts):
        share += total[:, at * both_rank:(at + 1) * both_rank]
    column = lax.broadcasted_iota(jnp.int32, (HS, both_rank), 1)
    share = adapter_factor * jnp.where(column < both_rank // 2, share[:HS], share[HS:])
    step = HS // dp
    for s, out_ref in enumerate(out_refs):
        turn = lax.rem(mine + s, dp)
        piece = share[:step]
        for j in range(1, dp):
            piece = jnp.where(turn == j, share[j * step:(j + 1) * step], piece)
        out_ref[...] = piece


def owner_kernel(inner, outer, up_ref, *refs):
    plane_refs = refs[:outer]
    key_ref, value_ref, low_grad_ref = refs[outer:]
    here = lax.axis_index("mp") // inner
    rows = key_ref.shape[0]
    rank = up_ref.shape[0] // 2
    for l, plane_ref in enumerate(plane_refs):
        columns = pl.ds(pl.multiple_of((here ^ l) * (inner * HS), LANES), inner * HS)
        keys = []
        values = []
        for p in range(inner):
            block = plane_ref[p * rows:(p + 1) * rows, :]
            keys.append(block[:, :HS])
            values.append(block[:, HS:])
        key_ref[:, columns] = jnp.concatenate(keys, axis=1)
        value_ref[:, columns] = jnp.concatenate(values, axis=1)
    up = up_ref[...]
    from_key = dot(key_ref[...], up, NT)
    from_value = dot(value_ref[...], up, NT)
    column = lax.broadcasted_iota(jnp.int32, from_key.shape, 1)
    low_grad_ref[...] = adapter_factor * jnp.where(column < rank, from_key, from_value)


def local(dp, mp, query, kv_cache, out_grad, source_lengths, target_lengths, low_rank, adapter_up_matrix):
    tgt_count = query.shape[0]
    src_count = kv_cache.shape[0]
    rows, both_rank = low_rank.shape
    width = adapter_up_matrix.shape[1]
    step = HS // dp
    inner = 1
    while inner * inner * 4 <= mp:
        inner *= 2
    inner = min(2 * inner, mp) if inner * inner < mp else inner
    outer = mp // inner
    assert outer & (outer - 1) == 0
    vmem = pl.BlockSpec(memory_space=pltpu.VMEM)
    hbm = pl.BlockSpec(memory_space=pl.ANY)
    params = pltpu.CompilerParams(vmem_limit_bytes=48 * 1024 * 1024)
    whole_vmem = pltpu.CompilerParams(vmem_limit_bytes=60 * 1024 * 1024)

    query_t = query.T
    grad_t = out_grad.T
    query_grad_t, sent = pl.pallas_call(
        functools.partial(attention_kernel, inner, outer),
        out_shape=[
            jax.ShapeDtypeStruct((HS, tgt_count), jnp.bfloat16),
            jax.ShapeDtypeStruct((inner, outer * rows + CUT, LANES), jnp.bfloat16),
        ],
        in_specs=[hbm] * 6,
        out_specs=[vmem] * 2,
        scratch_shapes=[
            pltpu.SMEM(source_lengths.shape, jnp.int32),
            pltpu.SMEM(target_lengths.shape, jnp.int32),
            pltpu.VMEM(query_t.shape, jnp.bfloat16),
            pltpu.VMEM(grad_t.shape, jnp.bfloat16),
            pltpu.VMEM(kv_cache.shape, jnp.bfloat16),
            pltpu.VMEM(low_rank.shape, jnp.bfloat16),
            pltpu.SemaphoreType.DMA((6,)),
        ],
        compiler_params=whole_vmem,
        name="attention_backward",
    )(source_lengths, target_lengths, query_t, grad_t, kv_cache, low_rank)

    planes = [[z * inner + p for p in range(inner)] for z in range(outer)]
    got = lax.all_to_all(sent, "mp", 0, 0, axis_index_groups=planes, tiled=True)

    plane_rows = inner * rows + inner * rows * both_rank // LANES
    relayed = pl.pallas_call(
        functools.partial(relay_kernel, inner, outer, both_rank),
        out_shape=[jax.ShapeDtypeStruct((plane_rows, LANES), jnp.bfloat16)] * outer,
        in_specs=[vmem],
        out_specs=[vmem] * outer,
        compiler_params=params,
        name="relay",
    )(got)
    arrived = [relayed[0]]
    for l in range(1, outer):
        route = [(m, ((m // inner) ^ l) * inner + m % inner) for m in range(mp)]
        arrived.append(lax.ppermute(relayed[l], "mp", route))

    shares = pl.pallas_call(
        functools.partial(share_kernel, inner, outer, both_rank, rows),
        out_shape=[jax.ShapeDtypeStruct((step, both_rank), jnp.float32)] * dp,
        in_specs=[vmem] * (1 + outer),
        out_specs=[vmem] * dp,
        compiler_params=params,
        name="adapter_shares",
    )(sent, *arrived)

    up_grad = None
    for s in range(dp):
        route = [(d * mp + h, h * dp + (d + s) % dp) for d in range(dp) for h in range(mp)]
        term = lax.ppermute(shares[s], ("dp", "mp"), route)
        up_grad = term if up_grad is None else up_grad + term

    key_gradient, value_grad, low_grad = pl.pallas_call(
        functools.partial(owner_kernel, inner, outer),
        out_shape=[
            jax.ShapeDtypeStruct((rows, width), jnp.bfloat16),
            jax.ShapeDtypeStruct((rows, width), jnp.bfloat16),
            jax.ShapeDtypeStruct((rows, both_rank), jnp.float32),
        ],
        in_specs=[vmem] * (1 + outer),
        out_specs=[vmem] * 3,
        compiler_params=params,
        name="owner_outputs",
    )(adapter_up_matrix, *arrived)
    return query_grad_t.T, key_gradient, value_grad, low_grad, up_grad


def solution(mesh):
    in_specs = (
        P("dp", "mp"),
        P("dp", "mp"),
        P("dp", "mp"),
        P("dp", None),
        P("dp", None),
        P(("dp", "mp"), None),
        P(),
    )
    out_specs = (
        P("dp", "mp"),
        P(("dp", "mp"), None),
        P(("dp", "mp"), None),
        P(("dp", "mp"), None),
        P(("dp", "mp"), None),
    )
    body = functools.partial(local, mesh.shape["dp"], mesh.shape["mp"])
    return jax.shard_map(body, mesh=mesh, in_specs=in_specs, out_specs=out_specs, check_vma=False)
```

```python
import functools

import jax
import jax.numpy as jnp
from jax import lax
from jax.experimental import pallas as pl
from jax.experimental.pallas import tpu as pltpu
from jax.sharding import PartitionSpec as P

HS = 64
LANES = 128

adapter_factor = 2.0

NT = (((1,), (1,)), ((), ()))
TN = (((0,), (0,)), ((), ()))


def dot(left, right, dims):
    return lax.dot_general(left, right, dims, preferred_element_type=jnp.float32)


def source_range(source_ref, target_ref, count):
    position = lax.broadcasted_iota(jnp.int32, (1, count), 1)
    first = jnp.zeros((1, count), jnp.int32)
    last = jnp.zeros((1, count), jnp.int32)
    target_start = jnp.int32(0)
    source_start = jnp.int32(0)
    for i in range(source_ref.shape[1]):
        source_end = source_start + source_ref[0, i]
        inside = position >= target_start
        first = jnp.where(inside, source_start, first)
        last = jnp.where(inside, source_end, last)
        target_start = target_start + target_ref[0, i]
        source_start = source_end
    return first, last


def attention_kernel(
    source_any, target_any, query_any, grad_any, kv_any,
    query_grad_ref, sent_ref,
    source_ref, target_ref, query_ref, grad_ref, kv_ref, sems,
):
    pairs = [
        (kv_any, kv_ref), (query_any, query_ref), (grad_any, grad_ref),
        (source_any, source_ref), (target_any, target_ref),
    ]
    copies = [
        pltpu.make_async_copy(here, there, sems.at[i]) for i, (here, there) in enumerate(pairs)
    ]
    for copy in copies:
        copy.start()
    for copy in copies:
        copy.wait()
    tgt_count = query_ref.shape[1]
    both = kv_ref[...]
    query_t = query_ref[...]
    grad_t = grad_ref[...]
    blank = jnp.zeros_like(query_t)
    query_wide = jnp.concatenate([query_t, blank], axis=0)
    grad_wide = jnp.concatenate([blank, grad_t], axis=0)
    scores = jnp.dot(both, query_wide, preferred_element_type=jnp.float32)
    dprob = jnp.dot(both, grad_wide, preferred_element_type=jnp.float32)
    first, last = source_range(source_ref, target_ref, tgt_count)
    position = lax.broadcasted_iota(jnp.int32, scores.shape, 0)
    allowed = jnp.logical_and(position >= first, position < last)
    expo = jnp.where(allowed, jnp.exp(scores), 0.0)
    total = jnp.sum(expo, axis=0, keepdims=True)
    delta = jnp.sum(expo * dprob, axis=0, keepdims=True) / total
    prob = expo * (1.0 / total)
    prob_low = prob.astype(jnp.bfloat16)
    dscore = (prob * (dprob - delta)).astype(jnp.bfloat16)
    both_grad = dot(dscore, query_wide, NT) + dot(prob_low, grad_wide, NT)
    both_low = both_grad.astype(jnp.bfloat16)
    rows = sent_ref.shape[1]
    for block in range(sent_ref.shape[0]):
        sent_ref[block] = both_low[block * rows:(block + 1) * rows]
    query_grad = dot(both, dscore, TN)
    query_grad_ref[...] = query_grad[:HS].astype(jnp.bfloat16)


def share_kernel(inner, outer, both_rank, sent_ref, *refs):
    plane_refs = refs[:outer]
    out_refs = refs[outer:]
    me = lax.axis_index("mp")
    here = me // inner
    place = lax.rem(me, inner)
    mine = lax.axis_index("dp")
    dp = len(out_refs)
    side = LANES // both_rank
    lane = lax.broadcasted_iota(jnp.int32, (2 * HS, LANES), 1) // both_rank
    total = jnp.zeros((2 * HS, LANES), jnp.float32)
    rows = sent_ref.shape[1]
    for group in range(inner // side):
        lows = [ref[group * rows:(group + 1) * rows, :] for ref in plane_refs]
        lows = jnp.concatenate(lows, axis=0)
        for at in range(side):
            k = group * side + at
            tokens = [sent_ref[(here ^ l) * inner + (place ^ k)] for l in range(outer)]
            product = dot(jnp.concatenate(tokens, axis=0), lows, TN)
            total += jnp.where(lane == at, product, 0.0)
    share = total[:, :both_rank]
    for at in range(1, side):
        share += total[:, at * both_rank:(at + 1) * both_rank]
    column = lax.broadcasted_iota(jnp.int32, (HS, both_rank), 1)
    share = adapter_factor * jnp.where(column < both_rank // 2, share[:HS], share[HS:])
    step = HS // dp
    for s, out_ref in enumerate(out_refs):
        turn = lax.rem(mine + s, dp)
        piece = share[:step]
        for j in range(1, dp):
            piece = jnp.where(turn == j, share[j * step:(j + 1) * step], piece)
        out_ref[...] = piece


def pack_kernel(*refs):
    side = LANES // refs[0].shape[1]
    rows = refs[0].shape[0]
    out_ref = refs[-1]
    for group in range((len(refs) - 1) // side):
        parts = [ref[...] for ref in refs[group * side:(group + 1) * side]]
        out_ref[group * rows:(group + 1) * rows, :] = jnp.concatenate(parts, axis=1)


def owner_kernel(up_ref, got_ref, *refs):
    share_refs = refs[:-4]
    key_ref, value_ref, low_grad_ref, up_grad_ref = refs[-4:]
    rank = up_ref.shape[0] // 2
    for pair in range(got_ref.shape[0] // 2):
        first = got_ref[2 * pair]
        second = got_ref[2 * pair + 1]
        columns = slice(2 * pair * HS, (2 * pair + 2) * HS)
        key_ref[:, columns] = jnp.concatenate([first[:, :HS], second[:, :HS]], axis=1)
        value_ref[:, columns] = jnp.concatenate([first[:, HS:], second[:, HS:]], axis=1)
    up = up_ref[...]
    from_key = dot(key_ref[...], up, NT)
    from_value = dot(value_ref[...], up, NT)
    column = lax.broadcasted_iota(jnp.int32, from_key.shape, 1)
    low_grad_ref[...] = adapter_factor * jnp.where(column < rank, from_key, from_value)
    total = share_refs[0][...]
    for share_ref in share_refs[1:]:
        total += share_ref[...]
    up_grad_ref[...] = total


def local(dp, mp, query, kv_cache, out_grad, source_lengths, target_lengths, low_rank, adapter_up_matrix):
    tgt_count = query.shape[0]
    src_count = kv_cache.shape[0]
    rows, both_rank = low_rank.shape
    width = adapter_up_matrix.shape[1]
    step = HS // dp
    side = LANES // both_rank
    inner = 4 if mp <= 16 else 8
    outer = mp // inner
    assert inner * outer == mp and outer & (outer - 1) == 0
    vmem = pl.BlockSpec(memory_space=pltpu.VMEM)
    hbm = pl.BlockSpec(memory_space=pl.ANY)
    params = pltpu.CompilerParams(vmem_limit_bytes=48 * 1024 * 1024)
    whole_vmem = pltpu.CompilerParams(vmem_limit_bytes=60 * 1024 * 1024)

    near = [low_rank]
    for k in range(1, inner):
        route = [(m, m ^ k) for m in range(mp)]
        near.append(lax.ppermute(low_rank, "mp", route))

    query_t = query.T
    grad_t = out_grad.T
    query_grad_t, sent = pl.pallas_call(
        attention_kernel,
        out_shape=[
            jax.ShapeDtypeStruct((HS, tgt_count), jnp.bfloat16),
            jax.ShapeDtypeStruct((mp, rows, LANES), jnp.bfloat16),
        ],
        in_specs=[hbm] * 5,
        out_specs=[vmem] * 2,
        scratch_shapes=[
            pltpu.SMEM(source_lengths.shape, jnp.int32),
            pltpu.SMEM(target_lengths.shape, jnp.int32),
            pltpu.VMEM(query_t.shape, jnp.bfloat16),
            pltpu.VMEM(grad_t.shape, jnp.bfloat16),
            pltpu.VMEM(kv_cache.shape, jnp.bfloat16),
            pltpu.SemaphoreType.DMA((5,)),
        ],
        compiler_params=whole_vmem,
        name="attention_backward",
    )(source_lengths, target_lengths, query_t, grad_t, kv_cache)

    got = lax.all_to_all(sent, "mp", 0, 0, tiled=True)

    packed = pl.pallas_call(
        pack_kernel,
        out_shape=jax.ShapeDtypeStruct((inner // side * rows, LANES), jnp.bfloat16),
        in_specs=[vmem] * inner,
        out_specs=vmem,
        compiler_params=params,
        name="pack_low_rank",
    )(*near)
    planes = [packed]
    for l in range(1, outer):
        route = [(m, ((m // inner) ^ l) * inner + m % inner) for m in range(mp)]
        planes.append(lax.ppermute(packed, "mp", route))

    shares = pl.pallas_call(
        functools.partial(share_kernel, inner, outer, both_rank),
        out_shape=[jax.ShapeDtypeStruct((step, both_rank), jnp.float32)] * dp,
        in_specs=[vmem] * (1 + outer),
        out_specs=[vmem] * dp,
        compiler_params=params,
        name="adapter_shares",
    )(sent, *planes)

    arrived = []
    for s in range(dp):
        route = [(d * mp + h, h * dp + (d + s) % dp) for d in range(dp) for h in range(mp)]
        arrived.append(lax.ppermute(shares[s], ("dp", "mp"), route))

    key_gradient, value_grad, low_grad, up_grad = pl.pallas_call(
        owner_kernel,
        out_shape=[
            jax.ShapeDtypeStruct((rows, width), jnp.bfloat16),
            jax.ShapeDtypeStruct((rows, width), jnp.bfloat16),
            jax.ShapeDtypeStruct((rows, both_rank), jnp.float32),
            jax.ShapeDtypeStruct((step, both_rank), jnp.float32),
        ],
        in_specs=[vmem] * (2 + dp),
        out_specs=[vmem] * 4,
        compiler_params=params,
        name="owner_outputs",
    )(adapter_up_matrix, got, *arrived)
    return query_grad_t.T, key_gradient, value_grad, low_grad, up_grad


def solution(mesh):
    in_specs = (
        P("dp", "mp"),
        P("dp", "mp"),
        P("dp", "mp"),
        P("dp", None),
        P("dp", None),
        P(("dp", "mp"), None),
        P(),
    )
    out_specs = (
        P("dp", "mp"),
        P(("dp", "mp"), None),
        P(("dp", "mp"), None),
        P(("dp", "mp"), None),
        P(("dp", "mp"), None),
    )
    body = functools.partial(local, mesh.shape["dp"], mesh.shape["mp"])
    return jax.shard_map(body, mesh=mesh, in_specs=in_specs, out_specs=out_specs, check_vma=False)
```

```python
import functools

import jax
import jax.numpy as jnp
from jax import lax
from jax.experimental import pallas as pl
from jax.experimental.pallas import tpu as pltpu
from jax.sharding import PartitionSpec as P

HS = 64
LANES = 128
CUT = 16

adapter_factor = 2.0

NT = (((1,), (1,)), ((), ()))
TN = (((0,), (0,)), ((), ()))


def dot(left, right, dims):
    return lax.dot_general(left, right, dims, preferred_element_type=jnp.float32)


def source_range(source_ref, target_ref, count):
    position = lax.broadcasted_iota(jnp.int32, (1, count), 1)
    first = jnp.zeros((1, count), jnp.int32)
    last = jnp.zeros((1, count), jnp.int32)
    target_start = jnp.int32(0)
    source_start = jnp.int32(0)
    for i in range(source_ref.shape[1]):
        source_end = source_start + source_ref[0, i]
        inside = position >= target_start
        first = jnp.where(inside, source_start, first)
        last = jnp.where(inside, source_end, last)
        target_start = target_start + target_ref[0, i]
        source_start = source_end
    return first, last


def attention_kernel(
    source_any, target_any, query_any, grad_any, kv_any, low_any,
    query_grad_ref, sent_ref,
    source_ref, target_ref, query_ref, grad_ref, kv_ref, low_ref, sems,
):
    pairs = [
        (kv_any, kv_ref), (query_any, query_ref), (grad_any, grad_ref),
        (source_any, source_ref), (target_any, target_ref), (low_any, low_ref),
    ]
    copies = [
        pltpu.make_async_copy(here, there, sems.at[i]) for i, (here, there) in enumerate(pairs)
    ]
    for copy in copies:
        copy.start()
    for copy in copies:
        copy.wait()
    tgt_count = query_ref.shape[1]
    both = kv_ref[...]
    query_t = query_ref[...]
    grad_t = grad_ref[...]
    blank = jnp.zeros_like(query_t)
    query_wide = jnp.concatenate([query_t, blank], axis=0)
    grad_wide = jnp.concatenate([blank, grad_t], axis=0)
    scores = jnp.dot(both, query_wide, preferred_element_type=jnp.float32)
    dprob = jnp.dot(both, grad_wide, preferred_element_type=jnp.float32)
    first, last = source_range(source_ref, target_ref, tgt_count)
    position = lax.broadcasted_iota(jnp.int32, scores.shape, 0)
    allowed = jnp.logical_and(position >= first, position < last)
    expo = jnp.where(allowed, jnp.exp(scores), 0.0)
    total = jnp.sum(expo, axis=0, keepdims=True)
    delta = jnp.sum(expo * dprob, axis=0, keepdims=True) / total
    prob = expo * (1.0 / total)
    prob_low = prob.astype(jnp.bfloat16)
    dscore = (prob * (dprob - delta)).astype(jnp.bfloat16)
    both_grad = dot(dscore, query_wide, NT) + dot(prob_low, grad_wide, NT)
    both_low = both_grad.astype(jnp.bfloat16)
    low = low_ref[...]
    rows, both_rank = low.shape
    spread = [low[at:at + CUT] for at in range(0, rows, CUT)]
    spread.append(jnp.zeros((CUT, LANES - rows // CUT * both_rank), jnp.bfloat16))
    spread = jnp.concatenate(spread, axis=1)
    for block in range(sent_ref.shape[0]):
        sent_ref[block, :rows, :] = both_low[block * rows:(block + 1) * rows]
        sent_ref[block, rows:, :] = spread
    query_grad = dot(both, dscore, TN)
    query_grad_ref[...] = query_grad[:HS].astype(jnp.bfloat16)


def share_kernel(rows, both_rank, sent_ref, got_ref, *out_refs):
    mine = lax.axis_index("dp")
    dp = len(out_refs)
    blocks = sent_ref.shape[0]
    tokens = jnp.concatenate([sent_ref[block, :rows, :] for block in range(blocks)], axis=0)
    lows = []
    for block in range(blocks):
        spread = got_ref[block, rows:, :]
        for at in range(rows // CUT):
            lows.append(spread[:, at * both_rank:(at + 1) * both_rank])
    share = dot(tokens, jnp.concatenate(lows, axis=0), TN)
    column = lax.broadcasted_iota(jnp.int32, (HS, both_rank), 1)
    share = adapter_factor * jnp.where(column < both_rank // 2, share[:HS], share[HS:])
    step = HS // dp
    for s, out_ref in enumerate(out_refs):
        turn = lax.rem(mine + s, dp)
        piece = share[:step]
        for j in range(1, dp):
            piece = jnp.where(turn == j, share[j * step:(j + 1) * step], piece)
        out_ref[...] = piece


def owner_kernel(up_ref, got_ref, key_ref, value_ref, low_grad_ref):
    rows = key_ref.shape[0]
    rank = up_ref.shape[0] // 2
    for pair in range(got_ref.shape[0] // 2):
        first = got_ref[2 * pair, :rows, :]
        second = got_ref[2 * pair + 1, :rows, :]
        columns = slice(2 * pair * HS, (2 * pair + 2) * HS)
        key_ref[:, columns] = jnp.concatenate([first[:, :HS], second[:, :HS]], axis=1)
        value_ref[:, columns] = jnp.concatenate([first[:, HS:], second[:, HS:]], axis=1)
    up = up_ref[...]
    from_key = dot(key_ref[...], up, NT)
    from_value = dot(value_ref[...], up, NT)
    column = lax.broadcasted_iota(jnp.int32, from_key.shape, 1)
    low_grad_ref[...] = adapter_factor * jnp.where(column < rank, from_key, from_value)


def local(dp, mp, query, kv_cache, out_grad, source_lengths, target_lengths, low_rank, adapter_up_matrix):
    tgt_count = query.shape[0]
    rows, both_rank = low_rank.shape
    width = adapter_up_matrix.shape[1]
    step = HS // dp
    vmem = pl.BlockSpec(memory_space=pltpu.VMEM)
    hbm = pl.BlockSpec(memory_space=pl.ANY)
    params = pltpu.CompilerParams(vmem_limit_bytes=48 * 1024 * 1024)
    whole_vmem = pltpu.CompilerParams(vmem_limit_bytes=60 * 1024 * 1024)

    query_t = query.T
    grad_t = out_grad.T
    query_grad_t, sent = pl.pallas_call(
        attention_kernel,
        out_shape=[
            jax.ShapeDtypeStruct((HS, tgt_count), jnp.bfloat16),
            jax.ShapeDtypeStruct((mp, rows + CUT, LANES), jnp.bfloat16),
        ],
        in_specs=[hbm] * 6,
        out_specs=[vmem] * 2,
        scratch_shapes=[
            pltpu.SMEM(source_lengths.shape, jnp.int32),
            pltpu.SMEM(target_lengths.shape, jnp.int32),
            pltpu.VMEM(query_t.shape, jnp.bfloat16),
            pltpu.VMEM(grad_t.shape, jnp.bfloat16),
            pltpu.VMEM(kv_cache.shape, jnp.bfloat16),
            pltpu.VMEM(low_rank.shape, jnp.bfloat16),
            pltpu.SemaphoreType.DMA((6,)),
        ],
        compiler_params=whole_vmem,
        name="attention_backward",
    )(source_lengths, target_lengths, query_t, grad_t, kv_cache, low_rank)

    got = lax.all_to_all(sent, "mp", 0, 0, tiled=True)

    shares = pl.pallas_call(
        functools.partial(share_kernel, rows, both_rank),
        out_shape=[jax.ShapeDtypeStruct((step, both_rank), jnp.float32)] * dp,
        in_specs=[vmem] * 2,
        out_specs=[vmem] * dp,
        compiler_params=params,
        name="adapter_shares",
    )(sent, got)

    up_grad = None
    for s in range(dp):
        route = [(d * mp + h, h * dp + (d + s) % dp) for d in range(dp) for h in range(mp)]
        term = lax.ppermute(shares[s], ("dp", "mp"), route)
        up_grad = term if up_grad is None else up_grad + term

    key_gradient, value_grad, low_grad = pl.pallas_call(
        owner_kernel,
        out_shape=[
            jax.ShapeDtypeStruct((rows, width), jnp.bfloat16),
            jax.ShapeDtypeStruct((rows, width), jnp.bfloat16),
            jax.ShapeDtypeStruct((rows, both_rank), jnp.float32),
        ],
        in_specs=[vmem] * 2,
        out_specs=[vmem] * 3,
        compiler_params=params,
        name="owner_outputs",
    )(adapter_up_matrix, got)
    return query_grad_t.T, key_gradient, value_grad, low_grad, up_grad


def solution(mesh):
    in_specs = (
        P("dp", "mp"),
        P("dp", "mp"),
        P("dp", "mp"),
        P("dp", None),
        P("dp", None),
        P(("dp", "mp"), None),
        P(),
    )
    out_specs = (
        P("dp", "mp"),
        P(("dp", "mp"), None),
        P(("dp", "mp"), None),
        P(("dp", "mp"), None),
        P(("dp", "mp"), None),
    )
    body = functools.partial(local, mesh.shape["dp"], mesh.shape["mp"])
    return jax.shard_map(body, mesh=mesh, in_specs=in_specs, out_specs=out_specs, check_vma=False)
```

```python
import functools

import jax
import jax.numpy as jnp
from jax import lax
from jax.experimental import pallas as pl
from jax.experimental.pallas import tpu as pltpu
from jax.sharding import PartitionSpec as P

HS = 64
LANES = 128
CUT = 16

adapter_factor = 2.0

NT = (((1,), (1,)), ((), ()))
TN = (((0,), (0,)), ((), ()))


def dot(left, right, dims):
    return lax.dot_general(left, right, dims, preferred_element_type=jnp.float32)


def source_range(source_ref, target_ref, count):
    position = lax.broadcasted_iota(jnp.int32, (1, count), 1)
    first = jnp.zeros((1, count), jnp.int32)
    last = jnp.zeros((1, count), jnp.int32)
    target_start = jnp.int32(0)
    source_start = jnp.int32(0)
    for i in range(source_ref.shape[1]):
        source_end = source_start + source_ref[0, i]
        inside = position >= target_start
        first = jnp.where(inside, source_start, first)
        last = jnp.where(inside, source_end, last)
        target_start = target_start + target_ref[0, i]
        source_start = source_end
    return first, last


def attention_kernel(
    rows, source_any, target_any, query_any, grad_any, kv_any, query_grad_ref, both_grad_ref, *refs
):
    *piece_refs, source_ref, target_ref, query_ref, grad_ref, kv_ref, pieces, sems = refs
    pairs = [
        (kv_any, kv_ref), (query_any, query_ref), (grad_any, grad_ref),
        (source_any, source_ref), (target_any, target_ref),
    ]
    copies = [
        pltpu.make_async_copy(here, there, sems.at[i]) for i, (here, there) in enumerate(pairs)
    ]
    for copy in copies:
        copy.start()
    for copy in copies:
        copy.wait()
    tgt_count = query_ref.shape[1]
    both = kv_ref[...]
    query_t = query_ref[...]
    grad_t = grad_ref[...]
    blank = jnp.zeros_like(query_t)
    query_wide = jnp.concatenate([query_t, blank], axis=0)
    grad_wide = jnp.concatenate([blank, grad_t], axis=0)
    scores = jnp.dot(both, query_wide, preferred_element_type=jnp.float32)
    dprob = jnp.dot(both, grad_wide, preferred_element_type=jnp.float32)
    first, last = source_range(source_ref, target_ref, tgt_count)
    position = lax.broadcasted_iota(jnp.int32, scores.shape, 0)
    allowed = jnp.logical_and(position >= first, position < last)
    expo = jnp.where(allowed, jnp.exp(scores), 0.0)
    total = jnp.sum(expo, axis=0, keepdims=True)
    delta = jnp.sum(expo * dprob, axis=0, keepdims=True) / total
    prob = expo * (1.0 / total)
    prob_low = prob.astype(jnp.bfloat16)
    dscore = (prob * (dprob - delta)).astype(jnp.bfloat16)
    both_grad = dot(dscore, query_wide, NT) + dot(prob_low, grad_wide, NT)
    both_low = both_grad.astype(jnp.bfloat16)
    blocks = both_grad_ref.shape[0]
    for block in range(blocks):
        both_grad_ref[block] = both_low[block * rows:(block + 1) * rows]

    order = []
    for start in range(0, rows, CUT):
        for block in range(blocks):
            order.append(both_low[block * rows + start:block * rows + start + CUT])
    turned = jnp.concatenate(order, axis=0).astype(jnp.float32).T.astype(jnp.bfloat16)
    mine = lax.axis_index("dp")
    dp = len(piece_refs)
    step = HS // dp
    for j in range(dp):
        pieces[j] = jnp.concatenate(
            [turned[j * step:(j + 1) * step], turned[HS + j * step:HS + (j + 1) * step]], axis=0
        )
    for s in range(dp):
        piece_refs[s][...] = pieces[lax.rem(mine + s, dp)]

    query_grad = dot(both, dscore, TN)
    query_grad_ref[...] = query_grad[:HS].astype(jnp.bfloat16)


def low_rank_kernel(rows, both_grad_ref, *refs):
    *low_refs, out_ref = refs
    mine = lax.axis_index("dp")
    dp = len(low_refs)
    both_rank = low_refs[0].shape[1]
    side = LANES // both_rank
    parts = []
    for pack in range(dp):
        low = low_refs[0][...]
        for s in range(1, dp):
            low = jnp.where(lax.rem(mine + dp - s, dp) == pack, low_refs[s][...], low)
        parts.extend(low[at:at + CUT] for at in range(0, rows, CUT))
    packed = [jnp.concatenate(parts[at:at + side], axis=1) for at in range(0, len(parts), side)]
    for block in range(out_ref.shape[0]):
        out_ref[block, :rows, :] = both_grad_ref[block]
        for group, part in enumerate(packed):
            out_ref[block, rows + group * CUT:rows + (group + 1) * CUT, :] = part


def owner_kernel(dp, mp, got_ref, up_ref, *refs):
    piece_refs = refs[:dp]
    key_ref, value_ref, low_grad_ref, up_grad_ref = refs[dp:dp + 4]
    rows = key_ref.shape[0]
    both_rank = up_ref.shape[0]
    rank = both_rank // 2
    for pair in range(mp // 2):
        first = got_ref[2 * pair, :rows, :]
        second = got_ref[2 * pair + 1, :rows, :]
        columns = slice(2 * pair * HS, (2 * pair + 2) * HS)
        key_ref[:, columns] = jnp.concatenate([first[:, :HS], second[:, :HS]], axis=1)
        value_ref[:, columns] = jnp.concatenate([first[:, HS:], second[:, HS:]], axis=1)
    up = up_ref[...]
    from_key = dot(key_ref[...], up, NT)
    from_value = dot(value_ref[...], up, NT)
    column = lax.broadcasted_iota(jnp.int32, from_key.shape, 1)
    low_grad_ref[...] = adapter_factor * jnp.where(column < rank, from_key, from_value)

    me = lax.axis_index("dp") * mp + lax.axis_index("mp")
    side = LANES // both_rank
    cuts = rows // CUT
    half = mp * CUT
    step = HS // dp
    lane = lax.broadcasted_iota(jnp.int32, (2 * step, LANES), 1) // both_rank
    total = jnp.zeros((2 * step, LANES), jnp.float32)
    lows = []
    for group in range(dp * cuts // side):
        at = rows + group * CUT
        lows.append(jnp.concatenate([got_ref[block, at:at + CUT, :] for block in range(mp)], axis=0))
    for s in range(dp):
        pack = lax.rem(lax.rem(me, dp) + dp - s, dp)
        for cut in range(cuts):
            piece = piece_refs[s][:, cut * half:(cut + 1) * half]
            slot = pack * cuts + cut
            for group, low in enumerate(lows):
                product = jnp.dot(piece, low, preferred_element_type=jnp.float32)
                total += jnp.where(lane + group * side == slot, product, 0.0)
    share = total[:, :both_rank]
    for at in range(1, side):
        share += total[:, at * both_rank:(at + 1) * both_rank]
    column = lax.broadcasted_iota(jnp.int32, (step, both_rank), 1)
    up_grad_ref[...] = adapter_factor * jnp.where(column < rank, share[:step], share[step:])


def local(dp, mp, query, kv_cache, out_grad, source_lengths, target_lengths, low_rank, adapter_up_matrix):
    tgt_count = query.shape[0]
    src_count = kv_cache.shape[0]
    rows, both_rank = low_rank.shape
    width = adapter_up_matrix.shape[1]
    step = HS // dp
    low_rows = dp * rows * both_rank // LANES
    vmem = pl.BlockSpec(memory_space=pltpu.VMEM)
    hbm = pl.BlockSpec(memory_space=pl.ANY)
    params = pltpu.CompilerParams(vmem_limit_bytes=48 * 1024 * 1024)
    whole_vmem = pltpu.CompilerParams(vmem_limit_bytes=60 * 1024 * 1024)

    seen = [low_rank]
    for s in range(1, dp):
        seen.append(lax.ppermute(low_rank, "dp", [(d, (d + s) % dp) for d in range(dp)]))

    query_t = query.T
    grad_t = out_grad.T
    query_grad_t, both_grad, *pieces = pl.pallas_call(
        functools.partial(attention_kernel, rows),
        out_shape=[
            jax.ShapeDtypeStruct((HS, tgt_count), jnp.bfloat16),
            jax.ShapeDtypeStruct((mp, rows, LANES), jnp.bfloat16),
        ] + [jax.ShapeDtypeStruct((2 * step, src_count), jnp.bfloat16)] * dp,
        in_specs=[hbm] * 5,
        out_specs=[vmem] * (2 + dp),
        scratch_shapes=[
            pltpu.SMEM(source_lengths.shape, jnp.int32),
            pltpu.SMEM(target_lengths.shape, jnp.int32),
            pltpu.VMEM(query_t.shape, jnp.bfloat16),
            pltpu.VMEM(grad_t.shape, jnp.bfloat16),
            pltpu.VMEM(kv_cache.shape, jnp.bfloat16),
            pltpu.VMEM((dp, 2 * step, src_count), jnp.bfloat16),
            pltpu.SemaphoreType.DMA((5,)),
        ],
        compiler_params=whole_vmem,
        cost_estimate=pl.CostEstimate(
            flops=10 * tgt_count * src_count * 2 * HS, bytes_accessed=2 ** 23, transcendentals=0
        ),
        name="attention_backward",
    )(source_lengths, target_lengths, query_t, grad_t, kv_cache)

    sent = pl.pallas_call(
        functools.partial(low_rank_kernel, rows),
        out_shape=jax.ShapeDtypeStruct((mp, rows + low_rows, LANES), jnp.bfloat16),
        in_specs=[vmem] * (1 + dp),
        out_specs=vmem,
        compiler_params=params,
        name="low_rank_rows",
    )(both_grad, *seen)
    got = lax.all_to_all(sent, "mp", split_axis=0, concat_axis=0, tiled=True)

    arrived = []
    for s in range(dp):
        route = [(d * mp + h, h * dp + (d + s) % dp) for d in range(dp) for h in range(mp)]
        arrived.append(lax.ppermute(pieces[s], ("dp", "mp"), route))

    key_gradient, value_grad, low_grad, up_grad = pl.pallas_call(
        functools.partial(owner_kernel, dp, mp),
        out_shape=[
            jax.ShapeDtypeStruct((rows, width), jnp.bfloat16),
            jax.ShapeDtypeStruct((rows, width), jnp.bfloat16),
            jax.ShapeDtypeStruct((rows, both_rank), jnp.float32),
            jax.ShapeDtypeStruct((step, both_rank), jnp.float32),
        ],
        in_specs=[vmem] * (2 + dp),
        out_specs=[vmem] * 4,
        compiler_params=params,
        name="owner_outputs",
    )(got, adapter_up_matrix, *arrived)
    return query_grad_t.T, key_gradient, value_grad, low_grad, up_grad


def solution(mesh):
    in_specs = (
        P("dp", "mp"),
        P("dp", "mp"),
        P("dp", "mp"),
        P("dp", None),
        P("dp", None),
        P(("dp", "mp"), None),
        P(),
    )
    out_specs = (
        P("dp", "mp"),
        P(("dp", "mp"), None),
        P(("dp", "mp"), None),
        P(("dp", "mp"), None),
        P(("dp", "mp"), None),
    )
    body = functools.partial(local, mesh.shape["dp"], mesh.shape["mp"])
    return jax.shard_map(body, mesh=mesh, in_specs=in_specs, out_specs=out_specs, check_vma=False)
```

```python
import functools

import jax
import jax.numpy as jnp
from jax import lax
from jax.experimental import pallas as pl
from jax.experimental.pallas import tpu as pltpu
from jax.sharding import PartitionSpec as P

HS = 64
LANES = 128
CUT = 16

adapter_factor = 2.0

NT = (((1,), (1,)), ((), ()))
TN = (((0,), (0,)), ((), ()))


def dot(left, right, dims):
    return lax.dot_general(left, right, dims, preferred_element_type=jnp.float32)


def spread_order(count):
    bits = count.bit_length() - 1
    assert count == 1 << bits
    return [sum(((i >> b) & 1) << (bits - 1 - b) for b in range(bits)) for i in range(count)]


def source_range(source_ref, target_ref, count):
    position = lax.broadcasted_iota(jnp.int32, (1, count), 1)
    first = jnp.zeros((1, count), jnp.int32)
    last = jnp.zeros((1, count), jnp.int32)
    target_start = jnp.int32(0)
    source_start = jnp.int32(0)
    for i in range(source_ref.shape[1]):
        source_end = source_start + source_ref[0, i]
        inside = position >= target_start
        first = jnp.where(inside, source_start, first)
        last = jnp.where(inside, source_end, last)
        target_start = target_start + target_ref[0, i]
        source_start = source_end
    return first, last


def attention_kernel(
    rows, source_any, target_any, query_any, grad_any, kv_any, query_grad_ref, both_grad_ref, *refs
):
    *piece_refs, source_ref, target_ref, query_ref, grad_ref, kv_ref, pieces, sems = refs
    pairs = [
        (kv_any, kv_ref), (query_any, query_ref), (grad_any, grad_ref),
        (source_any, source_ref), (target_any, target_ref),
    ]
    copies = [
        pltpu.make_async_copy(here, there, sems.at[i]) for i, (here, there) in enumerate(pairs)
    ]
    for copy in copies:
        copy.start()
    for copy in copies:
        copy.wait()
    tgt_count = query_ref.shape[1]
    both = kv_ref[...]
    query_t = query_ref[...]
    grad_t = grad_ref[...]
    blank = jnp.zeros_like(query_t)
    query_wide = jnp.concatenate([query_t, blank], axis=0)
    grad_wide = jnp.concatenate([blank, grad_t], axis=0)
    scores = jnp.dot(both, query_wide, preferred_element_type=jnp.float32)
    dprob = jnp.dot(both, grad_wide, preferred_element_type=jnp.float32)
    first, last = source_range(source_ref, target_ref, tgt_count)
    position = lax.broadcasted_iota(jnp.int32, scores.shape, 0)
    allowed = jnp.logical_and(position >= first, position < last)
    expo = jnp.where(allowed, jnp.exp(scores), 0.0)
    total = jnp.sum(expo, axis=0, keepdims=True)
    delta = jnp.sum(expo * dprob, axis=0, keepdims=True) / total
    prob = expo * (1.0 / total)
    prob_low = prob.astype(jnp.bfloat16)
    dscore = (prob * (dprob - delta)).astype(jnp.bfloat16)
    both_grad = dot(dscore, query_wide, NT) + dot(prob_low, grad_wide, NT)
    both_low = both_grad.astype(jnp.bfloat16)
    blocks = both_grad_ref.shape[0]
    for at, block in enumerate(spread_order(blocks)):
        both_grad_ref[at] = both_low[block * rows:(block + 1) * rows]

    order = []
    for start in range(0, rows, CUT):
        for block in range(blocks):
            order.append(both_low[block * rows + start:block * rows + start + CUT])
    turned = jnp.concatenate(order, axis=0).astype(jnp.float32).T.astype(jnp.bfloat16)
    mine = lax.axis_index("dp")
    dp = len(piece_refs)
    step = HS // dp
    for j in range(dp):
        pieces[j] = jnp.concatenate(
            [turned[j * step:(j + 1) * step], turned[HS + j * step:HS + (j + 1) * step]], axis=0
        )
    for s in range(dp):
        piece_refs[s][...] = pieces[lax.rem(mine + s, dp)]

    query_grad = dot(both, dscore, TN)
    query_grad_ref[...] = query_grad[:HS].astype(jnp.bfloat16)


def low_rank_kernel(rows, both_grad_ref, *refs):
    *low_refs, out_ref = refs
    mine = lax.axis_index("dp")
    dp = len(low_refs)
    both_rank = low_refs[0].shape[1]
    side = LANES // both_rank
    parts = []
    for pack in range(dp):
        low = low_refs[0][...]
        for s in range(1, dp):
            low = jnp.where(lax.rem(mine + dp - s, dp) == pack, low_refs[s][...], low)
        parts.extend(low[at:at + CUT] for at in range(0, rows, CUT))
    packed = [jnp.concatenate(parts[at:at + side], axis=1) for at in range(0, len(parts), side)]
    for block in range(out_ref.shape[0]):
        out_ref[block, :rows, :] = both_grad_ref[block]
        for group, part in enumerate(packed):
            out_ref[block, rows + group * CUT:rows + (group + 1) * CUT, :] = part


def owner_kernel(dp, mp, got_ref, up_ref, *refs):
    piece_refs = refs[:dp]
    key_ref, value_ref, low_grad_ref, up_grad_ref = refs[dp:dp + 4]
    rows = key_ref.shape[0]
    both_rank = up_ref.shape[0]
    rank = both_rank // 2
    places = spread_order(mp)
    for pair in range(mp // 2):
        first = got_ref[places.index(2 * pair), :rows, :]
        second = got_ref[places.index(2 * pair + 1), :rows, :]
        columns = slice(2 * pair * HS, (2 * pair + 2) * HS)
        key_ref[:, columns] = jnp.concatenate([first[:, :HS], second[:, :HS]], axis=1)
        value_ref[:, columns] = jnp.concatenate([first[:, HS:], second[:, HS:]], axis=1)
    up = up_ref[...]
    from_key = dot(key_ref[...], up, NT)
    from_value = dot(value_ref[...], up, NT)
    column = lax.broadcasted_iota(jnp.int32, from_key.shape, 1)
    low_grad_ref[...] = adapter_factor * jnp.where(column < rank, from_key, from_value)

    me = lax.axis_index("dp") * mp + lax.axis_index("mp")
    side = LANES // both_rank
    cuts = rows // CUT
    half = mp * CUT
    step = HS // dp
    lane = lax.broadcasted_iota(jnp.int32, (2 * step, LANES), 1) // both_rank
    total = jnp.zeros((2 * step, LANES), jnp.float32)
    lows = []
    for group in range(dp * cuts // side):
        at = rows + group * CUT
        lows.append(jnp.concatenate([got_ref[place, at:at + CUT, :] for place in places], axis=0))
    for s in range(dp):
        pack = lax.rem(lax.rem(me, dp) + dp - s, dp)
        for cut in range(cuts):
            piece = piece_refs[s][:, cut * half:(cut + 1) * half]
            slot = pack * cuts + cut
            for group, low in enumerate(lows):
                product = jnp.dot(piece, low, preferred_element_type=jnp.float32)
                total += jnp.where(lane + group * side == slot, product, 0.0)
    share = total[:, :both_rank]
    for at in range(1, side):
        share += total[:, at * both_rank:(at + 1) * both_rank]
    column = lax.broadcasted_iota(jnp.int32, (step, both_rank), 1)
    up_grad_ref[...] = adapter_factor * jnp.where(column < rank, share[:step], share[step:])


def local(dp, mp, query, kv_cache, out_grad, source_lengths, target_lengths, low_rank, adapter_up_matrix):
    tgt_count = query.shape[0]
    src_count = kv_cache.shape[0]
    rows, both_rank = low_rank.shape
    width = adapter_up_matrix.shape[1]
    step = HS // dp
    low_rows = dp * rows * both_rank // LANES
    vmem = pl.BlockSpec(memory_space=pltpu.VMEM)
    hbm = pl.BlockSpec(memory_space=pl.ANY)
    params = pltpu.CompilerParams(vmem_limit_bytes=48 * 1024 * 1024)
    whole_vmem = pltpu.CompilerParams(vmem_limit_bytes=60 * 1024 * 1024)

    seen = [low_rank]
    for s in range(1, dp):
        seen.append(lax.ppermute(low_rank, "dp", [(d, (d + s) % dp) for d in range(dp)]))

    query_t = query.T
    grad_t = out_grad.T
    query_grad_t, both_grad, *pieces = pl.pallas_call(
        functools.partial(attention_kernel, rows),
        out_shape=[
            jax.ShapeDtypeStruct((HS, tgt_count), jnp.bfloat16),
            jax.ShapeDtypeStruct((mp, rows, LANES), jnp.bfloat16),
        ] + [jax.ShapeDtypeStruct((2 * step, src_count), jnp.bfloat16)] * dp,
        in_specs=[hbm] * 5,
        out_specs=[vmem] * (2 + dp),
        scratch_shapes=[
            pltpu.SMEM(source_lengths.shape, jnp.int32),
            pltpu.SMEM(target_lengths.shape, jnp.int32),
            pltpu.VMEM(query_t.shape, jnp.bfloat16),
            pltpu.VMEM(grad_t.shape, jnp.bfloat16),
            pltpu.VMEM(kv_cache.shape, jnp.bfloat16),
            pltpu.VMEM((dp, 2 * step, src_count), jnp.bfloat16),
            pltpu.SemaphoreType.DMA((5,)),
        ],
        compiler_params=whole_vmem,
        cost_estimate=pl.CostEstimate(
            flops=10 * tgt_count * src_count * 2 * HS, bytes_accessed=2 ** 23, transcendentals=0
        ),
        name="attention_backward",
    )(source_lengths, target_lengths, query_t, grad_t, kv_cache)

    sent = pl.pallas_call(
        functools.partial(low_rank_kernel, rows),
        out_shape=jax.ShapeDtypeStruct((mp, rows + low_rows, LANES), jnp.bfloat16),
        in_specs=[vmem] * (1 + dp),
        out_specs=vmem,
        compiler_params=params,
        name="low_rank_rows",
    )(both_grad, *seen)
    got = lax.all_to_all(
        sent, "mp", split_axis=0, concat_axis=0, axis_index_groups=[spread_order(mp)], tiled=True
    )

    arrived = []
    for s in range(dp):
        route = [(d * mp + h, h * dp + (d + s) % dp) for d in range(dp) for h in range(mp)]
        arrived.append(lax.ppermute(pieces[s], ("dp", "mp"), route))

    key_gradient, value_grad, low_grad, up_grad = pl.pallas_call(
        functools.partial(owner_kernel, dp, mp),
        out_shape=[
            jax.ShapeDtypeStruct((rows, width), jnp.bfloat16),
            jax.ShapeDtypeStruct((rows, width), jnp.bfloat16),
            jax.ShapeDtypeStruct((rows, both_rank), jnp.float32),
            jax.ShapeDtypeStruct((step, both_rank), jnp.float32),
        ],
        in_specs=[vmem] * (2 + dp),
        out_specs=[vmem] * 4,
        compiler_params=params,
        name="owner_outputs",
    )(got, adapter_up_matrix, *arrived)
    return query_grad_t.T, key_gradient, value_grad, low_grad, up_grad


def solution(mesh):
    in_specs = (
        P("dp", "mp"),
        P("dp", "mp"),
        P("dp", "mp"),
        P("dp", None),
        P("dp", None),
        P(("dp", "mp"), None),
        P(),
    )
    out_specs = (
        P("dp", "mp"),
        P(("dp", "mp"), None),
        P(("dp", "mp"), None),
        P(("dp", "mp"), None),
        P(("dp", "mp"), None),
    )
    body = functools.partial(local, mesh.shape["dp"], mesh.shape["mp"])
    return jax.shard_map(body, mesh=mesh, in_specs=in_specs, out_specs=out_specs, check_vma=False)
```

```python
import functools

import jax
import jax.numpy as jnp
from jax import lax
from jax.experimental import pallas as pl
from jax.experimental.pallas import tpu as pltpu
from jax.sharding import PartitionSpec as P

HS = 64
LANES = 128
CUT = 16

adapter_factor = 2.0

NT = (((1,), (1,)), ((), ()))
TN = (((0,), (0,)), ((), ()))


def dot(left, right, dims):
    return lax.dot_general(left, right, dims, preferred_element_type=jnp.float32)


def group_order(count):
    quarter = count // 4
    bits = quarter.bit_length() - 1
    assert count == 4 << bits
    turned = [sum(((i >> b) & 1) << (bits - 1 - b) for b in range(bits)) for i in range(quarter)]
    order = []
    for low, high in ((1, 2), (0, 3)):
        for i in range(0, quarter, 2):
            first, second = turned[i], turned[i + 1]
            order += [low * quarter + first, high * quarter + second]
            order += [low * quarter + second, high * quarter + first]
    return order


def source_range(source_ref, target_ref, count):
    position = lax.broadcasted_iota(jnp.int32, (1, count), 1)
    first = jnp.zeros((1, count), jnp.int32)
    last = jnp.zeros((1, count), jnp.int32)
    target_start = jnp.int32(0)
    source_start = jnp.int32(0)
    for i in range(source_ref.shape[1]):
        source_end = source_start + source_ref[0, i]
        inside = position >= target_start
        first = jnp.where(inside, source_start, first)
        last = jnp.where(inside, source_end, last)
        target_start = target_start + target_ref[0, i]
        source_start = source_end
    return first, last


def attention_kernel(
    source_any, target_any, query_any, grad_any, kv_any, low_any,
    query_grad_ref, sent_ref,
    source_ref, target_ref, query_ref, grad_ref, kv_ref, low_ref, sems,
):
    pairs = [
        (kv_any, kv_ref), (query_any, query_ref), (grad_any, grad_ref),
        (source_any, source_ref), (target_any, target_ref), (low_any, low_ref),
    ]
    copies = [
        pltpu.make_async_copy(here, there, sems.at[i]) for i, (here, there) in enumerate(pairs)
    ]
    for copy in copies:
        copy.start()
    for copy in copies:
        copy.wait()
    tgt_count = query_ref.shape[1]
    both = kv_ref[...]
    query_t = query_ref[...]
    grad_t = grad_ref[...]
    blank = jnp.zeros_like(query_t)
    query_wide = jnp.concatenate([query_t, blank], axis=0)
    grad_wide = jnp.concatenate([blank, grad_t], axis=0)
    scores = jnp.dot(both, query_wide, preferred_element_type=jnp.float32)
    dprob = jnp.dot(both, grad_wide, preferred_element_type=jnp.float32)
    first, last = source_range(source_ref, target_ref, tgt_count)
    position = lax.broadcasted_iota(jnp.int32, scores.shape, 0)
    allowed = jnp.logical_and(position >= first, position < last)
    expo = jnp.where(allowed, jnp.exp(scores), 0.0)
    total = jnp.sum(expo, axis=0, keepdims=True)
    delta = jnp.sum(expo * dprob, axis=0, keepdims=True) / total
    prob = expo * (1.0 / total)
    prob_low = prob.astype(jnp.bfloat16)
    dscore = (prob * (dprob - delta)).astype(jnp.bfloat16)
    both_grad = dot(dscore, query_wide, NT) + dot(prob_low, grad_wide, NT)
    both_low = both_grad.astype(jnp.bfloat16)
    low = low_ref[...]
    rows, both_rank = low.shape
    spread = [low[at:at + CUT] for at in range(0, rows, CUT)]
    spread.append(jnp.zeros((CUT, LANES - rows // CUT * both_rank), jnp.bfloat16))
    spread = jnp.concatenate(spread, axis=1)
    for at, block in enumerate(group_order(sent_ref.shape[0])):
        sent_ref[at, :rows, :] = both_low[block * rows:(block + 1) * rows]
        sent_ref[at, rows:, :] = spread
    query_grad = dot(both, dscore, TN)
    query_grad_ref[...] = query_grad[:HS].astype(jnp.bfloat16)


def share_kernel(rows, both_rank, sent_ref, got_ref, *out_refs):
    mine = lax.axis_index("dp")
    dp = len(out_refs)
    blocks = sent_ref.shape[0]
    tokens = jnp.concatenate([sent_ref[block, :rows, :] for block in range(blocks)], axis=0)
    lows = []
    for block in range(blocks):
        spread = got_ref[block, rows:, :]
        for at in range(rows // CUT):
            lows.append(spread[:, at * both_rank:(at + 1) * both_rank])
    share = dot(tokens, jnp.concatenate(lows, axis=0), TN)
    column = lax.broadcasted_iota(jnp.int32, (HS, both_rank), 1)
    share = adapter_factor * jnp.where(column < both_rank // 2, share[:HS], share[HS:])
    step = HS // dp
    for s, out_ref in enumerate(out_refs):
        turn = lax.rem(mine + s, dp)
        piece = share[:step]
        for j in range(1, dp):
            piece = jnp.where(turn == j, share[j * step:(j + 1) * step], piece)
        out_ref[...] = piece


def owner_kernel(up_ref, got_ref, key_ref, value_ref, low_grad_ref):
    rows = key_ref.shape[0]
    rank = up_ref.shape[0] // 2
    order = group_order(got_ref.shape[0])
    for pair in range(len(order) // 2):
        first = got_ref[order.index(2 * pair), :rows, :]
        second = got_ref[order.index(2 * pair + 1), :rows, :]
        columns = slice(2 * pair * HS, (2 * pair + 2) * HS)
        key_ref[:, columns] = jnp.concatenate([first[:, :HS], second[:, :HS]], axis=1)
        value_ref[:, columns] = jnp.concatenate([first[:, HS:], second[:, HS:]], axis=1)
    up = up_ref[...]
    from_key = dot(key_ref[...], up, NT)
    from_value = dot(value_ref[...], up, NT)
    column = lax.broadcasted_iota(jnp.int32, from_key.shape, 1)
    low_grad_ref[...] = adapter_factor * jnp.where(column < rank, from_key, from_value)


def local(dp, mp, query, kv_cache, out_grad, source_lengths, target_lengths, low_rank, adapter_up_matrix):
    tgt_count = query.shape[0]
    rows, both_rank = low_rank.shape
    width = adapter_up_matrix.shape[1]
    step = HS // dp
    vmem = pl.BlockSpec(memory_space=pltpu.VMEM)
    hbm = pl.BlockSpec(memory_space=pl.ANY)
    params = pltpu.CompilerParams(vmem_limit_bytes=48 * 1024 * 1024)
    whole_vmem = pltpu.CompilerParams(vmem_limit_bytes=60 * 1024 * 1024)

    query_t = query.T
    grad_t = out_grad.T
    query_grad_t, sent = pl.pallas_call(
        attention_kernel,
        out_shape=[
            jax.ShapeDtypeStruct((HS, tgt_count), jnp.bfloat16),
            jax.ShapeDtypeStruct((mp, rows + CUT, LANES), jnp.bfloat16),
        ],
        in_specs=[hbm] * 6,
        out_specs=[vmem] * 2,
        scratch_shapes=[
            pltpu.SMEM(source_lengths.shape, jnp.int32),
            pltpu.SMEM(target_lengths.shape, jnp.int32),
            pltpu.VMEM(query_t.shape, jnp.bfloat16),
            pltpu.VMEM(grad_t.shape, jnp.bfloat16),
            pltpu.VMEM(kv_cache.shape, jnp.bfloat16),
            pltpu.VMEM(low_rank.shape, jnp.bfloat16),
            pltpu.SemaphoreType.DMA((6,)),
        ],
        compiler_params=whole_vmem,
        name="attention_backward",
    )(source_lengths, target_lengths, query_t, grad_t, kv_cache, low_rank)

    got = lax.all_to_all(sent, "mp", 0, 0, axis_index_groups=[group_order(mp)], tiled=True)

    shares = pl.pallas_call(
        functools.partial(share_kernel, rows, both_rank),
        out_shape=[jax.ShapeDtypeStruct((step, both_rank), jnp.float32)] * dp,
        in_specs=[vmem] * 2,
        out_specs=[vmem] * dp,
        compiler_params=params,
        name="adapter_shares",
    )(sent, got)

    up_grad = None
    for s in range(dp):
        route = [(d * mp + h, h * dp + (d + s) % dp) for d in range(dp) for h in range(mp)]
        term = lax.ppermute(shares[s], ("dp", "mp"), route)
        up_grad = term if up_grad is None else up_grad + term

    key_gradient, value_grad, low_grad = pl.pallas_call(
        owner_kernel,
        out_shape=[
            jax.ShapeDtypeStruct((rows, width), jnp.bfloat16),
            jax.ShapeDtypeStruct((rows, width), jnp.bfloat16),
            jax.ShapeDtypeStruct((rows, both_rank), jnp.float32),
        ],
        in_specs=[vmem] * 2,
        out_specs=[vmem] * 3,
        compiler_params=params,
        name="owner_outputs",
    )(adapter_up_matrix, got)
    return query_grad_t.T, key_gradient, value_grad, low_grad, up_grad


def solution(mesh):
    in_specs = (
        P("dp", "mp"),
        P("dp", "mp"),
        P("dp", "mp"),
        P("dp", None),
        P("dp", None),
        P(("dp", "mp"), None),
        P(),
    )
    out_specs = (
        P("dp", "mp"),
        P(("dp", "mp"), None),
        P(("dp", "mp"), None),
        P(("dp", "mp"), None),
        P(("dp", "mp"), None),
    )
    body = functools.partial(local, mesh.shape["dp"], mesh.shape["mp"])
    return jax.shard_map(body, mesh=mesh, in_specs=in_specs, out_specs=out_specs, check_vma=False)
```

```python
import functools

import jax
import jax.numpy as jnp
from jax import lax
from jax.experimental import pallas as pl
from jax.experimental.pallas import tpu as pltpu
from jax.sharding import PartitionSpec as P

HS = 64
LANES = 128
CUT = 16

adapter_factor = 2.0

NT = (((1,), (1,)), ((), ()))
TN = (((0,), (0,)), ((), ()))


def dot(left, right, dims):
    return lax.dot_general(left, right, dims, preferred_element_type=jnp.float32)


def group_order(count):
    quarter = count // 4
    bits = quarter.bit_length() - 1
    assert count == 4 << bits
    turned = [sum(((i >> b) & 1) << (bits - 1 - b) for b in range(bits)) for i in range(quarter)]
    order = []
    for low, high in ((1, 2), (0, 3)):
        for i in range(0, quarter, 2):
            first, second = turned[i], turned[i + 1]
            order += [low * quarter + first, high * quarter + second]
            order += [low * quarter + second, high * quarter + first]
    return order


def source_range(source_ref, target_ref, count):
    position = lax.broadcasted_iota(jnp.int32, (1, count), 1)
    first = jnp.zeros((1, count), jnp.int32)
    last = jnp.zeros((1, count), jnp.int32)
    target_start = jnp.int32(0)
    source_start = jnp.int32(0)
    for i in range(source_ref.shape[1]):
        source_end = source_start + source_ref[0, i]
        inside = position >= target_start
        first = jnp.where(inside, source_start, first)
        last = jnp.where(inside, source_end, last)
        target_start = target_start + target_ref[0, i]
        source_start = source_end
    return first, last


def attention_kernel(
    rows, source_any, target_any, query_any, grad_any, kv_any, query_grad_ref, both_grad_ref, *refs
):
    *piece_refs, source_ref, target_ref, query_ref, grad_ref, kv_ref, pieces, sems = refs
    pairs = [
        (kv_any, kv_ref), (query_any, query_ref), (grad_any, grad_ref),
        (source_any, source_ref), (target_any, target_ref),
    ]
    copies = [
        pltpu.make_async_copy(here, there, sems.at[i]) for i, (here, there) in enumerate(pairs)
    ]
    for copy in copies:
        copy.start()
    for copy in copies:
        copy.wait()
    tgt_count = query_ref.shape[1]
    both = kv_ref[...]
    query_t = query_ref[...]
    grad_t = grad_ref[...]
    blank = jnp.zeros_like(query_t)
    query_wide = jnp.concatenate([query_t, blank], axis=0)
    grad_wide = jnp.concatenate([blank, grad_t], axis=0)
    scores = jnp.dot(both, query_wide, preferred_element_type=jnp.float32)
    dprob = jnp.dot(both, grad_wide, preferred_element_type=jnp.float32)
    first, last = source_range(source_ref, target_ref, tgt_count)
    position = lax.broadcasted_iota(jnp.int32, scores.shape, 0)
    allowed = jnp.logical_and(position >= first, position < last)
    expo = jnp.where(allowed, jnp.exp(scores), 0.0)
    total = jnp.sum(expo, axis=0, keepdims=True)
    delta = jnp.sum(expo * dprob, axis=0, keepdims=True) / total
    prob = expo * (1.0 / total)
    prob_low = prob.astype(jnp.bfloat16)
    dscore = (prob * (dprob - delta)).astype(jnp.bfloat16)
    both_grad = dot(dscore, query_wide, NT) + dot(prob_low, grad_wide, NT)
    both_low = both_grad.astype(jnp.bfloat16)
    blocks = both_grad_ref.shape[0]
    for at, block in enumerate(group_order(blocks)):
        both_grad_ref[at] = both_low[block * rows:(block + 1) * rows]

    order = []
    for start in range(0, rows, CUT):
        for block in range(blocks):
            order.append(both_low[block * rows + start:block * rows + start + CUT])
    turned = jnp.concatenate(order, axis=0).astype(jnp.float32).T.astype(jnp.bfloat16)
    mine = lax.axis_index("dp")
    dp = len(piece_refs)
    step = HS // dp
    for j in range(dp):
        pieces[j] = jnp.concatenate(
            [turned[j * step:(j + 1) * step], turned[HS + j * step:HS + (j + 1) * step]], axis=0
        )
    for s in range(dp):
        piece_refs[s][...] = pieces[lax.rem(mine + s, dp)]

    query_grad = dot(both, dscore, TN)
    query_grad_ref[...] = query_grad[:HS].astype(jnp.bfloat16)


def low_rank_kernel(rows, both_grad_ref, *refs):
    *low_refs, out_ref = refs
    mine = lax.axis_index("dp")
    dp = len(low_refs)
    both_rank = low_refs[0].shape[1]
    side = LANES // both_rank
    parts = []
    for pack in range(dp):
        low = low_refs[0][...]
        for s in range(1, dp):
            low = jnp.where(lax.rem(mine + dp - s, dp) == pack, low_refs[s][...], low)
        parts.extend(low[at:at + CUT] for at in range(0, rows, CUT))
    packed = [jnp.concatenate(parts[at:at + side], axis=1) for at in range(0, len(parts), side)]
    for block in range(out_ref.shape[0]):
        out_ref[block, :rows, :] = both_grad_ref[block]
        for group, part in enumerate(packed):
            out_ref[block, rows + group * CUT:rows + (group + 1) * CUT, :] = part


def owner_kernel(dp, mp, got_ref, up_ref, *refs):
    piece_refs = refs[:dp]
    key_ref, value_ref, low_grad_ref, up_grad_ref = refs[dp:dp + 4]
    rows = key_ref.shape[0]
    both_rank = up_ref.shape[0]
    rank = both_rank // 2
    order = group_order(mp)
    places = [order.index(block) for block in range(mp)]
    for pair in range(mp // 2):
        first = got_ref[places[2 * pair], :rows, :]
        second = got_ref[places[2 * pair + 1], :rows, :]
        columns = slice(2 * pair * HS, (2 * pair + 2) * HS)
        key_ref[:, columns] = jnp.concatenate([first[:, :HS], second[:, :HS]], axis=1)
        value_ref[:, columns] = jnp.concatenate([first[:, HS:], second[:, HS:]], axis=1)
    up = up_ref[...]
    from_key = dot(key_ref[...], up, NT)
    from_value = dot(value_ref[...], up, NT)
    column = lax.broadcasted_iota(jnp.int32, from_key.shape, 1)
    low_grad_ref[...] = adapter_factor * jnp.where(column < rank, from_key, from_value)

    me = lax.axis_index("dp") * mp + lax.axis_index("mp")
    side = LANES // both_rank
    cuts = rows // CUT
    half = mp * CUT
    step = HS // dp
    lane = lax.broadcasted_iota(jnp.int32, (2 * step, LANES), 1) // both_rank
    total = jnp.zeros((2 * step, LANES), jnp.float32)
    lows = []
    for group in range(dp * cuts // side):
        at = rows + group * CUT
        lows.append(jnp.concatenate([got_ref[place, at:at + CUT, :] for place in places], axis=0))
    for s in range(dp):
        pack = lax.rem(lax.rem(me, dp) + dp - s, dp)
        for cut in range(cuts):
            piece = piece_refs[s][:, cut * half:(cut + 1) * half]
            slot = pack * cuts + cut
            for group, low in enumerate(lows):
                product = jnp.dot(piece, low, preferred_element_type=jnp.float32)
                total += jnp.where(lane + group * side == slot, product, 0.0)
    share = total[:, :both_rank]
    for at in range(1, side):
        share += total[:, at * both_rank:(at + 1) * both_rank]
    column = lax.broadcasted_iota(jnp.int32, (step, both_rank), 1)
    up_grad_ref[...] = adapter_factor * jnp.where(column < rank, share[:step], share[step:])


def local(dp, mp, query, kv_cache, out_grad, source_lengths, target_lengths, low_rank, adapter_up_matrix):
    tgt_count = query.shape[0]
    src_count = kv_cache.shape[0]
    rows, both_rank = low_rank.shape
    width = adapter_up_matrix.shape[1]
    step = HS // dp
    low_rows = dp * rows * both_rank // LANES
    vmem = pl.BlockSpec(memory_space=pltpu.VMEM)
    hbm = pl.BlockSpec(memory_space=pl.ANY)
    params = pltpu.CompilerParams(vmem_limit_bytes=48 * 1024 * 1024)
    whole_vmem = pltpu.CompilerParams(vmem_limit_bytes=60 * 1024 * 1024)

    seen = [low_rank]
    for s in range(1, dp):
        seen.append(lax.ppermute(low_rank, "dp", [(d, (d + s) % dp) for d in range(dp)]))

    query_t = query.T
    grad_t = out_grad.T
    query_grad_t, both_grad, *pieces = pl.pallas_call(
        functools.partial(attention_kernel, rows),
        out_shape=[
            jax.ShapeDtypeStruct((HS, tgt_count), jnp.bfloat16),
            jax.ShapeDtypeStruct((mp, rows, LANES), jnp.bfloat16),
        ] + [jax.ShapeDtypeStruct((2 * step, src_count), jnp.bfloat16)] * dp,
        in_specs=[hbm] * 5,
        out_specs=[vmem] * (2 + dp),
        scratch_shapes=[
            pltpu.SMEM(source_lengths.shape, jnp.int32),
            pltpu.SMEM(target_lengths.shape, jnp.int32),
            pltpu.VMEM(query_t.shape, jnp.bfloat16),
            pltpu.VMEM(grad_t.shape, jnp.bfloat16),
            pltpu.VMEM(kv_cache.shape, jnp.bfloat16),
            pltpu.VMEM((dp, 2 * step, src_count), jnp.bfloat16),
            pltpu.SemaphoreType.DMA((5,)),
        ],
        compiler_params=whole_vmem,
        cost_estimate=pl.CostEstimate(
            flops=10 * tgt_count * src_count * 2 * HS, bytes_accessed=2 ** 23, transcendentals=0
        ),
        name="attention_backward",
    )(source_lengths, target_lengths, query_t, grad_t, kv_cache)

    sent = pl.pallas_call(
        functools.partial(low_rank_kernel, rows),
        out_shape=jax.ShapeDtypeStruct((mp, rows + low_rows, LANES), jnp.bfloat16),
        in_specs=[vmem] * (1 + dp),
        out_specs=vmem,
        compiler_params=params,
        name="low_rank_rows",
    )(both_grad, *seen)
    got = lax.all_to_all(
        sent, "mp", split_axis=0, concat_axis=0, axis_index_groups=[group_order(mp)], tiled=True
    )

    arrived = []
    for s in range(dp):
        route = [(d * mp + h, h * dp + (d + s) % dp) for d in range(dp) for h in range(mp)]
        arrived.append(lax.ppermute(pieces[s], ("dp", "mp"), route))

    key_gradient, value_grad, low_grad, up_grad = pl.pallas_call(
        functools.partial(owner_kernel, dp, mp),
        out_shape=[
            jax.ShapeDtypeStruct((rows, width), jnp.bfloat16),
            jax.ShapeDtypeStruct((rows, width), jnp.bfloat16),
            jax.ShapeDtypeStruct((rows, both_rank), jnp.float32),
            jax.ShapeDtypeStruct((step, both_rank), jnp.float32),
        ],
        in_specs=[vmem] * (2 + dp),
        out_specs=[vmem] * 4,
        compiler_params=params,
        name="owner_outputs",
    )(got, adapter_up_matrix, *arrived)
    return query_grad_t.T, key_gradient, value_grad, low_grad, up_grad


def solution(mesh):
    in_specs = (
        P("dp", "mp"),
        P("dp", "mp"),
        P("dp", "mp"),
        P("dp", None),
        P("dp", None),
        P(("dp", "mp"), None),
        P(),
    )
    out_specs = (
        P("dp", "mp"),
        P(("dp", "mp"), None),
        P(("dp", "mp"), None),
        P(("dp", "mp"), None),
        P(("dp", "mp"), None),
    )
    body = functools.partial(local, mesh.shape["dp"], mesh.shape["mp"])
    return jax.shard_map(body, mesh=mesh, in_specs=in_specs, out_specs=out_specs, check_vma=False)
```

```python
import functools

import jax
import jax.numpy as jnp
from jax import lax
from jax.experimental import pallas as pl
from jax.experimental.pallas import tpu as pltpu
from jax.sharding import PartitionSpec as P

HS = 64
LANES = 128
CUT = 16

adapter_factor = 2.0

NT = (((1,), (1,)), ((), ()))
TN = (((0,), (0,)), ((), ()))


def dot(left, right, dims):
    return lax.dot_general(left, right, dims, preferred_element_type=jnp.float32)


def group_order(count):
    quarter = count // 4
    bits = quarter.bit_length() - 1
    assert count == 4 << bits
    turned = [sum(((i >> b) & 1) << (bits - 1 - b) for b in range(bits)) for i in range(quarter)]
    order = []
    for low, high in ((1, 2), (0, 3)):
        for i in range(0, quarter, 2):
            first, second = turned[i], turned[i + 1]
            order += [low * quarter + first, high * quarter + second]
            order += [low * quarter + second, high * quarter + first]
    return order


def source_range(source_ref, target_ref, count):
    position = lax.broadcasted_iota(jnp.int32, (1, count), 1)
    first = jnp.zeros((1, count), jnp.int32)
    last = jnp.zeros((1, count), jnp.int32)
    target_start = jnp.int32(0)
    source_start = jnp.int32(0)
    for i in range(source_ref.shape[1]):
        source_end = source_start + source_ref[0, i]
        inside = position >= target_start
        first = jnp.where(inside, source_start, first)
        last = jnp.where(inside, source_end, last)
        target_start = target_start + target_ref[0, i]
        source_start = source_end
    return first, last


def attention_kernel(
    rows, source_any, target_any, query_any, grad_any, kv_any, query_grad_ref, both_grad_ref, *refs
):
    *piece_refs, source_ref, target_ref, query_ref, grad_ref, kv_ref, pieces, sems = refs
    pairs = [
        (kv_any, kv_ref), (query_any, query_ref), (grad_any, grad_ref),
        (source_any, source_ref), (target_any, target_ref),
    ]
    copies = [
        pltpu.make_async_copy(here, there, sems.at[i]) for i, (here, there) in enumerate(pairs)
    ]
    for copy in copies:
        copy.start()
    for copy in copies:
        copy.wait()
    tgt_count = query_ref.shape[1]
    both = kv_ref[...]
    query_t = query_ref[...]
    grad_t = grad_ref[...]
    blank = jnp.zeros_like(query_t)
    query_wide = jnp.concatenate([query_t, blank], axis=0)
    grad_wide = jnp.concatenate([blank, grad_t], axis=0)
    scores = jnp.dot(both, query_wide, preferred_element_type=jnp.float32)
    dprob = jnp.dot(both, grad_wide, preferred_element_type=jnp.float32)
    first, last = source_range(source_ref, target_ref, tgt_count)
    position = lax.broadcasted_iota(jnp.int32, scores.shape, 0)
    allowed = jnp.logical_and(position >= first, position < last)
    expo = jnp.where(allowed, jnp.exp(scores), 0.0)
    total = jnp.sum(expo, axis=0, keepdims=True)
    delta = jnp.sum(expo * dprob, axis=0, keepdims=True) / total
    prob = expo * (1.0 / total)
    prob_low = prob.astype(jnp.bfloat16)
    dscore = (prob * (dprob - delta)).astype(jnp.bfloat16)
    both_grad = dot(dscore, query_wide, NT) + dot(prob_low, grad_wide, NT)
    both_low = both_grad.astype(jnp.bfloat16)
    blocks = both_grad_ref.shape[0]
    for at, block in enumerate(group_order(blocks)):
        both_grad_ref[at] = both_low[block * rows:(block + 1) * rows]

    order = []
    for start in range(0, rows, CUT):
        for block in range(blocks):
            order.append(both_low[block * rows + start:block * rows + start + CUT])
    turned = jnp.concatenate(order, axis=0).astype(jnp.float32).T.astype(jnp.bfloat16)
    mine = lax.axis_index("dp")
    dp = len(piece_refs)
    step = HS // dp
    for j in range(dp):
        pieces[j] = jnp.concatenate(
            [turned[j * step:(j + 1) * step], turned[HS + j * step:HS + (j + 1) * step]], axis=0
        )
    for s in range(dp):
        piece_refs[s][...] = pieces[lax.rem(mine + s, dp)]

    query_grad = dot(both, dscore, TN)
    query_grad_ref[...] = query_grad[:HS].astype(jnp.bfloat16)


def low_rank_kernel(rows, both_grad_ref, *refs):
    *low_refs, out_ref = refs
    mine = lax.axis_index("dp")
    dp = len(low_refs)
    both_rank = low_refs[0].shape[1]
    side = LANES // both_rank
    parts = []
    for pack in range(dp):
        low = low_refs[0][...]
        for s in range(1, dp):
            low = jnp.where(lax.rem(mine + dp - s, dp) == pack, low_refs[s][...], low)
        parts.extend(low[at:at + CUT] for at in range(0, rows, CUT))
    packed = [jnp.concatenate(parts[at:at + side], axis=1) for at in range(0, len(parts), side)]
    for block in range(out_ref.shape[0]):
        out_ref[block, :rows, :] = both_grad_ref[block]
        for group, part in enumerate(packed):
            out_ref[block, rows + group * CUT:rows + (group + 1) * CUT, :] = part


def order_kernel(*refs):
    *arrived_refs, out_ref = refs
    dp = len(arrived_refs)
    me = lax.axis_index("dp") * lax.axis_size("mp") + lax.axis_index("mp")
    for s, arrived_ref in enumerate(arrived_refs):
        out_ref[lax.rem(lax.rem(me, dp) + dp - s, dp)] = arrived_ref[...]


def owner_kernel(dp, mp, got_ref, up_ref, pieces_ref, key_ref, value_ref, low_grad_ref, up_grad_ref):
    rows = key_ref.shape[0]
    both_rank = up_ref.shape[0]
    rank = both_rank // 2
    order = group_order(mp)
    places = [order.index(block) for block in range(mp)]
    for pair in range(mp // 2):
        first = got_ref[places[2 * pair], :rows, :]
        second = got_ref[places[2 * pair + 1], :rows, :]
        columns = slice(2 * pair * HS, (2 * pair + 2) * HS)
        key_ref[:, columns] = jnp.concatenate([first[:, :HS], second[:, :HS]], axis=1)
        value_ref[:, columns] = jnp.concatenate([first[:, HS:], second[:, HS:]], axis=1)
    up = up_ref[...]
    from_key = dot(key_ref[...], up, NT)
    from_value = dot(value_ref[...], up, NT)
    column = lax.broadcasted_iota(jnp.int32, from_key.shape, 1)
    low_grad_ref[...] = adapter_factor * jnp.where(column < rank, from_key, from_value)

    side = LANES // both_rank
    cuts = rows // CUT
    half = mp * CUT
    step = HS // dp
    lane = lax.broadcasted_iota(jnp.int32, (2 * step, LANES), 1) // both_rank
    total = jnp.zeros((2 * step, LANES), jnp.float32)
    lows = []
    for group in range(dp * cuts // side):
        at = rows + group * CUT
        lows.append(jnp.concatenate([got_ref[place, at:at + CUT, :] for place in places], axis=0))
    for pack in range(dp):
        for cut in range(cuts):
            piece = pieces_ref[pack, :, cut * half:(cut + 1) * half]
            slot = pack * cuts + cut
            product = jnp.dot(piece, lows[slot // side], preferred_element_type=jnp.float32)
            total += jnp.where(lane == slot % side, product, 0.0)
    share = total[:, :both_rank]
    for at in range(1, side):
        share += total[:, at * both_rank:(at + 1) * both_rank]
    column = lax.broadcasted_iota(jnp.int32, (step, both_rank), 1)
    up_grad_ref[...] = adapter_factor * jnp.where(column < rank, share[:step], share[step:])


def local(dp, mp, query, kv_cache, out_grad, source_lengths, target_lengths, low_rank, adapter_up_matrix):
    tgt_count = query.shape[0]
    src_count = kv_cache.shape[0]
    rows, both_rank = low_rank.shape
    width = adapter_up_matrix.shape[1]
    step = HS // dp
    low_rows = dp * rows * both_rank // LANES
    vmem = pl.BlockSpec(memory_space=pltpu.VMEM)
    hbm = pl.BlockSpec(memory_space=pl.ANY)
    params = pltpu.CompilerParams(vmem_limit_bytes=48 * 1024 * 1024)
    whole_vmem = pltpu.CompilerParams(vmem_limit_bytes=60 * 1024 * 1024)

    seen = [low_rank]
    for s in range(1, dp):
        seen.append(lax.ppermute(low_rank, "dp", [(d, (d + s) % dp) for d in range(dp)]))

    query_t = query.T
    grad_t = out_grad.T
    query_grad_t, both_grad, *pieces = pl.pallas_call(
        functools.partial(attention_kernel, rows),
        out_shape=[
            jax.ShapeDtypeStruct((HS, tgt_count), jnp.bfloat16),
            jax.ShapeDtypeStruct((mp, rows, LANES), jnp.bfloat16),
        ] + [jax.ShapeDtypeStruct((2 * step, src_count), jnp.bfloat16)] * dp,
        in_specs=[hbm] * 5,
        out_specs=[vmem] * (2 + dp),
        scratch_shapes=[
            pltpu.SMEM(source_lengths.shape, jnp.int32),
            pltpu.SMEM(target_lengths.shape, jnp.int32),
            pltpu.VMEM(query_t.shape, jnp.bfloat16),
            pltpu.VMEM(grad_t.shape, jnp.bfloat16),
            pltpu.VMEM(kv_cache.shape, jnp.bfloat16),
            pltpu.VMEM((dp, 2 * step, src_count), jnp.bfloat16),
            pltpu.SemaphoreType.DMA((5,)),
        ],
        compiler_params=whole_vmem,
        cost_estimate=pl.CostEstimate(
            flops=10 * tgt_count * src_count * 2 * HS, bytes_accessed=2 ** 23, transcendentals=0
        ),
        name="attention_backward",
    )(source_lengths, target_lengths, query_t, grad_t, kv_cache)

    sent = pl.pallas_call(
        functools.partial(low_rank_kernel, rows),
        out_shape=jax.ShapeDtypeStruct((mp, rows + low_rows, LANES), jnp.bfloat16),
        in_specs=[vmem] * (1 + dp),
        out_specs=vmem,
        compiler_params=params,
        name="low_rank_rows",
    )(both_grad, *seen)
    got = lax.all_to_all(
        sent, "mp", split_axis=0, concat_axis=0, axis_index_groups=[group_order(mp)], tiled=True
    )

    arrived = []
    for s in range(dp):
        route = [(d * mp + h, h * dp + (d + s) % dp) for d in range(dp) for h in range(mp)]
        arrived.append(lax.ppermute(pieces[s], ("dp", "mp"), route))

    pieces = pl.pallas_call(
        order_kernel,
        out_shape=jax.ShapeDtypeStruct((dp, 2 * step, src_count), jnp.bfloat16),
        in_specs=[vmem] * dp,
        out_specs=vmem,
        compiler_params=params,
        cost_estimate=pl.CostEstimate(
            flops=2 ** 36, bytes_accessed=2 ** 28, transcendentals=0
        ),
        name="order_pieces",
    )(*arrived)

    key_gradient, value_grad, low_grad, up_grad = pl.pallas_call(
        functools.partial(owner_kernel, dp, mp),
        out_shape=[
            jax.ShapeDtypeStruct((rows, width), jnp.bfloat16),
            jax.ShapeDtypeStruct((rows, width), jnp.bfloat16),
            jax.ShapeDtypeStruct((rows, both_rank), jnp.float32),
            jax.ShapeDtypeStruct((step, both_rank), jnp.float32),
        ],
        in_specs=[vmem] * 3,
        out_specs=[vmem] * 4,
        compiler_params=params,
        name="owner_outputs",
    )(got, adapter_up_matrix, pieces)
    return query_grad_t.T, key_gradient, value_grad, low_grad, up_grad


def solution(mesh):
    in_specs = (
        P("dp", "mp"),
        P("dp", "mp"),
        P("dp", "mp"),
        P("dp", None),
        P("dp", None),
        P(("dp", "mp"), None),
        P(),
    )
    out_specs = (
        P("dp", "mp"),
        P(("dp", "mp"), None),
        P(("dp", "mp"), None),
        P(("dp", "mp"), None),
        P(("dp", "mp"), None),
    )
    body = functools.partial(local, mesh.shape["dp"], mesh.shape["mp"])
    return jax.shard_map(body, mesh=mesh, in_specs=in_specs, out_specs=out_specs, check_vma=False)
```

```python
import functools

import jax
import jax.numpy as jnp
from jax import lax
from jax.experimental import pallas as pl
from jax.experimental.pallas import tpu as pltpu
from jax.sharding import PartitionSpec as P

HS = 64
LANES = 128
CUT = 8

adapter_factor = 2.0

NT = (((1,), (1,)), ((), ()))
TN = (((0,), (0,)), ((), ()))


def dot(left, right, dims):
    return lax.dot_general(left, right, dims, preferred_element_type=jnp.float32)


def group_order(count):
    quarter = count // 4
    bits = quarter.bit_length() - 1
    assert count == 4 << bits
    turned = [sum(((i >> b) & 1) << (bits - 1 - b) for b in range(bits)) for i in range(quarter)]
    order = []
    for low, high in ((1, 2), (0, 3)):
        for i in range(0, quarter, 2):
            first, second = turned[i], turned[i + 1]
            order += [low * quarter + first, high * quarter + second]
            order += [low * quarter + second, high * quarter + first]
    return order


def source_range(source_ref, target_ref, count):
    position = lax.broadcasted_iota(jnp.int32, (1, count), 1)
    first = jnp.zeros((1, count), jnp.int32)
    last = jnp.zeros((1, count), jnp.int32)
    target_start = jnp.int32(0)
    source_start = jnp.int32(0)
    for i in range(source_ref.shape[1]):
        source_end = source_start + source_ref[0, i]
        inside = position >= target_start
        first = jnp.where(inside, source_start, first)
        last = jnp.where(inside, source_end, last)
        target_start = target_start + target_ref[0, i]
        source_start = source_end
    return first, last


def attention_kernel(
    source_any, target_any, query_any, grad_any, kv_any, low_any, query_grad_ref, sent_ref, *refs
):
    *piece_refs, source_ref, target_ref, query_ref, grad_ref, kv_ref, low_ref, pieces, sems = refs
    pairs = [
        (kv_any, kv_ref), (query_any, query_ref), (grad_any, grad_ref),
        (source_any, source_ref), (target_any, target_ref), (low_any, low_ref),
    ]
    copies = [
        pltpu.make_async_copy(here, there, sems.at[i]) for i, (here, there) in enumerate(pairs)
    ]
    for copy in copies:
        copy.start()
    for copy in copies:
        copy.wait()
    tgt_count = query_ref.shape[1]
    both = kv_ref[...]
    query_t = query_ref[...]
    grad_t = grad_ref[...]
    blank = jnp.zeros_like(query_t)
    query_wide = jnp.concatenate([query_t, blank], axis=0)
    grad_wide = jnp.concatenate([blank, grad_t], axis=0)
    scores = jnp.dot(both, query_wide, preferred_element_type=jnp.float32)
    dprob = jnp.dot(both, grad_wide, preferred_element_type=jnp.float32)
    first, last = source_range(source_ref, target_ref, tgt_count)
    position = lax.broadcasted_iota(jnp.int32, scores.shape, 0)
    allowed = jnp.logical_and(position >= first, position < last)
    expo = jnp.where(allowed, jnp.exp(scores), 0.0)
    total = jnp.sum(expo, axis=0, keepdims=True)
    delta = jnp.sum(expo * dprob, axis=0, keepdims=True) / total
    prob = expo * (1.0 / total)
    prob_low = prob.astype(jnp.bfloat16)
    dscore = (prob * (dprob - delta)).astype(jnp.bfloat16)
    both_grad = dot(dscore, query_wide, NT) + dot(prob_low, grad_wide, NT)
    both_low = both_grad.astype(jnp.bfloat16)
    low = low_ref[...].astype(jnp.float32)
    rows = low.shape[0]
    blocks = sent_ref.shape[0]
    packed = jnp.concatenate([low[at:at + CUT] for at in range(0, rows, CUT)], axis=1)
    packed = packed.astype(jnp.bfloat16)
    for at, block in enumerate(group_order(blocks)):
        sent_ref[at, :rows, :] = both_low[block * rows:(block + 1) * rows]
        sent_ref[at, rows:, :] = packed

    wide = both_low.astype(jnp.float32)
    parts = []
    for start in range(0, rows, CUT):
        for block in range(blocks):
            parts.append(wide[block * rows + start:block * rows + start + CUT])
    turned = jnp.concatenate(parts, axis=0).T.astype(jnp.bfloat16)
    dp = len(piece_refs)
    step = HS // dp
    for j in range(dp):
        pieces[j] = jnp.concatenate(
            [turned[j * step:(j + 1) * step], turned[HS + j * step:HS + (j + 1) * step]], axis=0
        )
    first_piece = lax.axis_index("mp") // (blocks // dp)
    for s in range(dp):
        piece_refs[s][...] = pieces[lax.rem(first_piece + s, dp)]

    query_grad = dot(both, dscore, TN)
    query_grad_ref[...] = query_grad[:HS].astype(jnp.bfloat16)


def order_kernel(*refs):
    *arrived_refs, out_ref = refs
    dp = len(arrived_refs)
    mine = lax.rem(lax.axis_index("mp"), dp)
    for s, arrived_ref in enumerate(arrived_refs):
        out_ref[lax.rem(mine + dp - s, dp)] = arrived_ref[...]


def share_kernel(rows, both_rank, got_ref, pieces_ref, *out_refs):
    dp, piece_rows, _ = pieces_ref.shape
    blocks = got_ref.shape[0]
    order = group_order(blocks)
    lows = [
        got_ref[order.index(block), rows:, :].astype(jnp.float32) for block in range(blocks)
    ]
    lows = jnp.concatenate(lows, axis=0).astype(jnp.bfloat16)
    columns = jnp.concatenate([pieces_ref[e] for e in range(dp)], axis=0)
    share = None
    for cut in range(rows // CUT):
        tokens = columns[:, cut * blocks * CUT:(cut + 1) * blocks * CUT]
        product = jnp.dot(tokens, lows, preferred_element_type=jnp.float32)
        part = product[:, cut * both_rank:(cut + 1) * both_rank]
        share = part if share is None else share + part
    step = piece_rows // 2
    column = lax.broadcasted_iota(jnp.int32, (step, both_rank), 1)
    shares = []
    for e in range(dp):
        keys = share[e * piece_rows:e * piece_rows + step]
        values = share[e * piece_rows + step:(e + 1) * piece_rows]
        shares.append(adapter_factor * jnp.where(column < both_rank // 2, keys, values))
    mine = lax.axis_index("dp")
    for s, out_ref in enumerate(out_refs):
        turn = lax.rem(mine + s, dp)
        chosen = shares[0]
        for e in range(1, dp):
            chosen = jnp.where(turn == e, shares[e], chosen)
        out_ref[...] = chosen


def owner_kernel(got_ref, up_ref, key_ref, value_ref, low_grad_ref):
    rows = key_ref.shape[0]
    rank = up_ref.shape[0] // 2
    order = group_order(got_ref.shape[0])
    for pair in range(len(order) // 2):
        first = got_ref[order.index(2 * pair), :rows, :]
        second = got_ref[order.index(2 * pair + 1), :rows, :]
        columns = slice(2 * pair * HS, (2 * pair + 2) * HS)
        key_ref[:, columns] = jnp.concatenate([first[:, :HS], second[:, :HS]], axis=1)
        value_ref[:, columns] = jnp.concatenate([first[:, HS:], second[:, HS:]], axis=1)
    up = up_ref[...]
    from_key = dot(key_ref[...], up, NT)
    from_value = dot(value_ref[...], up, NT)
    column = lax.broadcasted_iota(jnp.int32, from_key.shape, 1)
    low_grad_ref[...] = adapter_factor * jnp.where(column < rank, from_key, from_value)


def local(dp, mp, query, kv_cache, out_grad, source_lengths, target_lengths, low_rank, adapter_up_matrix):
    tgt_count = query.shape[0]
    src_count = kv_cache.shape[0]
    rows, both_rank = low_rank.shape
    width = adapter_up_matrix.shape[1]
    step = HS // dp
    assert rows // CUT * both_rank == LANES
    vmem = pl.BlockSpec(memory_space=pltpu.VMEM)
    hbm = pl.BlockSpec(memory_space=pl.ANY)
    params = pltpu.CompilerParams(vmem_limit_bytes=48 * 1024 * 1024)
    whole_vmem = pltpu.CompilerParams(vmem_limit_bytes=60 * 1024 * 1024)

    query_t = query.T
    grad_t = out_grad.T
    query_grad_t, sent, *pieces = pl.pallas_call(
        attention_kernel,
        out_shape=[
            jax.ShapeDtypeStruct((HS, tgt_count), jnp.bfloat16),
            jax.ShapeDtypeStruct((mp, rows + CUT, LANES), jnp.bfloat16),
        ] + [jax.ShapeDtypeStruct((2 * step, src_count), jnp.bfloat16)] * dp,
        in_specs=[hbm] * 6,
        out_specs=[vmem] * (2 + dp),
        scratch_shapes=[
            pltpu.SMEM(source_lengths.shape, jnp.int32),
            pltpu.SMEM(target_lengths.shape, jnp.int32),
            pltpu.VMEM(query_t.shape, jnp.bfloat16),
            pltpu.VMEM(grad_t.shape, jnp.bfloat16),
            pltpu.VMEM(kv_cache.shape, jnp.bfloat16),
            pltpu.VMEM(low_rank.shape, jnp.bfloat16),
            pltpu.VMEM((dp, 2 * step, src_count), jnp.bfloat16),
            pltpu.SemaphoreType.DMA((6,)),
        ],
        compiler_params=whole_vmem,
        name="attention_backward",
    )(source_lengths, target_lengths, query_t, grad_t, kv_cache, low_rank)

    arrived = []
    for s in range(dp):
        route = [(h, (h * dp + (h // (mp // dp) + s) % dp) % mp) for h in range(mp)]
        arrived.append(lax.ppermute(pieces[s], "mp", route))
    ordered = pl.pallas_call(
        order_kernel,
        out_shape=jax.ShapeDtypeStruct((dp, 2 * step, src_count), jnp.bfloat16),
        in_specs=[vmem] * dp,
        out_specs=vmem,
        compiler_params=params,
        cost_estimate=pl.CostEstimate(flops=2 ** 36, bytes_accessed=2 ** 28, transcendentals=0),
        name="order_pieces",
    )(*arrived)

    got = lax.all_to_all(sent, "mp", 0, 0, axis_index_groups=[group_order(mp)], tiled=True)

    shares = pl.pallas_call(
        functools.partial(share_kernel, rows, both_rank),
        out_shape=[jax.ShapeDtypeStruct((step, both_rank), jnp.float32)] * dp,
        in_specs=[vmem] * 2,
        out_specs=[vmem] * dp,
        compiler_params=params,
        name="adapter_shares",
    )(got, ordered)
    up_grad = shares[0]
    for s in range(1, dp):
        route = [(d, (d + s) % dp) for d in range(dp)]
        up_grad = up_grad + lax.ppermute(shares[s], "dp", route)

    key_gradient, value_grad, low_grad = pl.pallas_call(
        owner_kernel,
        out_shape=[
            jax.ShapeDtypeStruct((rows, width), jnp.bfloat16),
            jax.ShapeDtypeStruct((rows, width), jnp.bfloat16),
            jax.ShapeDtypeStruct((rows, both_rank), jnp.float32),
        ],
        in_specs=[vmem] * 2,
        out_specs=[vmem] * 3,
        compiler_params=params,
        name="owner_outputs",
    )(got, adapter_up_matrix)
    return query_grad_t.T, key_gradient, value_grad, low_grad, up_grad


def solution(mesh):
    in_specs = (
        P("dp", "mp"),
        P("dp", "mp"),
        P("dp", "mp"),
        P("dp", None),
        P("dp", None),
        P(("dp", "mp"), None),
        P(),
    )
    out_specs = (
        P("dp", "mp"),
        P(("dp", "mp"), None),
        P(("dp", "mp"), None),
        P(("dp", "mp"), None),
        P(("dp", "mp"), None),
    )
    body = functools.partial(local, mesh.shape["dp"], mesh.shape["mp"])
    return jax.shard_map(body, mesh=mesh, in_specs=in_specs, out_specs=out_specs, check_vma=False)
```

```python
import functools

import jax
import jax.numpy as jnp
from jax import lax
from jax.experimental import pallas as pl
from jax.experimental.pallas import tpu as pltpu
from jax.sharding import PartitionSpec as P

HS = 64
LANES = 128
CUT = 8

adapter_factor = 2.0

NT = (((1,), (1,)), ((), ()))
TN = (((0,), (0,)), ((), ()))


def dot(left, right, dims):
    return lax.dot_general(left, right, dims, preferred_element_type=jnp.float32)


def group_order(count):
    quarter = count // 4
    bits = quarter.bit_length() - 1
    assert count == 4 << bits
    turned = [sum(((i >> b) & 1) << (bits - 1 - b) for b in range(bits)) for i in range(quarter)]
    order = []
    for low, high in ((1, 2), (0, 3)):
        for i in range(0, quarter, 2):
            first, second = turned[i], turned[i + 1]
            order += [low * quarter + first, high * quarter + second]
            order += [low * quarter + second, high * quarter + first]
    return [count - 1 - place for place in order]


def source_range(source_ref, target_ref, count):
    position = lax.broadcasted_iota(jnp.int32, (1, count), 1)
    first = jnp.zeros((1, count), jnp.int32)
    last = jnp.zeros((1, count), jnp.int32)
    target_start = jnp.int32(0)
    source_start = jnp.int32(0)
    for i in range(source_ref.shape[1]):
        source_end = source_start + source_ref[0, i]
        inside = position >= target_start
        first = jnp.where(inside, source_start, first)
        last = jnp.where(inside, source_end, last)
        target_start = target_start + target_ref[0, i]
        source_start = source_end
    return first, last


def attention_kernel(
    source_any, target_any, query_any, grad_any, kv_any, low_any, query_grad_ref, sent_ref, turned_ref,
    source_ref, target_ref, query_ref, grad_ref, kv_ref, low_ref, sems,
):
    pairs = [
        (kv_any, kv_ref), (query_any, query_ref), (grad_any, grad_ref),
        (source_any, source_ref), (target_any, target_ref), (low_any, low_ref),
    ]
    copies = [
        pltpu.make_async_copy(here, there, sems.at[i]) for i, (here, there) in enumerate(pairs)
    ]
    for copy in copies:
        copy.start()
    for copy in copies:
        copy.wait()
    tgt_count = query_ref.shape[1]
    both = kv_ref[...]
    query_t = query_ref[...]
    grad_t = grad_ref[...]
    blank = jnp.zeros_like(query_t)
    query_wide = jnp.concatenate([query_t, blank], axis=0)
    grad_wide = jnp.concatenate([blank, grad_t], axis=0)
    scores = jnp.dot(both, query_wide, preferred_element_type=jnp.float32)
    dprob = jnp.dot(both, grad_wide, preferred_element_type=jnp.float32)
    first, last = source_range(source_ref, target_ref, tgt_count)
    position = lax.broadcasted_iota(jnp.int32, scores.shape, 0)
    allowed = jnp.logical_and(position >= first, position < last)
    expo = jnp.where(allowed, jnp.exp(scores), 0.0)
    total = jnp.sum(expo, axis=0, keepdims=True)
    delta = jnp.sum(expo * dprob, axis=0, keepdims=True) / total
    prob = expo * (1.0 / total)
    prob_low = prob.astype(jnp.bfloat16)
    dscore = (prob * (dprob - delta)).astype(jnp.bfloat16)
    both_grad = dot(dscore, query_wide, NT) + dot(prob_low, grad_wide, NT)
    both_low = both_grad.astype(jnp.bfloat16)
    low = low_ref[...].astype(jnp.float32)
    rows = low.shape[0]
    blocks = sent_ref.shape[0]
    packed = jnp.concatenate([low[at:at + CUT] for at in range(0, rows, CUT)], axis=1)
    packed = packed.astype(jnp.bfloat16)
    for at, block in enumerate(group_order(blocks)):
        sent_ref[at, :rows, :] = both_low[block * rows:(block + 1) * rows]
        sent_ref[at, rows:, :] = packed

    wide = both_low.astype(jnp.float32)
    parts = []
    for start in range(0, rows, CUT):
        for block in range(blocks):
            parts.append(wide[block * rows + start:block * rows + start + CUT])
    turned_ref[...] = jnp.concatenate(parts, axis=0).T.astype(jnp.bfloat16)

    query_grad = dot(both, dscore, TN)
    query_grad_ref[...] = query_grad[:HS].astype(jnp.bfloat16)


def keep_kernel(arrived_ref, out_ref):
    out_ref[...] = arrived_ref[...]


def share_kernel(rows, both_rank, got_ref, turned_ref, *out_refs):
    blocks = got_ref.shape[0]
    order = group_order(blocks)
    lows = [
        got_ref[order.index(block), rows:, :].astype(jnp.float32) for block in range(blocks)
    ]
    lows = jnp.concatenate(lows, axis=0).astype(jnp.bfloat16)
    share = None
    for cut in range(rows // CUT):
        tokens = turned_ref[:, cut * blocks * CUT:(cut + 1) * blocks * CUT]
        product = jnp.dot(tokens, lows, preferred_element_type=jnp.float32)
        part = product[:, cut * both_rank:(cut + 1) * both_rank]
        share = part if share is None else share + part
    column = lax.broadcasted_iota(jnp.int32, (HS, both_rank), 1)
    share = adapter_factor * jnp.where(column < both_rank // 2, share[:HS], share[HS:])
    mine = lax.axis_index("dp")
    dp = len(out_refs)
    step = HS // dp
    for s, out_ref in enumerate(out_refs):
        turn = lax.rem(mine + s, dp)
        chosen = share[:step]
        for j in range(1, dp):
            chosen = jnp.where(turn == j, share[j * step:(j + 1) * step], chosen)
        out_ref[...] = chosen


def owner_kernel(got_ref, up_ref, key_ref, value_ref, low_grad_ref):
    rows = key_ref.shape[0]
    rank = up_ref.shape[0] // 2
    order = group_order(got_ref.shape[0])
    for pair in range(len(order) // 2):
        first = got_ref[order.index(2 * pair), :rows, :]
        second = got_ref[order.index(2 * pair + 1), :rows, :]
        columns = slice(2 * pair * HS, (2 * pair + 2) * HS)
        key_ref[:, columns] = jnp.concatenate([first[:, :HS], second[:, :HS]], axis=1)
        value_ref[:, columns] = jnp.concatenate([first[:, HS:], second[:, HS:]], axis=1)
    up = up_ref[...]
    from_key = dot(key_ref[...], up, NT)
    from_value = dot(value_ref[...], up, NT)
    column = lax.broadcasted_iota(jnp.int32, from_key.shape, 1)
    low_grad_ref[...] = adapter_factor * jnp.where(column < rank, from_key, from_value)


def local(dp, mp, query, kv_cache, out_grad, source_lengths, target_lengths, low_rank, adapter_up_matrix):
    tgt_count = query.shape[0]
    src_count = kv_cache.shape[0]
    rows, both_rank = low_rank.shape
    width = adapter_up_matrix.shape[1]
    step = HS // dp
    assert rows // CUT * both_rank == LANES
    vmem = pl.BlockSpec(memory_space=pltpu.VMEM)
    hbm = pl.BlockSpec(memory_space=pl.ANY)
    params = pltpu.CompilerParams(vmem_limit_bytes=48 * 1024 * 1024)
    whole_vmem = pltpu.CompilerParams(vmem_limit_bytes=60 * 1024 * 1024)

    query_t = query.T
    grad_t = out_grad.T
    query_grad_t, sent, turned = pl.pallas_call(
        attention_kernel,
        out_shape=[
            jax.ShapeDtypeStruct((HS, tgt_count), jnp.bfloat16),
            jax.ShapeDtypeStruct((mp, rows + CUT, LANES), jnp.bfloat16),
            jax.ShapeDtypeStruct((2 * HS, src_count), jnp.bfloat16),
        ],
        in_specs=[hbm] * 6,
        out_specs=[vmem] * 3,
        scratch_shapes=[
            pltpu.SMEM(source_lengths.shape, jnp.int32),
            pltpu.SMEM(target_lengths.shape, jnp.int32),
            pltpu.VMEM(query_t.shape, jnp.bfloat16),
            pltpu.VMEM(grad_t.shape, jnp.bfloat16),
            pltpu.VMEM(kv_cache.shape, jnp.bfloat16),
            pltpu.VMEM(low_rank.shape, jnp.bfloat16),
            pltpu.SemaphoreType.DMA((6,)),
        ],
        compiler_params=whole_vmem,
        name="attention_backward",
    )(source_lengths, target_lengths, query_t, grad_t, kv_cache, low_rank)

    route = [(h, h * dp % mp + h * dp // mp) for h in range(mp)]
    arrived = pl.pallas_call(
        keep_kernel,
        out_shape=jax.ShapeDtypeStruct(turned.shape, turned.dtype),
        in_specs=[vmem],
        out_specs=vmem,
        compiler_params=params,
        cost_estimate=pl.CostEstimate(flops=2 ** 36, bytes_accessed=2 ** 28, transcendentals=0),
        name="keep_columns",
    )(lax.ppermute(turned, "mp", route))

    got = lax.all_to_all(sent, "mp", 0, 0, axis_index_groups=[group_order(mp)], tiled=True)

    shares = pl.pallas_call(
        functools.partial(share_kernel, rows, both_rank),
        out_shape=[jax.ShapeDtypeStruct((step, both_rank), jnp.float32)] * dp,
        in_specs=[vmem] * 2,
        out_specs=[vmem] * dp,
        compiler_params=params,
        name="adapter_shares",
    )(got, arrived)
    up_grad = None
    for s in range(dp):
        route = [
            (d * mp + m, m % dp * mp + m - m % dp + (d + s) % dp)
            for d in range(dp) for m in range(mp)
        ]
        term = lax.ppermute(shares[s], ("dp", "mp"), route)
        up_grad = term if up_grad is None else up_grad + term

    key_gradient, value_grad, low_grad = pl.pallas_call(
        owner_kernel,
        out_shape=[
            jax.ShapeDtypeStruct((rows, width), jnp.bfloat16),
            jax.ShapeDtypeStruct((rows, width), jnp.bfloat16),
            jax.ShapeDtypeStruct((rows, both_rank), jnp.float32),
        ],
        in_specs=[vmem] * 2,
        out_specs=[vmem] * 3,
        compiler_params=params,
        name="owner_outputs",
    )(got, adapter_up_matrix)
    return query_grad_t.T, key_gradient, value_grad, low_grad, up_grad


def solution(mesh):
    in_specs = (
        P("dp", "mp"),
        P("dp", "mp"),
        P("dp", "mp"),
        P("dp", None),
        P("dp", None),
        P(("dp", "mp"), None),
        P(),
    )
    out_specs = (
        P("dp", "mp"),
        P(("dp", "mp"), None),
        P(("dp", "mp"), None),
        P(("dp", "mp"), None),
        P(("dp", "mp"), None),
    )
    body = functools.partial(local, mesh.shape["dp"], mesh.shape["mp"])
    return jax.shard_map(body, mesh=mesh, in_specs=in_specs, out_specs=out_specs, check_vma=False)
```

```python
import functools

import jax
import jax.numpy as jnp
from jax import lax
from jax.experimental import pallas as pl
from jax.experimental.pallas import tpu as pltpu
from jax.sharding import PartitionSpec as P

HS = 64
LANES = 128
CUT = 8

adapter_factor = 2.0

NT = (((1,), (1,)), ((), ()))
TN = (((0,), (0,)), ((), ()))


def dot(left, right, dims):
    return lax.dot_general(left, right, dims, preferred_element_type=jnp.float32)


def group_order(count):
    quarter = count // 4
    bits = quarter.bit_length() - 1
    assert count == 4 << bits
    turned = [sum(((i >> b) & 1) << (bits - 1 - b) for b in range(bits)) for i in range(quarter)]
    order = []
    for low, high in ((1, 2), (0, 3)):
        for i in range(0, quarter, 2):
            first, second = turned[i], turned[i + 1]
            order += [low * quarter + first, high * quarter + second]
            order += [low * quarter + second, high * quarter + first]
    return [count - 1 - place for place in order]


def source_range(source_ref, target_ref, count):
    position = lax.broadcasted_iota(jnp.int32, (1, count), 1)
    first = jnp.zeros((1, count), jnp.int32)
    last = jnp.zeros((1, count), jnp.int32)
    target_start = jnp.int32(0)
    source_start = jnp.int32(0)
    for i in range(source_ref.shape[1]):
        source_end = source_start + source_ref[0, i]
        inside = position >= target_start
        first = jnp.where(inside, source_start, first)
        last = jnp.where(inside, source_end, last)
        target_start = target_start + target_ref[0, i]
        source_start = source_end
    return first, last


def attention_kernel(
    source_any, target_any, query_any, grad_any, kv_any, low_any, query_grad_ref, sent_ref, turned_ref,
    source_ref, target_ref, query_ref, grad_ref, kv_ref, low_ref, sems,
):
    pairs = [
        (kv_any, kv_ref), (query_any, query_ref), (grad_any, grad_ref),
        (source_any, source_ref), (target_any, target_ref), (low_any, low_ref),
    ]
    copies = [
        pltpu.make_async_copy(here, there, sems.at[i]) for i, (here, there) in enumerate(pairs)
    ]
    for copy in copies:
        copy.start()
    for copy in copies:
        copy.wait()
    tgt_count = query_ref.shape[1]
    both = kv_ref[...]
    query_t = query_ref[...]
    grad_t = grad_ref[...]
    blank = jnp.zeros_like(query_t)
    query_wide = jnp.concatenate([query_t, blank], axis=0)
    grad_wide = jnp.concatenate([blank, grad_t], axis=0)
    scores = jnp.dot(both, query_wide, preferred_element_type=jnp.float32)
    dprob = jnp.dot(both, grad_wide, preferred_element_type=jnp.float32)
    first, last = source_range(source_ref, target_ref, tgt_count)
    position = lax.broadcasted_iota(jnp.int32, scores.shape, 0)
    allowed = jnp.logical_and(position >= first, position < last)
    expo = jnp.where(allowed, jnp.exp(scores), 0.0)
    total = jnp.sum(expo, axis=0, keepdims=True)
    delta = jnp.sum(expo * dprob, axis=0, keepdims=True) / total
    prob = expo * (1.0 / total)
    prob_low = prob.astype(jnp.bfloat16)
    dscore = (prob * (dprob - delta)).astype(jnp.bfloat16)
    both_grad = dot(dscore, query_wide, NT) + dot(prob_low, grad_wide, NT)
    both_low = both_grad.astype(jnp.bfloat16)
    low = low_ref[...].astype(jnp.float32)
    rows = low.shape[0]
    blocks = sent_ref.shape[0]
    packed = jnp.concatenate([low[at:at + CUT] for at in range(0, rows, CUT)], axis=1)
    packed = packed.astype(jnp.bfloat16)
    for at, block in enumerate(group_order(blocks)):
        sent_ref[at, :rows, :] = both_low[block * rows:(block + 1) * rows]
        sent_ref[at, rows:, :] = packed

    wide = both_low.astype(jnp.float32)
    parts = []
    for start in range(0, rows, CUT):
        for block in range(blocks):
            parts.append(wide[block * rows + start:block * rows + start + CUT])
    turned_ref[...] = jnp.concatenate(parts, axis=0).T.astype(jnp.bfloat16)

    query_grad = dot(both, dscore, TN)
    query_grad_ref[...] = query_grad[:HS].astype(jnp.bfloat16)


def split_kernel(turned_ref, *out_refs):
    dp = len(out_refs)
    step = HS // dp
    turned = turned_ref[...].astype(jnp.float32)
    pieces = []
    for j in range(dp):
        rows = [turned[j * step:(j + 1) * step], turned[HS + j * step:HS + (j + 1) * step]]
        pieces.append(jnp.concatenate(rows, axis=0))
    mine = lax.rem(lax.axis_index("mp"), dp)
    for s, out_ref in enumerate(out_refs):
        turn = lax.rem(mine + s, dp)
        chosen = pieces[0]
        for j in range(1, dp):
            chosen = jnp.where(turn == j, pieces[j], chosen)
        out_ref[...] = chosen.astype(jnp.bfloat16)


def order_kernel(*refs):
    *arrived_refs, out_ref = refs
    dp = len(arrived_refs)
    mine = lax.rem(lax.axis_index("mp"), dp)
    for s, arrived_ref in enumerate(arrived_refs):
        out_ref[lax.rem(mine + dp - s, dp)] = arrived_ref[...]


def share_kernel(rows, both_rank, got_ref, pieces_ref, *out_refs):
    dp, piece_rows, _ = pieces_ref.shape
    blocks = got_ref.shape[0]
    order = group_order(blocks)
    lows = [
        got_ref[order.index(block), rows:, :].astype(jnp.float32) for block in range(blocks)
    ]
    lows = jnp.concatenate(lows, axis=0).astype(jnp.bfloat16)
    columns = jnp.concatenate([pieces_ref[e] for e in range(dp)], axis=0)
    share = None
    for cut in range(rows // CUT):
        tokens = columns[:, cut * blocks * CUT:(cut + 1) * blocks * CUT]
        product = jnp.dot(tokens, lows, preferred_element_type=jnp.float32)
        part = product[:, cut * both_rank:(cut + 1) * both_rank]
        share = part if share is None else share + part
    step = piece_rows // 2
    column = lax.broadcasted_iota(jnp.int32, (step, both_rank), 1)
    shares = []
    for e in range(dp):
        keys = share[e * piece_rows:e * piece_rows + step]
        values = share[e * piece_rows + step:(e + 1) * piece_rows]
        shares.append(adapter_factor * jnp.where(column < both_rank // 2, keys, values))
    mine = lax.axis_index("dp")
    for s, out_ref in enumerate(out_refs):
        turn = lax.rem(mine + s, dp)
        chosen = shares[0]
        for e in range(1, dp):
            chosen = jnp.where(turn == e, shares[e], chosen)
        out_ref[...] = chosen


def owner_kernel(got_ref, up_ref, key_ref, value_ref, low_grad_ref):
    rows = key_ref.shape[0]
    rank = up_ref.shape[0] // 2
    order = group_order(got_ref.shape[0])
    for pair in range(len(order) // 2):
        first = got_ref[order.index(2 * pair), :rows, :]
        second = got_ref[order.index(2 * pair + 1), :rows, :]
        columns = slice(2 * pair * HS, (2 * pair + 2) * HS)
        key_ref[:, columns] = jnp.concatenate([first[:, :HS], second[:, :HS]], axis=1)
        value_ref[:, columns] = jnp.concatenate([first[:, HS:], second[:, HS:]], axis=1)
    up = up_ref[...]
    from_key = dot(key_ref[...], up, NT)
    from_value = dot(value_ref[...], up, NT)
    column = lax.broadcasted_iota(jnp.int32, from_key.shape, 1)
    low_grad_ref[...] = adapter_factor * jnp.where(column < rank, from_key, from_value)


def local(dp, mp, query, kv_cache, out_grad, source_lengths, target_lengths, low_rank, adapter_up_matrix):
    tgt_count = query.shape[0]
    src_count = kv_cache.shape[0]
    rows, both_rank = low_rank.shape
    width = adapter_up_matrix.shape[1]
    step = HS // dp
    assert rows // CUT * both_rank == LANES
    vmem = pl.BlockSpec(memory_space=pltpu.VMEM)
    hbm = pl.BlockSpec(memory_space=pl.ANY)
    params = pltpu.CompilerParams(vmem_limit_bytes=48 * 1024 * 1024)
    whole_vmem = pltpu.CompilerParams(vmem_limit_bytes=60 * 1024 * 1024)

    query_t = query.T
    grad_t = out_grad.T
    query_grad_t, sent, turned = pl.pallas_call(
        attention_kernel,
        out_shape=[
            jax.ShapeDtypeStruct((HS, tgt_count), jnp.bfloat16),
            jax.ShapeDtypeStruct((mp, rows + CUT, LANES), jnp.bfloat16),
            jax.ShapeDtypeStruct((2 * HS, src_count), jnp.bfloat16),
        ],
        in_specs=[hbm] * 6,
        out_specs=[vmem] * 3,
        scratch_shapes=[
            pltpu.SMEM(source_lengths.shape, jnp.int32),
            pltpu.SMEM(target_lengths.shape, jnp.int32),
            pltpu.VMEM(query_t.shape, jnp.bfloat16),
            pltpu.VMEM(grad_t.shape, jnp.bfloat16),
            pltpu.VMEM(kv_cache.shape, jnp.bfloat16),
            pltpu.VMEM(low_rank.shape, jnp.bfloat16),
            pltpu.SemaphoreType.DMA((6,)),
        ],
        compiler_params=whole_vmem,
        name="attention_backward",
    )(source_lengths, target_lengths, query_t, grad_t, kv_cache, low_rank)

    route = [(h, h * dp % mp + h * dp // mp) for h in range(mp)]
    pieces = pl.pallas_call(
        split_kernel,
        out_shape=[jax.ShapeDtypeStruct((2 * step, src_count), jnp.bfloat16)] * dp,
        in_specs=[vmem],
        out_specs=[vmem] * dp,
        compiler_params=params,
        cost_estimate=pl.CostEstimate(flops=2 ** 36, bytes_accessed=2 ** 28, transcendentals=0),
        name="split_columns",
    )(lax.ppermute(turned, "mp", route))
    arrived = [pieces[0]]
    for s in range(1, dp):
        route = [(m, m - m % dp + (m + s) % dp) for m in range(mp)]
        arrived.append(lax.ppermute(pieces[s], "mp", route))
    ordered = pl.pallas_call(
        order_kernel,
        out_shape=jax.ShapeDtypeStruct((dp, 2 * step, src_count), jnp.bfloat16),
        in_specs=[vmem] * dp,
        out_specs=vmem,
        compiler_params=params,
        name="order_pieces",
    )(*arrived)

    got = lax.all_to_all(sent, "mp", 0, 0, axis_index_groups=[group_order(mp)], tiled=True)

    shares = pl.pallas_call(
        functools.partial(share_kernel, rows, both_rank),
        out_shape=[jax.ShapeDtypeStruct((step, both_rank), jnp.float32)] * dp,
        in_specs=[vmem] * 2,
        out_specs=[vmem] * dp,
        compiler_params=params,
        name="adapter_shares",
    )(got, ordered)
    up_grad = shares[0]
    for s in range(1, dp):
        route = [(d, (d + s) % dp) for d in range(dp)]
        up_grad = up_grad + lax.ppermute(shares[s], "dp", route)

    key_gradient, value_grad, low_grad = pl.pallas_call(
        owner_kernel,
        out_shape=[
            jax.ShapeDtypeStruct((rows, width), jnp.bfloat16),
            jax.ShapeDtypeStruct((rows, width), jnp.bfloat16),
            jax.ShapeDtypeStruct((rows, both_rank), jnp.float32),
        ],
        in_specs=[vmem] * 2,
        out_specs=[vmem] * 3,
        compiler_params=params,
        name="owner_outputs",
    )(got, adapter_up_matrix)
    return query_grad_t.T, key_gradient, value_grad, low_grad, up_grad


def solution(mesh):
    in_specs = (
        P("dp", "mp"),
        P("dp", "mp"),
        P("dp", "mp"),
        P("dp", None),
        P("dp", None),
        P(("dp", "mp"), None),
        P(),
    )
    out_specs = (
        P("dp", "mp"),
        P(("dp", "mp"), None),
        P(("dp", "mp"), None),
        P(("dp", "mp"), None),
        P(("dp", "mp"), None),
    )
    body = functools.partial(local, mesh.shape["dp"], mesh.shape["mp"])
    return jax.shard_map(body, mesh=mesh, in_specs=in_specs, out_specs=out_specs, check_vma=False)
```

```python
import functools

import jax
import jax.numpy as jnp
from jax import lax
from jax.experimental import pallas as pl
from jax.experimental.pallas import tpu as pltpu
from jax.sharding import PartitionSpec as P

HS = 64
LANES = 128
CUT = 8

adapter_factor = 2.0

NT = (((1,), (1,)), ((), ()))
TN = (((0,), (0,)), ((), ()))


def dot(left, right, dims):
    return lax.dot_general(left, right, dims, preferred_element_type=jnp.float32)


def group_order(count):
    quarter = count // 4
    bits = quarter.bit_length() - 1
    assert count == 4 << bits
    turned = [sum(((i >> b) & 1) << (bits - 1 - b) for b in range(bits)) for i in range(quarter)]
    order = []
    for low, high in ((1, 2), (0, 3)):
        for i in range(0, quarter, 2):
            first, second = turned[i], turned[i + 1]
            order += [low * quarter + first, high * quarter + second]
            order += [low * quarter + second, high * quarter + first]
    return [count - 1 - place for place in order]


def source_range(source_ref, target_ref, count):
    position = lax.broadcasted_iota(jnp.int32, (1, count), 1)
    first = jnp.zeros((1, count), jnp.int32)
    last = jnp.zeros((1, count), jnp.int32)
    target_start = jnp.int32(0)
    source_start = jnp.int32(0)
    for i in range(source_ref.shape[1]):
        source_end = source_start + source_ref[0, i]
        inside = position >= target_start
        first = jnp.where(inside, source_start, first)
        last = jnp.where(inside, source_end, last)
        target_start = target_start + target_ref[0, i]
        source_start = source_end
    return first, last


def attention_kernel(
    source_any, target_any, query_any, grad_any, kv_any, low_any, query_grad_ref, sent_ref, turned_ref,
    source_ref, target_ref, query_ref, grad_ref, kv_ref, low_ref, sems,
):
    pairs = [
        (kv_any, kv_ref), (query_any, query_ref), (grad_any, grad_ref),
        (source_any, source_ref), (target_any, target_ref), (low_any, low_ref),
    ]
    copies = [
        pltpu.make_async_copy(here, there, sems.at[i]) for i, (here, there) in enumerate(pairs)
    ]
    for copy in copies:
        copy.start()
    for copy in copies:
        copy.wait()
    tgt_count = query_ref.shape[1]
    both = kv_ref[...]
    query_t = query_ref[...]
    grad_t = grad_ref[...]
    blank = jnp.zeros_like(query_t)
    query_wide = jnp.concatenate([query_t, blank], axis=0)
    grad_wide = jnp.concatenate([blank, grad_t], axis=0)
    scores = jnp.dot(both, query_wide, preferred_element_type=jnp.float32)
    dprob = jnp.dot(both, grad_wide, preferred_element_type=jnp.float32)
    first, last = source_range(source_ref, target_ref, tgt_count)
    position = lax.broadcasted_iota(jnp.int32, scores.shape, 0)
    allowed = jnp.logical_and(position >= first, position < last)
    expo = jnp.where(allowed, jnp.exp(scores), 0.0)
    total = jnp.sum(expo, axis=0, keepdims=True)
    delta = jnp.sum(expo * dprob, axis=0, keepdims=True) / total
    prob = expo * (1.0 / total)
    prob_low = prob.astype(jnp.bfloat16)
    dscore = (prob * (dprob - delta)).astype(jnp.bfloat16)
    both_grad = dot(dscore, query_wide, NT) + dot(prob_low, grad_wide, NT)
    both_low = both_grad.astype(jnp.bfloat16)
    low = low_ref[...].astype(jnp.float32)
    rows = low.shape[0]
    blocks = sent_ref.shape[0]
    packed = jnp.concatenate([low[at:at + CUT] for at in range(0, rows, CUT)], axis=1)
    packed = packed.astype(jnp.bfloat16)
    for at, block in enumerate(group_order(blocks)):
        sent_ref[at, :rows, :] = both_low[block * rows:(block + 1) * rows]
        sent_ref[at, rows:, :] = packed

    wide = both_low.astype(jnp.float32)
    parts = []
    for start in range(0, rows, CUT):
        for block in range(blocks):
            parts.append(wide[block * rows + start:block * rows + start + CUT])
    turned_ref[...] = jnp.concatenate(parts, axis=0).T.astype(jnp.bfloat16)

    query_grad = dot(both, dscore, TN)
    query_grad_ref[...] = query_grad[:HS].astype(jnp.bfloat16)


def split_kernel(turned_ref, *out_refs):
    dp = len(out_refs)
    step = HS // dp
    turned = turned_ref[...].astype(jnp.float32)
    pieces = []
    for j in range(dp):
        rows = [turned[j * step:(j + 1) * step], turned[HS + j * step:HS + (j + 1) * step]]
        pieces.append(jnp.concatenate(rows, axis=0))
    e = lax.rem(lax.axis_index("mp"), dp)
    pack = lax.axis_index("dp")
    for s, out_ref in enumerate(out_refs):
        turn = lax.rem(2 * e + s + dp - pack, dp)
        chosen = pieces[0]
        for j in range(1, dp):
            chosen = jnp.where(turn == j, pieces[j], chosen)
        out_ref[...] = chosen.astype(jnp.bfloat16)


def order_kernel(*refs):
    *arrived_refs, out_ref = refs
    dp = len(arrived_refs)
    mine = lax.rem(lax.axis_index("mp"), dp)
    for s, arrived_ref in enumerate(arrived_refs):
        out_ref[lax.rem(mine + dp - s, dp)] = arrived_ref[...]


def share_kernel(rows, both_rank, got_ref, pieces_ref, *out_refs):
    dp, piece_rows, _ = pieces_ref.shape
    blocks = got_ref.shape[0]
    order = group_order(blocks)
    lows = [
        got_ref[order.index(block), rows:, :].astype(jnp.float32) for block in range(blocks)
    ]
    lows = jnp.concatenate(lows, axis=0).astype(jnp.bfloat16)
    columns = jnp.concatenate([pieces_ref[e] for e in range(dp)], axis=0)
    share = None
    for cut in range(rows // CUT):
        tokens = columns[:, cut * blocks * CUT:(cut + 1) * blocks * CUT]
        product = jnp.dot(tokens, lows, preferred_element_type=jnp.float32)
        part = product[:, cut * both_rank:(cut + 1) * both_rank]
        share = part if share is None else share + part
    step = piece_rows // 2
    column = lax.broadcasted_iota(jnp.int32, (step, both_rank), 1)
    shares = []
    for e in range(dp):
        keys = share[e * piece_rows:e * piece_rows + step]
        values = share[e * piece_rows + step:(e + 1) * piece_rows]
        shares.append(adapter_factor * jnp.where(column < both_rank // 2, keys, values))
    mine = lax.axis_index("dp")
    for s, out_ref in enumerate(out_refs):
        turn = lax.rem(mine + s, dp)
        chosen = shares[0]
        for e in range(1, dp):
            chosen = jnp.where(turn == e, shares[e], chosen)
        out_ref[...] = chosen


def owner_kernel(got_ref, up_ref, key_ref, value_ref, low_grad_ref):
    rows = key_ref.shape[0]
    rank = up_ref.shape[0] // 2
    order = group_order(got_ref.shape[0])
    for pair in range(len(order) // 2):
        first = got_ref[order.index(2 * pair), :rows, :]
        second = got_ref[order.index(2 * pair + 1), :rows, :]
        columns = slice(2 * pair * HS, (2 * pair + 2) * HS)
        key_ref[:, columns] = jnp.concatenate([first[:, :HS], second[:, :HS]], axis=1)
        value_ref[:, columns] = jnp.concatenate([first[:, HS:], second[:, HS:]], axis=1)
    up = up_ref[...]
    from_key = dot(key_ref[...], up, NT)
    from_value = dot(value_ref[...], up, NT)
    column = lax.broadcasted_iota(jnp.int32, from_key.shape, 1)
    low_grad_ref[...] = adapter_factor * jnp.where(column < rank, from_key, from_value)


def local(dp, mp, query, kv_cache, out_grad, source_lengths, target_lengths, low_rank, adapter_up_matrix):
    tgt_count = query.shape[0]
    src_count = kv_cache.shape[0]
    rows, both_rank = low_rank.shape
    width = adapter_up_matrix.shape[1]
    step = HS // dp
    assert rows // CUT * both_rank == LANES
    vmem = pl.BlockSpec(memory_space=pltpu.VMEM)
    hbm = pl.BlockSpec(memory_space=pl.ANY)
    params = pltpu.CompilerParams(vmem_limit_bytes=48 * 1024 * 1024)
    whole_vmem = pltpu.CompilerParams(vmem_limit_bytes=60 * 1024 * 1024)

    query_t = query.T
    grad_t = out_grad.T
    query_grad_t, sent, turned = pl.pallas_call(
        attention_kernel,
        out_shape=[
            jax.ShapeDtypeStruct((HS, tgt_count), jnp.bfloat16),
            jax.ShapeDtypeStruct((mp, rows + CUT, LANES), jnp.bfloat16),
            jax.ShapeDtypeStruct((2 * HS, src_count), jnp.bfloat16),
        ],
        in_specs=[hbm] * 6,
        out_specs=[vmem] * 3,
        scratch_shapes=[
            pltpu.SMEM(source_lengths.shape, jnp.int32),
            pltpu.SMEM(target_lengths.shape, jnp.int32),
            pltpu.VMEM(query_t.shape, jnp.bfloat16),
            pltpu.VMEM(grad_t.shape, jnp.bfloat16),
            pltpu.VMEM(kv_cache.shape, jnp.bfloat16),
            pltpu.VMEM(low_rank.shape, jnp.bfloat16),
            pltpu.SemaphoreType.DMA((6,)),
        ],
        compiler_params=whole_vmem,
        name="attention_backward",
    )(source_lengths, target_lengths, query_t, grad_t, kv_cache, low_rank)

    route = [(h, h * dp % mp + h * dp // mp) for h in range(mp)]
    pieces = pl.pallas_call(
        split_kernel,
        out_shape=[jax.ShapeDtypeStruct((2 * step, src_count), jnp.bfloat16)] * dp,
        in_specs=[vmem],
        out_specs=[vmem] * dp,
        compiler_params=params,
        cost_estimate=pl.CostEstimate(flops=2 ** 36, bytes_accessed=2 ** 28, transcendentals=0),
        name="split_columns",
    )(lax.ppermute(turned, "mp", route))
    arrived = [pieces[0]]
    for s in range(1, dp):
        route = [(m, m - m % dp + (m + s) % dp) for m in range(mp)]
        arrived.append(lax.ppermute(pieces[s], "mp", route))
    ordered = pl.pallas_call(
        order_kernel,
        out_shape=jax.ShapeDtypeStruct((dp, 2 * step, src_count), jnp.bfloat16),
        in_specs=[vmem] * dp,
        out_specs=vmem,
        compiler_params=params,
        name="order_pieces",
    )(*arrived)

    got = lax.all_to_all(sent, "mp", 0, 0, axis_index_groups=[group_order(mp)], tiled=True)

    shares = pl.pallas_call(
        functools.partial(share_kernel, rows, both_rank),
        out_shape=[jax.ShapeDtypeStruct((step, both_rank), jnp.float32)] * dp,
        in_specs=[vmem] * 2,
        out_specs=[vmem] * dp,
        compiler_params=params,
        name="adapter_shares",
    )(got, ordered)
    up_grad = shares[0]
    for s in range(1, dp):
        route = [
            (d * mp + m, (d + s) % dp * mp + m - m % dp + (m + s) % dp)
            for d in range(dp) for m in range(mp)
        ]
        up_grad = up_grad + lax.ppermute(shares[s], ("dp", "mp"), route)

    key_gradient, value_grad, low_grad = pl.pallas_call(
        owner_kernel,
        out_shape=[
            jax.ShapeDtypeStruct((rows, width), jnp.bfloat16),
            jax.ShapeDtypeStruct((rows, width), jnp.bfloat16),
            jax.ShapeDtypeStruct((rows, both_rank), jnp.float32),
        ],
        in_specs=[vmem] * 2,
        out_specs=[vmem] * 3,
        compiler_params=params,
        name="owner_outputs",
    )(got, adapter_up_matrix)
    return query_grad_t.T, key_gradient, value_grad, low_grad, up_grad


def solution(mesh):
    in_specs = (
        P("dp", "mp"),
        P("dp", "mp"),
        P("dp", "mp"),
        P("dp", None),
        P("dp", None),
        P(("dp", "mp"), None),
        P(),
    )
    out_specs = (
        P("dp", "mp"),
        P(("dp", "mp"), None),
        P(("dp", "mp"), None),
        P(("dp", "mp"), None),
        P(("dp", "mp"), None),
    )
    body = functools.partial(local, mesh.shape["dp"], mesh.shape["mp"])
    return jax.shard_map(body, mesh=mesh, in_specs=in_specs, out_specs=out_specs, check_vma=False)
```

```python
import functools

import jax
import jax.numpy as jnp
from jax import lax
from jax.experimental import pallas as pl
from jax.experimental.pallas import tpu as pltpu
from jax.sharding import PartitionSpec as P

HS = 64
LANES = 128
CUT = 8

adapter_factor = 2.0

NT = (((1,), (1,)), ((), ()))
TN = (((0,), (0,)), ((), ()))


def dot(left, right, dims):
    return lax.dot_general(left, right, dims, preferred_element_type=jnp.float32)


def group_order(count):
    quarter = count // 4
    bits = quarter.bit_length() - 1
    assert count == 4 << bits
    turned = [sum(((i >> b) & 1) << (bits - 1 - b) for b in range(bits)) for i in range(quarter)]
    order = []
    for low, high in ((2, 1), (0, 3)):
        for i in range(0, quarter, 2):
            first, second = turned[i], turned[i + 1]
            order += [low * quarter + first, high * quarter + second]
            order += [low * quarter + second, high * quarter + first]
    return [count - 1 - place for place in order]


def source_range(source_ref, target_ref, count):
    position = lax.broadcasted_iota(jnp.int32, (1, count), 1)
    first = jnp.zeros((1, count), jnp.int32)
    last = jnp.zeros((1, count), jnp.int32)
    target_start = jnp.int32(0)
    source_start = jnp.int32(0)
    for i in range(source_ref.shape[1]):
        source_end = source_start + source_ref[0, i]
        inside = position >= target_start
        first = jnp.where(inside, source_start, first)
        last = jnp.where(inside, source_end, last)
        target_start = target_start + target_ref[0, i]
        source_start = source_end
    return first, last


def attention_kernel(
    source_any, target_any, query_any, grad_any, kv_any, low_any, query_grad_ref, sent_ref, turned_ref,
    source_ref, target_ref, query_ref, grad_ref, kv_ref, low_ref, sems,
):
    pairs = [
        (kv_any, kv_ref), (query_any, query_ref), (grad_any, grad_ref),
        (source_any, source_ref), (target_any, target_ref), (low_any, low_ref),
    ]
    copies = [
        pltpu.make_async_copy(here, there, sems.at[i]) for i, (here, there) in enumerate(pairs)
    ]
    for copy in copies:
        copy.start()
    for copy in copies:
        copy.wait()
    tgt_count = query_ref.shape[1]
    both = kv_ref[...]
    query_t = query_ref[...]
    grad_t = grad_ref[...]
    blank = jnp.zeros_like(query_t)
    query_wide = jnp.concatenate([query_t, blank], axis=0)
    grad_wide = jnp.concatenate([blank, grad_t], axis=0)
    scores = jnp.dot(both, query_wide, preferred_element_type=jnp.float32)
    dprob = jnp.dot(both, grad_wide, preferred_element_type=jnp.float32)
    first, last = source_range(source_ref, target_ref, tgt_count)
    position = lax.broadcasted_iota(jnp.int32, scores.shape, 0)
    allowed = jnp.logical_and(position >= first, position < last)
    expo = jnp.where(allowed, jnp.exp(scores), 0.0)
    total = jnp.sum(expo, axis=0, keepdims=True)
    delta = jnp.sum(expo * dprob, axis=0, keepdims=True) / total
    prob = expo * (1.0 / total)
    prob_low = prob.astype(jnp.bfloat16)
    dscore = (prob * (dprob - delta)).astype(jnp.bfloat16)
    both_grad = dot(dscore, query_wide, NT) + dot(prob_low, grad_wide, NT)
    both_low = both_grad.astype(jnp.bfloat16)
    low = low_ref[...].astype(jnp.float32)
    rows = low.shape[0]
    blocks = sent_ref.shape[0]
    packed = jnp.concatenate([low[at:at + CUT] for at in range(0, rows, CUT)], axis=1)
    packed = packed.astype(jnp.bfloat16)
    for at, block in enumerate(group_order(blocks)):
        sent_ref[at, :rows, :] = both_low[block * rows:(block + 1) * rows]
        sent_ref[at, rows:, :] = packed

    wide = both_low.astype(jnp.float32)
    parts = []
    for start in range(0, rows, CUT):
        for block in range(blocks):
            parts.append(wide[block * rows + start:block * rows + start + CUT])
    turned_ref[...] = jnp.concatenate(parts, axis=0).T.astype(jnp.bfloat16)

    query_grad = dot(both, dscore, TN)
    query_grad_ref[...] = query_grad[:HS].astype(jnp.bfloat16)


def split_kernel(turned_ref, *out_refs):
    dp = len(out_refs)
    step = HS // dp
    turned = turned_ref[...].astype(jnp.float32)
    pieces = []
    for j in range(dp):
        rows = [turned[j * step:(j + 1) * step], turned[HS + j * step:HS + (j + 1) * step]]
        pieces.append(jnp.concatenate(rows, axis=0))
    e = lax.rem(lax.axis_index("mp"), dp)
    pack = lax.axis_index("dp")
    for s, out_ref in enumerate(out_refs):
        turn = lax.rem(2 * e + s + dp - pack, dp)
        chosen = pieces[0]
        for j in range(1, dp):
            chosen = jnp.where(turn == j, pieces[j], chosen)
        out_ref[...] = chosen.astype(jnp.bfloat16)


def order_kernel(*refs):
    *arrived_refs, out_ref = refs
    dp = len(arrived_refs)
    mine = lax.rem(lax.axis_index("mp"), dp)
    for s, arrived_ref in enumerate(arrived_refs):
        out_ref[lax.rem(mine + dp - s, dp)] = arrived_ref[...]


def share_kernel(rows, both_rank, got_ref, pieces_ref, *out_refs):
    dp, piece_rows, _ = pieces_ref.shape
    blocks = got_ref.shape[0]
    order = group_order(blocks)
    lows = [
        got_ref[order.index(block), rows:, :].astype(jnp.float32) for block in range(blocks)
    ]
    lows = jnp.concatenate(lows, axis=0).astype(jnp.bfloat16)
    columns = jnp.concatenate([pieces_ref[e] for e in range(dp)], axis=0)
    share = None
    for cut in range(rows // CUT):
        tokens = columns[:, cut * blocks * CUT:(cut + 1) * blocks * CUT]
        product = jnp.dot(tokens, lows, preferred_element_type=jnp.float32)
        part = product[:, cut * both_rank:(cut + 1) * both_rank]
        share = part if share is None else share + part
    step = piece_rows // 2
    column = lax.broadcasted_iota(jnp.int32, (step, both_rank), 1)
    shares = []
    for e in range(dp):
        keys = share[e * piece_rows:e * piece_rows + step]
        values = share[e * piece_rows + step:(e + 1) * piece_rows]
        shares.append(adapter_factor * jnp.where(column < both_rank // 2, keys, values))
    mine = lax.axis_index("dp")
    for s, out_ref in enumerate(out_refs):
        turn = lax.rem(mine + s, dp)
        chosen = shares[0]
        for e in range(1, dp):
            chosen = jnp.where(turn == e, shares[e], chosen)
        out_ref[...] = chosen


def owner_kernel(got_ref, up_ref, key_ref, value_ref, low_grad_ref):
    rows = key_ref.shape[0]
    rank = up_ref.shape[0] // 2
    order = group_order(got_ref.shape[0])
    for pair in range(len(order) // 2):
        first = got_ref[order.index(2 * pair), :rows, :]
        second = got_ref[order.index(2 * pair + 1), :rows, :]
        columns = slice(2 * pair * HS, (2 * pair + 2) * HS)
        key_ref[:, columns] = jnp.concatenate([first[:, :HS], second[:, :HS]], axis=1)
        value_ref[:, columns] = jnp.concatenate([first[:, HS:], second[:, HS:]], axis=1)
    up = up_ref[...]
    from_key = dot(key_ref[...], up, NT)
    from_value = dot(value_ref[...], up, NT)
    column = lax.broadcasted_iota(jnp.int32, from_key.shape, 1)
    low_grad_ref[...] = adapter_factor * jnp.where(column < rank, from_key, from_value)


def local(dp, mp, query, kv_cache, out_grad, source_lengths, target_lengths, low_rank, adapter_up_matrix):
    tgt_count = query.shape[0]
    src_count = kv_cache.shape[0]
    rows, both_rank = low_rank.shape
    width = adapter_up_matrix.shape[1]
    step = HS // dp
    assert rows // CUT * both_rank == LANES
    vmem = pl.BlockSpec(memory_space=pltpu.VMEM)
    hbm = pl.BlockSpec(memory_space=pl.ANY)
    params = pltpu.CompilerParams(vmem_limit_bytes=48 * 1024 * 1024)
    whole_vmem = pltpu.CompilerParams(vmem_limit_bytes=60 * 1024 * 1024)

    query_t = query.T
    grad_t = out_grad.T
    query_grad_t, sent, turned = pl.pallas_call(
        attention_kernel,
        out_shape=[
            jax.ShapeDtypeStruct((HS, tgt_count), jnp.bfloat16),
            jax.ShapeDtypeStruct((mp, rows + CUT, LANES), jnp.bfloat16),
            jax.ShapeDtypeStruct((2 * HS, src_count), jnp.bfloat16),
        ],
        in_specs=[hbm] * 6,
        out_specs=[vmem] * 3,
        scratch_shapes=[
            pltpu.SMEM(source_lengths.shape, jnp.int32),
            pltpu.SMEM(target_lengths.shape, jnp.int32),
            pltpu.VMEM(query_t.shape, jnp.bfloat16),
            pltpu.VMEM(grad_t.shape, jnp.bfloat16),
            pltpu.VMEM(kv_cache.shape, jnp.bfloat16),
            pltpu.VMEM(low_rank.shape, jnp.bfloat16),
            pltpu.SemaphoreType.DMA((6,)),
        ],
        compiler_params=whole_vmem,
        name="attention_backward",
    )(source_lengths, target_lengths, query_t, grad_t, kv_cache, low_rank)

    route = [(h, h * dp % mp + h * dp // mp) for h in range(mp)]
    pieces = pl.pallas_call(
        split_kernel,
        out_shape=[jax.ShapeDtypeStruct((2 * step, src_count), jnp.bfloat16)] * dp,
        in_specs=[vmem],
        out_specs=[vmem] * dp,
        compiler_params=params,
        cost_estimate=pl.CostEstimate(flops=2 ** 36, bytes_accessed=2 ** 28, transcendentals=0),
        name="split_columns",
    )(lax.ppermute(turned, "mp", route))
    arrived = [pieces[0]]
    for s in range(1, dp):
        route = [(m, m - m % dp + (m + s) % dp) for m in range(mp)]
        arrived.append(lax.ppermute(pieces[s], "mp", route))
    ordered = pl.pallas_call(
        order_kernel,
        out_shape=jax.ShapeDtypeStruct((dp, 2 * step, src_count), jnp.bfloat16),
        in_specs=[vmem] * dp,
        out_specs=vmem,
        compiler_params=params,
        name="order_pieces",
    )(*arrived)

    got = lax.all_to_all(sent, "mp", 0, 0, axis_index_groups=[group_order(mp)], tiled=True)

    shares = pl.pallas_call(
        functools.partial(share_kernel, rows, both_rank),
        out_shape=[jax.ShapeDtypeStruct((step, both_rank), jnp.float32)] * dp,
        in_specs=[vmem] * 2,
        out_specs=[vmem] * dp,
        compiler_params=params,
        name="adapter_shares",
    )(got, ordered)
    up_grad = shares[0]
    for s in range(1, dp):
        route = [
            (d * mp + m, (d + s) % dp * mp + m - m % dp + (m + s) % dp)
            for d in range(dp) for m in range(mp)
        ]
        up_grad = up_grad + lax.ppermute(shares[s], ("dp", "mp"), route)

    key_gradient, value_grad, low_grad = pl.pallas_call(
        owner_kernel,
        out_shape=[
            jax.ShapeDtypeStruct((rows, width), jnp.bfloat16),
            jax.ShapeDtypeStruct((rows, width), jnp.bfloat16),
            jax.ShapeDtypeStruct((rows, both_rank), jnp.float32),
        ],
        in_specs=[vmem] * 2,
        out_specs=[vmem] * 3,
        compiler_params=params,
        name="owner_outputs",
    )(got, adapter_up_matrix)
    return query_grad_t.T, key_gradient, value_grad, low_grad, up_grad


def solution(mesh):
    in_specs = (
        P("dp", "mp"),
        P("dp", "mp"),
        P("dp", "mp"),
        P("dp", None),
        P("dp", None),
        P(("dp", "mp"), None),
        P(),
    )
    out_specs = (
        P("dp", "mp"),
        P(("dp", "mp"), None),
        P(("dp", "mp"), None),
        P(("dp", "mp"), None),
        P(("dp", "mp"), None),
    )
    body = functools.partial(local, mesh.shape["dp"], mesh.shape["mp"])
    return jax.shard_map(body, mesh=mesh, in_specs=in_specs, out_specs=out_specs, check_vma=False)
```

```python
import functools

import jax
import jax.numpy as jnp
from jax import lax
from jax.experimental import pallas as pl
from jax.experimental.pallas import tpu as pltpu
from jax.sharding import PartitionSpec as P

HS = 64
LANES = 128
CUT = 8

adapter_factor = 2.0

NT = (((1,), (1,)), ((), ()))
TN = (((0,), (0,)), ((), ()))


def dot(left, right, dims):
    return lax.dot_general(left, right, dims, preferred_element_type=jnp.float32)


def group_order(count):
    quarter = count // 4
    bits = quarter.bit_length() - 1
    assert count == 4 << bits
    turned = [sum(((i >> b) & 1) << (bits - 1 - b) for b in range(bits)) for i in range(quarter)]
    order = []
    for near, far in ((2, 3), (1, 0)):
        for i in range(quarter):
            order.append(near * quarter + turned[quarter - 1 - i])
            order.append(far * quarter + turned[(quarter - 1 - i) ^ 1])
    return order


def source_range(source_ref, target_ref, count):
    position = lax.broadcasted_iota(jnp.int32, (1, count), 1)
    first = jnp.zeros((1, count), jnp.int32)
    last = jnp.zeros((1, count), jnp.int32)
    target_start = jnp.int32(0)
    source_start = jnp.int32(0)
    for i in range(source_ref.shape[1]):
        source_end = source_start + source_ref[0, i]
        inside = position >= target_start
        first = jnp.where(inside, source_start, first)
        last = jnp.where(inside, source_end, last)
        target_start = target_start + target_ref[0, i]
        source_start = source_end
    return first, last


def attention_kernel(
    source_any, target_any, query_any, grad_any, kv_any, low_any, query_grad_ref, sent_ref, turned_ref,
    source_ref, target_ref, query_ref, grad_ref, kv_ref, low_ref, sems,
):
    pairs = [
        (kv_any, kv_ref), (query_any, query_ref), (grad_any, grad_ref),
        (source_any, source_ref), (target_any, target_ref), (low_any, low_ref),
    ]
    copies = [
        pltpu.make_async_copy(here, there, sems.at[i]) for i, (here, there) in enumerate(pairs)
    ]
    for copy in copies:
        copy.start()
    for copy in copies:
        copy.wait()
    tgt_count = query_ref.shape[1]
    both = kv_ref[...]
    query_t = query_ref[...]
    grad_t = grad_ref[...]
    blank = jnp.zeros_like(query_t)
    query_wide = jnp.concatenate([query_t, blank], axis=0)
    grad_wide = jnp.concatenate([blank, grad_t], axis=0)
    scores = jnp.dot(both, query_wide, preferred_element_type=jnp.float32)
    dprob = jnp.dot(both, grad_wide, preferred_element_type=jnp.float32)
    first, last = source_range(source_ref, target_ref, tgt_count)
    position = lax.broadcasted_iota(jnp.int32, scores.shape, 0)
    allowed = jnp.logical_and(position >= first, position < last)
    expo = jnp.where(allowed, jnp.exp(scores), 0.0)
    total = jnp.sum(expo, axis=0, keepdims=True)
    delta = jnp.sum(expo * dprob, axis=0, keepdims=True) / total
    prob = expo * (1.0 / total)
    prob_low = prob.astype(jnp.bfloat16)
    dscore = (prob * (dprob - delta)).astype(jnp.bfloat16)
    both_grad = dot(dscore, query_wide, NT) + dot(prob_low, grad_wide, NT)
    both_low = both_grad.astype(jnp.bfloat16)
    low = low_ref[...].astype(jnp.float32)
    rows = low.shape[0]
    blocks = sent_ref.shape[0]
    packed = jnp.concatenate([low[at:at + CUT] for at in range(0, rows, CUT)], axis=1)
    packed = packed.astype(jnp.bfloat16)
    for at, block in enumerate(group_order(blocks)):
        sent_ref[at, :rows, :] = both_low[block * rows:(block + 1) * rows]
        sent_ref[at, rows:, :] = packed

    wide = both_low.astype(jnp.float32)
    parts = []
    for start in range(0, rows, CUT):
        for block in range(blocks):
            parts.append(wide[block * rows + start:block * rows + start + CUT])
    turned_ref[...] = jnp.concatenate(parts, axis=0).T.astype(jnp.bfloat16)

    query_grad = dot(both, dscore, TN)
    query_grad_ref[...] = query_grad[:HS].astype(jnp.bfloat16)


def split_kernel(turned_ref, *out_refs):
    dp = len(out_refs)
    step = HS // dp
    turned = turned_ref[...].astype(jnp.float32)
    pieces = []
    for j in range(dp):
        rows = [turned[j * step:(j + 1) * step], turned[HS + j * step:HS + (j + 1) * step]]
        pieces.append(jnp.concatenate(rows, axis=0))
    e = lax.rem(lax.axis_index("mp"), dp)
    pack = lax.axis_index("dp")
    for s, out_ref in enumerate(out_refs):
        turn = lax.rem(2 * e + s + dp - pack, dp)
        chosen = pieces[0]
        for j in range(1, dp):
            chosen = jnp.where(turn == j, pieces[j], chosen)
        out_ref[...] = chosen.astype(jnp.bfloat16)


def order_kernel(*refs):
    *arrived_refs, out_ref = refs
    dp = len(arrived_refs)
    mine = lax.rem(lax.axis_index("mp"), dp)
    for s, arrived_ref in enumerate(arrived_refs):
        out_ref[lax.rem(mine + dp - s, dp)] = arrived_ref[...]


def share_kernel(rows, both_rank, got_ref, pieces_ref, *out_refs):
    dp, piece_rows, _ = pieces_ref.shape
    blocks = got_ref.shape[0]
    order = group_order(blocks)
    lows = [
        got_ref[order.index(block), rows:, :].astype(jnp.float32) for block in range(blocks)
    ]
    lows = jnp.concatenate(lows, axis=0).astype(jnp.bfloat16)
    columns = jnp.concatenate([pieces_ref[e] for e in range(dp)], axis=0)
    share = None
    for cut in range(rows // CUT):
        tokens = columns[:, cut * blocks * CUT:(cut + 1) * blocks * CUT]
        product = jnp.dot(tokens, lows, preferred_element_type=jnp.float32)
        part = product[:, cut * both_rank:(cut + 1) * both_rank]
        share = part if share is None else share + part
    step = piece_rows // 2
    column = lax.broadcasted_iota(jnp.int32, (step, both_rank), 1)
    shares = []
    for e in range(dp):
        keys = share[e * piece_rows:e * piece_rows + step]
        values = share[e * piece_rows + step:(e + 1) * piece_rows]
        shares.append(adapter_factor * jnp.where(column < both_rank // 2, keys, values))
    mine = lax.axis_index("dp")
    for s, out_ref in enumerate(out_refs):
        turn = lax.rem(mine + s, dp)
        chosen = shares[0]
        for e in range(1, dp):
            chosen = jnp.where(turn == e, shares[e], chosen)
        out_ref[...] = chosen


def owner_kernel(got_ref, up_ref, key_ref, value_ref, low_grad_ref):
    rows = key_ref.shape[0]
    rank = up_ref.shape[0] // 2
    order = group_order(got_ref.shape[0])
    for pair in range(len(order) // 2):
        first = got_ref[order.index(2 * pair), :rows, :]
        second = got_ref[order.index(2 * pair + 1), :rows, :]
        columns = slice(2 * pair * HS, (2 * pair + 2) * HS)
        key_ref[:, columns] = jnp.concatenate([first[:, :HS], second[:, :HS]], axis=1)
        value_ref[:, columns] = jnp.concatenate([first[:, HS:], second[:, HS:]], axis=1)
    up = up_ref[...]
    from_key = dot(key_ref[...], up, NT)
    from_value = dot(value_ref[...], up, NT)
    column = lax.broadcasted_iota(jnp.int32, from_key.shape, 1)
    low_grad_ref[...] = adapter_factor * jnp.where(column < rank, from_key, from_value)


def local(dp, mp, query, kv_cache, out_grad, source_lengths, target_lengths, low_rank, adapter_up_matrix):
    tgt_count = query.shape[0]
    src_count = kv_cache.shape[0]
    rows, both_rank = low_rank.shape
    width = adapter_up_matrix.shape[1]
    step = HS // dp
    assert rows // CUT * both_rank == LANES
    vmem = pl.BlockSpec(memory_space=pltpu.VMEM)
    hbm = pl.BlockSpec(memory_space=pl.ANY)
    params = pltpu.CompilerParams(vmem_limit_bytes=48 * 1024 * 1024)
    whole_vmem = pltpu.CompilerParams(vmem_limit_bytes=60 * 1024 * 1024)

    query_t = query.T
    grad_t = out_grad.T
    query_grad_t, sent, turned = pl.pallas_call(
        attention_kernel,
        out_shape=[
            jax.ShapeDtypeStruct((HS, tgt_count), jnp.bfloat16),
            jax.ShapeDtypeStruct((mp, rows + CUT, LANES), jnp.bfloat16),
            jax.ShapeDtypeStruct((2 * HS, src_count), jnp.bfloat16),
        ],
        in_specs=[hbm] * 6,
        out_specs=[vmem] * 3,
        scratch_shapes=[
            pltpu.SMEM(source_lengths.shape, jnp.int32),
            pltpu.SMEM(target_lengths.shape, jnp.int32),
            pltpu.VMEM(query_t.shape, jnp.bfloat16),
            pltpu.VMEM(grad_t.shape, jnp.bfloat16),
            pltpu.VMEM(kv_cache.shape, jnp.bfloat16),
            pltpu.VMEM(low_rank.shape, jnp.bfloat16),
            pltpu.SemaphoreType.DMA((6,)),
        ],
        compiler_params=whole_vmem,
        name="attention_backward",
    )(source_lengths, target_lengths, query_t, grad_t, kv_cache, low_rank)

    route = [(h, h * dp % mp + h * dp // mp) for h in range(mp)]
    pieces = pl.pallas_call(
        split_kernel,
        out_shape=[jax.ShapeDtypeStruct((2 * step, src_count), jnp.bfloat16)] * dp,
        in_specs=[vmem],
        out_specs=[vmem] * dp,
        compiler_params=params,
        cost_estimate=pl.CostEstimate(flops=2 ** 36, bytes_accessed=2 ** 28, transcendentals=0),
        name="split_columns",
    )(lax.ppermute(turned, "mp", route))
    arrived = [pieces[0]]
    for s in range(1, dp):
        route = [(m, m - m % dp + (m + s) % dp) for m in range(mp)]
        arrived.append(lax.ppermute(pieces[s], "mp", route))
    ordered = pl.pallas_call(
        order_kernel,
        out_shape=jax.ShapeDtypeStruct((dp, 2 * step, src_count), jnp.bfloat16),
        in_specs=[vmem] * dp,
        out_specs=vmem,
        compiler_params=params,
        name="order_pieces",
    )(*arrived)

    got = lax.all_to_all(sent, "mp", 0, 0, axis_index_groups=[group_order(mp)], tiled=True)

    shares = pl.pallas_call(
        functools.partial(share_kernel, rows, both_rank),
        out_shape=[jax.ShapeDtypeStruct((step, both_rank), jnp.float32)] * dp,
        in_specs=[vmem] * 2,
        out_specs=[vmem] * dp,
        compiler_params=params,
        name="adapter_shares",
    )(got, ordered)
    up_grad = shares[0]
    for s in range(1, dp):
        route = [
            (d * mp + m, (d + s) % dp * mp + m - m % dp + (m + s) % dp)
            for d in range(dp) for m in range(mp)
        ]
        up_grad = up_grad + lax.ppermute(shares[s], ("dp", "mp"), route)

    key_gradient, value_grad, low_grad = pl.pallas_call(
        owner_kernel,
        out_shape=[
            jax.ShapeDtypeStruct((rows, width), jnp.bfloat16),
            jax.ShapeDtypeStruct((rows, width), jnp.bfloat16),
            jax.ShapeDtypeStruct((rows, both_rank), jnp.float32),
        ],
        in_specs=[vmem] * 2,
        out_specs=[vmem] * 3,
        compiler_params=params,
        name="owner_outputs",
    )(got, adapter_up_matrix)
    return query_grad_t.T, key_gradient, value_grad, low_grad, up_grad


def solution(mesh):
    in_specs = (
        P("dp", "mp"),
        P("dp", "mp"),
        P("dp", "mp"),
        P("dp", None),
        P("dp", None),
        P(("dp", "mp"), None),
        P(),
    )
    out_specs = (
        P("dp", "mp"),
        P(("dp", "mp"), None),
        P(("dp", "mp"), None),
        P(("dp", "mp"), None),
        P(("dp", "mp"), None),
    )
    body = functools.partial(local, mesh.shape["dp"], mesh.shape["mp"])
    return jax.shard_map(body, mesh=mesh, in_specs=in_specs, out_specs=out_specs, check_vma=False)
```

```python
import functools

import jax
import jax.numpy as jnp
from jax import lax
from jax.experimental import pallas as pl
from jax.experimental.pallas import tpu as pltpu
from jax.sharding import PartitionSpec as P

HS = 64
LANES = 128
CUT = 8

adapter_factor = 2.0

NT = (((1,), (1,)), ((), ()))
TN = (((0,), (0,)), ((), ()))


def dot(left, right, dims):
    return lax.dot_general(left, right, dims, preferred_element_type=jnp.float32)


def group_order(count):
    quarter = count // 4
    bits = quarter.bit_length() - 1
    assert count == 4 << bits
    turned = [sum(((i >> b) & 1) << (bits - 1 - b) for b in range(bits)) for i in range(quarter)]
    order = []
    for near, far in ((2, 3), (1, 0)):
        for i in range(quarter):
            order.append(near * quarter + turned[quarter - 1 - i])
            order.append(far * quarter + turned[(quarter - 1 - i) ^ 1])
    return order


def source_range(source_ref, target_ref, count):
    position = lax.broadcasted_iota(jnp.int32, (1, count), 1)
    first = jnp.zeros((1, count), jnp.int32)
    last = jnp.zeros((1, count), jnp.int32)
    target_start = jnp.int32(0)
    source_start = jnp.int32(0)
    for i in range(source_ref.shape[1]):
        source_end = source_start + source_ref[0, i]
        inside = position >= target_start
        first = jnp.where(inside, source_start, first)
        last = jnp.where(inside, source_end, last)
        target_start = target_start + target_ref[0, i]
        source_start = source_end
    return first, last


def attention_kernel(
    source_any, target_any, query_any, grad_any, kv_any, low_any,
    query_grad_any, sent_any, turned_any,
    source_ref, target_ref, query_ref, grad_ref, kv_ref, low_ref,
    expo_ref, dprob_ref, query_grad_ref, sent_ref, turned_ref, in_sems, out_sems,
):
    tgt_count = query_ref.shape[1]
    src_count = kv_ref.shape[0]
    rows = low_ref.shape[0]
    blocks = src_count // rows
    per_chunk = LANES // rows
    chunks = src_count // LANES
    order = group_order(blocks)
    pairs = [
        (query_any, query_ref), (grad_any, grad_ref),
        (source_any, source_ref), (target_any, target_ref), (low_any, low_ref),
    ]
    for chunk in range(chunks):
        part = pl.ds(chunk * LANES, LANES)
        pairs.append((kv_any.at[part, :], kv_ref.at[part, :]))
    copies = [
        pltpu.make_async_copy(here, there, in_sems.at[i]) for i, (here, there) in enumerate(pairs)
    ]
    for copy in copies:
        copy.start()
    for copy in copies[:5]:
        copy.wait()

    first, last = source_range(source_ref, target_ref, tgt_count)
    query_t = query_ref[...]
    grad_t = grad_ref[...]
    blank = jnp.zeros_like(query_t)
    query_wide = jnp.concatenate([query_t, blank], axis=0)
    grad_wide = jnp.concatenate([blank, grad_t], axis=0)
    wide = jnp.concatenate([query_wide, grad_wide], axis=1)
    total = jnp.zeros((1, tgt_count), jnp.float32)
    weighted = jnp.zeros((1, tgt_count), jnp.float32)
    for chunk in range(chunks):
        copies[5 + chunk].wait()
        part = slice(chunk * LANES, (chunk + 1) * LANES)
        product = jnp.dot(kv_ref[part, :], wide, preferred_element_type=jnp.float32)
        dprob = product[:, tgt_count:]
        position = chunk * LANES + lax.broadcasted_iota(jnp.int32, (LANES, tgt_count), 0)
        allowed = jnp.logical_and(position >= first, position < last)
        expo = jnp.where(allowed, jnp.exp(product[:, :tgt_count]), 0.0)
        total += jnp.sum(expo, axis=0, keepdims=True)
        weighted += jnp.sum(expo * dprob, axis=0, keepdims=True)
        expo_ref[part, :] = expo
        dprob_ref[part, :] = dprob
    inverse = 1.0 / total
    delta = weighted * inverse

    low = low_ref[...].astype(jnp.float32)
    packed = jnp.concatenate([low[at:at + CUT] for at in range(0, rows, CUT)], axis=1)
    packed = packed.astype(jnp.bfloat16)
    query_grad = jnp.zeros((2 * HS, tgt_count), jnp.float32)
    sends = []
    for chunk in range(chunks):
        part = slice(chunk * LANES, (chunk + 1) * LANES)
        prob = expo_ref[part, :] * inverse
        dscore = (prob * (dprob_ref[part, :] - delta)).astype(jnp.bfloat16)
        both = jnp.concatenate([dscore, prob.astype(jnp.bfloat16)], axis=1)
        both_grad = dot(both, wide, NT)
        both_low = both_grad.astype(jnp.bfloat16)
        for at in range(per_chunk):
            place = order.index(chunk * per_chunk + at)
            sent_ref[place, :rows, :] = both_low[at * rows:(at + 1) * rows]
            sent_ref[place, rows:, :] = packed
            sends.append((sent_ref.at[place], sent_any.at[place]))
        exact = both_low.astype(jnp.float32)
        parts = [
            exact[at * rows + start:at * rows + start + CUT]
            for start in range(0, rows, CUT) for at in range(per_chunk)
        ]
        turned_ref[:, part] = jnp.concatenate(parts, axis=0).T.astype(jnp.bfloat16)
        sends.append((turned_ref.at[:, part], turned_any.at[:, part]))
        query_grad += dot(kv_ref[part, :], dscore, TN)
        if chunk == chunks - 1:
            query_grad_ref[...] = query_grad[:HS].astype(jnp.bfloat16)
            sends.append((query_grad_ref, query_grad_any))
        begun = chunk * (per_chunk + 1)
        for i in range(begun, len(sends)):
            pltpu.make_async_copy(*sends[i], out_sems.at[i]).start()
    for i, pair in enumerate(sends):
        pltpu.make_async_copy(*pair, out_sems.at[i]).wait()


def split_kernel(turned_ref, *out_refs):
    dp = len(out_refs)
    step = HS // dp
    turned = turned_ref[...].astype(jnp.float32)
    pieces = []
    for j in range(dp):
        rows = [turned[j * step:(j + 1) * step], turned[HS + j * step:HS + (j + 1) * step]]
        pieces.append(jnp.concatenate(rows, axis=0))
    e = lax.rem(lax.axis_index("mp"), dp)
    pack = lax.axis_index("dp")
    for s, out_ref in enumerate(out_refs):
        turn = lax.rem(2 * e + s + dp - pack, dp)
        chosen = pieces[0]
        for j in range(1, dp):
            chosen = jnp.where(turn == j, pieces[j], chosen)
        out_ref[...] = chosen.astype(jnp.bfloat16)


def order_kernel(*refs):
    *arrived_refs, out_ref = refs
    dp = len(arrived_refs)
    mine = lax.rem(lax.axis_index("mp"), dp)
    for s, arrived_ref in enumerate(arrived_refs):
        out_ref[lax.rem(mine + dp - s, dp)] = arrived_ref[...]


def share_kernel(rows, both_rank, got_ref, pieces_ref, *out_refs):
    dp, piece_rows, _ = pieces_ref.shape
    blocks = got_ref.shape[0]
    order = group_order(blocks)
    lows = [
        got_ref[order.index(block), rows:, :].astype(jnp.float32) for block in range(blocks)
    ]
    parts = []
    per_chunk = LANES // rows
    for at in range(0, blocks, per_chunk):
        low = jnp.concatenate(lows[at:at + per_chunk], axis=0)
        for cut in range(rows // CUT):
            parts.append(low[:, cut * both_rank:(cut + 1) * both_rank])
    lows = jnp.concatenate(parts, axis=0).astype(jnp.bfloat16)
    columns = jnp.concatenate([pieces_ref[e] for e in range(dp)], axis=0)
    share = jnp.dot(columns, lows, preferred_element_type=jnp.float32)
    step = piece_rows // 2
    column = lax.broadcasted_iota(jnp.int32, (step, both_rank), 1)
    shares = []
    for e in range(dp):
        keys = share[e * piece_rows:e * piece_rows + step]
        values = share[e * piece_rows + step:(e + 1) * piece_rows]
        shares.append(adapter_factor * jnp.where(column < both_rank // 2, keys, values))
    mine = lax.axis_index("dp")
    for s, out_ref in enumerate(out_refs):
        turn = lax.rem(mine + s, dp)
        chosen = shares[0]
        for e in range(1, dp):
            chosen = jnp.where(turn == e, shares[e], chosen)
        out_ref[...] = chosen


def owner_kernel(got_ref, up_ref, key_ref, value_ref, low_grad_ref):
    rows = key_ref.shape[0]
    rank = up_ref.shape[0] // 2
    order = group_order(got_ref.shape[0])
    for pair in range(len(order) // 2):
        first = got_ref[order.index(2 * pair), :rows, :]
        second = got_ref[order.index(2 * pair + 1), :rows, :]
        columns = slice(2 * pair * HS, (2 * pair + 2) * HS)
        key_ref[:, columns] = jnp.concatenate([first[:, :HS], second[:, :HS]], axis=1)
        value_ref[:, columns] = jnp.concatenate([first[:, HS:], second[:, HS:]], axis=1)
    up = up_ref[...]
    from_key = dot(key_ref[...], up, NT)
    from_value = dot(value_ref[...], up, NT)
    column = lax.broadcasted_iota(jnp.int32, from_key.shape, 1)
    low_grad_ref[...] = adapter_factor * jnp.where(column < rank, from_key, from_value)


def local(dp, mp, query, kv_cache, out_grad, source_lengths, target_lengths, low_rank, adapter_up_matrix):
    tgt_count = query.shape[0]
    src_count = kv_cache.shape[0]
    rows, both_rank = low_rank.shape
    width = adapter_up_matrix.shape[1]
    step = HS // dp
    assert rows // CUT * both_rank == LANES and mp * rows == src_count
    vmem = pl.BlockSpec(memory_space=pltpu.VMEM)
    hbm = pl.BlockSpec(memory_space=pl.ANY)
    params = pltpu.CompilerParams(vmem_limit_bytes=48 * 1024 * 1024)
    whole_vmem = pltpu.CompilerParams(vmem_limit_bytes=60 * 1024 * 1024)

    query_t = query.T
    grad_t = out_grad.T
    query_grad_t, sent, turned = pl.pallas_call(
        attention_kernel,
        out_shape=[
            jax.ShapeDtypeStruct((HS, tgt_count), jnp.bfloat16),
            jax.ShapeDtypeStruct((mp, rows + CUT, LANES), jnp.bfloat16),
            jax.ShapeDtypeStruct((2 * HS, src_count), jnp.bfloat16),
        ],
        in_specs=[hbm] * 6,
        out_specs=[hbm] * 3,
        scratch_shapes=[
            pltpu.SMEM(source_lengths.shape, jnp.int32),
            pltpu.SMEM(target_lengths.shape, jnp.int32),
            pltpu.VMEM(query_t.shape, jnp.bfloat16),
            pltpu.VMEM(grad_t.shape, jnp.bfloat16),
            pltpu.VMEM(kv_cache.shape, jnp.bfloat16),
            pltpu.VMEM(low_rank.shape, jnp.bfloat16),
            pltpu.VMEM((src_count, tgt_count), jnp.float32),
            pltpu.VMEM((src_count, tgt_count), jnp.float32),
            pltpu.VMEM(query_t.shape, jnp.bfloat16),
            pltpu.VMEM((mp, rows + CUT, LANES), jnp.bfloat16),
            pltpu.VMEM((2 * HS, src_count), jnp.bfloat16),
            pltpu.SemaphoreType.DMA((5 + src_count // LANES,)),
            pltpu.SemaphoreType.DMA((mp + src_count // LANES + 1,)),
        ],
        compiler_params=whole_vmem,
        name="attention_backward",
    )(source_lengths, target_lengths, query_t, grad_t, kv_cache, low_rank)

    route = [(h, h * dp % mp + h * dp // mp) for h in range(mp)]
    pieces = pl.pallas_call(
        split_kernel,
        out_shape=[jax.ShapeDtypeStruct((2 * step, src_count), jnp.bfloat16)] * dp,
        in_specs=[vmem],
        out_specs=[vmem] * dp,
        compiler_params=params,
        cost_estimate=pl.CostEstimate(flops=2 ** 36, bytes_accessed=2 ** 28, transcendentals=0),
        name="split_columns",
    )(lax.ppermute(turned, "mp", route))
    arrived = [pieces[0]]
    for s in range(1, dp):
        route = [(m, m - m % dp + (m + s) % dp) for m in range(mp)]
        arrived.append(lax.ppermute(pieces[s], "mp", route))
    ordered = pl.pallas_call(
        order_kernel,
        out_shape=jax.ShapeDtypeStruct((dp, 2 * step, src_count), jnp.bfloat16),
        in_specs=[vmem] * dp,
        out_specs=vmem,
        compiler_params=params,
        name="order_pieces",
    )(*arrived)

    got = lax.all_to_all(sent, "mp", 0, 0, axis_index_groups=[group_order(mp)], tiled=True)

    shares = pl.pallas_call(
        functools.partial(share_kernel, rows, both_rank),
        out_shape=[jax.ShapeDtypeStruct((step, both_rank), jnp.float32)] * dp,
        in_specs=[vmem] * 2,
        out_specs=[vmem] * dp,
        compiler_params=params,
        name="adapter_shares",
    )(got, ordered)
    up_grad = shares[0]
    for s in range(1, dp):
        route = [
            (d * mp + m, (d + s) % dp * mp + m - m % dp + (m + s) % dp)
            for d in range(dp) for m in range(mp)
        ]
        up_grad = up_grad + lax.ppermute(shares[s], ("dp", "mp"), route)

    key_gradient, value_grad, low_grad = pl.pallas_call(
        owner_kernel,
        out_shape=[
            jax.ShapeDtypeStruct((rows, width), jnp.bfloat16),
            jax.ShapeDtypeStruct((rows, width), jnp.bfloat16),
            jax.ShapeDtypeStruct((rows, both_rank), jnp.float32),
        ],
        in_specs=[vmem] * 2,
        out_specs=[vmem] * 3,
        compiler_params=params,
        name="owner_outputs",
    )(got, adapter_up_matrix)
    return query_grad_t.T, key_gradient, value_grad, low_grad, up_grad


def solution(mesh):
    in_specs = (
        P("dp", "mp"),
        P("dp", "mp"),
        P("dp", "mp"),
        P("dp", None),
        P("dp", None),
        P(("dp", "mp"), None),
        P(),
    )
    out_specs = (
        P("dp", "mp"),
        P(("dp", "mp"), None),
        P(("dp", "mp"), None),
        P(("dp", "mp"), None),
        P(("dp", "mp"), None),
    )
    body = functools.partial(local, mesh.shape["dp"], mesh.shape["mp"])
    return jax.shard_map(body, mesh=mesh, in_specs=in_specs, out_specs=out_specs, check_vma=False)
```

```python
import functools

import jax
import jax.numpy as jnp
from jax import lax
from jax.experimental import pallas as pl
from jax.experimental.pallas import tpu as pltpu
from jax.sharding import PartitionSpec as P

HS = 64
LANES = 128
CUT = 8

adapter_factor = 2.0

NT = (((1,), (1,)), ((), ()))
TN = (((0,), (0,)), ((), ()))


def dot(left, right, dims):
    return lax.dot_general(left, right, dims, preferred_element_type=jnp.float32)


def group_order(count):
    quarter = count // 4
    bits = quarter.bit_length() - 1
    assert count == 4 << bits
    turned = [sum(((i >> b) & 1) << (bits - 1 - b) for b in range(bits)) for i in range(quarter)]
    order = []
    for near, far in ((2, 3), (1, 0)):
        for i in range(quarter):
            order.append(near * quarter + turned[quarter - 1 - i])
            order.append(far * quarter + turned[(quarter - 1 - i) ^ 1])
    return order


def source_range(source_ref, target_ref, count):
    position = lax.broadcasted_iota(jnp.int32, (1, count), 1)
    first = jnp.zeros((1, count), jnp.int32)
    last = jnp.zeros((1, count), jnp.int32)
    target_start = jnp.int32(0)
    source_start = jnp.int32(0)
    for i in range(source_ref.shape[1]):
        source_end = source_start + source_ref[0, i]
        inside = position >= target_start
        first = jnp.where(inside, source_start, first)
        last = jnp.where(inside, source_end, last)
        target_start = target_start + target_ref[0, i]
        source_start = source_end
    return first, last


def attention_kernel(
    source_any, target_any, query_any, grad_any, kv_any, low_any,
    query_grad_any, sent_any, turned_any,
    source_ref, target_ref, query_ref, grad_ref, kv_ref, low_ref,
    query_grad_ref, sent_ref, turned_ref, sems, out_sems,
):
    pairs = [
        (kv_any, kv_ref), (query_any, query_ref), (grad_any, grad_ref),
        (source_any, source_ref), (target_any, target_ref), (low_any, low_ref),
    ]
    copies = [
        pltpu.make_async_copy(here, there, sems.at[i]) for i, (here, there) in enumerate(pairs)
    ]
    for copy in copies:
        copy.start()
    for copy in copies:
        copy.wait()
    tgt_count = query_ref.shape[1]
    both = kv_ref[...]
    query_t = query_ref[...]
    grad_t = grad_ref[...]
    blank = jnp.zeros_like(query_t)
    query_wide = jnp.concatenate([query_t, blank], axis=0)
    grad_wide = jnp.concatenate([blank, grad_t], axis=0)
    wide = jnp.concatenate([query_wide, grad_wide], axis=1)
    product = jnp.dot(both, wide, preferred_element_type=jnp.float32)
    scores = product[:, :tgt_count]
    dprob = product[:, tgt_count:]
    first, last = source_range(source_ref, target_ref, tgt_count)
    position = lax.broadcasted_iota(jnp.int32, scores.shape, 0)
    allowed = jnp.logical_and(position >= first, position < last)
    expo = jnp.where(allowed, jnp.exp(scores), 0.0)
    inverse = 1.0 / jnp.sum(expo, axis=0, keepdims=True)
    delta = jnp.sum(expo * dprob, axis=0, keepdims=True) * inverse
    prob = expo * inverse
    dscore = (prob * (dprob - delta)).astype(jnp.bfloat16)
    both_grad = dot(jnp.concatenate([dscore, prob.astype(jnp.bfloat16)], axis=1), wide, NT)
    both_low = both_grad.astype(jnp.bfloat16)
    low = low_ref[...].astype(jnp.float32)
    rows = low.shape[0]
    blocks = sent_ref.shape[0]
    packed = jnp.concatenate([low[at:at + CUT] for at in range(0, rows, CUT)], axis=1)
    packed = packed.astype(jnp.bfloat16)
    for at, block in enumerate(group_order(blocks)):
        sent_ref[at, :rows, :] = both_low[block * rows:(block + 1) * rows]
        sent_ref[at, rows:, :] = packed
    sent_copy = pltpu.make_async_copy(sent_ref, sent_any, out_sems.at[0])
    sent_copy.start()

    exact = both_low.astype(jnp.float32)
    parts = []
    for start in range(0, rows, CUT):
        for block in range(blocks):
            parts.append(exact[block * rows + start:block * rows + start + CUT])
    turned_ref[...] = jnp.concatenate(parts, axis=0).T.astype(jnp.bfloat16)
    turned_copy = pltpu.make_async_copy(turned_ref, turned_any, out_sems.at[1])
    turned_copy.start()

    query_grad = dot(both, dscore, TN)
    query_grad_ref[...] = query_grad[:HS].astype(jnp.bfloat16)
    query_copy = pltpu.make_async_copy(query_grad_ref, query_grad_any, out_sems.at[2])
    query_copy.start()
    sent_copy.wait()
    turned_copy.wait()
    query_copy.wait()


def split_kernel(turned_ref, *out_refs):
    dp = len(out_refs)
    step = HS // dp
    turned = turned_ref[...].astype(jnp.float32)
    pieces = []
    for j in range(dp):
        rows = [turned[j * step:(j + 1) * step], turned[HS + j * step:HS + (j + 1) * step]]
        pieces.append(jnp.concatenate(rows, axis=0))
    e = lax.rem(lax.axis_index("mp"), dp)
    pack = lax.axis_index("dp")
    for s, out_ref in enumerate(out_refs):
        turn = lax.rem(2 * e + s + dp - pack, dp)
        chosen = pieces[0]
        for j in range(1, dp):
            chosen = jnp.where(turn == j, pieces[j], chosen)
        out_ref[...] = chosen.astype(jnp.bfloat16)


def order_kernel(*refs):
    *arrived_refs, out_ref = refs
    dp = len(arrived_refs)
    mine = lax.rem(lax.axis_index("mp"), dp)
    for s, arrived_ref in enumerate(arrived_refs):
        out_ref[lax.rem(mine + dp - s, dp)] = arrived_ref[...]


def share_kernel(rows, both_rank, got_ref, pieces_ref, *out_refs):
    dp, piece_rows, _ = pieces_ref.shape
    blocks = got_ref.shape[0]
    order = group_order(blocks)
    lows = [
        got_ref[order.index(block), rows:, :].astype(jnp.float32) for block in range(blocks)
    ]
    lows = jnp.concatenate(lows, axis=0).astype(jnp.bfloat16)
    columns = jnp.concatenate([pieces_ref[e] for e in range(dp)], axis=0)
    share = None
    for cut in range(rows // CUT):
        tokens = columns[:, cut * blocks * CUT:(cut + 1) * blocks * CUT]
        product = jnp.dot(tokens, lows, preferred_element_type=jnp.float32)
        part = product[:, cut * both_rank:(cut + 1) * both_rank]
        share = part if share is None else share + part
    step = piece_rows // 2
    column = lax.broadcasted_iota(jnp.int32, (step, both_rank), 1)
    shares = []
    for e in range(dp):
        keys = share[e * piece_rows:e * piece_rows + step]
        values = share[e * piece_rows + step:(e + 1) * piece_rows]
        shares.append(adapter_factor * jnp.where(column < both_rank // 2, keys, values))
    mine = lax.axis_index("dp")
    for s, out_ref in enumerate(out_refs):
        turn = lax.rem(mine + s, dp)
        chosen = shares[0]
        for e in range(1, dp):
            chosen = jnp.where(turn == e, shares[e], chosen)
        out_ref[...] = chosen


def owner_kernel(got_ref, up_ref, key_ref, value_ref, low_grad_ref):
    rows = key_ref.shape[0]
    rank = up_ref.shape[0] // 2
    order = group_order(got_ref.shape[0])
    for pair in range(len(order) // 2):
        first = got_ref[order.index(2 * pair), :rows, :]
        second = got_ref[order.index(2 * pair + 1), :rows, :]
        columns = slice(2 * pair * HS, (2 * pair + 2) * HS)
        key_ref[:, columns] = jnp.concatenate([first[:, :HS], second[:, :HS]], axis=1)
        value_ref[:, columns] = jnp.concatenate([first[:, HS:], second[:, HS:]], axis=1)
    up = up_ref[...]
    from_key = dot(key_ref[...], up, NT)
    from_value = dot(value_ref[...], up, NT)
    column = lax.broadcasted_iota(jnp.int32, from_key.shape, 1)
    low_grad_ref[...] = adapter_factor * jnp.where(column < rank, from_key, from_value)


def local(dp, mp, query, kv_cache, out_grad, source_lengths, target_lengths, low_rank, adapter_up_matrix):
    tgt_count = query.shape[0]
    src_count = kv_cache.shape[0]
    rows, both_rank = low_rank.shape
    width = adapter_up_matrix.shape[1]
    step = HS // dp
    assert rows // CUT * both_rank == LANES
    vmem = pl.BlockSpec(memory_space=pltpu.VMEM)
    hbm = pl.BlockSpec(memory_space=pl.ANY)
    params = pltpu.CompilerParams(vmem_limit_bytes=48 * 1024 * 1024)
    whole_vmem = pltpu.CompilerParams(vmem_limit_bytes=60 * 1024 * 1024)

    query_t = query.T
    grad_t = out_grad.T
    query_grad_t, sent, turned = pl.pallas_call(
        attention_kernel,
        out_shape=[
            jax.ShapeDtypeStruct((HS, tgt_count), jnp.bfloat16),
            jax.ShapeDtypeStruct((mp, rows + CUT, LANES), jnp.bfloat16),
            jax.ShapeDtypeStruct((2 * HS, src_count), jnp.bfloat16),
        ],
        in_specs=[hbm] * 6,
        out_specs=[hbm] * 3,
        scratch_shapes=[
            pltpu.SMEM(source_lengths.shape, jnp.int32),
            pltpu.SMEM(target_lengths.shape, jnp.int32),
            pltpu.VMEM(query_t.shape, jnp.bfloat16),
            pltpu.VMEM(grad_t.shape, jnp.bfloat16),
            pltpu.VMEM(kv_cache.shape, jnp.bfloat16),
            pltpu.VMEM(low_rank.shape, jnp.bfloat16),
            pltpu.VMEM(query_t.shape, jnp.bfloat16),
            pltpu.VMEM((mp, rows + CUT, LANES), jnp.bfloat16),
            pltpu.VMEM((2 * HS, src_count), jnp.bfloat16),
            pltpu.SemaphoreType.DMA((6,)),
            pltpu.SemaphoreType.DMA((3,)),
        ],
        compiler_params=whole_vmem,
        name="attention_backward",
    )(source_lengths, target_lengths, query_t, grad_t, kv_cache, low_rank)

    route = [(h, h * dp % mp + h * dp // mp) for h in range(mp)]
    pieces = pl.pallas_call(
        split_kernel,
        out_shape=[jax.ShapeDtypeStruct((2 * step, src_count), jnp.bfloat16)] * dp,
        in_specs=[vmem],
        out_specs=[vmem] * dp,
        compiler_params=params,
        cost_estimate=pl.CostEstimate(flops=2 ** 36, bytes_accessed=2 ** 28, transcendentals=0),
        name="split_columns",
    )(lax.ppermute(turned, "mp", route))
    arrived = [pieces[0]]
    for s in range(1, dp):
        route = [(m, m - m % dp + (m + s) % dp) for m in range(mp)]
        arrived.append(lax.ppermute(pieces[s], "mp", route))
    ordered = pl.pallas_call(
        order_kernel,
        out_shape=jax.ShapeDtypeStruct((dp, 2 * step, src_count), jnp.bfloat16),
        in_specs=[vmem] * dp,
        out_specs=vmem,
        compiler_params=params,
        name="order_pieces",
    )(*arrived)

    got = lax.all_to_all(sent, "mp", 0, 0, axis_index_groups=[group_order(mp)], tiled=True)

    shares = pl.pallas_call(
        functools.partial(share_kernel, rows, both_rank),
        out_shape=[jax.ShapeDtypeStruct((step, both_rank), jnp.float32)] * dp,
        in_specs=[vmem] * 2,
        out_specs=[vmem] * dp,
        compiler_params=params,
        name="adapter_shares",
    )(got, ordered)
    up_grad = shares[0]
    for s in range(1, dp):
        route = [
            (d * mp + m, (d + s) % dp * mp + m - m % dp + (m + s) % dp)
            for d in range(dp) for m in range(mp)
        ]
        up_grad = up_grad + lax.ppermute(shares[s], ("dp", "mp"), route)

    key_gradient, value_grad, low_grad = pl.pallas_call(
        owner_kernel,
        out_shape=[
            jax.ShapeDtypeStruct((rows, width), jnp.bfloat16),
            jax.ShapeDtypeStruct((rows, width), jnp.bfloat16),
            jax.ShapeDtypeStruct((rows, both_rank), jnp.float32),
        ],
        in_specs=[vmem] * 2,
        out_specs=[vmem] * 3,
        compiler_params=params,
        name="owner_outputs",
    )(got, adapter_up_matrix)
    return query_grad_t.T, key_gradient, value_grad, low_grad, up_grad


def solution(mesh):
    in_specs = (
        P("dp", "mp"),
        P("dp", "mp"),
        P("dp", "mp"),
        P("dp", None),
        P("dp", None),
        P(("dp", "mp"), None),
        P(),
    )
    out_specs = (
        P("dp", "mp"),
        P(("dp", "mp"), None),
        P(("dp", "mp"), None),
        P(("dp", "mp"), None),
        P(("dp", "mp"), None),
    )
    body = functools.partial(local, mesh.shape["dp"], mesh.shape["mp"])
    return jax.shard_map(body, mesh=mesh, in_specs=in_specs, out_specs=out_specs, check_vma=False)
```

```python
import functools

import jax
import jax.numpy as jnp
from jax import lax
from jax.experimental import pallas as pl
from jax.experimental.pallas import tpu as pltpu
from jax.sharding import PartitionSpec as P

HS = 64
LANES = 128
CUT = 8

adapter_factor = 2.0

NT = (((1,), (1,)), ((), ()))
TN = (((0,), (0,)), ((), ()))


def dot(left, right, dims):
    return lax.dot_general(left, right, dims, preferred_element_type=jnp.float32)


def group_order(count):
    quarter = count // 4
    bits = quarter.bit_length() - 1
    assert count == 4 << bits
    turned = [sum(((i >> b) & 1) << (bits - 1 - b) for b in range(bits)) for i in range(quarter)]
    order = []
    for near, far in ((2, 3), (1, 0)):
        for i in range(quarter):
            order.append(near * quarter + turned[quarter - 1 - i])
            order.append(far * quarter + turned[(quarter - 1 - i) ^ 1])
    return order


def source_range(source_ref, target_ref, count):
    position = lax.broadcasted_iota(jnp.int32, (1, count), 1)
    first = jnp.zeros((1, count), jnp.int32)
    last = jnp.zeros((1, count), jnp.int32)
    target_start = jnp.int32(0)
    source_start = jnp.int32(0)
    for i in range(source_ref.shape[1]):
        source_end = source_start + source_ref[0, i]
        inside = position >= target_start
        first = jnp.where(inside, source_start, first)
        last = jnp.where(inside, source_end, last)
        target_start = target_start + target_ref[0, i]
        source_start = source_end
    return first, last


def attention_kernel(
    source_any, target_any, query_any, grad_any, kv_any, low_any, query_grad_ref, sent_ref, both_grad_ref,
    source_ref, target_ref, query_ref, grad_ref, kv_ref, low_ref, sems,
):
    pairs = [
        (kv_any, kv_ref), (query_any, query_ref), (grad_any, grad_ref),
        (source_any, source_ref), (target_any, target_ref), (low_any, low_ref),
    ]
    copies = [
        pltpu.make_async_copy(here, there, sems.at[i]) for i, (here, there) in enumerate(pairs)
    ]
    for copy in copies:
        copy.start()
    for copy in copies:
        copy.wait()
    tgt_count = query_ref.shape[1]
    both = kv_ref[...]
    query_t = query_ref[...]
    grad_t = grad_ref[...]
    blank = jnp.zeros_like(query_t)
    query_wide = jnp.concatenate([query_t, blank], axis=0)
    grad_wide = jnp.concatenate([blank, grad_t], axis=0)
    scores = jnp.dot(both, query_wide, preferred_element_type=jnp.float32)
    dprob = jnp.dot(both, grad_wide, preferred_element_type=jnp.float32)
    first, last = source_range(source_ref, target_ref, tgt_count)
    position = lax.broadcasted_iota(jnp.int32, scores.shape, 0)
    allowed = jnp.logical_and(position >= first, position < last)
    expo = jnp.where(allowed, jnp.exp(scores), 0.0)
    total = jnp.sum(expo, axis=0, keepdims=True)
    delta = jnp.sum(expo * dprob, axis=0, keepdims=True) / total
    prob = expo * (1.0 / total)
    prob_low = prob.astype(jnp.bfloat16)
    dscore = (prob * (dprob - delta)).astype(jnp.bfloat16)
    both_grad = dot(dscore, query_wide, NT) + dot(prob_low, grad_wide, NT)
    both_low = both_grad.astype(jnp.bfloat16)
    low = low_ref[...].astype(jnp.float32)
    rows = low.shape[0]
    blocks = sent_ref.shape[0]
    packed = jnp.concatenate([low[at:at + CUT] for at in range(0, rows, CUT)], axis=1)
    packed = packed.astype(jnp.bfloat16)
    for at, block in enumerate(group_order(blocks)):
        sent_ref[at, :rows, :] = both_low[block * rows:(block + 1) * rows]
        sent_ref[at, rows:, :] = packed

    both_grad_ref[...] = both_low
    query_grad = dot(both, dscore, TN)
    query_grad_ref[...] = query_grad[:HS].astype(jnp.bfloat16)


def split_kernel(rows, both_grad_ref, *out_refs):
    dp = len(out_refs)
    step = HS // dp
    exact = both_grad_ref[...].astype(jnp.float32)
    parts = []
    for start in range(0, rows, CUT):
        for block in range(0, exact.shape[0], rows):
            parts.append(exact[block + start:block + start + CUT])
    turned = jnp.concatenate(parts, axis=0).T
    pieces = []
    for j in range(dp):
        halves = [turned[j * step:(j + 1) * step], turned[HS + j * step:HS + (j + 1) * step]]
        pieces.append(jnp.concatenate(halves, axis=0))
    e = lax.rem(lax.axis_index("mp"), dp)
    pack = lax.axis_index("dp")
    for s, out_ref in enumerate(out_refs):
        turn = lax.rem(2 * e + s + dp - pack, dp)
        chosen = pieces[0]
        for j in range(1, dp):
            chosen = jnp.where(turn == j, pieces[j], chosen)
        out_ref[...] = chosen.astype(jnp.bfloat16)


def order_kernel(*refs):
    *arrived_refs, out_ref = refs
    dp = len(arrived_refs)
    mine = lax.rem(lax.axis_index("mp"), dp)
    for s, arrived_ref in enumerate(arrived_refs):
        out_ref[lax.rem(mine + dp - s, dp)] = arrived_ref[...]


def share_kernel(rows, both_rank, got_ref, pieces_ref, *out_refs):
    dp, piece_rows, _ = pieces_ref.shape
    blocks = got_ref.shape[0]
    order = group_order(blocks)
    lows = [
        got_ref[order.index(block), rows:, :].astype(jnp.float32) for block in range(blocks)
    ]
    lows = jnp.concatenate(lows, axis=0).astype(jnp.bfloat16)
    columns = jnp.concatenate([pieces_ref[e] for e in range(dp)], axis=0)
    share = None
    for cut in range(rows // CUT):
        tokens = columns[:, cut * blocks * CUT:(cut + 1) * blocks * CUT]
        product = jnp.dot(tokens, lows, preferred_element_type=jnp.float32)
        part = product[:, cut * both_rank:(cut + 1) * both_rank]
        share = part if share is None else share + part
    step = piece_rows // 2
    column = lax.broadcasted_iota(jnp.int32, (step, both_rank), 1)
    shares = []
    for e in range(dp):
        keys = share[e * piece_rows:e * piece_rows + step]
        values = share[e * piece_rows + step:(e + 1) * piece_rows]
        shares.append(adapter_factor * jnp.where(column < both_rank // 2, keys, values))
    mine = lax.axis_index("dp")
    for s, out_ref in enumerate(out_refs):
        turn = lax.rem(mine + s, dp)
        chosen = shares[0]
        for e in range(1, dp):
            chosen = jnp.where(turn == e, shares[e], chosen)
        out_ref[...] = chosen


def owner_kernel(got_ref, up_ref, key_ref, value_ref, low_grad_ref):
    rows = key_ref.shape[0]
    rank = up_ref.shape[0] // 2
    order = group_order(got_ref.shape[0])
    for pair in range(len(order) // 2):
        first = got_ref[order.index(2 * pair), :rows, :]
        second = got_ref[order.index(2 * pair + 1), :rows, :]
        columns = slice(2 * pair * HS, (2 * pair + 2) * HS)
        key_ref[:, columns] = jnp.concatenate([first[:, :HS], second[:, :HS]], axis=1)
        value_ref[:, columns] = jnp.concatenate([first[:, HS:], second[:, HS:]], axis=1)
    up = up_ref[...]
    from_key = dot(key_ref[...], up, NT)
    from_value = dot(value_ref[...], up, NT)
    column = lax.broadcasted_iota(jnp.int32, from_key.shape, 1)
    low_grad_ref[...] = adapter_factor * jnp.where(column < rank, from_key, from_value)


def local(dp, mp, query, kv_cache, out_grad, source_lengths, target_lengths, low_rank, adapter_up_matrix):
    tgt_count = query.shape[0]
    src_count = kv_cache.shape[0]
    rows, both_rank = low_rank.shape
    width = adapter_up_matrix.shape[1]
    step = HS // dp
    assert rows // CUT * both_rank == LANES
    vmem = pl.BlockSpec(memory_space=pltpu.VMEM)
    hbm = pl.BlockSpec(memory_space=pl.ANY)
    params = pltpu.CompilerParams(vmem_limit_bytes=48 * 1024 * 1024)
    whole_vmem = pltpu.CompilerParams(vmem_limit_bytes=60 * 1024 * 1024)

    query_t = query.T
    grad_t = out_grad.T
    query_grad_t, sent, both_grad = pl.pallas_call(
        attention_kernel,
        out_shape=[
            jax.ShapeDtypeStruct((HS, tgt_count), jnp.bfloat16),
            jax.ShapeDtypeStruct((mp, rows + CUT, LANES), jnp.bfloat16),
            jax.ShapeDtypeStruct((src_count, 2 * HS), jnp.bfloat16),
        ],
        in_specs=[hbm] * 6,
        out_specs=[vmem] * 3,
        scratch_shapes=[
            pltpu.SMEM(source_lengths.shape, jnp.int32),
            pltpu.SMEM(target_lengths.shape, jnp.int32),
            pltpu.VMEM(query_t.shape, jnp.bfloat16),
            pltpu.VMEM(grad_t.shape, jnp.bfloat16),
            pltpu.VMEM(kv_cache.shape, jnp.bfloat16),
            pltpu.VMEM(low_rank.shape, jnp.bfloat16),
            pltpu.SemaphoreType.DMA((6,)),
        ],
        compiler_params=whole_vmem,
        name="attention_backward",
    )(source_lengths, target_lengths, query_t, grad_t, kv_cache, low_rank)

    route = [(h, h * dp % mp + h * dp // mp) for h in range(mp)]
    pieces = pl.pallas_call(
        functools.partial(split_kernel, rows),
        out_shape=[jax.ShapeDtypeStruct((2 * step, src_count), jnp.bfloat16)] * dp,
        in_specs=[vmem],
        out_specs=[vmem] * dp,
        compiler_params=params,
        cost_estimate=pl.CostEstimate(flops=2 ** 36, bytes_accessed=2 ** 28, transcendentals=0),
        name="split_columns",
    )(lax.ppermute(both_grad, "mp", route))
    arrived = [pieces[0]]
    for s in range(1, dp):
        route = [(m, m - m % dp + (m + s) % dp) for m in range(mp)]
        arrived.append(lax.ppermute(pieces[s], "mp", route))
    ordered = pl.pallas_call(
        order_kernel,
        out_shape=jax.ShapeDtypeStruct((dp, 2 * step, src_count), jnp.bfloat16),
        in_specs=[vmem] * dp,
        out_specs=vmem,
        compiler_params=params,
        name="order_pieces",
    )(*arrived)

    got = lax.all_to_all(sent, "mp", 0, 0, axis_index_groups=[group_order(mp)], tiled=True)

    shares = pl.pallas_call(
        functools.partial(share_kernel, rows, both_rank),
        out_shape=[jax.ShapeDtypeStruct((step, both_rank), jnp.float32)] * dp,
        in_specs=[vmem] * 2,
        out_specs=[vmem] * dp,
        compiler_params=params,
        name="adapter_shares",
    )(got, ordered)
    up_grad = shares[0]
    for s in range(1, dp):
        route = [
            (d * mp + m, (d + s) % dp * mp + m - m % dp + (m + s) % dp)
            for d in range(dp) for m in range(mp)
        ]
        up_grad = up_grad + lax.ppermute(shares[s], ("dp", "mp"), route)

    key_gradient, value_grad, low_grad = pl.pallas_call(
        owner_kernel,
        out_shape=[
            jax.ShapeDtypeStruct((rows, width), jnp.bfloat16),
            jax.ShapeDtypeStruct((rows, width), jnp.bfloat16),
            jax.ShapeDtypeStruct((rows, both_rank), jnp.float32),
        ],
        in_specs=[vmem] * 2,
        out_specs=[vmem] * 3,
        compiler_params=params,
        name="owner_outputs",
    )(got, adapter_up_matrix)
    return query_grad_t.T, key_gradient, value_grad, low_grad, up_grad


def solution(mesh):
    in_specs = (
        P("dp", "mp"),
        P("dp", "mp"),
        P("dp", "mp"),
        P("dp", None),
        P("dp", None),
        P(("dp", "mp"), None),
        P(),
    )
    out_specs = (
        P("dp", "mp"),
        P(("dp", "mp"), None),
        P(("dp", "mp"), None),
        P(("dp", "mp"), None),
        P(("dp", "mp"), None),
    )
    body = functools.partial(local, mesh.shape["dp"], mesh.shape["mp"])
    return jax.shard_map(body, mesh=mesh, in_specs=in_specs, out_specs=out_specs, check_vma=False)
```

```python
import functools

import jax
import jax.numpy as jnp
from jax import lax
from jax.experimental import pallas as pl
from jax.experimental.pallas import tpu as pltpu
from jax.sharding import PartitionSpec as P

HS = 64
LANES = 128
CUT = 8

adapter_factor = 2.0

NT = (((1,), (1,)), ((), ()))
TN = (((0,), (0,)), ((), ()))


def dot(left, right, dims):
    return lax.dot_general(left, right, dims, preferred_element_type=jnp.float32)


def group_order(count):
    quarter = count // 4
    bits = quarter.bit_length() - 1
    assert count == 4 << bits
    turned = [sum(((i >> b) & 1) << (bits - 1 - b) for b in range(bits)) for i in range(quarter)]
    order = []
    for near, far in ((2, 3), (1, 0)):
        for i in range(quarter):
            order.append(near * quarter + turned[quarter - 1 - i])
            order.append(far * quarter + turned[(quarter - 1 - i) ^ 1])
    return order


def source_range(source_ref, target_ref, count):
    position = lax.broadcasted_iota(jnp.int32, (1, count), 1)
    first = jnp.zeros((1, count), jnp.int32)
    last = jnp.zeros((1, count), jnp.int32)
    target_start = jnp.int32(0)
    source_start = jnp.int32(0)
    for i in range(source_ref.shape[1]):
        source_end = source_start + source_ref[0, i]
        inside = position >= target_start
        first = jnp.where(inside, source_start, first)
        last = jnp.where(inside, source_end, last)
        target_start = target_start + target_ref[0, i]
        source_start = source_end
    return first, last


PARTS = 4


def cut_copies(source, target):
    size = target.shape[0] // PARTS
    return [(source.at[pl.ds(i * size, size)], target.at[pl.ds(i * size, size)]) for i in range(PARTS)]


def attention_kernel(
    source_any, target_any, query_any, grad_any, kv_any, low_any,
    query_grad_any, sent_any, both_grad_any,
    source_ref, target_ref, query_ref, grad_ref, kv_ref, low_ref,
    query_grad_ref, sent_ref, both_grad_ref, sems, out_sems,
):
    pairs = cut_copies(kv_any, kv_ref) + [
        (query_any, query_ref), (grad_any, grad_ref),
        (source_any, source_ref), (target_any, target_ref), (low_any, low_ref),
    ]
    copies = [
        pltpu.make_async_copy(here, there, sems.at[i]) for i, (here, there) in enumerate(pairs)
    ]
    for copy in copies:
        copy.start()
    for copy in copies:
        copy.wait()
    tgt_count = query_ref.shape[1]
    both = kv_ref[...]
    query_t = query_ref[...]
    grad_t = grad_ref[...]
    blank = jnp.zeros_like(query_t)
    query_wide = jnp.concatenate([query_t, blank], axis=0)
    grad_wide = jnp.concatenate([blank, grad_t], axis=0)
    scores = jnp.dot(both, query_wide, preferred_element_type=jnp.float32)
    dprob = jnp.dot(both, grad_wide, preferred_element_type=jnp.float32)
    first, last = source_range(source_ref, target_ref, tgt_count)
    position = lax.broadcasted_iota(jnp.int32, scores.shape, 0)
    allowed = jnp.logical_and(position >= first, position < last)
    expo = jnp.where(allowed, jnp.exp(scores), 0.0)
    total = jnp.sum(expo, axis=0, keepdims=True)
    delta = jnp.sum(expo * dprob, axis=0, keepdims=True) / total
    prob = expo * (1.0 / total)
    prob_low = prob.astype(jnp.bfloat16)
    dscore = (prob * (dprob - delta)).astype(jnp.bfloat16)
    both_grad = dot(dscore, query_wide, NT) + dot(prob_low, grad_wide, NT)
    both_low = both_grad.astype(jnp.bfloat16)
    low = low_ref[...].astype(jnp.float32)
    rows = low.shape[0]
    blocks = sent_ref.shape[0]
    packed = jnp.concatenate([low[at:at + CUT] for at in range(0, rows, CUT)], axis=1)
    packed = packed.astype(jnp.bfloat16)
    for at, block in enumerate(group_order(blocks)):
        sent_ref[at, :rows, :] = both_low[block * rows:(block + 1) * rows]
        sent_ref[at, rows:, :] = packed

    both_grad_ref[...] = both_low
    query_grad = dot(both, dscore, TN)
    query_grad_ref[...] = query_grad[:HS].astype(jnp.bfloat16)
    pairs = cut_copies(sent_ref, sent_any) + cut_copies(both_grad_ref, both_grad_any)
    pairs.append((query_grad_ref, query_grad_any))
    copies = [
        pltpu.make_async_copy(here, there, out_sems.at[i]) for i, (here, there) in enumerate(pairs)
    ]
    for copy in copies:
        copy.start()
    for copy in copies:
        copy.wait()


def split_kernel(rows, both_grad_ref, *out_refs):
    dp = len(out_refs)
    step = HS // dp
    exact = both_grad_ref[...].astype(jnp.float32)
    parts = []
    for start in range(0, rows, CUT):
        for block in range(0, exact.shape[0], rows):
            parts.append(exact[block + start:block + start + CUT])
    turned = jnp.concatenate(parts, axis=0).T
    pieces = []
    for j in range(dp):
        halves = [turned[j * step:(j + 1) * step], turned[HS + j * step:HS + (j + 1) * step]]
        pieces.append(jnp.concatenate(halves, axis=0))
    e = lax.rem(lax.axis_index("mp"), dp)
    pack = lax.axis_index("dp")
    for s, out_ref in enumerate(out_refs):
        turn = lax.rem(2 * e + s + dp - pack, dp)
        chosen = pieces[0]
        for j in range(1, dp):
            chosen = jnp.where(turn == j, pieces[j], chosen)
        out_ref[...] = chosen.astype(jnp.bfloat16)


def order_kernel(*refs):
    *arrived_refs, out_ref = refs
    dp = len(arrived_refs)
    mine = lax.rem(lax.axis_index("mp"), dp)
    for s, arrived_ref in enumerate(arrived_refs):
        out_ref[lax.rem(mine + dp - s, dp)] = arrived_ref[...]


def share_kernel(rows, both_rank, got_ref, pieces_ref, *out_refs):
    dp, piece_rows, _ = pieces_ref.shape
    blocks = got_ref.shape[0]
    order = group_order(blocks)
    lows = [
        got_ref[order.index(block), rows:, :].astype(jnp.float32) for block in range(blocks)
    ]
    lows = jnp.concatenate(lows, axis=0).astype(jnp.bfloat16)
    columns = jnp.concatenate([pieces_ref[e] for e in range(dp)], axis=0)
    share = None
    for cut in range(rows // CUT):
        tokens = columns[:, cut * blocks * CUT:(cut + 1) * blocks * CUT]
        product = jnp.dot(tokens, lows, preferred_element_type=jnp.float32)
        part = product[:, cut * both_rank:(cut + 1) * both_rank]
        share = part if share is None else share + part
    step = piece_rows // 2
    column = lax.broadcasted_iota(jnp.int32, (step, both_rank), 1)
    shares = []
    for e in range(dp):
        keys = share[e * piece_rows:e * piece_rows + step]
        values = share[e * piece_rows + step:(e + 1) * piece_rows]
        shares.append(adapter_factor * jnp.where(column < both_rank // 2, keys, values))
    mine = lax.axis_index("dp")
    for s, out_ref in enumerate(out_refs):
        turn = lax.rem(mine + s, dp)
        chosen = shares[0]
        for e in range(1, dp):
            chosen = jnp.where(turn == e, shares[e], chosen)
        out_ref[...] = chosen


def owner_kernel(got_ref, up_ref, key_ref, value_ref, low_grad_ref):
    rows = key_ref.shape[0]
    rank = up_ref.shape[0] // 2
    order = group_order(got_ref.shape[0])
    for pair in range(len(order) // 2):
        first = got_ref[order.index(2 * pair), :rows, :]
        second = got_ref[order.index(2 * pair + 1), :rows, :]
        columns = slice(2 * pair * HS, (2 * pair + 2) * HS)
        key_ref[:, columns] = jnp.concatenate([first[:, :HS], second[:, :HS]], axis=1)
        value_ref[:, columns] = jnp.concatenate([first[:, HS:], second[:, HS:]], axis=1)
    up = up_ref[...]
    from_key = dot(key_ref[...], up, NT)
    from_value = dot(value_ref[...], up, NT)
    column = lax.broadcasted_iota(jnp.int32, from_key.shape, 1)
    low_grad_ref[...] = adapter_factor * jnp.where(column < rank, from_key, from_value)


def local(dp, mp, query, kv_cache, out_grad, source_lengths, target_lengths, low_rank, adapter_up_matrix):
    tgt_count = query.shape[0]
    src_count = kv_cache.shape[0]
    rows, both_rank = low_rank.shape
    width = adapter_up_matrix.shape[1]
    step = HS // dp
    assert rows // CUT * both_rank == LANES
    vmem = pl.BlockSpec(memory_space=pltpu.VMEM)
    hbm = pl.BlockSpec(memory_space=pl.ANY)
    params = pltpu.CompilerParams(vmem_limit_bytes=48 * 1024 * 1024)
    whole_vmem = pltpu.CompilerParams(vmem_limit_bytes=60 * 1024 * 1024)

    query_t = query.T
    grad_t = out_grad.T
    query_grad_t, sent, both_grad = pl.pallas_call(
        attention_kernel,
        out_shape=[
            jax.ShapeDtypeStruct((HS, tgt_count), jnp.bfloat16),
            jax.ShapeDtypeStruct((mp, rows + CUT, LANES), jnp.bfloat16),
            jax.ShapeDtypeStruct((src_count, 2 * HS), jnp.bfloat16),
        ],
        in_specs=[hbm] * 6,
        out_specs=[hbm] * 3,
        scratch_shapes=[
            pltpu.SMEM(source_lengths.shape, jnp.int32),
            pltpu.SMEM(target_lengths.shape, jnp.int32),
            pltpu.VMEM(query_t.shape, jnp.bfloat16),
            pltpu.VMEM(grad_t.shape, jnp.bfloat16),
            pltpu.VMEM(kv_cache.shape, jnp.bfloat16),
            pltpu.VMEM(low_rank.shape, jnp.bfloat16),
            pltpu.VMEM(query_t.shape, jnp.bfloat16),
            pltpu.VMEM((mp, rows + CUT, LANES), jnp.bfloat16),
            pltpu.VMEM((src_count, 2 * HS), jnp.bfloat16),
            pltpu.SemaphoreType.DMA((PARTS + 5,)),
            pltpu.SemaphoreType.DMA((2 * PARTS + 1,)),
        ],
        compiler_params=whole_vmem,
        name="attention_backward",
    )(source_lengths, target_lengths, query_t, grad_t, kv_cache, low_rank)

    route = [(h, h * dp % mp + h * dp // mp) for h in range(mp)]
    pieces = pl.pallas_call(
        functools.partial(split_kernel, rows),
        out_shape=[jax.ShapeDtypeStruct((2 * step, src_count), jnp.bfloat16)] * dp,
        in_specs=[vmem],
        out_specs=[vmem] * dp,
        compiler_params=params,
        cost_estimate=pl.CostEstimate(flops=2 ** 36, bytes_accessed=2 ** 28, transcendentals=0),
        name="split_columns",
    )(lax.ppermute(both_grad, "mp", route))
    arrived = [pieces[0]]
    for s in range(1, dp):
        route = [(m, m - m % dp + (m + s) % dp) for m in range(mp)]
        arrived.append(lax.ppermute(pieces[s], "mp", route))
    ordered = pl.pallas_call(
        order_kernel,
        out_shape=jax.ShapeDtypeStruct((dp, 2 * step, src_count), jnp.bfloat16),
        in_specs=[vmem] * dp,
        out_specs=vmem,
        compiler_params=params,
        name="order_pieces",
    )(*arrived)

    got = lax.all_to_all(sent, "mp", 0, 0, axis_index_groups=[group_order(mp)], tiled=True)

    shares = pl.pallas_call(
        functools.partial(share_kernel, rows, both_rank),
        out_shape=[jax.ShapeDtypeStruct((step, both_rank), jnp.float32)] * dp,
        in_specs=[vmem] * 2,
        out_specs=[vmem] * dp,
        compiler_params=params,
        name="adapter_shares",
    )(got, ordered)
    up_grad = shares[0]
    for s in range(1, dp):
        route = [
            (d * mp + m, (d + s) % dp * mp + m - m % dp + (m + s) % dp)
            for d in range(dp) for m in range(mp)
        ]
        up_grad = up_grad + lax.ppermute(shares[s], ("dp", "mp"), route)

    key_gradient, value_grad, low_grad = pl.pallas_call(
        owner_kernel,
        out_shape=[
            jax.ShapeDtypeStruct((rows, width), jnp.bfloat16),
            jax.ShapeDtypeStruct((rows, width), jnp.bfloat16),
            jax.ShapeDtypeStruct((rows, both_rank), jnp.float32),
        ],
        in_specs=[vmem] * 2,
        out_specs=[vmem] * 3,
        compiler_params=params,
        name="owner_outputs",
    )(got, adapter_up_matrix)
    return query_grad_t.T, key_gradient, value_grad, low_grad, up_grad


def solution(mesh):
    in_specs = (
        P("dp", "mp"),
        P("dp", "mp"),
        P("dp", "mp"),
        P("dp", None),
        P("dp", None),
        P(("dp", "mp"), None),
        P(),
    )
    out_specs = (
        P("dp", "mp"),
        P(("dp", "mp"), None),
        P(("dp", "mp"), None),
        P(("dp", "mp"), None),
        P(("dp", "mp"), None),
    )
    body = functools.partial(local, mesh.shape["dp"], mesh.shape["mp"])
    return jax.shard_map(body, mesh=mesh, in_specs=in_specs, out_specs=out_specs, check_vma=False)
```

```python
import functools

import jax
import jax.numpy as jnp
from jax import lax
from jax.experimental import pallas as pl
from jax.experimental.pallas import tpu as pltpu
from jax.sharding import PartitionSpec as P

HS = 64
LANES = 128
CUT = 8

adapter_factor = 2.0

NT = (((1,), (1,)), ((), ()))
TN = (((0,), (0,)), ((), ()))


def dot(left, right, dims):
    return lax.dot_general(left, right, dims, preferred_element_type=jnp.float32)


def group_order(count):
    quarter = count // 4
    bits = quarter.bit_length() - 1
    assert count == 4 << bits
    turned = [sum(((i >> b) & 1) << (bits - 1 - b) for b in range(bits)) for i in range(quarter)]
    order = []
    for near, far in ((2, 3), (1, 0)):
        for i in range(quarter):
            order.append(near * quarter + turned[quarter - 1 - i])
            order.append(far * quarter + turned[(quarter - 1 - i) ^ 1])
    return order


def source_range(source_ref, target_ref, count):
    position = lax.broadcasted_iota(jnp.int32, (1, count), 1)
    first = jnp.zeros((1, count), jnp.int32)
    last = jnp.zeros((1, count), jnp.int32)
    target_start = jnp.int32(0)
    source_start = jnp.int32(0)
    for i in range(source_ref.shape[1]):
        source_end = source_start + source_ref[0, i]
        inside = position >= target_start
        first = jnp.where(inside, source_start, first)
        last = jnp.where(inside, source_end, last)
        target_start = target_start + target_ref[0, i]
        source_start = source_end
    return first, last


def attention_kernel(
    source_any, target_any, query_any, grad_any, kv_any, low_any, query_grad_ref, sent_ref, both_grad_ref,
    source_ref, target_ref, query_ref, grad_ref, kv_ref, low_ref, sems,
):
    pairs = [
        (kv_any, kv_ref), (query_any, query_ref), (grad_any, grad_ref),
        (source_any, source_ref), (target_any, target_ref), (low_any, low_ref),
    ]
    copies = [
        pltpu.make_async_copy(here, there, sems.at[i]) for i, (here, there) in enumerate(pairs)
    ]
    for copy in copies:
        copy.start()
    for copy in copies:
        copy.wait()
    tgt_count = query_ref.shape[1]
    both = kv_ref[...]
    query_t = query_ref[...]
    grad_t = grad_ref[...]
    blank = jnp.zeros_like(query_t)
    query_wide = jnp.concatenate([query_t, blank], axis=0)
    grad_wide = jnp.concatenate([blank, grad_t], axis=0)
    first, last = source_range(source_ref, target_ref, tgt_count)
    half = both.shape[0] // 2
    parts = [both[:half], both[half:]]
    scores = [jnp.dot(part, query_wide, preferred_element_type=jnp.float32) for part in parts]
    dprobs = [jnp.dot(part, grad_wide, preferred_element_type=jnp.float32) for part in parts]
    expos = []
    for i, score in enumerate(scores):
        position = i * half + lax.broadcasted_iota(jnp.int32, score.shape, 0)
        allowed = jnp.logical_and(position >= first, position < last)
        expos.append(jnp.where(allowed, jnp.exp(score), 0.0))
    inverse = 1.0 / sum(jnp.sum(expo, axis=0, keepdims=True) for expo in expos)
    weighted = sum(
        jnp.sum(expo * dprob, axis=0, keepdims=True) for expo, dprob in zip(expos, dprobs)
    )
    delta = weighted * inverse
    probs = [expo * inverse for expo in expos]
    dscores = [
        (prob * (dprob - delta)).astype(jnp.bfloat16) for prob, dprob in zip(probs, dprobs)
    ]
    both_low = jnp.concatenate([
        (dot(dscore, query_wide, NT) + dot(prob.astype(jnp.bfloat16), grad_wide, NT))
        .astype(jnp.bfloat16)
        for dscore, prob in zip(dscores, probs)
    ], axis=0)
    low = low_ref[...].astype(jnp.float32)
    rows = low.shape[0]
    blocks = sent_ref.shape[0]
    packed = jnp.concatenate([low[at:at + CUT] for at in range(0, rows, CUT)], axis=1)
    packed = packed.astype(jnp.bfloat16)
    for at, block in enumerate(group_order(blocks)):
        sent_ref[at, :rows, :] = both_low[block * rows:(block + 1) * rows]
        sent_ref[at, rows:, :] = packed

    both_grad_ref[...] = both_low
    query_grad = sum(dot(part, dscore, TN) for part, dscore in zip(parts, dscores))
    query_grad_ref[...] = query_grad[:HS].astype(jnp.bfloat16)


def split_kernel(rows, both_grad_ref, *out_refs):
    dp = len(out_refs)
    step = HS // dp
    exact = both_grad_ref[...].astype(jnp.float32)
    parts = []
    for start in range(0, rows, CUT):
        for block in range(0, exact.shape[0], rows):
            parts.append(exact[block + start:block + start + CUT])
    turned = jnp.concatenate(parts, axis=0).T
    pieces = []
    for j in range(dp):
        halves = [turned[j * step:(j + 1) * step], turned[HS + j * step:HS + (j + 1) * step]]
        pieces.append(jnp.concatenate(halves, axis=0))
    e = lax.rem(lax.axis_index("mp"), dp)
    pack = lax.axis_index("dp")
    for s, out_ref in enumerate(out_refs):
        turn = lax.rem(2 * e + s + dp - pack, dp)
        chosen = pieces[0]
        for j in range(1, dp):
            chosen = jnp.where(turn == j, pieces[j], chosen)
        out_ref[...] = chosen.astype(jnp.bfloat16)


def order_kernel(*refs):
    *arrived_refs, out_ref = refs
    dp = len(arrived_refs)
    mine = lax.rem(lax.axis_index("mp"), dp)
    for s, arrived_ref in enumerate(arrived_refs):
        out_ref[lax.rem(mine + dp - s, dp)] = arrived_ref[...]


def share_kernel(rows, both_rank, got_ref, pieces_ref, *out_refs):
    dp, piece_rows, _ = pieces_ref.shape
    blocks = got_ref.shape[0]
    order = group_order(blocks)
    lows = [
        got_ref[order.index(block), rows:, :].astype(jnp.float32) for block in range(blocks)
    ]
    lows = jnp.concatenate(lows, axis=0).astype(jnp.bfloat16)
    columns = jnp.concatenate([pieces_ref[e] for e in range(dp)], axis=0)
    share = None
    for cut in range(rows // CUT):
        tokens = columns[:, cut * blocks * CUT:(cut + 1) * blocks * CUT]
        product = jnp.dot(tokens, lows, preferred_element_type=jnp.float32)
        part = product[:, cut * both_rank:(cut + 1) * both_rank]
        share = part if share is None else share + part
    step = piece_rows // 2
    column = lax.broadcasted_iota(jnp.int32, (step, both_rank), 1)
    shares = []
    for e in range(dp):
        keys = share[e * piece_rows:e * piece_rows + step]
        values = share[e * piece_rows + step:(e + 1) * piece_rows]
        shares.append(adapter_factor * jnp.where(column < both_rank // 2, keys, values))
    mine = lax.axis_index("dp")
    for s, out_ref in enumerate(out_refs):
        turn = lax.rem(mine + s, dp)
        chosen = shares[0]
        for e in range(1, dp):
            chosen = jnp.where(turn == e, shares[e], chosen)
        out_ref[...] = chosen


def owner_kernel(got_ref, up_ref, key_ref, value_ref, low_grad_ref):
    rows = key_ref.shape[0]
    rank = up_ref.shape[0] // 2
    order = group_order(got_ref.shape[0])
    for pair in range(len(order) // 2):
        first = got_ref[order.index(2 * pair), :rows, :]
        second = got_ref[order.index(2 * pair + 1), :rows, :]
        columns = slice(2 * pair * HS, (2 * pair + 2) * HS)
        key_ref[:, columns] = jnp.concatenate([first[:, :HS], second[:, :HS]], axis=1)
        value_ref[:, columns] = jnp.concatenate([first[:, HS:], second[:, HS:]], axis=1)
    up = up_ref[...]
    from_key = dot(key_ref[...], up, NT)
    from_value = dot(value_ref[...], up, NT)
    column = lax.broadcasted_iota(jnp.int32, from_key.shape, 1)
    low_grad_ref[...] = adapter_factor * jnp.where(column < rank, from_key, from_value)


def local(dp, mp, query, kv_cache, out_grad, source_lengths, target_lengths, low_rank, adapter_up_matrix):
    tgt_count = query.shape[0]
    src_count = kv_cache.shape[0]
    rows, both_rank = low_rank.shape
    width = adapter_up_matrix.shape[1]
    step = HS // dp
    assert rows // CUT * both_rank == LANES
    vmem = pl.BlockSpec(memory_space=pltpu.VMEM)
    hbm = pl.BlockSpec(memory_space=pl.ANY)
    params = pltpu.CompilerParams(vmem_limit_bytes=48 * 1024 * 1024)
    whole_vmem = pltpu.CompilerParams(vmem_limit_bytes=60 * 1024 * 1024)

    query_t = query.T
    grad_t = out_grad.T
    query_grad_t, sent, both_grad = pl.pallas_call(
        attention_kernel,
        out_shape=[
            jax.ShapeDtypeStruct((HS, tgt_count), jnp.bfloat16),
            jax.ShapeDtypeStruct((mp, rows + CUT, LANES), jnp.bfloat16),
            jax.ShapeDtypeStruct((src_count, 2 * HS), jnp.bfloat16),
        ],
        in_specs=[hbm] * 6,
        out_specs=[vmem] * 3,
        scratch_shapes=[
            pltpu.SMEM(source_lengths.shape, jnp.int32),
            pltpu.SMEM(target_lengths.shape, jnp.int32),
            pltpu.VMEM(query_t.shape, jnp.bfloat16),
            pltpu.VMEM(grad_t.shape, jnp.bfloat16),
            pltpu.VMEM(kv_cache.shape, jnp.bfloat16),
            pltpu.VMEM(low_rank.shape, jnp.bfloat16),
            pltpu.SemaphoreType.DMA((6,)),
        ],
        compiler_params=whole_vmem,
        name="attention_backward",
    )(source_lengths, target_lengths, query_t, grad_t, kv_cache, low_rank)

    route = [(h, h * dp % mp + h * dp // mp) for h in range(mp)]
    pieces = pl.pallas_call(
        functools.partial(split_kernel, rows),
        out_shape=[jax.ShapeDtypeStruct((2 * step, src_count), jnp.bfloat16)] * dp,
        in_specs=[vmem],
        out_specs=[vmem] * dp,
        compiler_params=params,
        cost_estimate=pl.CostEstimate(flops=2 ** 36, bytes_accessed=2 ** 28, transcendentals=0),
        name="split_columns",
    )(lax.ppermute(both_grad, "mp", route))
    arrived = [pieces[0]]
    for s in range(1, dp):
        route = [(m, m - m % dp + (m + s) % dp) for m in range(mp)]
        arrived.append(lax.ppermute(pieces[s], "mp", route))
    ordered = pl.pallas_call(
        order_kernel,
        out_shape=jax.ShapeDtypeStruct((dp, 2 * step, src_count), jnp.bfloat16),
        in_specs=[vmem] * dp,
        out_specs=vmem,
        compiler_params=params,
        name="order_pieces",
    )(*arrived)

    got = lax.all_to_all(sent, "mp", 0, 0, axis_index_groups=[group_order(mp)], tiled=True)

    shares = pl.pallas_call(
        functools.partial(share_kernel, rows, both_rank),
        out_shape=[jax.ShapeDtypeStruct((step, both_rank), jnp.float32)] * dp,
        in_specs=[vmem] * 2,
        out_specs=[vmem] * dp,
        compiler_params=params,
        name="adapter_shares",
    )(got, ordered)
    up_grad = shares[0]
    for s in range(1, dp):
        route = [
            (d * mp + m, (d + s) % dp * mp + m - m % dp + (m + s) % dp)
            for d in range(dp) for m in range(mp)
        ]
        up_grad = up_grad + lax.ppermute(shares[s], ("dp", "mp"), route)

    key_gradient, value_grad, low_grad = pl.pallas_call(
        owner_kernel,
        out_shape=[
            jax.ShapeDtypeStruct((rows, width), jnp.bfloat16),
            jax.ShapeDtypeStruct((rows, width), jnp.bfloat16),
            jax.ShapeDtypeStruct((rows, both_rank), jnp.float32),
        ],
        in_specs=[vmem] * 2,
        out_specs=[vmem] * 3,
        compiler_params=params,
        name="owner_outputs",
    )(got, adapter_up_matrix)
    return query_grad_t.T, key_gradient, value_grad, low_grad, up_grad


def solution(mesh):
    in_specs = (
        P("dp", "mp"),
        P("dp", "mp"),
        P("dp", "mp"),
        P("dp", None),
        P("dp", None),
        P(("dp", "mp"), None),
        P(),
    )
    out_specs = (
        P("dp", "mp"),
        P(("dp", "mp"), None),
        P(("dp", "mp"), None),
        P(("dp", "mp"), None),
        P(("dp", "mp"), None),
    )
    body = functools.partial(local, mesh.shape["dp"], mesh.shape["mp"])
    return jax.shard_map(body, mesh=mesh, in_specs=in_specs, out_specs=out_specs, check_vma=False)
```

```python
import functools

import jax
import jax.numpy as jnp
from jax import lax
from jax.experimental import pallas as pl
from jax.experimental.pallas import tpu as pltpu
from jax.sharding import PartitionSpec as P

HS = 64
LANES = 128
CUT = 8

adapter_factor = 2.0

NT = (((1,), (1,)), ((), ()))
TN = (((0,), (0,)), ((), ()))


def dot(left, right, dims):
    return lax.dot_general(left, right, dims, preferred_element_type=jnp.float32)


def group_order(count):
    quarter = count // 4
    bits = quarter.bit_length() - 1
    assert count == 4 << bits
    turned = [sum(((i >> b) & 1) << (bits - 1 - b) for b in range(bits)) for i in range(quarter)]
    order = []
    for near, far in ((2, 3), (1, 0)):
        for i in range(quarter):
            order.append(near * quarter + (turned[quarter - 1 - i] ^ (quarter // 2)))
            order.append(far * quarter + (turned[(quarter - 1 - i) ^ 1] ^ (quarter // 2)))
    return order


def source_range(source_ref, target_ref, count):
    position = lax.broadcasted_iota(jnp.int32, (1, count), 1)
    first = jnp.zeros((1, count), jnp.int32)
    last = jnp.zeros((1, count), jnp.int32)
    target_start = jnp.int32(0)
    source_start = jnp.int32(0)
    for i in range(source_ref.shape[1]):
        source_end = source_start + source_ref[0, i]
        inside = position >= target_start
        first = jnp.where(inside, source_start, first)
        last = jnp.where(inside, source_end, last)
        target_start = target_start + target_ref[0, i]
        source_start = source_end
    return first, last


def attention_kernel(
    source_any, target_any, query_any, grad_any, kv_any, low_any, query_grad_ref, sent_ref, both_grad_ref,
    source_ref, target_ref, query_ref, grad_ref, kv_ref, low_ref, sems,
):
    pairs = [
        (kv_any, kv_ref), (query_any, query_ref), (grad_any, grad_ref),
        (source_any, source_ref), (target_any, target_ref), (low_any, low_ref),
    ]
    copies = [
        pltpu.make_async_copy(here, there, sems.at[i]) for i, (here, there) in enumerate(pairs)
    ]
    for copy in copies:
        copy.start()
    for copy in copies:
        copy.wait()
    tgt_count = query_ref.shape[1]
    both = kv_ref[...]
    query_t = query_ref[...]
    grad_t = grad_ref[...]
    blank = jnp.zeros_like(query_t)
    query_wide = jnp.concatenate([query_t, blank], axis=0)
    grad_wide = jnp.concatenate([blank, grad_t], axis=0)
    first, last = source_range(source_ref, target_ref, tgt_count)
    half = both.shape[0] // 2
    parts = [both[:half], both[half:]]
    scores = [jnp.dot(part, query_wide, preferred_element_type=jnp.float32) for part in parts]
    dprobs = [jnp.dot(part, grad_wide, preferred_element_type=jnp.float32) for part in parts]
    expos = []
    for i, score in enumerate(scores):
        position = i * half + lax.broadcasted_iota(jnp.int32, score.shape, 0)
        allowed = jnp.logical_and(position >= first, position < last)
        expos.append(jnp.where(allowed, jnp.exp(score), 0.0))
    inverse = 1.0 / sum(jnp.sum(expo, axis=0, keepdims=True) for expo in expos)
    weighted = sum(
        jnp.sum(expo * dprob, axis=0, keepdims=True) for expo, dprob in zip(expos, dprobs)
    )
    delta = weighted * inverse
    probs = [expo * inverse for expo in expos]
    dscores = [
        (prob * (dprob - delta)).astype(jnp.bfloat16) for prob, dprob in zip(probs, dprobs)
    ]
    both_low = jnp.concatenate([
        (dot(dscore, query_wide, NT) + dot(prob.astype(jnp.bfloat16), grad_wide, NT))
        .astype(jnp.bfloat16)
        for dscore, prob in zip(dscores, probs)
    ], axis=0)
    low = low_ref[...].astype(jnp.float32)
    rows = low.shape[0]
    blocks = sent_ref.shape[0]
    packed = jnp.concatenate([low[at:at + CUT] for at in range(0, rows, CUT)], axis=1)
    packed = packed.astype(jnp.bfloat16)
    for at, block in enumerate(group_order(blocks)):
        sent_ref[at, :rows, :] = both_low[block * rows:(block + 1) * rows]
        sent_ref[at, rows:, :] = packed

    both_grad_ref[...] = both_low
    query_grad = sum(dot(part, dscore, TN) for part, dscore in zip(parts, dscores))
    query_grad_ref[...] = query_grad[:HS].astype(jnp.bfloat16)


def split_kernel(rows, both_grad_ref, *out_refs):
    dp = len(out_refs)
    step = HS // dp
    exact = both_grad_ref[...].astype(jnp.float32)
    parts = []
    for start in range(0, rows, CUT):
        for block in range(0, exact.shape[0], rows):
            parts.append(exact[block + start:block + start + CUT])
    turned = jnp.concatenate(parts, axis=0).T
    pieces = []
    for j in range(dp):
        halves = [turned[j * step:(j + 1) * step], turned[HS + j * step:HS + (j + 1) * step]]
        pieces.append(jnp.concatenate(halves, axis=0))
    e = lax.rem(lax.axis_index("mp"), dp)
    pack = lax.axis_index("dp")
    for s, out_ref in enumerate(out_refs):
        turn = lax.rem(2 * e + s + dp - pack, dp)
        chosen = pieces[0]
        for j in range(1, dp):
            chosen = jnp.where(turn == j, pieces[j], chosen)
        out_ref[...] = chosen.astype(jnp.bfloat16)


def order_kernel(*refs):
    *arrived_refs, out_ref = refs
    dp = len(arrived_refs)
    mine = lax.rem(lax.axis_index("mp"), dp)
    for s, arrived_ref in enumerate(arrived_refs):
        out_ref[lax.rem(mine + dp - s, dp)] = arrived_ref[...]


def share_kernel(rows, both_rank, got_ref, pieces_ref, *out_refs):
    dp, piece_rows, _ = pieces_ref.shape
    blocks = got_ref.shape[0]
    order = group_order(blocks)
    lows = [
        got_ref[order.index(block), rows:, :].astype(jnp.float32) for block in range(blocks)
    ]
    lows = jnp.concatenate(lows, axis=0).astype(jnp.bfloat16)
    columns = jnp.concatenate([pieces_ref[e] for e in range(dp)], axis=0)
    share = None
    for cut in range(rows // CUT):
        tokens = columns[:, cut * blocks * CUT:(cut + 1) * blocks * CUT]
        product = jnp.dot(tokens, lows, preferred_element_type=jnp.float32)
        part = product[:, cut * both_rank:(cut + 1) * both_rank]
        share = part if share is None else share + part
    step = piece_rows // 2
    column = lax.broadcasted_iota(jnp.int32, (step, both_rank), 1)
    shares = []
    for e in range(dp):
        keys = share[e * piece_rows:e * piece_rows + step]
        values = share[e * piece_rows + step:(e + 1) * piece_rows]
        shares.append(adapter_factor * jnp.where(column < both_rank // 2, keys, values))
    mine = lax.axis_index("dp")
    for s, out_ref in enumerate(out_refs):
        turn = lax.rem(mine + s, dp)
        chosen = shares[0]
        for e in range(1, dp):
            chosen = jnp.where(turn == e, shares[e], chosen)
        out_ref[...] = chosen


def owner_kernel(got_ref, up_ref, key_ref, value_ref, low_grad_ref):
    rows = key_ref.shape[0]
    rank = up_ref.shape[0] // 2
    order = group_order(got_ref.shape[0])
    for pair in range(len(order) // 2):
        first = got_ref[order.index(2 * pair), :rows, :]
        second = got_ref[order.index(2 * pair + 1), :rows, :]
        columns = slice(2 * pair * HS, (2 * pair + 2) * HS)
        key_ref[:, columns] = jnp.concatenate([first[:, :HS], second[:, :HS]], axis=1)
        value_ref[:, columns] = jnp.concatenate([first[:, HS:], second[:, HS:]], axis=1)
    up = up_ref[...]
    from_key = dot(key_ref[...], up, NT)
    from_value = dot(value_ref[...], up, NT)
    column = lax.broadcasted_iota(jnp.int32, from_key.shape, 1)
    low_grad_ref[...] = adapter_factor * jnp.where(column < rank, from_key, from_value)


def local(dp, mp, query, kv_cache, out_grad, source_lengths, target_lengths, low_rank, adapter_up_matrix):
    tgt_count = query.shape[0]
    src_count = kv_cache.shape[0]
    rows, both_rank = low_rank.shape
    width = adapter_up_matrix.shape[1]
    step = HS // dp
    assert rows // CUT * both_rank == LANES
    vmem = pl.BlockSpec(memory_space=pltpu.VMEM)
    hbm = pl.BlockSpec(memory_space=pl.ANY)
    params = pltpu.CompilerParams(vmem_limit_bytes=48 * 1024 * 1024)
    whole_vmem = pltpu.CompilerParams(vmem_limit_bytes=60 * 1024 * 1024)

    query_t = query.T
    grad_t = out_grad.T
    query_grad_t, sent, both_grad = pl.pallas_call(
        attention_kernel,
        out_shape=[
            jax.ShapeDtypeStruct((HS, tgt_count), jnp.bfloat16),
            jax.ShapeDtypeStruct((mp, rows + CUT, LANES), jnp.bfloat16),
            jax.ShapeDtypeStruct((src_count, 2 * HS), jnp.bfloat16),
        ],
        in_specs=[hbm] * 6,
        out_specs=[vmem] * 3,
        scratch_shapes=[
            pltpu.SMEM(source_lengths.shape, jnp.int32),
            pltpu.SMEM(target_lengths.shape, jnp.int32),
            pltpu.VMEM(query_t.shape, jnp.bfloat16),
            pltpu.VMEM(grad_t.shape, jnp.bfloat16),
            pltpu.VMEM(kv_cache.shape, jnp.bfloat16),
            pltpu.VMEM(low_rank.shape, jnp.bfloat16),
            pltpu.SemaphoreType.DMA((6,)),
        ],
        compiler_params=whole_vmem,
        name="attention_backward",
    )(source_lengths, target_lengths, query_t, grad_t, kv_cache, low_rank)

    route = [(h, h * dp % mp + h * dp // mp) for h in range(mp)]
    pieces = pl.pallas_call(
        functools.partial(split_kernel, rows),
        out_shape=[jax.ShapeDtypeStruct((2 * step, src_count), jnp.bfloat16)] * dp,
        in_specs=[vmem],
        out_specs=[vmem] * dp,
        compiler_params=params,
        cost_estimate=pl.CostEstimate(flops=2 ** 36, bytes_accessed=2 ** 28, transcendentals=0),
        name="split_columns",
    )(lax.ppermute(both_grad, "mp", route))
    arrived = [pieces[0]]
    for s in range(1, dp):
        route = [(m, m - m % dp + (m + s) % dp) for m in range(mp)]
        arrived.append(lax.ppermute(pieces[s], "mp", route))
    ordered = pl.pallas_call(
        order_kernel,
        out_shape=jax.ShapeDtypeStruct((dp, 2 * step, src_count), jnp.bfloat16),
        in_specs=[vmem] * dp,
        out_specs=vmem,
        compiler_params=params,
        name="order_pieces",
    )(*arrived)

    got = lax.all_to_all(sent, "mp", 0, 0, axis_index_groups=[group_order(mp)], tiled=True)

    shares = pl.pallas_call(
        functools.partial(share_kernel, rows, both_rank),
        out_shape=[jax.ShapeDtypeStruct((step, both_rank), jnp.float32)] * dp,
        in_specs=[vmem] * 2,
        out_specs=[vmem] * dp,
        compiler_params=params,
        name="adapter_shares",
    )(got, ordered)
    up_grad = shares[0]
    for s in range(1, dp):
        route = [
            (d * mp + m, (d + s) % dp * mp + m - m % dp + (m + s) % dp)
            for d in range(dp) for m in range(mp)
        ]
        up_grad = up_grad + lax.ppermute(shares[s], ("dp", "mp"), route)

    key_gradient, value_grad, low_grad = pl.pallas_call(
        owner_kernel,
        out_shape=[
            jax.ShapeDtypeStruct((rows, width), jnp.bfloat16),
            jax.ShapeDtypeStruct((rows, width), jnp.bfloat16),
            jax.ShapeDtypeStruct((rows, both_rank), jnp.float32),
        ],
        in_specs=[vmem] * 2,
        out_specs=[vmem] * 3,
        compiler_params=params,
        name="owner_outputs",
    )(got, adapter_up_matrix)
    return query_grad_t.T, key_gradient, value_grad, low_grad, up_grad


def solution(mesh):
    in_specs = (
        P("dp", "mp"),
        P("dp", "mp"),
        P("dp", "mp"),
        P("dp", None),
        P("dp", None),
        P(("dp", "mp"), None),
        P(),
    )
    out_specs = (
        P("dp", "mp"),
        P(("dp", "mp"), None),
        P(("dp", "mp"), None),
        P(("dp", "mp"), None),
        P(("dp", "mp"), None),
    )
    body = functools.partial(local, mesh.shape["dp"], mesh.shape["mp"])
    return jax.shard_map(body, mesh=mesh, in_specs=in_specs, out_specs=out_specs, check_vma=False)
```

```python
import functools

import jax
import jax.numpy as jnp
from jax import lax
from jax.experimental import pallas as pl
from jax.experimental.pallas import tpu as pltpu
from jax.sharding import PartitionSpec as P

HS = 64
LANES = 128
CUT = 8

adapter_factor = 2.0

NT = (((1,), (1,)), ((), ()))
TN = (((0,), (0,)), ((), ()))


def dot(left, right, dims):
    return lax.dot_general(left, right, dims, preferred_element_type=jnp.float32)


def group_order(count):
    quarter = count // 4
    bits = quarter.bit_length() - 1
    assert count == 4 << bits
    turned = [sum(((i >> b) & 1) << (bits - 1 - b) for b in range(bits)) for i in range(quarter)]
    order = []
    for near, far in ((3, 2), (0, 1)):
        for i in range(quarter):
            order.append(near * quarter + turned[quarter - 1 - i])
            order.append(far * quarter + turned[(quarter - 1 - i) ^ 1])
    return order


def source_range(source_ref, target_ref, count):
    position = lax.broadcasted_iota(jnp.int32, (1, count), 1)
    first = jnp.zeros((1, count), jnp.int32)
    last = jnp.zeros((1, count), jnp.int32)
    target_start = jnp.int32(0)
    source_start = jnp.int32(0)
    for i in range(source_ref.shape[1]):
        source_end = source_start + source_ref[0, i]
        inside = position >= target_start
        first = jnp.where(inside, source_start, first)
        last = jnp.where(inside, source_end, last)
        target_start = target_start + target_ref[0, i]
        source_start = source_end
    return first, last


def attention_kernel(
    source_any, target_any, query_any, grad_any, kv_any, low_any, query_grad_ref, sent_ref, both_grad_ref,
    source_ref, target_ref, query_ref, grad_ref, kv_ref, low_ref, sems,
):
    pairs = [
        (kv_any, kv_ref), (query_any, query_ref), (grad_any, grad_ref),
        (source_any, source_ref), (target_any, target_ref), (low_any, low_ref),
    ]
    copies = [
        pltpu.make_async_copy(here, there, sems.at[i]) for i, (here, there) in enumerate(pairs)
    ]
    for copy in copies:
        copy.start()
    for copy in copies:
        copy.wait()
    tgt_count = query_ref.shape[1]
    both = kv_ref[...]
    query_t = query_ref[...]
    grad_t = grad_ref[...]
    blank = jnp.zeros_like(query_t)
    query_wide = jnp.concatenate([query_t, blank], axis=0)
    grad_wide = jnp.concatenate([blank, grad_t], axis=0)
    first, last = source_range(source_ref, target_ref, tgt_count)
    half = both.shape[0] // 2
    parts = [both[:half], both[half:]]
    scores = [jnp.dot(part, query_wide, preferred_element_type=jnp.float32) for part in parts]
    dprobs = [jnp.dot(part, grad_wide, preferred_element_type=jnp.float32) for part in parts]
    expos = []
    for i, score in enumerate(scores):
        position = i * half + lax.broadcasted_iota(jnp.int32, score.shape, 0)
        allowed = jnp.logical_and(position >= first, position < last)
        expos.append(jnp.where(allowed, jnp.exp(score), 0.0))
    inverse = 1.0 / sum(jnp.sum(expo, axis=0, keepdims=True) for expo in expos)
    weighted = sum(
        jnp.sum(expo * dprob, axis=0, keepdims=True) for expo, dprob in zip(expos, dprobs)
    )
    delta = weighted * inverse
    probs = [expo * inverse for expo in expos]
    dscores = [
        (prob * (dprob - delta)).astype(jnp.bfloat16) for prob, dprob in zip(probs, dprobs)
    ]
    both_low = jnp.concatenate([
        (dot(dscore, query_wide, NT) + dot(prob.astype(jnp.bfloat16), grad_wide, NT))
        .astype(jnp.bfloat16)
        for dscore, prob in zip(dscores, probs)
    ], axis=0)
    low = low_ref[...].astype(jnp.float32)
    rows = low.shape[0]
    blocks = sent_ref.shape[0]
    packed = jnp.concatenate([low[at:at + CUT] for at in range(0, rows, CUT)], axis=1)
    packed = packed.astype(jnp.bfloat16)
    for at, block in enumerate(group_order(blocks)):
        sent_ref[at, :rows, :] = both_low[block * rows:(block + 1) * rows]
        sent_ref[at, rows:, :] = packed

    both_grad_ref[...] = both_low
    query_grad = sum(dot(part, dscore, TN) for part, dscore in zip(parts, dscores))
    query_grad_ref[...] = query_grad[:HS].astype(jnp.bfloat16)


def split_kernel(rows, both_grad_ref, *out_refs):
    dp = len(out_refs)
    step = HS // dp
    exact = both_grad_ref[...].astype(jnp.float32)
    parts = []
    for start in range(0, rows, CUT):
        for block in range(0, exact.shape[0], rows):
            parts.append(exact[block + start:block + start + CUT])
    turned = jnp.concatenate(parts, axis=0).T
    pieces = []
    for j in range(dp):
        halves = [turned[j * step:(j + 1) * step], turned[HS + j * step:HS + (j + 1) * step]]
        pieces.append(jnp.concatenate(halves, axis=0))
    e = lax.rem(lax.axis_index("mp"), dp)
    pack = lax.axis_index("dp")
    for s, out_ref in enumerate(out_refs):
        turn = lax.rem(2 * e + s + dp - pack, dp)
        chosen = pieces[0]
        for j in range(1, dp):
            chosen = jnp.where(turn == j, pieces[j], chosen)
        out_ref[...] = chosen.astype(jnp.bfloat16)


def order_kernel(*refs):
    *arrived_refs, out_ref = refs
    dp = len(arrived_refs)
    mine = lax.rem(lax.axis_index("mp"), dp)
    for s, arrived_ref in enumerate(arrived_refs):
        out_ref[lax.rem(mine + dp - s, dp)] = arrived_ref[...]


def share_kernel(rows, both_rank, got_ref, pieces_ref, *out_refs):
    dp, piece_rows, _ = pieces_ref.shape
    blocks = got_ref.shape[0]
    order = group_order(blocks)
    lows = [
        got_ref[order.index(block), rows:, :].astype(jnp.float32) for block in range(blocks)
    ]
    lows = jnp.concatenate(lows, axis=0).astype(jnp.bfloat16)
    columns = jnp.concatenate([pieces_ref[e] for e in range(dp)], axis=0)
    share = None
    for cut in range(rows // CUT):
        tokens = columns[:, cut * blocks * CUT:(cut + 1) * blocks * CUT]
        product = jnp.dot(tokens, lows, preferred_element_type=jnp.float32)
        part = product[:, cut * both_rank:(cut + 1) * both_rank]
        share = part if share is None else share + part
    step = piece_rows // 2
    column = lax.broadcasted_iota(jnp.int32, (step, both_rank), 1)
    shares = []
    for e in range(dp):
        keys = share[e * piece_rows:e * piece_rows + step]
        values = share[e * piece_rows + step:(e + 1) * piece_rows]
        shares.append(adapter_factor * jnp.where(column < both_rank // 2, keys, values))
    mine = lax.axis_index("dp")
    for s, out_ref in enumerate(out_refs):
        turn = lax.rem(mine + s, dp)
        chosen = shares[0]
        for e in range(1, dp):
            chosen = jnp.where(turn == e, shares[e], chosen)
        out_ref[...] = chosen


def owner_kernel(got_ref, up_ref, key_ref, value_ref, low_grad_ref):
    rows = key_ref.shape[0]
    rank = up_ref.shape[0] // 2
    order = group_order(got_ref.shape[0])
    for pair in range(len(order) // 2):
        first = got_ref[order.index(2 * pair), :rows, :]
        second = got_ref[order.index(2 * pair + 1), :rows, :]
        columns = slice(2 * pair * HS, (2 * pair + 2) * HS)
        key_ref[:, columns] = jnp.concatenate([first[:, :HS], second[:, :HS]], axis=1)
        value_ref[:, columns] = jnp.concatenate([first[:, HS:], second[:, HS:]], axis=1)
    up = up_ref[...]
    from_key = dot(key_ref[...], up, NT)
    from_value = dot(value_ref[...], up, NT)
    column = lax.broadcasted_iota(jnp.int32, from_key.shape, 1)
    low_grad_ref[...] = adapter_factor * jnp.where(column < rank, from_key, from_value)


def local(dp, mp, query, kv_cache, out_grad, source_lengths, target_lengths, low_rank, adapter_up_matrix):
    tgt_count = query.shape[0]
    src_count = kv_cache.shape[0]
    rows, both_rank = low_rank.shape
    width = adapter_up_matrix.shape[1]
    step = HS // dp
    assert rows // CUT * both_rank == LANES
    vmem = pl.BlockSpec(memory_space=pltpu.VMEM)
    hbm = pl.BlockSpec(memory_space=pl.ANY)
    params = pltpu.CompilerParams(vmem_limit_bytes=48 * 1024 * 1024)
    whole_vmem = pltpu.CompilerParams(vmem_limit_bytes=60 * 1024 * 1024)

    query_t = query.T
    grad_t = out_grad.T
    query_grad_t, sent, both_grad = pl.pallas_call(
        attention_kernel,
        out_shape=[
            jax.ShapeDtypeStruct((HS, tgt_count), jnp.bfloat16),
            jax.ShapeDtypeStruct((mp, rows + CUT, LANES), jnp.bfloat16),
            jax.ShapeDtypeStruct((src_count, 2 * HS), jnp.bfloat16),
        ],
        in_specs=[hbm] * 6,
        out_specs=[vmem] * 3,
        scratch_shapes=[
            pltpu.SMEM(source_lengths.shape, jnp.int32),
            pltpu.SMEM(target_lengths.shape, jnp.int32),
            pltpu.VMEM(query_t.shape, jnp.bfloat16),
            pltpu.VMEM(grad_t.shape, jnp.bfloat16),
            pltpu.VMEM(kv_cache.shape, jnp.bfloat16),
            pltpu.VMEM(low_rank.shape, jnp.bfloat16),
            pltpu.SemaphoreType.DMA((6,)),
        ],
        compiler_params=whole_vmem,
        name="attention_backward",
    )(source_lengths, target_lengths, query_t, grad_t, kv_cache, low_rank)

    route = [(h, h * dp % mp + h * dp // mp) for h in range(mp)]
    pieces = pl.pallas_call(
        functools.partial(split_kernel, rows),
        out_shape=[jax.ShapeDtypeStruct((2 * step, src_count), jnp.bfloat16)] * dp,
        in_specs=[vmem],
        out_specs=[vmem] * dp,
        compiler_params=params,
        cost_estimate=pl.CostEstimate(flops=2 ** 36, bytes_accessed=2 ** 28, transcendentals=0),
        name="split_columns",
    )(lax.ppermute(both_grad, "mp", route))
    arrived = [pieces[0]]
    for s in range(1, dp):
        route = [(m, m - m % dp + (m + s) % dp) for m in range(mp)]
        arrived.append(lax.ppermute(pieces[s], "mp", route))
    ordered = pl.pallas_call(
        order_kernel,
        out_shape=jax.ShapeDtypeStruct((dp, 2 * step, src_count), jnp.bfloat16),
        in_specs=[vmem] * dp,
        out_specs=vmem,
        compiler_params=params,
        name="order_pieces",
    )(*arrived)

    got = lax.all_to_all(sent, "mp", 0, 0, axis_index_groups=[group_order(mp)], tiled=True)

    shares = pl.pallas_call(
        functools.partial(share_kernel, rows, both_rank),
        out_shape=[jax.ShapeDtypeStruct((step, both_rank), jnp.float32)] * dp,
        in_specs=[vmem] * 2,
        out_specs=[vmem] * dp,
        compiler_params=params,
        name="adapter_shares",
    )(got, ordered)
    up_grad = shares[0]
    for s in range(1, dp):
        route = [
            (d * mp + m, (d + s) % dp * mp + m - m % dp + (m + s) % dp)
            for d in range(dp) for m in range(mp)
        ]
        up_grad = up_grad + lax.ppermute(shares[s], ("dp", "mp"), route)

    key_gradient, value_grad, low_grad = pl.pallas_call(
        owner_kernel,
        out_shape=[
            jax.ShapeDtypeStruct((rows, width), jnp.bfloat16),
            jax.ShapeDtypeStruct((rows, width), jnp.bfloat16),
            jax.ShapeDtypeStruct((rows, both_rank), jnp.float32),
        ],
        in_specs=[vmem] * 2,
        out_specs=[vmem] * 3,
        compiler_params=params,
        name="owner_outputs",
    )(got, adapter_up_matrix)
    return query_grad_t.T, key_gradient, value_grad, low_grad, up_grad


def solution(mesh):
    in_specs = (
        P("dp", "mp"),
        P("dp", "mp"),
        P("dp", "mp"),
        P("dp", None),
        P("dp", None),
        P(("dp", "mp"), None),
        P(),
    )
    out_specs = (
        P("dp", "mp"),
        P(("dp", "mp"), None),
        P(("dp", "mp"), None),
        P(("dp", "mp"), None),
        P(("dp", "mp"), None),
    )
    body = functools.partial(local, mesh.shape["dp"], mesh.shape["mp"])
    return jax.shard_map(body, mesh=mesh, in_specs=in_specs, out_specs=out_specs, check_vma=False)
```

```python
import functools

import jax
import jax.numpy as jnp
from jax import lax
from jax.experimental import pallas as pl
from jax.experimental.pallas import tpu as pltpu
from jax.sharding import PartitionSpec as P

HS = 64
LANES = 128
CUT = 8

adapter_factor = 2.0

NT = (((1,), (1,)), ((), ()))
TN = (((0,), (0,)), ((), ()))


def dot(left, right, dims):
    return lax.dot_general(left, right, dims, preferred_element_type=jnp.float32)


def group_order(count):
    quarter = count // 4
    bits = quarter.bit_length() - 1
    assert count == 4 << bits
    turned = [sum(((i >> b) & 1) << (bits - 1 - b) for b in range(bits)) for i in range(quarter)]
    order = []
    for near, far in ((2, 3), (1, 0)):
        for i in range(quarter):
            order.append(near * quarter + turned[quarter - 1 - i])
            order.append(far * quarter + turned[(quarter - 1 - i) ^ 1])
    return order


def source_range(source_ref, target_ref, count):
    position = lax.broadcasted_iota(jnp.int32, (1, count), 1)
    first = jnp.zeros((1, count), jnp.int32)
    last = jnp.zeros((1, count), jnp.int32)
    target_start = jnp.int32(0)
    source_start = jnp.int32(0)
    for i in range(source_ref.shape[1]):
        source_end = source_start + source_ref[0, i]
        inside = position >= target_start
        first = jnp.where(inside, source_start, first)
        last = jnp.where(inside, source_end, last)
        target_start = target_start + target_ref[0, i]
        source_start = source_end
    return first, last


def attention_kernel(
    source_any, target_any, query_any, grad_any, kv_any, low_any, query_grad_ref, sent_ref, both_grad_ref,
    source_ref, target_ref, query_ref, grad_ref, kv_ref, low_ref, sems,
):
    pairs = [
        (kv_any, kv_ref), (query_any, query_ref), (grad_any, grad_ref),
        (source_any, source_ref), (target_any, target_ref), (low_any, low_ref),
    ]
    copies = [
        pltpu.make_async_copy(here, there, sems.at[i]) for i, (here, there) in enumerate(pairs)
    ]
    for copy in copies:
        copy.start()
    for copy in copies:
        copy.wait()
    tgt_count = query_ref.shape[1]
    both = kv_ref[...]
    query_t = query_ref[...]
    grad_t = grad_ref[...]
    blank = jnp.zeros_like(query_t)
    query_wide = jnp.concatenate([query_t, blank], axis=0)
    grad_wide = jnp.concatenate([blank, grad_t], axis=0)
    first, last = source_range(source_ref, target_ref, tgt_count)
    half = both.shape[0] // 2
    parts = [both[:half], both[half:]]
    scores = [jnp.dot(part, query_wide, preferred_element_type=jnp.float32) for part in parts]
    dprobs = [jnp.dot(part, grad_wide, preferred_element_type=jnp.float32) for part in parts]
    expos = []
    for i, score in enumerate(scores):
        position = i * half + lax.broadcasted_iota(jnp.int32, score.shape, 0)
        allowed = jnp.logical_and(position >= first, position < last)
        expos.append(jnp.where(allowed, jnp.exp(score), 0.0))
    inverse = 1.0 / sum(jnp.sum(expo, axis=0, keepdims=True) for expo in expos)
    weighted = sum(
        jnp.sum(expo * dprob, axis=0, keepdims=True) for expo, dprob in zip(expos, dprobs)
    )
    delta = weighted * inverse
    probs = [expo * inverse for expo in expos]
    dscores = [
        (prob * (dprob - delta)).astype(jnp.bfloat16) for prob, dprob in zip(probs, dprobs)
    ]
    both_low = jnp.concatenate([
        (dot(dscore, query_wide, NT) + dot(prob.astype(jnp.bfloat16), grad_wide, NT))
        .astype(jnp.bfloat16)
        for dscore, prob in zip(dscores, probs)
    ], axis=0)
    low = low_ref[...].astype(jnp.float32)
    rows = low.shape[0]
    blocks = sent_ref.shape[0]
    packed = jnp.concatenate([low[at:at + CUT] for at in range(0, rows, CUT)], axis=1)
    packed = packed.astype(jnp.bfloat16)
    for at, block in enumerate(group_order(blocks)):
        sent_ref[at, :rows, :] = both_low[block * rows:(block + 1) * rows]
        sent_ref[at, rows:, :] = packed

    both_grad_ref[...] = both_low
    query_grad = sum(dot(part, dscore, TN) for part, dscore in zip(parts, dscores))
    query_grad_ref[...] = query_grad[:HS].astype(jnp.bfloat16)


def split_kernel(rows, both_grad_ref, *out_refs):
    dp = len(out_refs)
    step = HS // dp
    exact = both_grad_ref[...].astype(jnp.float32)
    parts = []
    for start in range(0, rows, CUT):
        for block in range(0, exact.shape[0], rows):
            parts.append(exact[block + start:block + start + CUT])
    turned = jnp.concatenate(parts, axis=0).T
    pieces = []
    for j in range(dp):
        halves = [turned[j * step:(j + 1) * step], turned[HS + j * step:HS + (j + 1) * step]]
        pieces.append(jnp.concatenate(halves, axis=0))
    pack = lax.axis_index("dp")
    for s, out_ref in enumerate(out_refs):
        turn = lax.rem(2 * dp - 1 + s - pack, dp)
        chosen = pieces[0]
        for j in range(1, dp):
            chosen = jnp.where(turn == j, pieces[j], chosen)
        out_ref[...] = chosen.astype(jnp.bfloat16)


def order_kernel(*refs):
    *arrived_refs, out_ref = refs
    dp = len(arrived_refs)
    mine = lax.rem(lax.axis_index("mp"), dp)
    for s, arrived_ref in enumerate(arrived_refs):
        out_ref[dp - 1 - lax.rem(mine + dp - s, dp)] = arrived_ref[...]


def share_kernel(rows, both_rank, got_ref, pieces_ref, *out_refs):
    dp, piece_rows, _ = pieces_ref.shape
    blocks = got_ref.shape[0]
    order = group_order(blocks)
    lows = [
        got_ref[order.index(block), rows:, :].astype(jnp.float32) for block in range(blocks)
    ]
    lows = jnp.concatenate(lows, axis=0).astype(jnp.bfloat16)
    columns = jnp.concatenate([pieces_ref[e] for e in range(dp)], axis=0)
    share = None
    for cut in range(rows // CUT):
        tokens = columns[:, cut * blocks * CUT:(cut + 1) * blocks * CUT]
        product = jnp.dot(tokens, lows, preferred_element_type=jnp.float32)
        part = product[:, cut * both_rank:(cut + 1) * both_rank]
        share = part if share is None else share + part
    step = piece_rows // 2
    column = lax.broadcasted_iota(jnp.int32, (step, both_rank), 1)
    shares = []
    for e in range(dp):
        keys = share[e * piece_rows:e * piece_rows + step]
        values = share[e * piece_rows + step:(e + 1) * piece_rows]
        shares.append(adapter_factor * jnp.where(column < both_rank // 2, keys, values))
    mine = lax.axis_index("dp")
    for s, out_ref in enumerate(out_refs):
        turn = lax.rem(mine + s, dp)
        chosen = shares[0]
        for e in range(1, dp):
            chosen = jnp.where(turn == e, shares[e], chosen)
        out_ref[...] = chosen


def owner_kernel(got_ref, up_ref, key_ref, value_ref, low_grad_ref):
    rows = key_ref.shape[0]
    rank = up_ref.shape[0] // 2
    order = group_order(got_ref.shape[0])
    for pair in range(len(order) // 2):
        first = got_ref[order.index(2 * pair), :rows, :]
        second = got_ref[order.index(2 * pair + 1), :rows, :]
        columns = slice(2 * pair * HS, (2 * pair + 2) * HS)
        key_ref[:, columns] = jnp.concatenate([first[:, :HS], second[:, :HS]], axis=1)
        value_ref[:, columns] = jnp.concatenate([first[:, HS:], second[:, HS:]], axis=1)
    up = up_ref[...]
    from_key = dot(key_ref[...], up, NT)
    from_value = dot(value_ref[...], up, NT)
    column = lax.broadcasted_iota(jnp.int32, from_key.shape, 1)
    low_grad_ref[...] = adapter_factor * jnp.where(column < rank, from_key, from_value)


def local(dp, mp, query, kv_cache, out_grad, source_lengths, target_lengths, low_rank, adapter_up_matrix):
    tgt_count = query.shape[0]
    src_count = kv_cache.shape[0]
    rows, both_rank = low_rank.shape
    width = adapter_up_matrix.shape[1]
    step = HS // dp
    assert rows // CUT * both_rank == LANES
    vmem = pl.BlockSpec(memory_space=pltpu.VMEM)
    hbm = pl.BlockSpec(memory_space=pl.ANY)
    params = pltpu.CompilerParams(vmem_limit_bytes=48 * 1024 * 1024)
    whole_vmem = pltpu.CompilerParams(vmem_limit_bytes=60 * 1024 * 1024)

    query_t = query.T
    grad_t = out_grad.T
    query_grad_t, sent, both_grad = pl.pallas_call(
        attention_kernel,
        out_shape=[
            jax.ShapeDtypeStruct((HS, tgt_count), jnp.bfloat16),
            jax.ShapeDtypeStruct((mp, rows + CUT, LANES), jnp.bfloat16),
            jax.ShapeDtypeStruct((src_count, 2 * HS), jnp.bfloat16),
        ],
        in_specs=[hbm] * 6,
        out_specs=[vmem] * 3,
        scratch_shapes=[
            pltpu.SMEM(source_lengths.shape, jnp.int32),
            pltpu.SMEM(target_lengths.shape, jnp.int32),
            pltpu.VMEM(query_t.shape, jnp.bfloat16),
            pltpu.VMEM(grad_t.shape, jnp.bfloat16),
            pltpu.VMEM(kv_cache.shape, jnp.bfloat16),
            pltpu.VMEM(low_rank.shape, jnp.bfloat16),
            pltpu.SemaphoreType.DMA((6,)),
        ],
        compiler_params=whole_vmem,
        name="attention_backward",
    )(source_lengths, target_lengths, query_t, grad_t, kv_cache, low_rank)

    route = [(h, h * dp % mp + dp - 1 - h * dp // mp) for h in range(mp)]
    pieces = pl.pallas_call(
        functools.partial(split_kernel, rows),
        out_shape=[jax.ShapeDtypeStruct((2 * step, src_count), jnp.bfloat16)] * dp,
        in_specs=[vmem],
        out_specs=[vmem] * dp,
        compiler_params=params,
        cost_estimate=pl.CostEstimate(flops=2 ** 36, bytes_accessed=2 ** 28, transcendentals=0),
        name="split_columns",
    )(lax.ppermute(both_grad, "mp", route))
    arrived = [pieces[0]]
    for s in range(1, dp):
        route = [(m, m - m % dp + (m + s) % dp) for m in range(mp)]
        arrived.append(lax.ppermute(pieces[s], "mp", route))
    ordered = pl.pallas_call(
        order_kernel,
        out_shape=jax.ShapeDtypeStruct((dp, 2 * step, src_count), jnp.bfloat16),
        in_specs=[vmem] * dp,
        out_specs=vmem,
        compiler_params=params,
        name="order_pieces",
    )(*arrived)

    got = lax.all_to_all(sent, "mp", 0, 0, axis_index_groups=[group_order(mp)], tiled=True)

    shares = pl.pallas_call(
        functools.partial(share_kernel, rows, both_rank),
        out_shape=[jax.ShapeDtypeStruct((step, both_rank), jnp.float32)] * dp,
        in_specs=[vmem] * 2,
        out_specs=[vmem] * dp,
        compiler_params=params,
        name="adapter_shares",
    )(got, ordered)
    up_grad = shares[0]
    for s in range(1, dp):
        route = [
            (d * mp + m, (d + s) % dp * mp + m - m % dp + (m + s) % dp)
            for d in range(dp) for m in range(mp)
        ]
        up_grad = up_grad + lax.ppermute(shares[s], ("dp", "mp"), route)

    key_gradient, value_grad, low_grad = pl.pallas_call(
        owner_kernel,
        out_shape=[
            jax.ShapeDtypeStruct((rows, width), jnp.bfloat16),
            jax.ShapeDtypeStruct((rows, width), jnp.bfloat16),
            jax.ShapeDtypeStruct((rows, both_rank), jnp.float32),
        ],
        in_specs=[vmem] * 2,
        out_specs=[vmem] * 3,
        compiler_params=params,
        name="owner_outputs",
    )(got, adapter_up_matrix)
    return query_grad_t.T, key_gradient, value_grad, low_grad, up_grad


def solution(mesh):
    in_specs = (
        P("dp", "mp"),
        P("dp", "mp"),
        P("dp", "mp"),
        P("dp", None),
        P("dp", None),
        P(("dp", "mp"), None),
        P(),
    )
    out_specs = (
        P("dp", "mp"),
        P(("dp", "mp"), None),
        P(("dp", "mp"), None),
        P(("dp", "mp"), None),
        P(("dp", "mp"), None),
    )
    body = functools.partial(local, mesh.shape["dp"], mesh.shape["mp"])
    return jax.shard_map(body, mesh=mesh, in_specs=in_specs, out_specs=out_specs, check_vma=False)
```

```python
import functools

import jax
import jax.numpy as jnp
from jax import lax
from jax.experimental import pallas as pl
from jax.experimental.pallas import tpu as pltpu
from jax.sharding import PartitionSpec as P

HS = 64
LANES = 128
CUT = 8

adapter_factor = 2.0

NT = (((1,), (1,)), ((), ()))
TN = (((0,), (0,)), ((), ()))


def dot(left, right, dims):
    return lax.dot_general(left, right, dims, preferred_element_type=jnp.float32)


def group_order(count):
    quarter = count // 4
    bits = quarter.bit_length() - 1
    assert count == 4 << bits
    turned = [sum(((i >> b) & 1) << (bits - 1 - b) for b in range(bits)) for i in range(quarter)]
    order = []
    for near, far in ((2, 3), (1, 0)):
        for i in range(quarter):
            order.append(near * quarter + turned[quarter - 1 - i])
            order.append(far * quarter + turned[(quarter - 1 - i) ^ 1])
    return order


def source_range(source_ref, target_ref, count):
    position = lax.broadcasted_iota(jnp.int32, (1, count), 1)
    first = jnp.zeros((1, count), jnp.int32)
    last = jnp.zeros((1, count), jnp.int32)
    target_start = jnp.int32(0)
    source_start = jnp.int32(0)
    for i in range(source_ref.shape[1]):
        source_end = source_start + source_ref[0, i]
        inside = position >= target_start
        first = jnp.where(inside, source_start, first)
        last = jnp.where(inside, source_end, last)
        target_start = target_start + target_ref[0, i]
        source_start = source_end
    return first, last


def attention_kernel(
    source_any, target_any, query_any, grad_any, kv_any, low_any, query_grad_ref, sent_ref, both_grad_ref,
    source_ref, target_ref, query_ref, grad_ref, kv_ref, low_ref, sems,
):
    pairs = [
        (kv_any, kv_ref), (query_any, query_ref), (grad_any, grad_ref),
        (source_any, source_ref), (target_any, target_ref), (low_any, low_ref),
    ]
    copies = [
        pltpu.make_async_copy(here, there, sems.at[i]) for i, (here, there) in enumerate(pairs)
    ]
    for copy in copies:
        copy.start()
    for copy in copies:
        copy.wait()
    tgt_count = query_ref.shape[1]
    both = kv_ref[...]
    query_t = query_ref[...]
    grad_t = grad_ref[...]
    blank = jnp.zeros_like(query_t)
    query_wide = jnp.concatenate([query_t, blank], axis=0)
    grad_wide = jnp.concatenate([blank, grad_t], axis=0)
    first, last = source_range(source_ref, target_ref, tgt_count)
    height = both.shape[0] // 4
    parts = [both[at:at + height] for at in range(0, both.shape[0], height)]
    scores = [jnp.dot(part, query_wide, preferred_element_type=jnp.float32) for part in parts]
    dprobs = [jnp.dot(part, grad_wide, preferred_element_type=jnp.float32) for part in parts]
    expos = []
    for i, score in enumerate(scores):
        position = i * height + lax.broadcasted_iota(jnp.int32, score.shape, 0)
        allowed = jnp.logical_and(position >= first, position < last)
        expos.append(jnp.where(allowed, jnp.exp(score), 0.0))
    inverse = 1.0 / sum(jnp.sum(expo, axis=0, keepdims=True) for expo in expos)
    weighted = sum(
        jnp.sum(expo * dprob, axis=0, keepdims=True) for expo, dprob in zip(expos, dprobs)
    )
    delta = weighted * inverse
    probs = [expo * inverse for expo in expos]
    dscores = [
        (prob * (dprob - delta)).astype(jnp.bfloat16) for prob, dprob in zip(probs, dprobs)
    ]
    both_low = jnp.concatenate([
        (dot(dscore, query_wide, NT) + dot(prob.astype(jnp.bfloat16), grad_wide, NT))
        .astype(jnp.bfloat16)
        for dscore, prob in zip(dscores, probs)
    ], axis=0)
    low = low_ref[...].astype(jnp.float32)
    rows = low.shape[0]
    blocks = sent_ref.shape[0]
    packed = jnp.concatenate([low[at:at + CUT] for at in range(0, rows, CUT)], axis=1)
    packed = packed.astype(jnp.bfloat16)
    for at, block in enumerate(group_order(blocks)):
        sent_ref[at, :rows, :] = both_low[block * rows:(block + 1) * rows]
        sent_ref[at, rows:, :] = packed

    both_grad_ref[...] = both_low
    query_grad = sum(dot(part, dscore, TN) for part, dscore in zip(parts, dscores))
    query_grad_ref[...] = query_grad[:HS].astype(jnp.bfloat16)


def split_kernel(rows, both_grad_ref, *out_refs):
    dp = len(out_refs)
    step = HS // dp
    exact = both_grad_ref[...].astype(jnp.float32)
    parts = []
    for start in range(0, rows, CUT):
        for block in range(0, exact.shape[0], rows):
            parts.append(exact[block + start:block + start + CUT])
    turned = jnp.concatenate(parts, axis=0).T
    pieces = []
    for j in range(dp):
        halves = [turned[j * step:(j + 1) * step], turned[HS + j * step:HS + (j + 1) * step]]
        pieces.append(jnp.concatenate(halves, axis=0))
    pack = lax.axis_index("dp")
    for s, out_ref in enumerate(out_refs):
        turn = lax.rem(2 * dp - 1 + s - pack, dp)
        chosen = pieces[0]
        for j in range(1, dp):
            chosen = jnp.where(turn == j, pieces[j], chosen)
        out_ref[...] = chosen.astype(jnp.bfloat16)


def order_kernel(*refs):
    *arrived_refs, out_ref = refs
    dp = len(arrived_refs)
    mine = lax.rem(lax.axis_index("mp"), dp)
    for s, arrived_ref in enumerate(arrived_refs):
        out_ref[dp - 1 - lax.rem(mine + dp - s, dp)] = arrived_ref[...]


def share_kernel(rows, both_rank, got_ref, pieces_ref, *out_refs):
    dp, piece_rows, _ = pieces_ref.shape
    blocks = got_ref.shape[0]
    order = group_order(blocks)
    lows = [
        got_ref[order.index(block), rows:, :].astype(jnp.float32) for block in range(blocks)
    ]
    lows = jnp.concatenate(lows, axis=0).astype(jnp.bfloat16)
    columns = jnp.concatenate([pieces_ref[e] for e in range(dp)], axis=0)
    share = None
    for cut in range(rows // CUT):
        tokens = columns[:, cut * blocks * CUT:(cut + 1) * blocks * CUT]
        product = jnp.dot(tokens, lows, preferred_element_type=jnp.float32)
        part = product[:, cut * both_rank:(cut + 1) * both_rank]
        share = part if share is None else share + part
    step = piece_rows // 2
    column = lax.broadcasted_iota(jnp.int32, (step, both_rank), 1)
    shares = []
    for e in range(dp):
        keys = share[e * piece_rows:e * piece_rows + step]
        values = share[e * piece_rows + step:(e + 1) * piece_rows]
        shares.append(adapter_factor * jnp.where(column < both_rank // 2, keys, values))
    mine = lax.axis_index("dp")
    for s, out_ref in enumerate(out_refs):
        turn = lax.rem(mine + s, dp)
        chosen = shares[0]
        for e in range(1, dp):
            chosen = jnp.where(turn == e, shares[e], chosen)
        out_ref[...] = chosen


def owner_kernel(got_ref, up_ref, key_ref, value_ref, low_grad_ref):
    rows = key_ref.shape[0]
    rank = up_ref.shape[0] // 2
    order = group_order(got_ref.shape[0])
    for pair in range(len(order) // 2):
        first = got_ref[order.index(2 * pair), :rows, :]
        second = got_ref[order.index(2 * pair + 1), :rows, :]
        columns = slice(2 * pair * HS, (2 * pair + 2) * HS)
        key_ref[:, columns] = jnp.concatenate([first[:, :HS], second[:, :HS]], axis=1)
        value_ref[:, columns] = jnp.concatenate([first[:, HS:], second[:, HS:]], axis=1)
    up = up_ref[...]
    from_key = dot(key_ref[...], up, NT)
    from_value = dot(value_ref[...], up, NT)
    column = lax.broadcasted_iota(jnp.int32, from_key.shape, 1)
    low_grad_ref[...] = adapter_factor * jnp.where(column < rank, from_key, from_value)


def local(dp, mp, query, kv_cache, out_grad, source_lengths, target_lengths, low_rank, adapter_up_matrix):
    tgt_count = query.shape[0]
    src_count = kv_cache.shape[0]
    rows, both_rank = low_rank.shape
    width = adapter_up_matrix.shape[1]
    step = HS // dp
    assert rows // CUT * both_rank == LANES
    vmem = pl.BlockSpec(memory_space=pltpu.VMEM)
    hbm = pl.BlockSpec(memory_space=pl.ANY)
    params = pltpu.CompilerParams(vmem_limit_bytes=48 * 1024 * 1024)
    whole_vmem = pltpu.CompilerParams(vmem_limit_bytes=60 * 1024 * 1024)

    query_t = query.T
    grad_t = out_grad.T
    query_grad_t, sent, both_grad = pl.pallas_call(
        attention_kernel,
        out_shape=[
            jax.ShapeDtypeStruct((HS, tgt_count), jnp.bfloat16),
            jax.ShapeDtypeStruct((mp, rows + CUT, LANES), jnp.bfloat16),
            jax.ShapeDtypeStruct((src_count, 2 * HS), jnp.bfloat16),
        ],
        in_specs=[hbm] * 6,
        out_specs=[vmem] * 3,
        scratch_shapes=[
            pltpu.SMEM(source_lengths.shape, jnp.int32),
            pltpu.SMEM(target_lengths.shape, jnp.int32),
            pltpu.VMEM(query_t.shape, jnp.bfloat16),
            pltpu.VMEM(grad_t.shape, jnp.bfloat16),
            pltpu.VMEM(kv_cache.shape, jnp.bfloat16),
            pltpu.VMEM(low_rank.shape, jnp.bfloat16),
            pltpu.SemaphoreType.DMA((6,)),
        ],
        compiler_params=whole_vmem,
        name="attention_backward",
    )(source_lengths, target_lengths, query_t, grad_t, kv_cache, low_rank)

    route = [(h, h * dp % mp + dp - 1 - h * dp // mp) for h in range(mp)]
    pieces = pl.pallas_call(
        functools.partial(split_kernel, rows),
        out_shape=[jax.ShapeDtypeStruct((2 * step, src_count), jnp.bfloat16)] * dp,
        in_specs=[vmem],
        out_specs=[vmem] * dp,
        compiler_params=params,
        cost_estimate=pl.CostEstimate(flops=2 ** 36, bytes_accessed=2 ** 28, transcendentals=0),
        name="split_columns",
    )(lax.ppermute(both_grad, "mp", route))
    arrived = [pieces[0]]
    for s in range(1, dp):
        route = [(m, m - m % dp + (m + s) % dp) for m in range(mp)]
        arrived.append(lax.ppermute(pieces[s], "mp", route))
    ordered = pl.pallas_call(
        order_kernel,
        out_shape=jax.ShapeDtypeStruct((dp, 2 * step, src_count), jnp.bfloat16),
        in_specs=[vmem] * dp,
        out_specs=vmem,
        compiler_params=params,
        name="order_pieces",
    )(*arrived)

    got = lax.all_to_all(sent, "mp", 0, 0, axis_index_groups=[group_order(mp)], tiled=True)

    shares = pl.pallas_call(
        functools.partial(share_kernel, rows, both_rank),
        out_shape=[jax.ShapeDtypeStruct((step, both_rank), jnp.float32)] * dp,
        in_specs=[vmem] * 2,
        out_specs=[vmem] * dp,
        compiler_params=params,
        name="adapter_shares",
    )(got, ordered)
    up_grad = shares[0]
    for s in range(1, dp):
        route = [
            (d * mp + m, (d + s) % dp * mp + m - m % dp + (m + s) % dp)
            for d in range(dp) for m in range(mp)
        ]
        up_grad = up_grad + lax.ppermute(shares[s], ("dp", "mp"), route)

    key_gradient, value_grad, low_grad = pl.pallas_call(
        owner_kernel,
        out_shape=[
            jax.ShapeDtypeStruct((rows, width), jnp.bfloat16),
            jax.ShapeDtypeStruct((rows, width), jnp.bfloat16),
            jax.ShapeDtypeStruct((rows, both_rank), jnp.float32),
        ],
        in_specs=[vmem] * 2,
        out_specs=[vmem] * 3,
        compiler_params=params,
        name="owner_outputs",
    )(got, adapter_up_matrix)
    return query_grad_t.T, key_gradient, value_grad, low_grad, up_grad


def solution(mesh):
    in_specs = (
        P("dp", "mp"),
        P("dp", "mp"),
        P("dp", "mp"),
        P("dp", None),
        P("dp", None),
        P(("dp", "mp"), None),
        P(),
    )
    out_specs = (
        P("dp", "mp"),
        P(("dp", "mp"), None),
        P(("dp", "mp"), None),
        P(("dp", "mp"), None),
        P(("dp", "mp"), None),
    )
    body = functools.partial(local, mesh.shape["dp"], mesh.shape["mp"])
    return jax.shard_map(body, mesh=mesh, in_specs=in_specs, out_specs=out_specs, check_vma=False)
```

```python
import functools

import jax
import jax.numpy as jnp
from jax import lax
from jax.experimental import pallas as pl
from jax.experimental.pallas import tpu as pltpu
from jax.sharding import PartitionSpec as P

HS = 64
LANES = 128
CUT = 8

adapter_factor = 2.0

NT = (((1,), (1,)), ((), ()))
TN = (((0,), (0,)), ((), ()))


def dot(left, right, dims):
    return lax.dot_general(left, right, dims, preferred_element_type=jnp.float32)


def group_order(count):
    quarter = count // 4
    bits = quarter.bit_length() - 1
    assert count == 4 << bits
    turned = [sum(((i >> b) & 1) << (bits - 1 - b) for b in range(bits)) for i in range(quarter)]
    order = []
    for near, far in ((2, 3), (1, 0)):
        for i in range(quarter):
            order.append(near * quarter + turned[quarter - 1 - i])
            order.append(far * quarter + turned[(quarter - 1 - i) ^ 1])
    return order


def source_range(source_ref, target_ref, count):
    position = lax.broadcasted_iota(jnp.int32, (1, count), 1)
    first = jnp.zeros((1, count), jnp.int32)
    last = jnp.zeros((1, count), jnp.int32)
    target_start = jnp.int32(0)
    source_start = jnp.int32(0)
    for i in range(source_ref.shape[1]):
        source_end = source_start + source_ref[0, i]
        inside = position >= target_start
        first = jnp.where(inside, source_start, first)
        last = jnp.where(inside, source_end, last)
        target_start = target_start + target_ref[0, i]
        source_start = source_end
    return first, last


def attention_kernel(
    source_any, target_any, query_any, grad_any, kv_any, low_any, query_grad_ref, sent_ref, *refs
):
    *piece_refs, source_ref, target_ref, query_ref, grad_ref, kv_ref, low_ref, pieces, sems = refs
    pairs = [
        (kv_any, kv_ref), (query_any, query_ref), (grad_any, grad_ref),
        (source_any, source_ref), (target_any, target_ref), (low_any, low_ref),
    ]
    copies = [
        pltpu.make_async_copy(here, there, sems.at[i]) for i, (here, there) in enumerate(pairs)
    ]
    for copy in copies:
        copy.start()
    for copy in copies:
        copy.wait()
    tgt_count = query_ref.shape[1]
    both = kv_ref[...]
    query_t = query_ref[...]
    grad_t = grad_ref[...]
    blank = jnp.zeros_like(query_t)
    query_wide = jnp.concatenate([query_t, blank], axis=0)
    grad_wide = jnp.concatenate([blank, grad_t], axis=0)
    first, last = source_range(source_ref, target_ref, tgt_count)
    half = both.shape[0] // 2
    parts = [both[:half], both[half:]]
    scores = [jnp.dot(part, query_wide, preferred_element_type=jnp.float32) for part in parts]
    dprobs = [jnp.dot(part, grad_wide, preferred_element_type=jnp.float32) for part in parts]
    expos = []
    for i, score in enumerate(scores):
        position = i * half + lax.broadcasted_iota(jnp.int32, score.shape, 0)
        allowed = jnp.logical_and(position >= first, position < last)
        expos.append(jnp.where(allowed, jnp.exp(score), 0.0))
    inverse = 1.0 / sum(jnp.sum(expo, axis=0, keepdims=True) for expo in expos)
    weighted = sum(
        jnp.sum(expo * dprob, axis=0, keepdims=True) for expo, dprob in zip(expos, dprobs)
    )
    delta = weighted * inverse
    probs = [expo * inverse for expo in expos]
    dscores = [
        (prob * (dprob - delta)).astype(jnp.bfloat16) for prob, dprob in zip(probs, dprobs)
    ]
    both_low = jnp.concatenate([
        (dot(dscore, query_wide, NT) + dot(prob.astype(jnp.bfloat16), grad_wide, NT))
        .astype(jnp.bfloat16)
        for dscore, prob in zip(dscores, probs)
    ], axis=0)
    low = low_ref[...].astype(jnp.float32)
    rows = low.shape[0]
    blocks = sent_ref.shape[0]
    packed = jnp.concatenate([low[at:at + CUT] for at in range(0, rows, CUT)], axis=1)
    packed = packed.astype(jnp.bfloat16)
    for at, block in enumerate(group_order(blocks)):
        sent_ref[at, :rows, :] = both_low[block * rows:(block + 1) * rows]
        sent_ref[at, rows:, :] = packed

    exact = both_low.astype(jnp.float32)
    ordered = [
        exact[block + start:block + start + CUT]
        for start in range(0, rows, CUT) for block in range(0, exact.shape[0], rows)
    ]
    turned = jnp.concatenate(ordered, axis=0).T.astype(jnp.bfloat16)
    dp = len(piece_refs)
    step = HS // dp
    for j in range(dp):
        halves = [turned[j * step:(j + 1) * step], turned[HS + j * step:HS + (j + 1) * step]]
        pieces[j] = jnp.concatenate(halves, axis=0)
    e = lax.axis_index("mp") // (blocks // dp)
    pack = lax.axis_index("dp")
    for s, piece_ref in enumerate(piece_refs):
        piece_ref[...] = pieces[lax.rem(2 * e + s + dp - pack, dp)]
    query_grad = sum(dot(part, dscore, TN) for part, dscore in zip(parts, dscores))
    query_grad_ref[...] = query_grad[:HS].astype(jnp.bfloat16)


def order_kernel(mp, *refs):
    out_ref = refs[-1]
    dp = (len(refs) - 1) // 2
    me = lax.axis_index("mp")
    place = lax.rem(me, dp)
    for s in range(dp):
        e = lax.rem(place + dp - s, dp)
        source = (e * mp + me - place) // dp
        out_ref[e] = jnp.where(source == me, refs[dp + s][...], refs[s][...])


def share_kernel(rows, both_rank, got_ref, pieces_ref, *out_refs):
    dp, piece_rows, _ = pieces_ref.shape
    blocks = got_ref.shape[0]
    order = group_order(blocks)
    lows = [
        got_ref[order.index(block), rows:, :].astype(jnp.float32) for block in range(blocks)
    ]
    lows = jnp.concatenate(lows, axis=0).astype(jnp.bfloat16)
    columns = jnp.concatenate([pieces_ref[e] for e in range(dp)], axis=0)
    share = None
    for cut in range(rows // CUT):
        tokens = columns[:, cut * blocks * CUT:(cut + 1) * blocks * CUT]
        product = jnp.dot(tokens, lows, preferred_element_type=jnp.float32)
        part = product[:, cut * both_rank:(cut + 1) * both_rank]
        share = part if share is None else share + part
    step = piece_rows // 2
    column = lax.broadcasted_iota(jnp.int32, (step, both_rank), 1)
    shares = []
    for e in range(dp):
        keys = share[e * piece_rows:e * piece_rows + step]
        values = share[e * piece_rows + step:(e + 1) * piece_rows]
        shares.append(adapter_factor * jnp.where(column < both_rank // 2, keys, values))
    mine = lax.axis_index("dp")
    for s, out_ref in enumerate(out_refs):
        turn = lax.rem(mine + s, dp)
        chosen = shares[0]
        for e in range(1, dp):
            chosen = jnp.where(turn == e, shares[e], chosen)
        out_ref[...] = chosen


def owner_kernel(got_ref, up_ref, key_ref, value_ref, low_grad_ref):
    rows = key_ref.shape[0]
    rank = up_ref.shape[0] // 2
    order = group_order(got_ref.shape[0])
    for pair in range(len(order) // 2):
        first = got_ref[order.index(2 * pair), :rows, :]
        second = got_ref[order.index(2 * pair + 1), :rows, :]
        columns = slice(2 * pair * HS, (2 * pair + 2) * HS)
        key_ref[:, columns] = jnp.concatenate([first[:, :HS], second[:, :HS]], axis=1)
        value_ref[:, columns] = jnp.concatenate([first[:, HS:], second[:, HS:]], axis=1)
    up = up_ref[...]
    from_key = dot(key_ref[...], up, NT)
    from_value = dot(value_ref[...], up, NT)
    column = lax.broadcasted_iota(jnp.int32, from_key.shape, 1)
    low_grad_ref[...] = adapter_factor * jnp.where(column < rank, from_key, from_value)


def local(dp, mp, query, kv_cache, out_grad, source_lengths, target_lengths, low_rank, adapter_up_matrix):
    tgt_count = query.shape[0]
    src_count = kv_cache.shape[0]
    rows, both_rank = low_rank.shape
    width = adapter_up_matrix.shape[1]
    step = HS // dp
    assert rows // CUT * both_rank == LANES
    vmem = pl.BlockSpec(memory_space=pltpu.VMEM)
    hbm = pl.BlockSpec(memory_space=pl.ANY)
    params = pltpu.CompilerParams(vmem_limit_bytes=48 * 1024 * 1024)
    whole_vmem = pltpu.CompilerParams(vmem_limit_bytes=60 * 1024 * 1024)

    query_t = query.T
    grad_t = out_grad.T
    query_grad_t, sent, *pieces = pl.pallas_call(
        attention_kernel,
        out_shape=[
            jax.ShapeDtypeStruct((HS, tgt_count), jnp.bfloat16),
            jax.ShapeDtypeStruct((mp, rows + CUT, LANES), jnp.bfloat16),
        ] + [jax.ShapeDtypeStruct((2 * step, src_count), jnp.bfloat16)] * dp,
        in_specs=[hbm] * 6,
        out_specs=[vmem] * (2 + dp),
        scratch_shapes=[
            pltpu.SMEM(source_lengths.shape, jnp.int32),
            pltpu.SMEM(target_lengths.shape, jnp.int32),
            pltpu.VMEM(query_t.shape, jnp.bfloat16),
            pltpu.VMEM(grad_t.shape, jnp.bfloat16),
            pltpu.VMEM(kv_cache.shape, jnp.bfloat16),
            pltpu.VMEM(low_rank.shape, jnp.bfloat16),
            pltpu.VMEM((dp, 2 * step, src_count), jnp.bfloat16),
            pltpu.SemaphoreType.DMA((6,)),
        ],
        compiler_params=whole_vmem,
        name="attention_backward",
    )(source_lengths, target_lengths, query_t, grad_t, kv_cache, low_rank)

    got = lax.all_to_all(sent, "mp", 0, 0, axis_index_groups=[group_order(mp)], tiled=True)

    arrived = []
    for s in range(dp):
        route = [
            (h, h * dp % mp + (h * dp // mp + s) % dp) for h in range(mp)
        ]
        route = [pair for pair in route if pair[0] != pair[1]]
        arrived.append(lax.ppermute(pieces[s], "mp", route))
    ordered = pl.pallas_call(
        functools.partial(order_kernel, mp),
        out_shape=jax.ShapeDtypeStruct((dp, 2 * step, src_count), jnp.bfloat16),
        in_specs=[vmem] * (2 * dp),
        out_specs=vmem,
        compiler_params=params,
        name="order_pieces",
    )(*arrived, *pieces)

    shares = pl.pallas_call(
        functools.partial(share_kernel, rows, both_rank),
        out_shape=[jax.ShapeDtypeStruct((step, both_rank), jnp.float32)] * dp,
        in_specs=[vmem] * 2,
        out_specs=[vmem] * dp,
        compiler_params=params,
        name="adapter_shares",
    )(got, ordered)
    up_grad = shares[0]
    for s in range(1, dp):
        route = [
            (d * mp + m, (d + s) % dp * mp + m - m % dp + (m + s) % dp)
            for d in range(dp) for m in range(mp)
        ]
        up_grad = up_grad + lax.ppermute(shares[s], ("dp", "mp"), route)

    key_gradient, value_grad, low_grad = pl.pallas_call(
        owner_kernel,
        out_shape=[
            jax.ShapeDtypeStruct((rows, width), jnp.bfloat16),
            jax.ShapeDtypeStruct((rows, width), jnp.bfloat16),
            jax.ShapeDtypeStruct((rows, both_rank), jnp.float32),
        ],
        in_specs=[vmem] * 2,
        out_specs=[vmem] * 3,
        compiler_params=params,
        name="owner_outputs",
    )(got, adapter_up_matrix)
    return query_grad_t.T, key_gradient, value_grad, low_grad, up_grad


def solution(mesh):
    in_specs = (
        P("dp", "mp"),
        P("dp", "mp"),
        P("dp", "mp"),
        P("dp", None),
        P("dp", None),
        P(("dp", "mp"), None),
        P(),
    )
    out_specs = (
        P("dp", "mp"),
        P(("dp", "mp"), None),
        P(("dp", "mp"), None),
        P(("dp", "mp"), None),
        P(("dp", "mp"), None),
    )
    body = functools.partial(local, mesh.shape["dp"], mesh.shape["mp"])
    return jax.shard_map(body, mesh=mesh, in_specs=in_specs, out_specs=out_specs, check_vma=False)
```

```python
import functools

import jax
import jax.numpy as jnp
from jax import lax
from jax.experimental import pallas as pl
from jax.experimental.pallas import tpu as pltpu
from jax.sharding import PartitionSpec as P

HS = 64
LANES = 128
CUT = 8

adapter_factor = 2.0

NT = (((1,), (1,)), ((), ()))
TN = (((0,), (0,)), ((), ()))


def dot(left, right, dims):
    return lax.dot_general(left, right, dims, preferred_element_type=jnp.float32)


def group_order(count):
    quarter = count // 4
    bits = quarter.bit_length() - 1
    assert count == 4 << bits
    turned = [sum(((i >> b) & 1) << (bits - 1 - b) for b in range(bits)) for i in range(quarter)]
    order = []
    for near, far in ((2, 3), (1, 0)):
        for i in range(quarter):
            order.append(near * quarter + (turned[quarter - 1 - i] ^ 1))
            order.append(far * quarter + (turned[(quarter - 1 - i) ^ 1] ^ 1))
    return order


def source_range(source_ref, target_ref, count):
    position = lax.broadcasted_iota(jnp.int32, (1, count), 1)
    first = jnp.zeros((1, count), jnp.int32)
    last = jnp.zeros((1, count), jnp.int32)
    target_start = jnp.int32(0)
    source_start = jnp.int32(0)
    for i in range(source_ref.shape[1]):
        source_end = source_start + source_ref[0, i]
        inside = position >= target_start
        first = jnp.where(inside, source_start, first)
        last = jnp.where(inside, source_end, last)
        target_start = target_start + target_ref[0, i]
        source_start = source_end
    return first, last


def attention_kernel(
    source_any, target_any, query_any, grad_any, kv_any, low_any, query_grad_ref, sent_ref, both_grad_ref,
    source_ref, target_ref, query_ref, grad_ref, kv_ref, low_ref, sems,
):
    pairs = [
        (kv_any, kv_ref), (query_any, query_ref), (grad_any, grad_ref),
        (source_any, source_ref), (target_any, target_ref), (low_any, low_ref),
    ]
    copies = [
        pltpu.make_async_copy(here, there, sems.at[i]) for i, (here, there) in enumerate(pairs)
    ]
    for copy in copies:
        copy.start()
    for copy in copies:
        copy.wait()
    tgt_count = query_ref.shape[1]
    both = kv_ref[...]
    query_t = query_ref[...]
    grad_t = grad_ref[...]
    blank = jnp.zeros_like(query_t)
    query_wide = jnp.concatenate([query_t, blank], axis=0)
    grad_wide = jnp.concatenate([blank, grad_t], axis=0)
    first, last = source_range(source_ref, target_ref, tgt_count)
    half = both.shape[0] // 2
    parts = [both[:half], both[half:]]
    scores = [jnp.dot(part, query_wide, preferred_element_type=jnp.float32) for part in parts]
    dprobs = [jnp.dot(part, grad_wide, preferred_element_type=jnp.float32) for part in parts]
    expos = []
    for i, score in enumerate(scores):
        position = i * half + lax.broadcasted_iota(jnp.int32, score.shape, 0)
        allowed = jnp.logical_and(position >= first, position < last)
        expos.append(jnp.where(allowed, jnp.exp(score), 0.0))
    inverse = 1.0 / sum(jnp.sum(expo, axis=0, keepdims=True) for expo in expos)
    weighted = sum(
        jnp.sum(expo * dprob, axis=0, keepdims=True) for expo, dprob in zip(expos, dprobs)
    )
    delta = weighted * inverse
    probs = [expo * inverse for expo in expos]
    dscores = [
        (prob * (dprob - delta)).astype(jnp.bfloat16) for prob, dprob in zip(probs, dprobs)
    ]
    both_low = jnp.concatenate([
        (dot(dscore, query_wide, NT) + dot(prob.astype(jnp.bfloat16), grad_wide, NT))
        .astype(jnp.bfloat16)
        for dscore, prob in zip(dscores, probs)
    ], axis=0)
    low = low_ref[...].astype(jnp.float32)
    rows = low.shape[0]
    blocks = sent_ref.shape[0]
    packed = jnp.concatenate([low[at:at + CUT] for at in range(0, rows, CUT)], axis=1)
    packed = packed.astype(jnp.bfloat16)
    for at, block in enumerate(group_order(blocks)):
        sent_ref[at, :rows, :] = both_low[block * rows:(block + 1) * rows]
        sent_ref[at, rows:, :] = packed

    both_grad_ref[...] = both_low
    query_grad = sum(dot(part, dscore, TN) for part, dscore in zip(parts, dscores))
    query_grad_ref[...] = query_grad[:HS].astype(jnp.bfloat16)


def split_kernel(rows, both_grad_ref, *out_refs):
    dp = len(out_refs)
    step = HS // dp
    exact = both_grad_ref[...].astype(jnp.float32)
    parts = []
    for start in range(0, rows, CUT):
        for block in range(0, exact.shape[0], rows):
            parts.append(exact[block + start:block + start + CUT])
    turned = jnp.concatenate(parts, axis=0).T
    pieces = []
    for j in range(dp):
        halves = [turned[j * step:(j + 1) * step], turned[HS + j * step:HS + (j + 1) * step]]
        pieces.append(jnp.concatenate(halves, axis=0))
    pack = lax.axis_index("dp")
    for s, out_ref in enumerate(out_refs):
        turn = lax.rem(2 * dp - 1 + s - pack, dp)
        chosen = pieces[0]
        for j in range(1, dp):
            chosen = jnp.where(turn == j, pieces[j], chosen)
        out_ref[...] = chosen.astype(jnp.bfloat16)


def order_kernel(*refs):
    *arrived_refs, out_ref = refs
    dp = len(arrived_refs)
    mine = lax.rem(lax.axis_index("mp"), dp)
    for s, arrived_ref in enumerate(arrived_refs):
        out_ref[dp - 1 - lax.rem(mine + dp - s, dp)] = arrived_ref[...]


def share_kernel(rows, both_rank, got_ref, pieces_ref, *out_refs):
    dp, piece_rows, _ = pieces_ref.shape
    blocks = got_ref.shape[0]
    order = group_order(blocks)
    lows = [
        got_ref[order.index(block), rows:, :].astype(jnp.float32) for block in range(blocks)
    ]
    lows = jnp.concatenate(lows, axis=0).astype(jnp.bfloat16)
    columns = jnp.concatenate([pieces_ref[e] for e in range(dp)], axis=0)
    share = None
    for cut in range(rows // CUT):
        tokens = columns[:, cut * blocks * CUT:(cut + 1) * blocks * CUT]
        product = jnp.dot(tokens, lows, preferred_element_type=jnp.float32)
        part = product[:, cut * both_rank:(cut + 1) * both_rank]
        share = part if share is None else share + part
    step = piece_rows // 2
    column = lax.broadcasted_iota(jnp.int32, (step, both_rank), 1)
    shares = []
    for e in range(dp):
        keys = share[e * piece_rows:e * piece_rows + step]
        values = share[e * piece_rows + step:(e + 1) * piece_rows]
        shares.append(adapter_factor * jnp.where(column < both_rank // 2, keys, values))
    mine = lax.axis_index("dp")
    for s, out_ref in enumerate(out_refs):
        turn = lax.rem(mine + s, dp)
        chosen = shares[0]
        for e in range(1, dp):
            chosen = jnp.where(turn == e, shares[e], chosen)
        out_ref[...] = chosen


def owner_kernel(got_ref, up_ref, key_ref, value_ref, low_grad_ref):
    rows = key_ref.shape[0]
    rank = up_ref.shape[0] // 2
    order = group_order(got_ref.shape[0])
    for pair in range(len(order) // 2):
        first = got_ref[order.index(2 * pair), :rows, :]
        second = got_ref[order.index(2 * pair + 1), :rows, :]
        columns = slice(2 * pair * HS, (2 * pair + 2) * HS)
        key_ref[:, columns] = jnp.concatenate([first[:, :HS], second[:, :HS]], axis=1)
        value_ref[:, columns] = jnp.concatenate([first[:, HS:], second[:, HS:]], axis=1)
    up = up_ref[...]
    from_key = dot(key_ref[...], up, NT)
    from_value = dot(value_ref[...], up, NT)
    column = lax.broadcasted_iota(jnp.int32, from_key.shape, 1)
    low_grad_ref[...] = adapter_factor * jnp.where(column < rank, from_key, from_value)


def local(dp, mp, query, kv_cache, out_grad, source_lengths, target_lengths, low_rank, adapter_up_matrix):
    tgt_count = query.shape[0]
    src_count = kv_cache.shape[0]
    rows, both_rank = low_rank.shape
    width = adapter_up_matrix.shape[1]
    step = HS // dp
    assert rows // CUT * both_rank == LANES
    vmem = pl.BlockSpec(memory_space=pltpu.VMEM)
    hbm = pl.BlockSpec(memory_space=pl.ANY)
    params = pltpu.CompilerParams(vmem_limit_bytes=48 * 1024 * 1024)
    whole_vmem = pltpu.CompilerParams(vmem_limit_bytes=60 * 1024 * 1024)

    query_t = query.T
    grad_t = out_grad.T
    query_grad_t, sent, both_grad = pl.pallas_call(
        attention_kernel,
        out_shape=[
            jax.ShapeDtypeStruct((HS, tgt_count), jnp.bfloat16),
            jax.ShapeDtypeStruct((mp, rows + CUT, LANES), jnp.bfloat16),
            jax.ShapeDtypeStruct((src_count, 2 * HS), jnp.bfloat16),
        ],
        in_specs=[hbm] * 6,
        out_specs=[vmem] * 3,
        scratch_shapes=[
            pltpu.SMEM(source_lengths.shape, jnp.int32),
            pltpu.SMEM(target_lengths.shape, jnp.int32),
            pltpu.VMEM(query_t.shape, jnp.bfloat16),
            pltpu.VMEM(grad_t.shape, jnp.bfloat16),
            pltpu.VMEM(kv_cache.shape, jnp.bfloat16),
            pltpu.VMEM(low_rank.shape, jnp.bfloat16),
            pltpu.SemaphoreType.DMA((6,)),
        ],
        compiler_params=whole_vmem,
        name="attention_backward",
    )(source_lengths, target_lengths, query_t, grad_t, kv_cache, low_rank)

    route = [(h, h * dp % mp + dp - 1 - h * dp // mp) for h in range(mp)]
    pieces = pl.pallas_call(
        functools.partial(split_kernel, rows),
        out_shape=[jax.ShapeDtypeStruct((2 * step, src_count), jnp.bfloat16)] * dp,
        in_specs=[vmem],
        out_specs=[vmem] * dp,
        compiler_params=params,
        cost_estimate=pl.CostEstimate(flops=2 ** 36, bytes_accessed=2 ** 28, transcendentals=0),
        name="split_columns",
    )(lax.ppermute(both_grad, "mp", route))
    arrived = [pieces[0]]
    for s in range(1, dp):
        route = [(m, m - m % dp + (m + s) % dp) for m in range(mp)]
        arrived.append(lax.ppermute(pieces[s], "mp", route))
    ordered = pl.pallas_call(
        order_kernel,
        out_shape=jax.ShapeDtypeStruct((dp, 2 * step, src_count), jnp.bfloat16),
        in_specs=[vmem] * dp,
        out_specs=vmem,
        compiler_params=params,
        name="order_pieces",
    )(*arrived)

    got = lax.all_to_all(sent, "mp", 0, 0, axis_index_groups=[group_order(mp)], tiled=True)

    shares = pl.pallas_call(
        functools.partial(share_kernel, rows, both_rank),
        out_shape=[jax.ShapeDtypeStruct((step, both_rank), jnp.float32)] * dp,
        in_specs=[vmem] * 2,
        out_specs=[vmem] * dp,
        compiler_params=params,
        name="adapter_shares",
    )(got, ordered)
    up_grad = shares[0]
    for s in range(1, dp):
        route = [
            (d * mp + m, (d + s) % dp * mp + m - m % dp + (m + s) % dp)
            for d in range(dp) for m in range(mp)
        ]
        up_grad = up_grad + lax.ppermute(shares[s], ("dp", "mp"), route)

    key_gradient, value_grad, low_grad = pl.pallas_call(
        owner_kernel,
        out_shape=[
            jax.ShapeDtypeStruct((rows, width), jnp.bfloat16),
            jax.ShapeDtypeStruct((rows, width), jnp.bfloat16),
            jax.ShapeDtypeStruct((rows, both_rank), jnp.float32),
        ],
        in_specs=[vmem] * 2,
        out_specs=[vmem] * 3,
        compiler_params=params,
        name="owner_outputs",
    )(got, adapter_up_matrix)
    return query_grad_t.T, key_gradient, value_grad, low_grad, up_grad


def solution(mesh):
    in_specs = (
        P("dp", "mp"),
        P("dp", "mp"),
        P("dp", "mp"),
        P("dp", None),
        P("dp", None),
        P(("dp", "mp"), None),
        P(),
    )
    out_specs = (
        P("dp", "mp"),
        P(("dp", "mp"), None),
        P(("dp", "mp"), None),
        P(("dp", "mp"), None),
        P(("dp", "mp"), None),
    )
    body = functools.partial(local, mesh.shape["dp"], mesh.shape["mp"])
    return jax.shard_map(body, mesh=mesh, in_specs=in_specs, out_specs=out_specs, check_vma=False)
```

```python
import functools

import jax
import jax.numpy as jnp
from jax import lax
from jax.experimental import pallas as pl
from jax.experimental.pallas import tpu as pltpu
from jax.sharding import PartitionSpec as P

HS = 64
LANES = 128
CUT = 8

adapter_factor = 2.0

NT = (((1,), (1,)), ((), ()))
TN = (((0,), (0,)), ((), ()))


def dot(left, right, dims):
    return lax.dot_general(left, right, dims, preferred_element_type=jnp.float32)


def group_order(count):
    quarter = count // 4
    bits = quarter.bit_length() - 1
    assert count == 4 << bits
    turned = [sum(((i >> b) & 1) << (bits - 1 - b) for b in range(bits)) for i in range(quarter)]
    order = []
    for place in reversed(turned):
        other = place ^ (quarter // 2)
        order += [2 * quarter + place, other, 3 * quarter + place, quarter + other]
    return order


def source_range(source_ref, target_ref, count):
    position = lax.broadcasted_iota(jnp.int32, (1, count), 1)
    first = jnp.zeros((1, count), jnp.int32)
    last = jnp.zeros((1, count), jnp.int32)
    target_start = jnp.int32(0)
    source_start = jnp.int32(0)
    for i in range(source_ref.shape[1]):
        source_end = source_start + source_ref[0, i]
        inside = position >= target_start
        first = jnp.where(inside, source_start, first)
        last = jnp.where(inside, source_end, last)
        target_start = target_start + target_ref[0, i]
        source_start = source_end
    return first, last


def attention_kernel(
    source_any, target_any, query_any, grad_any, kv_any, low_any, query_grad_ref, sent_ref, both_grad_ref,
    source_ref, target_ref, query_ref, grad_ref, kv_ref, low_ref, sems,
):
    pairs = [
        (kv_any, kv_ref), (query_any, query_ref), (grad_any, grad_ref),
        (source_any, source_ref), (target_any, target_ref), (low_any, low_ref),
    ]
    copies = [
        pltpu.make_async_copy(here, there, sems.at[i]) for i, (here, there) in enumerate(pairs)
    ]
    for copy in copies:
        copy.start()
    for copy in copies:
        copy.wait()
    tgt_count = query_ref.shape[1]
    both = kv_ref[...]
    query_t = query_ref[...]
    grad_t = grad_ref[...]
    blank = jnp.zeros_like(query_t)
    query_wide = jnp.concatenate([query_t, blank], axis=0)
    grad_wide = jnp.concatenate([blank, grad_t], axis=0)
    first, last = source_range(source_ref, target_ref, tgt_count)
    half = both.shape[0] // 2
    parts = [both[:half], both[half:]]
    scores = [jnp.dot(part, query_wide, preferred_element_type=jnp.float32) for part in parts]
    dprobs = [jnp.dot(part, grad_wide, preferred_element_type=jnp.float32) for part in parts]
    expos = []
    for i, score in enumerate(scores):
        position = i * half + lax.broadcasted_iota(jnp.int32, score.shape, 0)
        allowed = jnp.logical_and(position >= first, position < last)
        expos.append(jnp.where(allowed, jnp.exp(score), 0.0))
    inverse = 1.0 / sum(jnp.sum(expo, axis=0, keepdims=True) for expo in expos)
    weighted = sum(
        jnp.sum(expo * dprob, axis=0, keepdims=True) for expo, dprob in zip(expos, dprobs)
    )
    delta = weighted * inverse
    probs = [expo * inverse for expo in expos]
    dscores = [
        (prob * (dprob - delta)).astype(jnp.bfloat16) for prob, dprob in zip(probs, dprobs)
    ]
    both_low = jnp.concatenate([
        (dot(dscore, query_wide, NT) + dot(prob.astype(jnp.bfloat16), grad_wide, NT))
        .astype(jnp.bfloat16)
        for dscore, prob in zip(dscores, probs)
    ], axis=0)
    low = low_ref[...].astype(jnp.float32)
    rows = low.shape[0]
    blocks = sent_ref.shape[0]
    packed = jnp.concatenate([low[at:at + CUT] for at in range(0, rows, CUT)], axis=1)
    packed = packed.astype(jnp.bfloat16)
    for at, block in enumerate(group_order(blocks)):
        sent_ref[at, :rows, :] = both_low[block * rows:(block + 1) * rows]
        sent_ref[at, rows:, :] = packed

    both_grad_ref[...] = both_low
    query_grad = sum(dot(part, dscore, TN) for part, dscore in zip(parts, dscores))
    query_grad_ref[...] = query_grad[:HS].astype(jnp.bfloat16)


def split_kernel(rows, both_grad_ref, *out_refs):
    dp = len(out_refs)
    step = HS // dp
    exact = both_grad_ref[...].astype(jnp.float32)
    parts = []
    for start in range(0, rows, CUT):
        for block in range(0, exact.shape[0], rows):
            parts.append(exact[block + start:block + start + CUT])
    turned = jnp.concatenate(parts, axis=0).T
    pieces = []
    for j in range(dp):
        halves = [turned[j * step:(j + 1) * step], turned[HS + j * step:HS + (j + 1) * step]]
        pieces.append(jnp.concatenate(halves, axis=0))
    pack = lax.axis_index("dp")
    for s, out_ref in enumerate(out_refs):
        turn = lax.rem(2 * dp - 1 + s - pack, dp)
        chosen = pieces[0]
        for j in range(1, dp):
            chosen = jnp.where(turn == j, pieces[j], chosen)
        out_ref[...] = chosen.astype(jnp.bfloat16)


def order_kernel(*refs):
    *arrived_refs, out_ref = refs
    dp = len(arrived_refs)
    mine = lax.rem(lax.axis_index("mp"), dp)
    for s, arrived_ref in enumerate(arrived_refs):
        out_ref[dp - 1 - lax.rem(mine + dp - s, dp)] = arrived_ref[...]


def share_kernel(rows, both_rank, got_ref, pieces_ref, *out_refs):
    dp, piece_rows, _ = pieces_ref.shape
    blocks = got_ref.shape[0]
    order = group_order(blocks)
    lows = [
        got_ref[order.index(block), rows:, :].astype(jnp.float32) for block in range(blocks)
    ]
    lows = jnp.concatenate(lows, axis=0).astype(jnp.bfloat16)
    columns = jnp.concatenate([pieces_ref[e] for e in range(dp)], axis=0)
    share = None
    for cut in range(rows // CUT):
        tokens = columns[:, cut * blocks * CUT:(cut + 1) * blocks * CUT]
        product = jnp.dot(tokens, lows, preferred_element_type=jnp.float32)
        part = product[:, cut * both_rank:(cut + 1) * both_rank]
        share = part if share is None else share + part
    step = piece_rows // 2
    column = lax.broadcasted_iota(jnp.int32, (step, both_rank), 1)
    shares = []
    for e in range(dp):
        keys = share[e * piece_rows:e * piece_rows + step]
        values = share[e * piece_rows + step:(e + 1) * piece_rows]
        shares.append(adapter_factor * jnp.where(column < both_rank // 2, keys, values))
    mine = lax.axis_index("dp")
    for s, out_ref in enumerate(out_refs):
        turn = lax.rem(mine + s, dp)
        chosen = shares[0]
        for e in range(1, dp):
            chosen = jnp.where(turn == e, shares[e], chosen)
        out_ref[...] = chosen


def owner_kernel(got_ref, up_ref, key_ref, value_ref, low_grad_ref):
    rows = key_ref.shape[0]
    rank = up_ref.shape[0] // 2
    order = group_order(got_ref.shape[0])
    for pair in range(len(order) // 2):
        first = got_ref[order.index(2 * pair), :rows, :]
        second = got_ref[order.index(2 * pair + 1), :rows, :]
        columns = slice(2 * pair * HS, (2 * pair + 2) * HS)
        key_ref[:, columns] = jnp.concatenate([first[:, :HS], second[:, :HS]], axis=1)
        value_ref[:, columns] = jnp.concatenate([first[:, HS:], second[:, HS:]], axis=1)
    up = up_ref[...]
    from_key = dot(key_ref[...], up, NT)
    from_value = dot(value_ref[...], up, NT)
    column = lax.broadcasted_iota(jnp.int32, from_key.shape, 1)
    low_grad_ref[...] = adapter_factor * jnp.where(column < rank, from_key, from_value)


def local(dp, mp, query, kv_cache, out_grad, source_lengths, target_lengths, low_rank, adapter_up_matrix):
    tgt_count = query.shape[0]
    src_count = kv_cache.shape[0]
    rows, both_rank = low_rank.shape
    width = adapter_up_matrix.shape[1]
    step = HS // dp
    assert rows // CUT * both_rank == LANES
    vmem = pl.BlockSpec(memory_space=pltpu.VMEM)
    hbm = pl.BlockSpec(memory_space=pl.ANY)
    params = pltpu.CompilerParams(vmem_limit_bytes=48 * 1024 * 1024)
    whole_vmem = pltpu.CompilerParams(vmem_limit_bytes=60 * 1024 * 1024)

    query_t = query.T
    grad_t = out_grad.T
    query_grad_t, sent, both_grad = pl.pallas_call(
        attention_kernel,
        out_shape=[
            jax.ShapeDtypeStruct((HS, tgt_count), jnp.bfloat16),
            jax.ShapeDtypeStruct((mp, rows + CUT, LANES), jnp.bfloat16),
            jax.ShapeDtypeStruct((src_count, 2 * HS), jnp.bfloat16),
        ],
        in_specs=[hbm] * 6,
        out_specs=[vmem] * 3,
        scratch_shapes=[
            pltpu.SMEM(source_lengths.shape, jnp.int32),
            pltpu.SMEM(target_lengths.shape, jnp.int32),
            pltpu.VMEM(query_t.shape, jnp.bfloat16),
            pltpu.VMEM(grad_t.shape, jnp.bfloat16),
            pltpu.VMEM(kv_cache.shape, jnp.bfloat16),
            pltpu.VMEM(low_rank.shape, jnp.bfloat16),
            pltpu.SemaphoreType.DMA((6,)),
        ],
        compiler_params=whole_vmem,
        name="attention_backward",
    )(source_lengths, target_lengths, query_t, grad_t, kv_cache, low_rank)

    route = [(h, h * dp % mp + dp - 1 - h * dp // mp) for h in range(mp)]
    pieces = pl.pallas_call(
        functools.partial(split_kernel, rows),
        out_shape=[jax.ShapeDtypeStruct((2 * step, src_count), jnp.bfloat16)] * dp,
        in_specs=[vmem],
        out_specs=[vmem] * dp,
        compiler_params=params,
        cost_estimate=pl.CostEstimate(flops=2 ** 36, bytes_accessed=2 ** 28, transcendentals=0),
        name="split_columns",
    )(lax.ppermute(both_grad, "mp", route))
    arrived = [pieces[0]]
    for s in range(1, dp):
        route = [(m, m - m % dp + (m + s) % dp) for m in range(mp)]
        arrived.append(lax.ppermute(pieces[s], "mp", route))
    ordered = pl.pallas_call(
        order_kernel,
        out_shape=jax.ShapeDtypeStruct((dp, 2 * step, src_count), jnp.bfloat16),
        in_specs=[vmem] * dp,
        out_specs=vmem,
        compiler_params=params,
        name="order_pieces",
    )(*arrived)

    got = lax.all_to_all(sent, "mp", 0, 0, axis_index_groups=[group_order(mp)], tiled=True)

    shares = pl.pallas_call(
        functools.partial(share_kernel, rows, both_rank),
        out_shape=[jax.ShapeDtypeStruct((step, both_rank), jnp.float32)] * dp,
        in_specs=[vmem] * 2,
        out_specs=[vmem] * dp,
        compiler_params=params,
        name="adapter_shares",
    )(got, ordered)
    up_grad = shares[0]
    for s in range(1, dp):
        route = [
            (d * mp + m, (d + s) % dp * mp + m - m % dp + (m + s) % dp)
            for d in range(dp) for m in range(mp)
        ]
        up_grad = up_grad + lax.ppermute(shares[s], ("dp", "mp"), route)

    key_gradient, value_grad, low_grad = pl.pallas_call(
        owner_kernel,
        out_shape=[
            jax.ShapeDtypeStruct((rows, width), jnp.bfloat16),
            jax.ShapeDtypeStruct((rows, width), jnp.bfloat16),
            jax.ShapeDtypeStruct((rows, both_rank), jnp.float32),
        ],
        in_specs=[vmem] * 2,
        out_specs=[vmem] * 3,
        compiler_params=params,
        name="owner_outputs",
    )(got, adapter_up_matrix)
    return query_grad_t.T, key_gradient, value_grad, low_grad, up_grad


def solution(mesh):
    in_specs = (
        P("dp", "mp"),
        P("dp", "mp"),
        P("dp", "mp"),
        P("dp", None),
        P("dp", None),
        P(("dp", "mp"), None),
        P(),
    )
    out_specs = (
        P("dp", "mp"),
        P(("dp", "mp"), None),
        P(("dp", "mp"), None),
        P(("dp", "mp"), None),
        P(("dp", "mp"), None),
    )
    body = functools.partial(local, mesh.shape["dp"], mesh.shape["mp"])
    return jax.shard_map(body, mesh=mesh, in_specs=in_specs, out_specs=out_specs, check_vma=False)
```

```python
import functools

import jax
import jax.numpy as jnp
from jax import lax
from jax.experimental import pallas as pl
from jax.experimental.pallas import tpu as pltpu
from jax.sharding import PartitionSpec as P

HS = 64
LANES = 128
CUT = 8

adapter_factor = 2.0

NT = (((1,), (1,)), ((), ()))
TN = (((0,), (0,)), ((), ()))


def dot(left, right, dims):
    return lax.dot_general(left, right, dims, preferred_element_type=jnp.float32)


def group_order(count):
    quarter = count // 4
    bits = quarter.bit_length() - 1
    assert count == 4 << bits
    turned = [sum(((i >> b) & 1) << (bits - 1 - b) for b in range(bits)) for i in range(quarter)]
    order = []
    for i, place in enumerate(reversed(turned)):
        order += [2 * quarter + place, 2 * i, 3 * quarter + place, 2 * i + 1]
    return order


def source_range(source_ref, target_ref, count):
    position = lax.broadcasted_iota(jnp.int32, (1, count), 1)
    first = jnp.zeros((1, count), jnp.int32)
    last = jnp.zeros((1, count), jnp.int32)
    target_start = jnp.int32(0)
    source_start = jnp.int32(0)
    for i in range(source_ref.shape[1]):
        source_end = source_start + source_ref[0, i]
        inside = position >= target_start
        first = jnp.where(inside, source_start, first)
        last = jnp.where(inside, source_end, last)
        target_start = target_start + target_ref[0, i]
        source_start = source_end
    return first, last


def attention_kernel(
    source_any, target_any, query_any, grad_any, kv_any, low_any, query_grad_ref, sent_ref, both_grad_ref,
    source_ref, target_ref, query_ref, grad_ref, kv_ref, low_ref, sems,
):
    pairs = [
        (kv_any, kv_ref), (query_any, query_ref), (grad_any, grad_ref),
        (source_any, source_ref), (target_any, target_ref), (low_any, low_ref),
    ]
    copies = [
        pltpu.make_async_copy(here, there, sems.at[i]) for i, (here, there) in enumerate(pairs)
    ]
    for copy in copies:
        copy.start()
    for copy in copies:
        copy.wait()
    tgt_count = query_ref.shape[1]
    both = kv_ref[...]
    query_t = query_ref[...]
    grad_t = grad_ref[...]
    blank = jnp.zeros_like(query_t)
    query_wide = jnp.concatenate([query_t, blank], axis=0)
    grad_wide = jnp.concatenate([blank, grad_t], axis=0)
    first, last = source_range(source_ref, target_ref, tgt_count)
    half = both.shape[0] // 2
    parts = [both[:half], both[half:]]
    scores = [jnp.dot(part, query_wide, preferred_element_type=jnp.float32) for part in parts]
    dprobs = [jnp.dot(part, grad_wide, preferred_element_type=jnp.float32) for part in parts]
    expos = []
    for i, score in enumerate(scores):
        position = i * half + lax.broadcasted_iota(jnp.int32, score.shape, 0)
        allowed = jnp.logical_and(position >= first, position < last)
        expos.append(jnp.where(allowed, jnp.exp(score), 0.0))
    inverse = 1.0 / sum(jnp.sum(expo, axis=0, keepdims=True) for expo in expos)
    weighted = sum(
        jnp.sum(expo * dprob, axis=0, keepdims=True) for expo, dprob in zip(expos, dprobs)
    )
    delta = weighted * inverse
    probs = [expo * inverse for expo in expos]
    dscores = [
        (prob * (dprob - delta)).astype(jnp.bfloat16) for prob, dprob in zip(probs, dprobs)
    ]
    both_low = jnp.concatenate([
        (dot(dscore, query_wide, NT) + dot(prob.astype(jnp.bfloat16), grad_wide, NT))
        .astype(jnp.bfloat16)
        for dscore, prob in zip(dscores, probs)
    ], axis=0)
    low = low_ref[...].astype(jnp.float32)
    rows = low.shape[0]
    blocks = sent_ref.shape[0]
    packed = jnp.concatenate([low[at:at + CUT] for at in range(0, rows, CUT)], axis=1)
    packed = packed.astype(jnp.bfloat16)
    for at, block in enumerate(group_order(blocks)):
        sent_ref[at, :rows, :] = both_low[block * rows:(block + 1) * rows]
        sent_ref[at, rows:, :] = packed

    both_grad_ref[...] = both_low
    query_grad = sum(dot(part, dscore, TN) for part, dscore in zip(parts, dscores))
    query_grad_ref[...] = query_grad[:HS].astype(jnp.bfloat16)


def split_kernel(rows, both_grad_ref, *out_refs):
    dp = len(out_refs)
    step = HS // dp
    exact = both_grad_ref[...].astype(jnp.float32)
    parts = []
    for start in range(0, rows, CUT):
        for block in range(0, exact.shape[0], rows):
            parts.append(exact[block + start:block + start + CUT])
    turned = jnp.concatenate(parts, axis=0).T
    pieces = []
    for j in range(dp):
        halves = [turned[j * step:(j + 1) * step], turned[HS + j * step:HS + (j + 1) * step]]
        pieces.append(jnp.concatenate(halves, axis=0))
    pack = lax.axis_index("dp")
    for s, out_ref in enumerate(out_refs):
        turn = lax.rem(2 * dp - 1 + s - pack, dp)
        chosen = pieces[0]
        for j in range(1, dp):
            chosen = jnp.where(turn == j, pieces[j], chosen)
        out_ref[...] = chosen.astype(jnp.bfloat16)


def order_kernel(*refs):
    *arrived_refs, out_ref = refs
    dp = len(arrived_refs)
    mine = lax.rem(lax.axis_index("mp"), dp)
    for s, arrived_ref in enumerate(arrived_refs):
        out_ref[dp - 1 - lax.rem(mine + dp - s, dp)] = arrived_ref[...]


def share_kernel(rows, both_rank, got_ref, pieces_ref, *out_refs):
    dp, piece_rows, _ = pieces_ref.shape
    blocks = got_ref.shape[0]
    order = group_order(blocks)
    lows = [
        got_ref[order.index(block), rows:, :].astype(jnp.float32) for block in range(blocks)
    ]
    lows = jnp.concatenate(lows, axis=0).astype(jnp.bfloat16)
    columns = jnp.concatenate([pieces_ref[e] for e in range(dp)], axis=0)
    share = None
    for cut in range(rows // CUT):
        tokens = columns[:, cut * blocks * CUT:(cut + 1) * blocks * CUT]
        product = jnp.dot(tokens, lows, preferred_element_type=jnp.float32)
        part = product[:, cut * both_rank:(cut + 1) * both_rank]
        share = part if share is None else share + part
    step = piece_rows // 2
    column = lax.broadcasted_iota(jnp.int32, (step, both_rank), 1)
    shares = []
    for e in range(dp):
        keys = share[e * piece_rows:e * piece_rows + step]
        values = share[e * piece_rows + step:(e + 1) * piece_rows]
        shares.append(adapter_factor * jnp.where(column < both_rank // 2, keys, values))
    mine = lax.axis_index("dp")
    for s, out_ref in enumerate(out_refs):
        turn = lax.rem(mine + s, dp)
        chosen = shares[0]
        for e in range(1, dp):
            chosen = jnp.where(turn == e, shares[e], chosen)
        out_ref[...] = chosen


def owner_kernel(got_ref, up_ref, key_ref, value_ref, low_grad_ref):
    rows = key_ref.shape[0]
    rank = up_ref.shape[0] // 2
    order = group_order(got_ref.shape[0])
    for pair in range(len(order) // 2):
        first = got_ref[order.index(2 * pair), :rows, :]
        second = got_ref[order.index(2 * pair + 1), :rows, :]
        columns = slice(2 * pair * HS, (2 * pair + 2) * HS)
        key_ref[:, columns] = jnp.concatenate([first[:, :HS], second[:, :HS]], axis=1)
        value_ref[:, columns] = jnp.concatenate([first[:, HS:], second[:, HS:]], axis=1)
    up = up_ref[...]
    from_key = dot(key_ref[...], up, NT)
    from_value = dot(value_ref[...], up, NT)
    column = lax.broadcasted_iota(jnp.int32, from_key.shape, 1)
    low_grad_ref[...] = adapter_factor * jnp.where(column < rank, from_key, from_value)


def local(dp, mp, query, kv_cache, out_grad, source_lengths, target_lengths, low_rank, adapter_up_matrix):
    tgt_count = query.shape[0]
    src_count = kv_cache.shape[0]
    rows, both_rank = low_rank.shape
    width = adapter_up_matrix.shape[1]
    step = HS // dp
    assert rows // CUT * both_rank == LANES
    vmem = pl.BlockSpec(memory_space=pltpu.VMEM)
    hbm = pl.BlockSpec(memory_space=pl.ANY)
    params = pltpu.CompilerParams(vmem_limit_bytes=48 * 1024 * 1024)
    whole_vmem = pltpu.CompilerParams(vmem_limit_bytes=60 * 1024 * 1024)

    query_t = query.T
    grad_t = out_grad.T
    query_grad_t, sent, both_grad = pl.pallas_call(
        attention_kernel,
        out_shape=[
            jax.ShapeDtypeStruct((HS, tgt_count), jnp.bfloat16),
            jax.ShapeDtypeStruct((mp, rows + CUT, LANES), jnp.bfloat16),
            jax.ShapeDtypeStruct((src_count, 2 * HS), jnp.bfloat16),
        ],
        in_specs=[hbm] * 6,
        out_specs=[vmem] * 3,
        scratch_shapes=[
            pltpu.SMEM(source_lengths.shape, jnp.int32),
            pltpu.SMEM(target_lengths.shape, jnp.int32),
            pltpu.VMEM(query_t.shape, jnp.bfloat16),
            pltpu.VMEM(grad_t.shape, jnp.bfloat16),
            pltpu.VMEM(kv_cache.shape, jnp.bfloat16),
            pltpu.VMEM(low_rank.shape, jnp.bfloat16),
            pltpu.SemaphoreType.DMA((6,)),
        ],
        compiler_params=whole_vmem,
        name="attention_backward",
    )(source_lengths, target_lengths, query_t, grad_t, kv_cache, low_rank)

    route = [(h, h * dp % mp + dp - 1 - h * dp // mp) for h in range(mp)]
    pieces = pl.pallas_call(
        functools.partial(split_kernel, rows),
        out_shape=[jax.ShapeDtypeStruct((2 * step, src_count), jnp.bfloat16)] * dp,
        in_specs=[vmem],
        out_specs=[vmem] * dp,
        compiler_params=params,
        cost_estimate=pl.CostEstimate(flops=2 ** 36, bytes_accessed=2 ** 28, transcendentals=0),
        name="split_columns",
    )(lax.ppermute(both_grad, "mp", route))
    arrived = [pieces[0]]
    for s in range(1, dp):
        route = [(m, m - m % dp + (m + s) % dp) for m in range(mp)]
        arrived.append(lax.ppermute(pieces[s], "mp", route))
    ordered = pl.pallas_call(
        order_kernel,
        out_shape=jax.ShapeDtypeStruct((dp, 2 * step, src_count), jnp.bfloat16),
        in_specs=[vmem] * dp,
        out_specs=vmem,
        compiler_params=params,
        name="order_pieces",
    )(*arrived)

    got = lax.all_to_all(sent, "mp", 0, 0, axis_index_groups=[group_order(mp)], tiled=True)

    shares = pl.pallas_call(
        functools.partial(share_kernel, rows, both_rank),
        out_shape=[jax.ShapeDtypeStruct((step, both_rank), jnp.float32)] * dp,
        in_specs=[vmem] * 2,
        out_specs=[vmem] * dp,
        compiler_params=params,
        name="adapter_shares",
    )(got, ordered)
    up_grad = shares[0]
    for s in range(1, dp):
        route = [
            (d * mp + m, (d + s) % dp * mp + m - m % dp + (m + s) % dp)
            for d in range(dp) for m in range(mp)
        ]
        up_grad = up_grad + lax.ppermute(shares[s], ("dp", "mp"), route)

    key_gradient, value_grad, low_grad = pl.pallas_call(
        owner_kernel,
        out_shape=[
            jax.ShapeDtypeStruct((rows, width), jnp.bfloat16),
            jax.ShapeDtypeStruct((rows, width), jnp.bfloat16),
            jax.ShapeDtypeStruct((rows, both_rank), jnp.float32),
        ],
        in_specs=[vmem] * 2,
        out_specs=[vmem] * 3,
        compiler_params=params,
        name="owner_outputs",
    )(got, adapter_up_matrix)
    return query_grad_t.T, key_gradient, value_grad, low_grad, up_grad


def solution(mesh):
    in_specs = (
        P("dp", "mp"),
        P("dp", "mp"),
        P("dp", "mp"),
        P("dp", None),
        P("dp", None),
        P(("dp", "mp"), None),
        P(),
    )
    out_specs = (
        P("dp", "mp"),
        P(("dp", "mp"), None),
        P(("dp", "mp"), None),
        P(("dp", "mp"), None),
        P(("dp", "mp"), None),
    )
    body = functools.partial(local, mesh.shape["dp"], mesh.shape["mp"])
    return jax.shard_map(body, mesh=mesh, in_specs=in_specs, out_specs=out_specs, check_vma=False)
```

```python
import functools

import jax
import jax.numpy as jnp
from jax import lax
from jax.experimental import pallas as pl
from jax.experimental.pallas import tpu as pltpu
from jax.sharding import PartitionSpec as P

HS = 64
LANES = 128
CUT = 8

adapter_factor = 2.0

NT = (((1,), (1,)), ((), ()))
TN = (((0,), (0,)), ((), ()))


def dot(left, right, dims):
    return lax.dot_general(left, right, dims, preferred_element_type=jnp.float32)


def group_order(count):
    quarter = count // 4
    bits = quarter.bit_length() - 1
    assert count == 4 << bits
    turned = [sum(((i >> b) & 1) << (bits - 1 - b) for b in range(bits)) for i in range(quarter)]
    order = []
    for i, place in enumerate(reversed(turned)):
        order += [2 * quarter + place, 2 * i, 3 * quarter + place, 2 * i + 1]
    return order


def source_range(source_ref, target_ref, count):
    position = lax.broadcasted_iota(jnp.int32, (1, count), 1)
    first = jnp.zeros((1, count), jnp.int32)
    last = jnp.zeros((1, count), jnp.int32)
    target_start = jnp.int32(0)
    source_start = jnp.int32(0)
    for i in range(source_ref.shape[1]):
        source_end = source_start + source_ref[0, i]
        inside = position >= target_start
        first = jnp.where(inside, source_start, first)
        last = jnp.where(inside, source_end, last)
        target_start = target_start + target_ref[0, i]
        source_start = source_end
    return first, last


def attention_kernel(
    source_any, target_any, query_any, grad_any, kv_any, low_any, query_grad_ref, sent_ref, both_grad_ref,
    source_ref, target_ref, query_ref, grad_ref, kv_ref, low_ref, sems,
):
    pairs = [
        (kv_any, kv_ref), (query_any, query_ref), (grad_any, grad_ref),
        (source_any, source_ref), (target_any, target_ref), (low_any, low_ref),
    ]
    copies = [
        pltpu.make_async_copy(here, there, sems.at[i]) for i, (here, there) in enumerate(pairs)
    ]
    for copy in copies:
        copy.start()
    for copy in copies:
        copy.wait()
    tgt_count = query_ref.shape[1]
    both = kv_ref[...]
    query_t = query_ref[...]
    grad_t = grad_ref[...]
    blank = jnp.zeros_like(query_t)
    query_wide = jnp.concatenate([query_t, blank], axis=0)
    grad_wide = jnp.concatenate([blank, grad_t], axis=0)
    first, last = source_range(source_ref, target_ref, tgt_count)
    half = both.shape[0] // 2
    parts = [both[:half], both[half:]]
    scores = [jnp.dot(part, query_wide, preferred_element_type=jnp.float32) for part in parts]
    dprobs = [jnp.dot(part, grad_wide, preferred_element_type=jnp.float32) for part in parts]
    expos = []
    for i, score in enumerate(scores):
        position = i * half + lax.broadcasted_iota(jnp.int32, score.shape, 0)
        allowed = jnp.logical_and(position >= first, position < last)
        expos.append(jnp.where(allowed, jnp.exp(score), 0.0))
    inverse = 1.0 / sum(jnp.sum(expo, axis=0, keepdims=True) for expo in expos)
    weighted = sum(
        jnp.sum(expo * dprob, axis=0, keepdims=True) for expo, dprob in zip(expos, dprobs)
    )
    delta = weighted * inverse
    probs = [expo * inverse for expo in expos]
    dscores = [
        (prob * (dprob - delta)).astype(jnp.bfloat16) for prob, dprob in zip(probs, dprobs)
    ]
    both_low = jnp.concatenate([
        (dot(dscore, query_wide, NT) + dot(prob.astype(jnp.bfloat16), grad_wide, NT))
        .astype(jnp.bfloat16)
        for dscore, prob in zip(dscores, probs)
    ], axis=0)
    low = low_ref[...].astype(jnp.float32)
    rows = low.shape[0]
    blocks = sent_ref.shape[0]
    packed = jnp.concatenate([low[at:at + CUT] for at in range(0, rows, CUT)], axis=1)
    packed = packed.astype(jnp.bfloat16)
    for at, block in enumerate(group_order(blocks)):
        sent_ref[at, :rows, :] = both_low[block * rows:(block + 1) * rows]
        sent_ref[at, rows:, :] = packed

    both_grad_ref[...] = both_low
    query_grad = sum(dot(part, dscore, TN) for part, dscore in zip(parts, dscores))
    query_grad_ref[...] = query_grad[:HS].astype(jnp.bfloat16)


def split_kernel(rows, both_grad_ref, *out_refs):
    dp = len(out_refs)
    step = HS // dp
    exact = both_grad_ref[...].astype(jnp.float32)
    parts = []
    for start in range(0, rows, CUT):
        for block in range(0, exact.shape[0], rows):
            parts.append(exact[block + start:block + start + CUT])
    turned = jnp.concatenate(parts, axis=0).T
    pieces = []
    for j in range(dp):
        halves = [turned[j * step:(j + 1) * step], turned[HS + j * step:HS + (j + 1) * step]]
        pieces.append(jnp.concatenate(halves, axis=0))
    pack = lax.axis_index("dp")
    for s, out_ref in enumerate(out_refs):
        turn = lax.rem(2 * dp - 1 + s - pack, dp)
        chosen = pieces[0]
        for j in range(1, dp):
            chosen = jnp.where(turn == j, pieces[j], chosen)
        out_ref[...] = chosen.astype(jnp.bfloat16)


def order_kernel(*refs):
    *arrived_refs, out_ref = refs
    dp = len(arrived_refs)
    mine = lax.rem(lax.axis_index("mp"), dp)
    for s, arrived_ref in enumerate(arrived_refs):
        out_ref[dp - 1 - lax.rem(mine + dp - s, dp)] = arrived_ref[...]


def share_kernel(rows, both_rank, got_ref, pieces_ref, *out_refs):
    dp, piece_rows, _ = pieces_ref.shape
    blocks = got_ref.shape[0]
    order = group_order(blocks)
    lows = [
        got_ref[order.index(block), rows:, :].astype(jnp.float32) for block in range(blocks)
    ]
    lows = jnp.concatenate(lows, axis=0).astype(jnp.bfloat16)
    columns = jnp.concatenate([pieces_ref[e] for e in range(dp)], axis=0)
    cuts = rows // CUT
    width = blocks * CUT
    stacked = [columns[:, cut * width:(cut + 1) * width] for cut in range(cuts)]
    product = jnp.dot(
        jnp.concatenate(stacked, axis=0), lows, preferred_element_type=jnp.float32
    )
    height = dp * piece_rows
    share = sum(
        product[cut * height:(cut + 1) * height, cut * both_rank:(cut + 1) * both_rank]
        for cut in range(cuts)
    )
    step = piece_rows // 2
    column = lax.broadcasted_iota(jnp.int32, (step, both_rank), 1)
    shares = []
    for e in range(dp):
        keys = share[e * piece_rows:e * piece_rows + step]
        values = share[e * piece_rows + step:(e + 1) * piece_rows]
        shares.append(adapter_factor * jnp.where(column < both_rank // 2, keys, values))
    mine = lax.axis_index("dp")
    for s, out_ref in enumerate(out_refs):
        turn = lax.rem(mine + s, dp)
        chosen = shares[0]
        for e in range(1, dp):
            chosen = jnp.where(turn == e, shares[e], chosen)
        out_ref[...] = chosen


def owner_kernel(got_ref, up_ref, key_ref, value_ref, low_grad_ref):
    rows = key_ref.shape[0]
    rank = up_ref.shape[0] // 2
    order = group_order(got_ref.shape[0])
    for pair in range(len(order) // 2):
        first = got_ref[order.index(2 * pair), :rows, :]
        second = got_ref[order.index(2 * pair + 1), :rows, :]
        columns = slice(2 * pair * HS, (2 * pair + 2) * HS)
        key_ref[:, columns] = jnp.concatenate([first[:, :HS], second[:, :HS]], axis=1)
        value_ref[:, columns] = jnp.concatenate([first[:, HS:], second[:, HS:]], axis=1)
    up = up_ref[...]
    from_key = dot(key_ref[...], up, NT)
    from_value = dot(value_ref[...], up, NT)
    column = lax.broadcasted_iota(jnp.int32, from_key.shape, 1)
    low_grad_ref[...] = adapter_factor * jnp.where(column < rank, from_key, from_value)


def local(dp, mp, query, kv_cache, out_grad, source_lengths, target_lengths, low_rank, adapter_up_matrix):
    tgt_count = query.shape[0]
    src_count = kv_cache.shape[0]
    rows, both_rank = low_rank.shape
    width = adapter_up_matrix.shape[1]
    step = HS // dp
    assert rows // CUT * both_rank == LANES
    vmem = pl.BlockSpec(memory_space=pltpu.VMEM)
    hbm = pl.BlockSpec(memory_space=pl.ANY)
    params = pltpu.CompilerParams(vmem_limit_bytes=48 * 1024 * 1024)
    whole_vmem = pltpu.CompilerParams(vmem_limit_bytes=60 * 1024 * 1024)

    query_t = query.T
    grad_t = out_grad.T
    query_grad_t, sent, both_grad = pl.pallas_call(
        attention_kernel,
        out_shape=[
            jax.ShapeDtypeStruct((HS, tgt_count), jnp.bfloat16),
            jax.ShapeDtypeStruct((mp, rows + CUT, LANES), jnp.bfloat16),
            jax.ShapeDtypeStruct((src_count, 2 * HS), jnp.bfloat16),
        ],
        in_specs=[hbm] * 6,
        out_specs=[vmem] * 3,
        scratch_shapes=[
            pltpu.SMEM(source_lengths.shape, jnp.int32),
            pltpu.SMEM(target_lengths.shape, jnp.int32),
            pltpu.VMEM(query_t.shape, jnp.bfloat16),
            pltpu.VMEM(grad_t.shape, jnp.bfloat16),
            pltpu.VMEM(kv_cache.shape, jnp.bfloat16),
            pltpu.VMEM(low_rank.shape, jnp.bfloat16),
            pltpu.SemaphoreType.DMA((6,)),
        ],
        compiler_params=whole_vmem,
        name="attention_backward",
    )(source_lengths, target_lengths, query_t, grad_t, kv_cache, low_rank)

    route = [(h, h * dp % mp + dp - 1 - h * dp // mp) for h in range(mp)]
    pieces = pl.pallas_call(
        functools.partial(split_kernel, rows),
        out_shape=[jax.ShapeDtypeStruct((2 * step, src_count), jnp.bfloat16)] * dp,
        in_specs=[vmem],
        out_specs=[vmem] * dp,
        compiler_params=params,
        cost_estimate=pl.CostEstimate(flops=2 ** 36, bytes_accessed=2 ** 28, transcendentals=0),
        name="split_columns",
    )(lax.ppermute(both_grad, "mp", route))
    arrived = [pieces[0]]
    for s in range(1, dp):
        route = [(m, m - m % dp + (m + s) % dp) for m in range(mp)]
        arrived.append(lax.ppermute(pieces[s], "mp", route))
    ordered = pl.pallas_call(
        order_kernel,
        out_shape=jax.ShapeDtypeStruct((dp, 2 * step, src_count), jnp.bfloat16),
        in_specs=[vmem] * dp,
        out_specs=vmem,
        compiler_params=params,
        name="order_pieces",
    )(*arrived)

    got = lax.all_to_all(sent, "mp", 0, 0, axis_index_groups=[group_order(mp)], tiled=True)

    shares = pl.pallas_call(
        functools.partial(share_kernel, rows, both_rank),
        out_shape=[jax.ShapeDtypeStruct((step, both_rank), jnp.float32)] * dp,
        in_specs=[vmem] * 2,
        out_specs=[vmem] * dp,
        compiler_params=params,
        name="adapter_shares",
    )(got, ordered)
    up_grad = shares[0]
    for s in range(1, dp):
        route = [
            (d * mp + m, (d + s) % dp * mp + m - m % dp + (m + s) % dp)
            for d in range(dp) for m in range(mp)
        ]
        up_grad = up_grad + lax.ppermute(shares[s], ("dp", "mp"), route)

    key_gradient, value_grad, low_grad = pl.pallas_call(
        owner_kernel,
        out_shape=[
            jax.ShapeDtypeStruct((rows, width), jnp.bfloat16),
            jax.ShapeDtypeStruct((rows, width), jnp.bfloat16),
            jax.ShapeDtypeStruct((rows, both_rank), jnp.float32),
        ],
        in_specs=[vmem] * 2,
        out_specs=[vmem] * 3,
        compiler_params=params,
        name="owner_outputs",
    )(got, adapter_up_matrix)
    return query_grad_t.T, key_gradient, value_grad, low_grad, up_grad


def solution(mesh):
    in_specs = (
        P("dp", "mp"),
        P("dp", "mp"),
        P("dp", "mp"),
        P("dp", None),
        P("dp", None),
        P(("dp", "mp"), None),
        P(),
    )
    out_specs = (
        P("dp", "mp"),
        P(("dp", "mp"), None),
        P(("dp", "mp"), None),
        P(("dp", "mp"), None),
        P(("dp", "mp"), None),
    )
    body = functools.partial(local, mesh.shape["dp"], mesh.shape["mp"])
    return jax.shard_map(body, mesh=mesh, in_specs=in_specs, out_specs=out_specs, check_vma=False)
```

```python
import functools

import jax
import jax.numpy as jnp
from jax import lax
from jax.experimental import pallas as pl
from jax.experimental.pallas import tpu as pltpu
from jax.sharding import PartitionSpec as P

HS = 64
LANES = 128
CUT = 8

adapter_factor = 2.0

NT = (((1,), (1,)), ((), ()))
TN = (((0,), (0,)), ((), ()))


def dot(left, right, dims):
    return lax.dot_general(left, right, dims, preferred_element_type=jnp.float32)


def group_order(count):
    quarter = count // 4
    bits = quarter.bit_length() - 1
    assert count == 4 << bits
    turned = [sum(((i >> b) & 1) << (bits - 1 - b) for b in range(bits)) for i in range(quarter)]
    order = []
    for i, place in enumerate(reversed(turned)):
        order += [2 * quarter + place, 2 * i, 3 * quarter + place, 2 * i + 1]
    return order


def source_range(source_ref, target_ref, count):
    position = lax.broadcasted_iota(jnp.int32, (1, count), 1)
    first = jnp.zeros((1, count), jnp.int32)
    last = jnp.zeros((1, count), jnp.int32)
    target_start = jnp.int32(0)
    source_start = jnp.int32(0)
    for i in range(source_ref.shape[1]):
        source_end = source_start + source_ref[0, i]
        inside = position >= target_start
        first = jnp.where(inside, source_start, first)
        last = jnp.where(inside, source_end, last)
        target_start = target_start + target_ref[0, i]
        source_start = source_end
    return first, last


def attention_kernel(
    source_any, target_any, query_any, grad_any, kv_any, low_any, query_grad_ref, sent_ref,
    source_ref, target_ref, query_ref, grad_ref, kv_ref, low_ref, sems,
):
    pairs = [
        (kv_any, kv_ref), (query_any, query_ref), (grad_any, grad_ref),
        (source_any, source_ref), (target_any, target_ref), (low_any, low_ref),
    ]
    copies = [
        pltpu.make_async_copy(here, there, sems.at[i]) for i, (here, there) in enumerate(pairs)
    ]
    for copy in copies:
        copy.start()
    for copy in copies:
        copy.wait()
    tgt_count = query_ref.shape[1]
    both = kv_ref[...]
    query_t = query_ref[...]
    grad_t = grad_ref[...]
    blank = jnp.zeros_like(query_t)
    query_wide = jnp.concatenate([query_t, blank], axis=0)
    grad_wide = jnp.concatenate([blank, grad_t], axis=0)
    first, last = source_range(source_ref, target_ref, tgt_count)
    half = both.shape[0] // 2
    parts = [both[:half], both[half:]]
    scores = [jnp.dot(part, query_wide, preferred_element_type=jnp.float32) for part in parts]
    dprobs = [jnp.dot(part, grad_wide, preferred_element_type=jnp.float32) for part in parts]
    expos = []
    for i, score in enumerate(scores):
        position = i * half + lax.broadcasted_iota(jnp.int32, score.shape, 0)
        allowed = jnp.logical_and(position >= first, position < last)
        expos.append(jnp.where(allowed, jnp.exp(score), 0.0))
    inverse = 1.0 / sum(jnp.sum(expo, axis=0, keepdims=True) for expo in expos)
    weighted = sum(
        jnp.sum(expo * dprob, axis=0, keepdims=True) for expo, dprob in zip(expos, dprobs)
    )
    delta = weighted * inverse
    probs = [expo * inverse for expo in expos]
    dscores = [
        (prob * (dprob - delta)).astype(jnp.bfloat16) for prob, dprob in zip(probs, dprobs)
    ]
    both_low = jnp.concatenate([
        (dot(dscore, query_wide, NT) + dot(prob.astype(jnp.bfloat16), grad_wide, NT))
        .astype(jnp.bfloat16)
        for dscore, prob in zip(dscores, probs)
    ], axis=0)
    low = low_ref[...].astype(jnp.float32)
    rows = low.shape[0]
    blocks = sent_ref.shape[0]
    packed = jnp.concatenate([low[at:at + CUT] for at in range(0, rows, CUT)], axis=1)
    packed = packed.astype(jnp.bfloat16)
    for at, block in enumerate(group_order(blocks)):
        sent_ref[at, :rows, :] = both_low[block * rows:(block + 1) * rows]
        sent_ref[at, rows:, :] = packed

    query_grad = sum(dot(part, dscore, TN) for part, dscore in zip(parts, dscores))
    query_grad_ref[...] = query_grad[:HS].astype(jnp.bfloat16)


def split_kernel(rows, blocks_ref, *out_refs):
    dp = len(out_refs)
    step = HS // dp
    order = group_order(blocks_ref.shape[0])
    exact = [
        blocks_ref[order.index(block), :rows, :].astype(jnp.float32) for block in range(len(order))
    ]
    parts = [part[start:start + CUT] for start in range(0, rows, CUT) for part in exact]
    turned = jnp.concatenate(parts, axis=0).T
    pieces = []
    for j in range(dp):
        halves = [turned[j * step:(j + 1) * step], turned[HS + j * step:HS + (j + 1) * step]]
        pieces.append(jnp.concatenate(halves, axis=0))
    pack = lax.axis_index("dp")
    for s, out_ref in enumerate(out_refs):
        turn = lax.rem(2 * dp - 1 + s - pack, dp)
        chosen = pieces[0]
        for j in range(1, dp):
            chosen = jnp.where(turn == j, pieces[j], chosen)
        out_ref[...] = chosen.astype(jnp.bfloat16)


def order_kernel(*refs):
    *arrived_refs, out_ref = refs
    dp = len(arrived_refs)
    mine = lax.rem(lax.axis_index("mp"), dp)
    for s, arrived_ref in enumerate(arrived_refs):
        out_ref[dp - 1 - lax.rem(mine + dp - s, dp)] = arrived_ref[...]


def share_kernel(rows, both_rank, got_ref, pieces_ref, *out_refs):
    dp, piece_rows, _ = pieces_ref.shape
    blocks = got_ref.shape[0]
    order = group_order(blocks)
    lows = [
        got_ref[order.index(block), rows:, :].astype(jnp.float32) for block in range(blocks)
    ]
    lows = jnp.concatenate(lows, axis=0).astype(jnp.bfloat16)
    columns = jnp.concatenate([pieces_ref[e] for e in range(dp)], axis=0)
    cuts = rows // CUT
    width = blocks * CUT
    stacked = [columns[:, cut * width:(cut + 1) * width] for cut in range(cuts)]
    product = jnp.dot(
        jnp.concatenate(stacked, axis=0), lows, preferred_element_type=jnp.float32
    )
    height = dp * piece_rows
    share = sum(
        product[cut * height:(cut + 1) * height, cut * both_rank:(cut + 1) * both_rank]
        for cut in range(cuts)
    )
    step = piece_rows // 2
    column = lax.broadcasted_iota(jnp.int32, (step, both_rank), 1)
    shares = []
    for e in range(dp):
        keys = share[e * piece_rows:e * piece_rows + step]
        values = share[e * piece_rows + step:(e + 1) * piece_rows]
        shares.append(adapter_factor * jnp.where(column < both_rank // 2, keys, values))
    mine = lax.axis_index("dp")
    for s, out_ref in enumerate(out_refs):
        turn = lax.rem(mine + s, dp)
        chosen = shares[0]
        for e in range(1, dp):
            chosen = jnp.where(turn == e, shares[e], chosen)
        out_ref[...] = chosen


def owner_kernel(got_ref, up_ref, key_ref, value_ref, low_grad_ref):
    rows = key_ref.shape[0]
    rank = up_ref.shape[0] // 2
    order = group_order(got_ref.shape[0])
    for pair in range(len(order) // 2):
        first = got_ref[order.index(2 * pair), :rows, :]
        second = got_ref[order.index(2 * pair + 1), :rows, :]
        columns = slice(2 * pair * HS, (2 * pair + 2) * HS)
        key_ref[:, columns] = jnp.concatenate([first[:, :HS], second[:, :HS]], axis=1)
        value_ref[:, columns] = jnp.concatenate([first[:, HS:], second[:, HS:]], axis=1)
    up = up_ref[...]
    from_key = dot(key_ref[...], up, NT)
    from_value = dot(value_ref[...], up, NT)
    column = lax.broadcasted_iota(jnp.int32, from_key.shape, 1)
    low_grad_ref[...] = adapter_factor * jnp.where(column < rank, from_key, from_value)


def local(dp, mp, query, kv_cache, out_grad, source_lengths, target_lengths, low_rank, adapter_up_matrix):
    tgt_count = query.shape[0]
    src_count = kv_cache.shape[0]
    rows, both_rank = low_rank.shape
    width = adapter_up_matrix.shape[1]
    step = HS // dp
    assert rows // CUT * both_rank == LANES
    vmem = pl.BlockSpec(memory_space=pltpu.VMEM)
    hbm = pl.BlockSpec(memory_space=pl.ANY)
    params = pltpu.CompilerParams(vmem_limit_bytes=48 * 1024 * 1024)
    whole_vmem = pltpu.CompilerParams(vmem_limit_bytes=60 * 1024 * 1024)

    query_t = query.T
    grad_t = out_grad.T
    query_grad_t, sent = pl.pallas_call(
        attention_kernel,
        out_shape=[
            jax.ShapeDtypeStruct((HS, tgt_count), jnp.bfloat16),
            jax.ShapeDtypeStruct((mp, rows + CUT, LANES), jnp.bfloat16),
        ],
        in_specs=[hbm] * 6,
        out_specs=[vmem] * 2,
        scratch_shapes=[
            pltpu.SMEM(source_lengths.shape, jnp.int32),
            pltpu.SMEM(target_lengths.shape, jnp.int32),
            pltpu.VMEM(query_t.shape, jnp.bfloat16),
            pltpu.VMEM(grad_t.shape, jnp.bfloat16),
            pltpu.VMEM(kv_cache.shape, jnp.bfloat16),
            pltpu.VMEM(low_rank.shape, jnp.bfloat16),
            pltpu.SemaphoreType.DMA((6,)),
        ],
        compiler_params=whole_vmem,
        name="attention_backward",
    )(source_lengths, target_lengths, query_t, grad_t, kv_cache, low_rank)

    route = [(h, h * dp % mp + dp - 1 - h * dp // mp) for h in range(mp)]
    pieces = pl.pallas_call(
        functools.partial(split_kernel, rows),
        out_shape=[jax.ShapeDtypeStruct((2 * step, src_count), jnp.bfloat16)] * dp,
        in_specs=[vmem],
        out_specs=[vmem] * dp,
        compiler_params=params,
        cost_estimate=pl.CostEstimate(flops=2 ** 36, bytes_accessed=2 ** 28, transcendentals=0),
        name="split_columns",
    )(lax.ppermute(sent, "mp", route))
    arrived = [pieces[0]]
    for s in range(1, dp):
        route = [(m, m - m % dp + (m + s) % dp) for m in range(mp)]
        arrived.append(lax.ppermute(pieces[s], "mp", route))
    ordered = pl.pallas_call(
        order_kernel,
        out_shape=jax.ShapeDtypeStruct((dp, 2 * step, src_count), jnp.bfloat16),
        in_specs=[vmem] * dp,
        out_specs=vmem,
        compiler_params=params,
        name="order_pieces",
    )(*arrived)

    got = lax.all_to_all(sent, "mp", 0, 0, axis_index_groups=[group_order(mp)], tiled=True)

    shares = pl.pallas_call(
        functools.partial(share_kernel, rows, both_rank),
        out_shape=[jax.ShapeDtypeStruct((step, both_rank), jnp.float32)] * dp,
        in_specs=[vmem] * 2,
        out_specs=[vmem] * dp,
        compiler_params=params,
        name="adapter_shares",
    )(got, ordered)
    up_grad = shares[0]
    for s in range(1, dp):
        route = [
            (d * mp + m, (d + s) % dp * mp + m - m % dp + (m + s) % dp)
            for d in range(dp) for m in range(mp)
        ]
        up_grad = up_grad + lax.ppermute(shares[s], ("dp", "mp"), route)

    key_gradient, value_grad, low_grad = pl.pallas_call(
        owner_kernel,
        out_shape=[
            jax.ShapeDtypeStruct((rows, width), jnp.bfloat16),
            jax.ShapeDtypeStruct((rows, width), jnp.bfloat16),
            jax.ShapeDtypeStruct((rows, both_rank), jnp.float32),
        ],
        in_specs=[vmem] * 2,
        out_specs=[vmem] * 3,
        compiler_params=params,
        name="owner_outputs",
    )(got, adapter_up_matrix)
    return query_grad_t.T, key_gradient, value_grad, low_grad, up_grad


def solution(mesh):
    in_specs = (
        P("dp", "mp"),
        P("dp", "mp"),
        P("dp", "mp"),
        P("dp", None),
        P("dp", None),
        P(("dp", "mp"), None),
        P(),
    )
    out_specs = (
        P("dp", "mp"),
        P(("dp", "mp"), None),
        P(("dp", "mp"), None),
        P(("dp", "mp"), None),
        P(("dp", "mp"), None),
    )
    body = functools.partial(local, mesh.shape["dp"], mesh.shape["mp"])
    return jax.shard_map(body, mesh=mesh, in_specs=in_specs, out_specs=out_specs, check_vma=False)
```

```python
import functools

import jax
import jax.numpy as jnp
from jax import lax
from jax.experimental import pallas as pl
from jax.experimental.pallas import tpu as pltpu
from jax.sharding import PartitionSpec as P

HS = 64
LANES = 128
CUT = 8

adapter_factor = 2.0

NT = (((1,), (1,)), ((), ()))
TN = (((0,), (0,)), ((), ()))


def dot(left, right, dims):
    return lax.dot_general(left, right, dims, preferred_element_type=jnp.float32)


def group_order(count):
    quarter = count // 4
    bits = quarter.bit_length() - 1
    assert count == 4 << bits
    turned = [sum(((i >> b) & 1) << (bits - 1 - b) for b in range(bits)) for i in range(quarter)]
    order = []
    for i, place in enumerate(reversed(turned)):
        order += [2 * quarter + place, 2 * i, 3 * quarter + place, 2 * i + 1]
    return order


def source_range(source_ref, target_ref, count):
    position = lax.broadcasted_iota(jnp.int32, (1, count), 1)
    first = jnp.zeros((1, count), jnp.int32)
    last = jnp.zeros((1, count), jnp.int32)
    target_start = jnp.int32(0)
    source_start = jnp.int32(0)
    for i in range(source_ref.shape[1]):
        source_end = source_start + source_ref[0, i]
        inside = position >= target_start
        first = jnp.where(inside, source_start, first)
        last = jnp.where(inside, source_end, last)
        target_start = target_start + target_ref[0, i]
        source_start = source_end
    return first, last


def attention_kernel(
    source_any, target_any, query_any, grad_any, kv_any, low_any, query_grad_ref, sent_ref,
    source_ref, target_ref, query_ref, grad_ref, kv_ref, low_ref, sems,
):
    pairs = [
        (kv_any, kv_ref), (query_any, query_ref), (grad_any, grad_ref),
        (source_any, source_ref), (target_any, target_ref), (low_any, low_ref),
    ]
    copies = [
        pltpu.make_async_copy(here, there, sems.at[i]) for i, (here, there) in enumerate(pairs)
    ]
    for copy in copies:
        copy.start()
    for copy in copies:
        copy.wait()
    tgt_count = query_ref.shape[1]
    both = kv_ref[...]
    query_t = query_ref[...]
    grad_t = grad_ref[...]
    blank = jnp.zeros_like(query_t)
    query_wide = jnp.concatenate([query_t, blank], axis=0)
    grad_wide = jnp.concatenate([blank, grad_t], axis=0)
    first, last = source_range(source_ref, target_ref, tgt_count)
    half = both.shape[0] // 2
    parts = [both[:half], both[half:]]
    scores = [jnp.dot(part, query_wide, preferred_element_type=jnp.float32) for part in parts]
    dprobs = [jnp.dot(part, grad_wide, preferred_element_type=jnp.float32) for part in parts]
    expos = []
    for i, score in enumerate(scores):
        position = i * half + lax.broadcasted_iota(jnp.int32, score.shape, 0)
        allowed = jnp.logical_and(position >= first, position < last)
        expos.append(jnp.where(allowed, jnp.exp(score), 0.0))
    inverse = 1.0 / sum(jnp.sum(expo, axis=0, keepdims=True) for expo in expos)
    weighted = sum(
        jnp.sum(expo * dprob, axis=0, keepdims=True) for expo, dprob in zip(expos, dprobs)
    )
    delta = weighted * inverse
    probs = [expo * inverse for expo in expos]
    dscores = [
        (prob * (dprob - delta)).astype(jnp.bfloat16) for prob, dprob in zip(probs, dprobs)
    ]
    both_low = jnp.concatenate([
        (dot(dscore, query_wide, NT) + dot(prob.astype(jnp.bfloat16), grad_wide, NT))
        .astype(jnp.bfloat16)
        for dscore, prob in zip(dscores, probs)
    ], axis=0)
    low = low_ref[...].astype(jnp.float32)
    rows = low.shape[0]
    blocks = sent_ref.shape[0]
    packed = jnp.concatenate([low[at:at + CUT] for at in range(0, rows, CUT)], axis=1)
    packed = packed.astype(jnp.bfloat16)
    for at, block in enumerate(group_order(blocks)):
        sent_ref[at, :rows, :] = both_low[block * rows:(block + 1) * rows]
        sent_ref[at, rows:, :] = packed

    query_grad = sum(dot(part, dscore, TN) for part, dscore in zip(parts, dscores))
    query_grad_ref[...] = query_grad[:HS].astype(jnp.bfloat16)


def split_kernel(rows, blocks_ref, *out_refs):
    dp = len(out_refs)
    step = HS // dp
    order = group_order(blocks_ref.shape[0])
    exact = [
        blocks_ref[order.index(block), :rows, :].astype(jnp.float32) for block in range(len(order))
    ]
    parts = [part[start:start + CUT] for start in range(0, rows, CUT) for part in exact]
    turned = jnp.concatenate(parts, axis=0).T
    pieces = []
    for j in range(dp):
        halves = [turned[j * step:(j + 1) * step], turned[HS + j * step:HS + (j + 1) * step]]
        pieces.append(jnp.concatenate(halves, axis=0))
    pack = lax.axis_index("dp")
    for s, out_ref in enumerate(out_refs):
        turn = lax.rem(2 * dp - 1 + s - pack, dp)
        chosen = pieces[0]
        for j in range(1, dp):
            chosen = jnp.where(turn == j, pieces[j], chosen)
        out_ref[...] = chosen.astype(jnp.bfloat16)


def order_kernel(*refs):
    *arrived_refs, out_ref = refs
    dp = len(arrived_refs)
    mine = lax.rem(lax.axis_index("mp"), dp)
    for s, arrived_ref in enumerate(arrived_refs):
        out_ref[dp - 1 - lax.rem(mine + dp - s, dp)] = arrived_ref[...]


def share_kernel(rows, both_rank, got_ref, pieces_ref, *out_refs):
    dp, piece_rows, _ = pieces_ref.shape
    blocks = got_ref.shape[0]
    order = group_order(blocks)
    lows = [
        got_ref[order.index(block), rows:, :].astype(jnp.float32) for block in range(blocks)
    ]
    lows = jnp.concatenate(lows, axis=0).astype(jnp.bfloat16)
    columns = jnp.concatenate([pieces_ref[e] for e in range(dp)], axis=0)
    cuts = rows // CUT
    width = blocks * CUT
    stacked = [columns[:, cut * width:(cut + 1) * width] for cut in range(cuts)]
    product = jnp.dot(
        jnp.concatenate(stacked, axis=0), lows, preferred_element_type=jnp.float32
    )
    height = dp * piece_rows
    share = sum(
        product[cut * height:(cut + 1) * height, cut * both_rank:(cut + 1) * both_rank]
        for cut in range(cuts)
    )
    step = piece_rows // 2
    column = lax.broadcasted_iota(jnp.int32, (step, both_rank), 1)
    shares = []
    for e in range(dp):
        keys = share[e * piece_rows:e * piece_rows + step]
        values = share[e * piece_rows + step:(e + 1) * piece_rows]
        shares.append(adapter_factor * jnp.where(column < both_rank // 2, keys, values))
    mine = lax.axis_index("dp")
    for s, out_ref in enumerate(out_refs):
        turn = lax.rem(mine + s, dp)
        chosen = shares[0]
        for e in range(1, dp):
            chosen = jnp.where(turn == e, shares[e], chosen)
        if s > 0:
            height = out_ref.shape[0]
            chosen = [chosen[at:at + height] for at in range(0, step, height)]
            chosen = jnp.concatenate(chosen, axis=1)
        out_ref[...] = chosen


def add_kernel(own_ref, *refs):
    *arrived_refs, out_ref = refs
    both_rank = own_ref.shape[1]
    total = own_ref[...]
    for arrived_ref in arrived_refs:
        arrived = arrived_ref[...]
        parts = [arrived[:, at:at + both_rank] for at in range(0, LANES, both_rank)]
        total += jnp.concatenate(parts, axis=0)
    out_ref[...] = total


def owner_kernel(got_ref, up_ref, key_ref, value_ref, low_grad_ref):
    rows = key_ref.shape[0]
    rank = up_ref.shape[0] // 2
    order = group_order(got_ref.shape[0])
    for pair in range(len(order) // 2):
        first = got_ref[order.index(2 * pair), :rows, :]
        second = got_ref[order.index(2 * pair + 1), :rows, :]
        columns = slice(2 * pair * HS, (2 * pair + 2) * HS)
        key_ref[:, columns] = jnp.concatenate([first[:, :HS], second[:, :HS]], axis=1)
        value_ref[:, columns] = jnp.concatenate([first[:, HS:], second[:, HS:]], axis=1)
    up = up_ref[...]
    from_key = dot(key_ref[...], up, NT)
    from_value = dot(value_ref[...], up, NT)
    column = lax.broadcasted_iota(jnp.int32, from_key.shape, 1)
    low_grad_ref[...] = adapter_factor * jnp.where(column < rank, from_key, from_value)


def local(dp, mp, query, kv_cache, out_grad, source_lengths, target_lengths, low_rank, adapter_up_matrix):
    tgt_count = query.shape[0]
    src_count = kv_cache.shape[0]
    rows, both_rank = low_rank.shape
    width = adapter_up_matrix.shape[1]
    step = HS // dp
    assert rows // CUT * both_rank == LANES
    vmem = pl.BlockSpec(memory_space=pltpu.VMEM)
    hbm = pl.BlockSpec(memory_space=pl.ANY)
    params = pltpu.CompilerParams(vmem_limit_bytes=48 * 1024 * 1024)
    whole_vmem = pltpu.CompilerParams(vmem_limit_bytes=60 * 1024 * 1024)

    query_t = query.T
    grad_t = out_grad.T
    query_grad_t, sent = pl.pallas_call(
        attention_kernel,
        out_shape=[
            jax.ShapeDtypeStruct((HS, tgt_count), jnp.bfloat16),
            jax.ShapeDtypeStruct((mp, rows + CUT, LANES), jnp.bfloat16),
        ],
        in_specs=[hbm] * 6,
        out_specs=[vmem] * 2,
        scratch_shapes=[
            pltpu.SMEM(source_lengths.shape, jnp.int32),
            pltpu.SMEM(target_lengths.shape, jnp.int32),
            pltpu.VMEM(query_t.shape, jnp.bfloat16),
            pltpu.VMEM(grad_t.shape, jnp.bfloat16),
            pltpu.VMEM(kv_cache.shape, jnp.bfloat16),
            pltpu.VMEM(low_rank.shape, jnp.bfloat16),
            pltpu.SemaphoreType.DMA((6,)),
        ],
        compiler_params=whole_vmem,
        name="attention_backward",
    )(source_lengths, target_lengths, query_t, grad_t, kv_cache, low_rank)

    route = [(h, h * dp % mp + dp - 1 - h * dp // mp) for h in range(mp)]
    pieces = pl.pallas_call(
        functools.partial(split_kernel, rows),
        out_shape=[jax.ShapeDtypeStruct((2 * step, src_count), jnp.bfloat16)] * dp,
        in_specs=[vmem],
        out_specs=[vmem] * dp,
        compiler_params=params,
        cost_estimate=pl.CostEstimate(flops=2 ** 36, bytes_accessed=2 ** 28, transcendentals=0),
        name="split_columns",
    )(lax.ppermute(sent, "mp", route))
    arrived = [pieces[0]]
    for s in range(1, dp):
        route = [(m, m - m % dp + (m + s) % dp) for m in range(mp)]
        arrived.append(lax.ppermute(pieces[s], "mp", route))
    ordered = pl.pallas_call(
        order_kernel,
        out_shape=jax.ShapeDtypeStruct((dp, 2 * step, src_count), jnp.bfloat16),
        in_specs=[vmem] * dp,
        out_specs=vmem,
        compiler_params=params,
        name="order_pieces",
    )(*arrived)

    got = lax.all_to_all(sent, "mp", 0, 0, axis_index_groups=[group_order(mp)], tiled=True)

    shares = pl.pallas_call(
        functools.partial(share_kernel, rows, both_rank),
        out_shape=[jax.ShapeDtypeStruct((step, both_rank), jnp.float32)]
        + [jax.ShapeDtypeStruct((step * both_rank // LANES, LANES), jnp.float32)] * (dp - 1),
        in_specs=[vmem] * 2,
        out_specs=[vmem] * dp,
        compiler_params=params,
        name="adapter_shares",
    )(got, ordered)
    crossed = []
    for s in range(1, dp):
        route = [
            (d * mp + m, (d + s) % dp * mp + m - m % dp + (m + s) % dp)
            for d in range(dp) for m in range(mp)
        ]
        crossed.append(lax.ppermute(shares[s], ("dp", "mp"), route))
    up_grad = pl.pallas_call(
        add_kernel,
        out_shape=jax.ShapeDtypeStruct((step, both_rank), jnp.float32),
        in_specs=[vmem] * dp,
        out_specs=vmem,
        compiler_params=params,
        name="add_shares",
    )(shares[0], *crossed)

    key_gradient, value_grad, low_grad = pl.pallas_call(
        owner_kernel,
        out_shape=[
            jax.ShapeDtypeStruct((rows, width), jnp.bfloat16),
            jax.ShapeDtypeStruct((rows, width), jnp.bfloat16),
            jax.ShapeDtypeStruct((rows, both_rank), jnp.float32),
        ],
        in_specs=[vmem] * 2,
        out_specs=[vmem] * 3,
        compiler_params=params,
        name="owner_outputs",
    )(got, adapter_up_matrix)
    return query_grad_t.T, key_gradient, value_grad, low_grad, up_grad


def solution(mesh):
    in_specs = (
        P("dp", "mp"),
        P("dp", "mp"),
        P("dp", "mp"),
        P("dp", None),
        P("dp", None),
        P(("dp", "mp"), None),
        P(),
    )
    out_specs = (
        P("dp", "mp"),
        P(("dp", "mp"), None),
        P(("dp", "mp"), None),
        P(("dp", "mp"), None),
        P(("dp", "mp"), None),
    )
    body = functools.partial(local, mesh.shape["dp"], mesh.shape["mp"])
    return jax.shard_map(body, mesh=mesh, in_specs=in_specs, out_specs=out_specs, check_vma=False)
```

```python
import functools

import jax
import jax.numpy as jnp
from jax import lax
from jax.experimental import pallas as pl
from jax.experimental.pallas import tpu as pltpu
from jax.sharding import PartitionSpec as P

HS = 64
LANES = 128
CUT = 8

adapter_factor = 2.0

NT = (((1,), (1,)), ((), ()))
TN = (((0,), (0,)), ((), ()))


def dot(left, right, dims):
    return lax.dot_general(left, right, dims, preferred_element_type=jnp.float32)


def group_order(count):
    quarter = count // 4
    bits = quarter.bit_length() - 1
    assert count == 4 << bits
    turned = [sum(((i >> b) & 1) << (bits - 1 - b) for b in range(bits)) for i in range(quarter)]
    order = []
    for i, place in enumerate(reversed(turned)):
        order += [2 * quarter + place, 2 * i, 2 * i + 1, 3 * quarter + place]
    return order


def source_range(source_ref, target_ref, count):
    position = lax.broadcasted_iota(jnp.int32, (1, count), 1)
    first = jnp.zeros((1, count), jnp.int32)
    last = jnp.zeros((1, count), jnp.int32)
    target_start = jnp.int32(0)
    source_start = jnp.int32(0)
    for i in range(source_ref.shape[1]):
        source_end = source_start + source_ref[0, i]
        inside = position >= target_start
        first = jnp.where(inside, source_start, first)
        last = jnp.where(inside, source_end, last)
        target_start = target_start + target_ref[0, i]
        source_start = source_end
    return first, last


def attention_kernel(
    source_any, target_any, query_any, grad_any, kv_any, low_any, query_grad_ref, sent_ref,
    source_ref, target_ref, query_ref, grad_ref, kv_ref, low_ref, sems,
):
    pairs = [
        (kv_any, kv_ref), (query_any, query_ref), (grad_any, grad_ref),
        (source_any, source_ref), (target_any, target_ref), (low_any, low_ref),
    ]
    copies = [
        pltpu.make_async_copy(here, there, sems.at[i]) for i, (here, there) in enumerate(pairs)
    ]
    for copy in copies:
        copy.start()
    for copy in copies:
        copy.wait()
    tgt_count = query_ref.shape[1]
    both = kv_ref[...]
    query_t = query_ref[...]
    grad_t = grad_ref[...]
    blank = jnp.zeros_like(query_t)
    query_wide = jnp.concatenate([query_t, blank], axis=0)
    grad_wide = jnp.concatenate([blank, grad_t], axis=0)
    first, last = source_range(source_ref, target_ref, tgt_count)
    half = both.shape[0] // 2
    parts = [both[:half], both[half:]]
    scores = [jnp.dot(part, query_wide, preferred_element_type=jnp.float32) for part in parts]
    dprobs = [jnp.dot(part, grad_wide, preferred_element_type=jnp.float32) for part in parts]
    expos = []
    for i, score in enumerate(scores):
        position = i * half + lax.broadcasted_iota(jnp.int32, score.shape, 0)
        allowed = jnp.logical_and(position >= first, position < last)
        expos.append(jnp.where(allowed, jnp.exp(score), 0.0))
    inverse = 1.0 / sum(jnp.sum(expo, axis=0, keepdims=True) for expo in expos)
    weighted = sum(
        jnp.sum(expo * dprob, axis=0, keepdims=True) for expo, dprob in zip(expos, dprobs)
    )
    delta = weighted * inverse
    probs = [expo * inverse for expo in expos]
    dscores = [
        (prob * (dprob - delta)).astype(jnp.bfloat16) for prob, dprob in zip(probs, dprobs)
    ]
    both_low = jnp.concatenate([
        (dot(dscore, query_wide, NT) + dot(prob.astype(jnp.bfloat16), grad_wide, NT))
        .astype(jnp.bfloat16)
        for dscore, prob in zip(dscores, probs)
    ], axis=0)
    low = low_ref[...].astype(jnp.float32)
    rows = low.shape[0]
    blocks = sent_ref.shape[0]
    packed = jnp.concatenate([low[at:at + CUT] for at in range(0, rows, CUT)], axis=1)
    packed = packed.astype(jnp.bfloat16)
    for at, block in enumerate(group_order(blocks)):
        sent_ref[at, :rows, :] = both_low[block * rows:(block + 1) * rows]
        sent_ref[at, rows:, :] = packed

    query_grad = sum(dot(part, dscore, TN) for part, dscore in zip(parts, dscores))
    query_grad_ref[...] = query_grad[:HS].astype(jnp.bfloat16)


def split_kernel(rows, blocks_ref, *out_refs):
    dp = len(out_refs)
    step = HS // dp
    order = group_order(blocks_ref.shape[0])
    exact = [
        blocks_ref[order.index(block), :rows, :].astype(jnp.float32) for block in range(len(order))
    ]
    parts = [part[start:start + CUT] for start in range(0, rows, CUT) for part in exact]
    turned = jnp.concatenate(parts, axis=0).T
    pieces = []
    for j in range(dp):
        halves = [turned[j * step:(j + 1) * step], turned[HS + j * step:HS + (j + 1) * step]]
        pieces.append(jnp.concatenate(halves, axis=0))
    pack = lax.axis_index("dp")
    for s, out_ref in enumerate(out_refs):
        turn = lax.rem(2 * dp - 1 + s - pack, dp)
        chosen = pieces[0]
        for j in range(1, dp):
            chosen = jnp.where(turn == j, pieces[j], chosen)
        out_ref[...] = chosen.astype(jnp.bfloat16)


def order_kernel(*refs):
    *arrived_refs, out_ref = refs
    dp = len(arrived_refs)
    mine = lax.rem(lax.axis_index("mp"), dp)
    for s, arrived_ref in enumerate(arrived_refs):
        out_ref[dp - 1 - lax.rem(mine + dp - s, dp)] = arrived_ref[...]


def share_kernel(rows, both_rank, got_ref, pieces_ref, *out_refs):
    dp, piece_rows, _ = pieces_ref.shape
    blocks = got_ref.shape[0]
    order = group_order(blocks)
    lows = [
        got_ref[order.index(block), rows:, :].astype(jnp.float32) for block in range(blocks)
    ]
    lows = jnp.concatenate(lows, axis=0).astype(jnp.bfloat16)
    columns = jnp.concatenate([pieces_ref[e] for e in range(dp)], axis=0)
    cuts = rows // CUT
    width = blocks * CUT
    stacked = [columns[:, cut * width:(cut + 1) * width] for cut in range(cuts)]
    product = jnp.dot(
        jnp.concatenate(stacked, axis=0), lows, preferred_element_type=jnp.float32
    )
    height = dp * piece_rows
    share = sum(
        product[cut * height:(cut + 1) * height, cut * both_rank:(cut + 1) * both_rank]
        for cut in range(cuts)
    )
    step = piece_rows // 2
    column = lax.broadcasted_iota(jnp.int32, (step, both_rank), 1)
    shares = []
    for e in range(dp):
        keys = share[e * piece_rows:e * piece_rows + step]
        values = share[e * piece_rows + step:(e + 1) * piece_rows]
        shares.append(adapter_factor * jnp.where(column < both_rank // 2, keys, values))
    mine = lax.axis_index("dp")
    for s, out_ref in enumerate(out_refs):
        turn = lax.rem(mine + s, dp)
        chosen = shares[0]
        for e in range(1, dp):
            chosen = jnp.where(turn == e, shares[e], chosen)
        out_ref[...] = chosen


def owner_kernel(got_ref, up_ref, key_ref, value_ref, low_grad_ref):
    rows = key_ref.shape[0]
    rank = up_ref.shape[0] // 2
    order = group_order(got_ref.shape[0])
    for pair in range(len(order) // 2):
        first = got_ref[order.index(2 * pair), :rows, :]
        second = got_ref[order.index(2 * pair + 1), :rows, :]
        columns = slice(2 * pair * HS, (2 * pair + 2) * HS)
        key_ref[:, columns] = jnp.concatenate([first[:, :HS], second[:, :HS]], axis=1)
        value_ref[:, columns] = jnp.concatenate([first[:, HS:], second[:, HS:]], axis=1)
    up = up_ref[...]
    from_key = dot(key_ref[...], up, NT)
    from_value = dot(value_ref[...], up, NT)
    column = lax.broadcasted_iota(jnp.int32, from_key.shape, 1)
    low_grad_ref[...] = adapter_factor * jnp.where(column < rank, from_key, from_value)


def local(dp, mp, query, kv_cache, out_grad, source_lengths, target_lengths, low_rank, adapter_up_matrix):
    tgt_count = query.shape[0]
    src_count = kv_cache.shape[0]
    rows, both_rank = low_rank.shape
    width = adapter_up_matrix.shape[1]
    step = HS // dp
    assert rows // CUT * both_rank == LANES
    vmem = pl.BlockSpec(memory_space=pltpu.VMEM)
    hbm = pl.BlockSpec(memory_space=pl.ANY)
    params = pltpu.CompilerParams(vmem_limit_bytes=48 * 1024 * 1024)
    whole_vmem = pltpu.CompilerParams(vmem_limit_bytes=60 * 1024 * 1024)

    query_t = query.T
    grad_t = out_grad.T
    query_grad_t, sent = pl.pallas_call(
        attention_kernel,
        out_shape=[
            jax.ShapeDtypeStruct((HS, tgt_count), jnp.bfloat16),
            jax.ShapeDtypeStruct((mp, rows + CUT, LANES), jnp.bfloat16),
        ],
        in_specs=[hbm] * 6,
        out_specs=[vmem] * 2,
        scratch_shapes=[
            pltpu.SMEM(source_lengths.shape, jnp.int32),
            pltpu.SMEM(target_lengths.shape, jnp.int32),
            pltpu.VMEM(query_t.shape, jnp.bfloat16),
            pltpu.VMEM(grad_t.shape, jnp.bfloat16),
            pltpu.VMEM(kv_cache.shape, jnp.bfloat16),
            pltpu.VMEM(low_rank.shape, jnp.bfloat16),
            pltpu.SemaphoreType.DMA((6,)),
        ],
        compiler_params=whole_vmem,
        name="attention_backward",
    )(source_lengths, target_lengths, query_t, grad_t, kv_cache, low_rank)

    route = [(h, h * dp % mp + dp - 1 - h * dp // mp) for h in range(mp)]
    pieces = pl.pallas_call(
        functools.partial(split_kernel, rows),
        out_shape=[jax.ShapeDtypeStruct((2 * step, src_count), jnp.bfloat16)] * dp,
        in_specs=[vmem],
        out_specs=[vmem] * dp,
        compiler_params=params,
        cost_estimate=pl.CostEstimate(flops=2 ** 36, bytes_accessed=2 ** 28, transcendentals=0),
        name="split_columns",
    )(lax.ppermute(sent, "mp", route))
    arrived = [pieces[0]]
    for s in range(1, dp):
        route = [(m, m - m % dp + (m + s) % dp) for m in range(mp)]
        arrived.append(lax.ppermute(pieces[s], "mp", route))
    ordered = pl.pallas_call(
        order_kernel,
        out_shape=jax.ShapeDtypeStruct((dp, 2 * step, src_count), jnp.bfloat16),
        in_specs=[vmem] * dp,
        out_specs=vmem,
        compiler_params=params,
        name="order_pieces",
    )(*arrived)

    got = lax.all_to_all(sent, "mp", 0, 0, axis_index_groups=[group_order(mp)], tiled=True)

    shares = pl.pallas_call(
        functools.partial(share_kernel, rows, both_rank),
        out_shape=[jax.ShapeDtypeStruct((step, both_rank), jnp.float32)] * dp,
        in_specs=[vmem] * 2,
        out_specs=[vmem] * dp,
        compiler_params=params,
        name="adapter_shares",
    )(got, ordered)
    up_grad = shares[0]
    for s in range(1, dp):
        route = [
            (d * mp + m, (d + s) % dp * mp + m - m % dp + (m + s) % dp)
            for d in range(dp) for m in range(mp)
        ]
        up_grad = up_grad + lax.ppermute(shares[s], ("dp", "mp"), route)

    key_gradient, value_grad, low_grad = pl.pallas_call(
        owner_kernel,
        out_shape=[
            jax.ShapeDtypeStruct((rows, width), jnp.bfloat16),
            jax.ShapeDtypeStruct((rows, width), jnp.bfloat16),
            jax.ShapeDtypeStruct((rows, both_rank), jnp.float32),
        ],
        in_specs=[vmem] * 2,
        out_specs=[vmem] * 3,
        compiler_params=params,
        name="owner_outputs",
    )(got, adapter_up_matrix)
    return query_grad_t.T, key_gradient, value_grad, low_grad, up_grad


def solution(mesh):
    in_specs = (
        P("dp", "mp"),
        P("dp", "mp"),
        P("dp", "mp"),
        P("dp", None),
        P("dp", None),
        P(("dp", "mp"), None),
        P(),
    )
    out_specs = (
        P("dp", "mp"),
        P(("dp", "mp"), None),
        P(("dp", "mp"), None),
        P(("dp", "mp"), None),
        P(("dp", "mp"), None),
    )
    body = functools.partial(local, mesh.shape["dp"], mesh.shape["mp"])
    return jax.shard_map(body, mesh=mesh, in_specs=in_specs, out_specs=out_specs, check_vma=False)
```

```python
import functools

import jax
import jax.numpy as jnp
from jax import lax
from jax.experimental import pallas as pl
from jax.experimental.pallas import tpu as pltpu
from jax.sharding import PartitionSpec as P

HS = 64
LANES = 128
CUT = 8

adapter_factor = 2.0

NT = (((1,), (1,)), ((), ()))
TN = (((0,), (0,)), ((), ()))


def dot(left, right, dims):
    return lax.dot_general(left, right, dims, preferred_element_type=jnp.float32)


def group_order(count):
    quarter = count // 4
    bits = quarter.bit_length() - 1
    assert count == 4 << bits
    turned = [sum(((i >> b) & 1) << (bits - 1 - b) for b in range(bits)) for i in range(quarter)]
    order = []
    for i, place in enumerate(reversed(turned)):
        lower = 4 * (i // 2) + i % 2
        order += [2 * quarter + place, lower, 3 * quarter + place, lower + 2]
    return order


def source_range(source_ref, target_ref, count):
    position = lax.broadcasted_iota(jnp.int32, (1, count), 1)
    first = jnp.zeros((1, count), jnp.int32)
    last = jnp.zeros((1, count), jnp.int32)
    target_start = jnp.int32(0)
    source_start = jnp.int32(0)
    for i in range(source_ref.shape[1]):
        source_end = source_start + source_ref[0, i]
        inside = position >= target_start
        first = jnp.where(inside, source_start, first)
        last = jnp.where(inside, source_end, last)
        target_start = target_start + target_ref[0, i]
        source_start = source_end
    return first, last


def attention_kernel(
    source_any, target_any, query_any, grad_any, kv_any, low_any, query_grad_ref, sent_ref,
    source_ref, target_ref, query_ref, grad_ref, kv_ref, low_ref, sems,
):
    pairs = [
        (kv_any, kv_ref), (query_any, query_ref), (grad_any, grad_ref),
        (source_any, source_ref), (target_any, target_ref), (low_any, low_ref),
    ]
    copies = [
        pltpu.make_async_copy(here, there, sems.at[i]) for i, (here, there) in enumerate(pairs)
    ]
    for copy in copies:
        copy.start()
    for copy in copies:
        copy.wait()
    tgt_count = query_ref.shape[1]
    both = kv_ref[...]
    query_t = query_ref[...]
    grad_t = grad_ref[...]
    blank = jnp.zeros_like(query_t)
    query_wide = jnp.concatenate([query_t, blank], axis=0)
    grad_wide = jnp.concatenate([blank, grad_t], axis=0)
    first, last = source_range(source_ref, target_ref, tgt_count)
    half = both.shape[0] // 2
    parts = [both[:half], both[half:]]
    scores = [jnp.dot(part, query_wide, preferred_element_type=jnp.float32) for part in parts]
    dprobs = [jnp.dot(part, grad_wide, preferred_element_type=jnp.float32) for part in parts]
    expos = []
    for i, score in enumerate(scores):
        position = i * half + lax.broadcasted_iota(jnp.int32, score.shape, 0)
        allowed = jnp.logical_and(position >= first, position < last)
        expos.append(jnp.where(allowed, jnp.exp(score), 0.0))
    inverse = 1.0 / sum(jnp.sum(expo, axis=0, keepdims=True) for expo in expos)
    weighted = sum(
        jnp.sum(expo * dprob, axis=0, keepdims=True) for expo, dprob in zip(expos, dprobs)
    )
    delta = weighted * inverse
    probs = [expo * inverse for expo in expos]
    dscores = [
        (prob * (dprob - delta)).astype(jnp.bfloat16) for prob, dprob in zip(probs, dprobs)
    ]
    both_low = jnp.concatenate([
        (dot(dscore, query_wide, NT) + dot(prob.astype(jnp.bfloat16), grad_wide, NT))
        .astype(jnp.bfloat16)
        for dscore, prob in zip(dscores, probs)
    ], axis=0)
    low = low_ref[...].astype(jnp.float32)
    rows = low.shape[0]
    blocks = sent_ref.shape[0]
    packed = jnp.concatenate([low[at:at + CUT] for at in range(0, rows, CUT)], axis=1)
    packed = packed.astype(jnp.bfloat16)
    for at, block in enumerate(group_order(blocks)):
        sent_ref[at, :rows, :] = both_low[block * rows:(block + 1) * rows]
        sent_ref[at, rows:, :] = packed

    query_grad = sum(dot(part, dscore, TN) for part, dscore in zip(parts, dscores))
    query_grad_ref[...] = query_grad[:HS].astype(jnp.bfloat16)


def split_kernel(rows, blocks_ref, *out_refs):
    dp = len(out_refs)
    step = HS // dp
    order = group_order(blocks_ref.shape[0])
    exact = [
        blocks_ref[order.index(block), :rows, :].astype(jnp.float32) for block in range(len(order))
    ]
    parts = [part[start:start + CUT] for start in range(0, rows, CUT) for part in exact]
    turned = jnp.concatenate(parts, axis=0).T
    pieces = []
    for j in range(dp):
        halves = [turned[j * step:(j + 1) * step], turned[HS + j * step:HS + (j + 1) * step]]
        pieces.append(jnp.concatenate(halves, axis=0))
    pack = lax.axis_index("dp")
    for s, out_ref in enumerate(out_refs):
        turn = lax.rem(2 * dp - 1 + s - pack, dp)
        chosen = pieces[0]
        for j in range(1, dp):
            chosen = jnp.where(turn == j, pieces[j], chosen)
        out_ref[...] = chosen.astype(jnp.bfloat16)


def order_kernel(*refs):
    *arrived_refs, out_ref = refs
    dp = len(arrived_refs)
    mine = lax.rem(lax.axis_index("mp"), dp)
    for s, arrived_ref in enumerate(arrived_refs):
        out_ref[dp - 1 - lax.rem(mine + dp - s, dp)] = arrived_ref[...]


def share_kernel(rows, both_rank, got_ref, pieces_ref, *out_refs):
    dp, piece_rows, _ = pieces_ref.shape
    blocks = got_ref.shape[0]
    order = group_order(blocks)
    lows = [
        got_ref[order.index(block), rows:, :].astype(jnp.float32) for block in range(blocks)
    ]
    lows = jnp.concatenate(lows, axis=0).astype(jnp.bfloat16)
    columns = jnp.concatenate([pieces_ref[e] for e in range(dp)], axis=0)
    cuts = rows // CUT
    width = blocks * CUT
    stacked = [columns[:, cut * width:(cut + 1) * width] for cut in range(cuts)]
    product = jnp.dot(
        jnp.concatenate(stacked, axis=0), lows, preferred_element_type=jnp.float32
    )
    height = dp * piece_rows
    share = sum(
        product[cut * height:(cut + 1) * height, cut * both_rank:(cut + 1) * both_rank]
        for cut in range(cuts)
    )
    step = piece_rows // 2
    column = lax.broadcasted_iota(jnp.int32, (step, both_rank), 1)
    shares = []
    for e in range(dp):
        keys = share[e * piece_rows:e * piece_rows + step]
        values = share[e * piece_rows + step:(e + 1) * piece_rows]
        shares.append(adapter_factor * jnp.where(column < both_rank // 2, keys, values))
    mine = lax.axis_index("dp")
    for s, out_ref in enumerate(out_refs):
        turn = lax.rem(mine + s, dp)
        chosen = shares[0]
        for e in range(1, dp):
            chosen = jnp.where(turn == e, shares[e], chosen)
        out_ref[...] = chosen


def owner_kernel(got_ref, up_ref, key_ref, value_ref, low_grad_ref):
    rows = key_ref.shape[0]
    rank = up_ref.shape[0] // 2
    order = group_order(got_ref.shape[0])
    for pair in range(len(order) // 2):
        first = got_ref[order.index(2 * pair), :rows, :]
        second = got_ref[order.index(2 * pair + 1), :rows, :]
        columns = slice(2 * pair * HS, (2 * pair + 2) * HS)
        key_ref[:, columns] = jnp.concatenate([first[:, :HS], second[:, :HS]], axis=1)
        value_ref[:, columns] = jnp.concatenate([first[:, HS:], second[:, HS:]], axis=1)
    up = up_ref[...]
    from_key = dot(key_ref[...], up, NT)
    from_value = dot(value_ref[...], up, NT)
    column = lax.broadcasted_iota(jnp.int32, from_key.shape, 1)
    low_grad_ref[...] = adapter_factor * jnp.where(column < rank, from_key, from_value)


def local(dp, mp, query, kv_cache, out_grad, source_lengths, target_lengths, low_rank, adapter_up_matrix):
    tgt_count = query.shape[0]
    src_count = kv_cache.shape[0]
    rows, both_rank = low_rank.shape
    width = adapter_up_matrix.shape[1]
    step = HS // dp
    assert rows // CUT * both_rank == LANES
    vmem = pl.BlockSpec(memory_space=pltpu.VMEM)
    hbm = pl.BlockSpec(memory_space=pl.ANY)
    params = pltpu.CompilerParams(vmem_limit_bytes=48 * 1024 * 1024)
    whole_vmem = pltpu.CompilerParams(vmem_limit_bytes=60 * 1024 * 1024)

    query_t = query.T
    grad_t = out_grad.T
    query_grad_t, sent = pl.pallas_call(
        attention_kernel,
        out_shape=[
            jax.ShapeDtypeStruct((HS, tgt_count), jnp.bfloat16),
            jax.ShapeDtypeStruct((mp, rows + CUT, LANES), jnp.bfloat16),
        ],
        in_specs=[hbm] * 6,
        out_specs=[vmem] * 2,
        scratch_shapes=[
            pltpu.SMEM(source_lengths.shape, jnp.int32),
            pltpu.SMEM(target_lengths.shape, jnp.int32),
            pltpu.VMEM(query_t.shape, jnp.bfloat16),
            pltpu.VMEM(grad_t.shape, jnp.bfloat16),
            pltpu.VMEM(kv_cache.shape, jnp.bfloat16),
            pltpu.VMEM(low_rank.shape, jnp.bfloat16),
            pltpu.SemaphoreType.DMA((6,)),
        ],
        compiler_params=whole_vmem,
        name="attention_backward",
    )(source_lengths, target_lengths, query_t, grad_t, kv_cache, low_rank)

    route = [(h, h * dp % mp + dp - 1 - h * dp // mp) for h in range(mp)]
    pieces = pl.pallas_call(
        functools.partial(split_kernel, rows),
        out_shape=[jax.ShapeDtypeStruct((2 * step, src_count), jnp.bfloat16)] * dp,
        in_specs=[vmem],
        out_specs=[vmem] * dp,
        compiler_params=params,
        cost_estimate=pl.CostEstimate(flops=2 ** 36, bytes_accessed=2 ** 28, transcendentals=0),
        name="split_columns",
    )(lax.ppermute(sent, "mp", route))
    arrived = [pieces[0]]
    for s in range(1, dp):
        route = [(m, m - m % dp + (m + s) % dp) for m in range(mp)]
        arrived.append(lax.ppermute(pieces[s], "mp", route))
    ordered = pl.pallas_call(
        order_kernel,
        out_shape=jax.ShapeDtypeStruct((dp, 2 * step, src_count), jnp.bfloat16),
        in_specs=[vmem] * dp,
        out_specs=vmem,
        compiler_params=params,
        name="order_pieces",
    )(*arrived)

    got = lax.all_to_all(sent, "mp", 0, 0, axis_index_groups=[group_order(mp)], tiled=True)

    shares = pl.pallas_call(
        functools.partial(share_kernel, rows, both_rank),
        out_shape=[jax.ShapeDtypeStruct((step, both_rank), jnp.float32)] * dp,
        in_specs=[vmem] * 2,
        out_specs=[vmem] * dp,
        compiler_params=params,
        name="adapter_shares",
    )(got, ordered)
    up_grad = shares[0]
    for s in range(1, dp):
        route = [
            (d * mp + m, (d + s) % dp * mp + m - m % dp + (m + s) % dp)
            for d in range(dp) for m in range(mp)
        ]
        up_grad = up_grad + lax.ppermute(shares[s], ("dp", "mp"), route)

    key_gradient, value_grad, low_grad = pl.pallas_call(
        owner_kernel,
        out_shape=[
            jax.ShapeDtypeStruct((rows, width), jnp.bfloat16),
            jax.ShapeDtypeStruct((rows, width), jnp.bfloat16),
            jax.ShapeDtypeStruct((rows, both_rank), jnp.float32),
        ],
        in_specs=[vmem] * 2,
        out_specs=[vmem] * 3,
        compiler_params=params,
        name="owner_outputs",
    )(got, adapter_up_matrix)
    return query_grad_t.T, key_gradient, value_grad, low_grad, up_grad


def solution(mesh):
    in_specs = (
        P("dp", "mp"),
        P("dp", "mp"),
        P("dp", "mp"),
        P("dp", None),
        P("dp", None),
        P(("dp", "mp"), None),
        P(),
    )
    out_specs = (
        P("dp", "mp"),
        P(("dp", "mp"), None),
        P(("dp", "mp"), None),
        P(("dp", "mp"), None),
        P(("dp", "mp"), None),
    )
    body = functools.partial(local, mesh.shape["dp"], mesh.shape["mp"])
    return jax.shard_map(body, mesh=mesh, in_specs=in_specs, out_specs=out_specs, check_vma=False)
```
